32 devices in a mesh: rows: 4 (over y, core), chan: 8 (over z, x).
Axes of the slice: x: 2, y: 2, z: 4, core: 2. Of those that a mesh axis runs over, the one named last changes fastest.
Arguments:
- tokens: float32 [16384, 1024], P(('rows', 'chan')), may hold values from -6 to 6
- segments: int32 [16384], P('rows'), may hold values from 0 to 32, as said below
- gelu_weight: bfloat16 [1024, 1536], P(None, 'chan'), may hold values from -0.1875 to 0.1875
- gelu_bias: bfloat16 [1536], P('chan'), may hold values from -3 to 3
- input_weight: bfloat16 [1024, 1536], P(None, 'chan'), may hold values from -0.1875 to 0.1875
- input_bias: bfloat16 [1536], P('chan'), may hold values from -3 to 3
- conv_taps: bfloat16 [4, 1536], P(None, 'chan'), may hold values from -3 to 3
- conv_bias: bfloat16 [1536], P('chan'), may hold values from -2 to 2
- decay_gate: bfloat16 [1536, 192], P('chan'), may hold values from -0.4375 to 0.4375
- decay_bias: bfloat16 [1536], P('chan'), may hold values from -3 to 3
- input_gate: bfloat16 [1536, 192], P('chan'), may hold values from -0.4375 to 0.4375
- ingate_bias: bfloat16 [1536], P('chan'), may hold values from -3 to 3
- decay_param: bfloat16 [1536], P('chan'), may hold values from -8 to -1
- out_weight: bfloat16 [1536, 1024], P('chan'), may hold values from -0.3125 to 0.3125
- mixer_gain: float32 [1024], replicated, may hold values from 0.5 to 1.5
- gate_weight: bfloat16 [1024, 3072], P(None, 'chan'), may hold values from -0.1875 to 0.1875
- up_weight: bfloat16 [1024, 3072], P(None, 'chan'), may hold values from -0.1875 to 0.1875
- down_weight: bfloat16 [3072, 1024], P('chan'), may hold values from -0.21875 to 0.21875
- feed_gain: float32 [1024], replicated, may hold values from 0.5 to 1.5
- cotangent: float32 [16384, 1024], P(('rows', 'chan'))
Outputs:
- block_output: float32 [16384, 1024], P(('rows', 'chan'))
- tokens_grad: float32 [16384, 1024], P(('rows', 'chan'))
- gelu_weight_grad: float32 [1024, 1536], P(None, 'chan')
- gelu_bias_grad: float32 [1536], P('chan')
- input_weight_grad: float32 [1024, 1536], P(None, 'chan')
- input_bias_grad: float32 [1536], P('chan')
- conv_taps_grad: float32 [4, 1536], P(None, 'chan')
- conv_bias_grad: float32 [1536], P('chan')
- decay_gate_grad: float32 [1536, 192], P('chan')
- decay_bias_grad: float32 [1536], P('chan')
- input_gate_grad: float32 [1536, 192], P('chan')
- ingate_bias_grad: float32 [1536], P('chan')
- decay_param_grad: float32 [1536], P('chan')
- out_weight_grad: float32 [1536, 1024], P('chan')
- mixer_gain_grad: float32 [1024], replicated
- gate_weight_grad: float32 [1024, 3072], P(None, 'chan')
- up_weight_grad: float32 [1024, 3072], P(None, 'chan')
- down_weight_grad: float32 [3072, 1024], P('chan')
- feed_gain_grad: float32 [1024], replicated
- mean_decay: float32 [1536], P('chan')
The draws below stay inside these ranges and needn't reach their ends.
Inputs may be any that keep to these rules, and one draw needn't show every extreme that they name: Each packed row of 4096 tokens holds 8 segments, the first beginning at the row's first token; numbers rise by one at each new segment, across rows too, and are 0 on a run of padding of at most 128 tokens at the row's end, which every row but the last has. The first 6 segments end within the row's first 512 tokens and the last one begins within its last 512 tokens.
All inputs are finite; a program needn't handle non-finite values.
Results may differ from the reference program's by a relative error of at most 0.0085.
Values may be sent and summed in bfloat16 or wider, within the bound.
No kernel may reach another device: no remote copies, remote signals or barrier semaphores. Data moves between devices by JAX's collectives and lax.ppermute only.
A program may use at most 448 MiB of HBM per device.

```python
import jax
import jax.numpy as jnp
from jax import lax

MODEL_WIDTH = 1024
R = 1536
FF = 3072
CONV = 4
BW = 192
SEGS = 8
TOK_DEV = 512
TOK_ROW = 4096
PACKED_ROW_LENGTH = 4096
TOTAL_TOKENS = 16384


def draw_segments(key, part):
    key = jax.random.fold_in(key, 11)
    first, second_half, third = jax.random.split(key, 3)
    packed_row_count = TOTAL_TOKENS // PACKED_ROW_LENGTH
    row_keys = jax.random.split(first, packed_row_count)
    picked = jax.vmap(lambda k: jax.random.permutation(k, TOK_DEV - 1) + 1)(row_keys)[:, :SEGS - 2]
    last_break = jax.random.randint(third, (packed_row_count,), PACKED_ROW_LENGTH - TOK_DEV + 1, PACKED_ROW_LENGTH - TOK_DEV // 2 + 1)
    token_position = jnp.arange(PACKED_ROW_LENGTH, dtype=jnp.int32)
    breaks = jnp.any(token_position[None, :, None] == picked[:, None, :], axis=-1) | (token_position == 0)[None, :] | (token_position[None, :] == last_break[:, None])
    numbers = jnp.cumsum(breaks.reshape(TOTAL_TOKENS).astype(jnp.int32))
    padding_length = jax.random.randint(second_half, (packed_row_count,), 1, TOK_DEV // 4 + 1)
    row_index = jnp.arange(packed_row_count, dtype=jnp.int32)
    padding_length = jnp.where(row_index == packed_row_count - 1, 0, padding_length)
    padded_tokens = token_position[None, :] >= PACKED_ROW_LENGTH - padding_length[:, None]
    return jnp.where(padded_tokens.reshape(TOTAL_TOKENS), 0, numbers).astype(jnp.int32)


def draw_cotangent(key, part):
    key = jax.random.fold_in(key, 23)
    first = jax.random.fold_in(key, 0)
    place = (jnp.arange(TOTAL_TOKENS) % TOK_ROW).astype(jnp.float32)
    factor = (0.5 + place / TOK_ROW)[:, None]
    values = jax.random.normal(first, (TOTAL_TOKENS, MODEL_WIDTH), jnp.float32)
    return (values * factor).astype(jnp.float32)


def level_of(own_key, extent, cuts, low, largest):
    def one(dim, shards_of):
        steps = jax.random.uniform(jax.random.fold_in(jax.random.fold_in(own_key, 6), dim), (shards_of,), jnp.float32, low / len(cuts), largest / len(cuts))
        return jnp.repeat(jnp.exp(steps), extent[dim] // shards_of).reshape((-1,) + (1,) * (len(extent) - dim - 1))

    level = one(*cuts[0])
    for cut in cuts[1:]:
        level = level * one(*cut)
    return level


def centred(own_key, shape, deviation, reach, pieces=(), kind=jnp.bfloat16):
    result = jax.random.normal(own_key, shape, jnp.float32) * deviation
    if len(pieces) > 0:
        result = level_of(own_key, shape, pieces, -0.22, 0.18) * result
    return jnp.clip(result, min=-reach, max=reach).astype(kind)


def setup_inputs(seed: int = 0) -> dict:
    streams_of = jax.random.split(jax.random.key(seed), 21)
    return {
        "tokens": centred(streams_of[0], (TOTAL_TOKENS, MODEL_WIDTH), 1.0, 6.0, ((0, 32),), jnp.float32),
        "segments": draw_segments(jax.random.fold_in(streams_of[20], 71), 0),
        "gelu_weight": centred(streams_of[2], (MODEL_WIDTH, R), MODEL_WIDTH ** -0.5, 0.1875, ((1, 8),)),
        "gelu_bias": centred(streams_of[3], (R,), 0.5, 3.0, ((0, 8),)),
        "input_weight": centred(streams_of[4], (MODEL_WIDTH, R), MODEL_WIDTH ** -0.5, 0.1875, ((1, 8),)),
        "input_bias": centred(streams_of[5], (R,), 0.5, 3.0, ((0, 8),)),
        "conv_taps": centred(streams_of[6], (CONV, R), 0.5, 3.0, ((1, 8),)),
        "conv_bias": centred(streams_of[7], (R,), 0.3, 2.0, ((0, 8),)),
        "decay_gate": centred(streams_of[8], (R, BW), BW ** -0.5, 0.4375, ((0, 8),)),
        "decay_bias": centred(streams_of[9], (R,), 0.5, 3.0, ((0, 8),)),
        "input_gate": centred(streams_of[10], (R, BW), BW ** -0.5, 0.4375, ((0, 8),)),
        "ingate_bias": centred(streams_of[11], (R,), 0.5, 3.0, ((0, 8),)),
        "decay_param": jnp.clip(-8.0 + 7.0 * jax.random.uniform(streams_of[12], (R,), jnp.float32) ** level_of(streams_of[12], (R,), ((0, 8),), -0.2, 0.2), -8.0, -1.0).astype(jnp.bfloat16),
        "out_weight": centred(streams_of[13], (R, MODEL_WIDTH), (R // 4) ** -0.5, 0.3125, ((0, 8),)),
        "mixer_gain": jnp.clip(1.0 + 0.1 * jax.random.normal(streams_of[14], (MODEL_WIDTH,), jnp.float32), 0.5, 1.5),
        "gate_weight": centred(streams_of[15], (MODEL_WIDTH, FF), MODEL_WIDTH ** -0.5, 0.1875, ((1, 8),)),
        "up_weight": centred(streams_of[16], (MODEL_WIDTH, FF), MODEL_WIDTH ** -0.5, 0.1875, ((1, 8),)),
        "down_weight": centred(streams_of[17], (FF, MODEL_WIDTH), (FF // 4) ** -0.5, 0.21875, ((0, 8),)),
        "feed_gain": jnp.clip(1.0 + 0.1 * jax.random.normal(streams_of[18], (MODEL_WIDTH,), jnp.float32), 0.5, 1.5),
        "cotangent": draw_cotangent(jax.random.fold_in(streams_of[20], 71), 0),
    }


@jax.custom_vjp
def low(v):
    return lax.optimization_barrier(v.astype(jnp.bfloat16)).astype(jnp.float32)

@jax.custom_vjp
def low_back(v):
    return v

def low_keep(v):
    return (low(v), None)

def low_pass(kept, grad):
    return (grad,)

def back_keep(v):
    return (v, None)

def back_low(kept, grad):
    return (low(grad),)
low.defvjp(low_keep, low_pass)
low_back.defvjp(back_keep, back_low)

def matmul(left, right):
    return jnp.dot(left, right, precision=lax.Precision.HIGHEST, preferred_element_type=jnp.float32)

def rms_norm(values, gain):
    return values * lax.rsqrt(lax.optimization_barrier(jnp.mean(values * values, axis=-1, keepdims=True)) + 1e-06) * gain

def combine_steps(earlier, later):
    return (earlier[0] * later[0], later[0] * earlier[1] + later[1])

def block_gate(conv, matrix, bias):
    length = conv.shape[0]
    channels = conv.shape[1]
    width = matrix.shape[1]
    blocks = matrix.shape[0] // width
    stacked = matrix.reshape(blocks, width, width)
    product = jnp.einsum('tnb,nbc->tnc', conv.reshape(length, blocks, width), stacked, precision=lax.Precision.HIGHEST)
    return jax.nn.sigmoid(product.reshape(length, channels) + bias)

def recurrent_mixer(branch_y, branch_u, segments, conv_taps, conv_bias, decay_gate, decay_bias, input_gate, ingate_bias, decay_param):
    channels = branch_u.shape[1]
    before = jnp.concatenate([jnp.full((1,), -1, jnp.int32), segments[:-1]])
    start = (segments != before)[:, None]
    conv = conv_bias + conv_taps[0] * branch_u
    for shift in range(1, conv_taps.shape[0]):
        moved = jnp.concatenate([jnp.zeros((shift, channels), jnp.float32), branch_u[:-shift]], 0)
        moved_seg = jnp.concatenate([jnp.full((shift,), -1, jnp.int32), segments[:-shift]])
        same = (segments == moved_seg)[:, None]
        conv = conv + jnp.where(same, conv_taps[shift] * moved, 0.0)
    conv = jnp.where((segments != 0)[:, None], conv, 0.0)
    rgate = block_gate(conv, decay_gate, decay_bias)
    igate = block_gate(conv, input_gate, ingate_bias)
    decay = jnp.exp(-8.0 * rgate * jax.nn.softplus(decay_param))
    scale = jnp.where(start, 1.0, jnp.sqrt(1.0 - decay * decay + 0.01))
    inject = conv * igate * scale
    carried = jnp.where(start, 0.0, decay)
    factors, states = lax.associative_scan(combine_steps, (carried, inject), axis=0)
    return (states * jax.nn.gelu(branch_y), lax.optimization_barrier(jnp.sum(decay, 0)))

def block_group(params, group_tokens, segments_per_group):
    gelu_weight, gelu_bias, input_weight, input_bias, conv_taps, conv_bias, decay_gate, decay_bias, input_gate, ingate_bias, decay_param, out_weight, mixer_gain, gate_weight, up_weight, down_weight, feed_gain = params
    normed = low(rms_norm(group_tokens, mixer_gain))
    branch_y = low_back(matmul(normed, gelu_weight) + gelu_bias)
    branch_u = low_back(matmul(normed, input_weight) + input_bias)
    mixed, decay_sum = recurrent_mixer(branch_y, branch_u, segments_per_group, conv_taps, conv_bias, decay_gate, decay_bias, input_gate, ingate_bias, decay_param)
    middle = group_tokens + low_back(matmul(low(mixed), out_weight))
    normed2 = low(rms_norm(middle, feed_gain))
    gate = low_back(matmul(normed2, gate_weight))
    upper = low_back(matmul(normed2, up_weight))
    hidden = low(jax.nn.gelu(gate) * upper)
    return (middle + low_back(matmul(hidden, down_weight)), decay_sum)

def reference(tokens, segments, gelu_weight, gelu_bias, input_weight, input_bias, conv_taps, conv_bias, decay_gate, decay_bias, input_gate, ingate_bias, decay_param, out_weight, mixer_gain, gate_weight, up_weight, down_weight, feed_gain, cotangent):
    params = tuple((p.astype(jnp.float32) for p in (gelu_weight, gelu_bias, input_weight, input_bias, conv_taps, conv_bias, decay_gate, decay_bias, input_gate, ingate_bias, decay_param, out_weight, mixer_gain, gate_weight, up_weight, down_weight, feed_gain)))
    segment_groups = TOTAL_TOKENS // PACKED_ROW_LENGTH
    segments_per_group = segments.reshape(segment_groups, PACKED_ROW_LENGTH)

    def forward(params, tokens):
        grouped_rows = tokens.reshape(segment_groups, PACKED_ROW_LENGTH, MODEL_WIDTH)

        def one_group(pair):
            return block_group(params, pair[0], pair[1])
        outputs, decay_sums = lax.map(jax.checkpoint(one_group), (grouped_rows, segments_per_group))
        return (outputs.reshape(TOTAL_TOKENS, MODEL_WIDTH), lax.optimization_barrier(jnp.sum(decay_sums, 0)))
    block_output, pullback, decay_sum = jax.vjp(forward, params, tokens, has_aux=True)
    param_grads, tokens_grad = pullback(cotangent)
    mean_decay = decay_sum / TOTAL_TOKENS
    return (block_output, tokens_grad) + tuple(param_grads[:12]) + (param_grads[12],) + tuple(param_grads[13:16]) + (param_grads[16], mean_decay)
```

```python
import jax
import jax.numpy as jnp
from jax import lax
from jax.sharding import PartitionSpec as P


def passed_along(value, axis, steps):
    count = lax.axis_size(axis)
    leading, last = (max(0, -steps), min(count, count - steps))
    return lax.ppermute(value, axis, [(source, source + steps) for source in range(leading, last)])


def entering(value, axis, join, backward):
    count, mine = (lax.axis_size(axis), lax.axis_index(axis))
    sign = -1 if backward else 1
    place = count - 1 - mine if backward else mine
    total = value
    reach = 1
    while reach < count:
        moved = passed_along(total, axis, sign * reach)
        longer = join(moved, total)
        total = jnp.where(place >= reach, longer, total)
        reach *= 2
    moved = passed_along(total, axis, sign)
    return moved[1]


def gathered(piece):
    parts = lax.axis_size("rows")
    share = piece.shape[0] // parts
    own = lax.dynamic_slice_in_dim(piece, lax.axis_index("rows") * share, share)
    return lax.all_gather(own, ("chan", "rows"), axis=0, tiled=True)


def summed_over_all(partial):
    own = lax.psum_scatter(partial, ("chan", "rows"), scatter_dimension=0, tiled=True)
    return lax.all_gather(own, "rows", axis=0, tiled=True).astype(jnp.float32)


def rms_norm(values, gain):
    return values * lax.rsqrt(jnp.mean(values * values, axis=-1, keepdims=True) + 1e-06) * gain


def combine_steps(earlier, later):
    return (earlier[0] * later[0], later[0] * earlier[1] + later[1])


def join_carries(earlier, later):
    return jnp.stack(combine_steps(earlier, later))


def block_gate(conv, matrix, bias):
    length = conv.shape[0]
    channels = conv.shape[1]
    width = matrix.shape[1]
    blocks = matrix.shape[0] // width
    stacked = matrix.reshape(blocks, width, width)
    product = jnp.einsum(
        "tnb,nbc->tnc",
        conv.reshape(length, blocks, width),
        stacked,
        precision=lax.Precision.HIGHEST,
    )
    return jax.nn.sigmoid(product.reshape(length, channels) + bias)


def mixer_block(
    branch_u,
    rim_u,
    window_segments,
    conv_taps,
    conv_bias,
    decay_gate,
    decay_bias,
    input_gate,
    ingate_bias,
    decay_param,
):
    rim = rim_u.shape[0]
    length = branch_u.shape[0]
    own = window_segments[rim:]
    start = (own != window_segments[rim - 1 : rim - 1 + length])[:, None]
    extended = jnp.concatenate([rim_u, branch_u], 0)
    conv = conv_bias + conv_taps[0] * branch_u
    for shift in range(1, rim + 1):
        moved = extended[rim - shift : rim - shift + length]
        same = (own == window_segments[rim - shift : rim - shift + length])[:, None]
        conv = conv + jnp.where(same, conv_taps[shift] * moved, 0.0)
    conv = jnp.where((own != 0)[:, None], conv, 0.0)
    rgate = block_gate(conv, decay_gate, decay_bias)
    igate = block_gate(conv, input_gate, ingate_bias)
    decay = jnp.exp(-8.0 * rgate * jax.nn.softplus(decay_param))
    scale = jnp.where(start, 1.0, jnp.sqrt(1.0 - decay * decay + 0.01))
    inject = conv * igate * scale
    carried = jnp.where(start, 0.0, decay)
    factors, states = lax.associative_scan(combine_steps, (carried, inject), axis=0)
    return ((states, factors), jnp.sum(decay, 0))


def inner(left, right):
    return lax.dot_general(
        left, right, (((0,), (0,)), ((), ())), preferred_element_type=jnp.float32
    )


def outer(left, right):
    return lax.dot_general(
        left, right, (((1,), (1,)), ((), ())), preferred_element_type=jnp.float32
    )


def activate(gate, upper):
    return jax.nn.gelu(gate) * upper


def local(
    tokens,
    segments,
    gelu_weight,
    gelu_bias,
    input_weight,
    input_bias,
    conv_taps,
    conv_bias,
    decay_gate,
    decay_bias,
    input_gate,
    ingate_bias,
    decay_param,
    out_weight,
    mixer_gain,
    gate_weight,
    up_weight,
    down_weight,
    feed_gain,
    cotangent,
):
    local_rows = tokens.shape[0]
    rim = conv_taps.shape[0] - 1
    offset = lax.axis_index("chan") * local_rows
    padded_segments = jnp.concatenate([jnp.full((rim,), -1, jnp.int32), segments])
    window_segments = lax.dynamic_slice_in_dim(padded_segments, offset, local_rows + rim)
    chans = lax.axis_size("chan")
    small = jnp.concatenate(
        [jnp.stack([gelu_bias, input_bias, conv_bias, decay_bias, ingate_bias, decay_param]), conv_taps]
    )
    branch_t = gathered(jnp.concatenate([gelu_weight.T, input_weight.T], 0))
    mixer_rest = gathered(jnp.concatenate([decay_gate, input_gate], 0))
    out_full = gathered(out_weight)
    feed_t = gathered(jnp.concatenate([gate_weight.T, up_weight.T, down_weight], 0))
    small_full = lax.all_gather(small, "chan", axis=1, tiled=True)
    vectors_low, taps_low = small_full[:6], small_full[6:]

    def parted(full, parts):
        each = full.reshape(chans, parts, -1, full.shape[1])
        return [each[:, part].reshape(-1, full.shape[1]) for part in range(parts)]

    gelu_t, input_t = parted(branch_t, 2)
    dgate_low, igate_low = parted(mixer_rest, 2)
    gate_t, up_t, down_full = parted(feed_t, 3)
    width = gelu_t.shape[0]
    taps_full = taps_low.astype(jnp.float32)
    dgate_full = dgate_low.astype(jnp.float32)
    igate_full = igate_low.astype(jnp.float32)
    vector_full = vectors_low.astype(jnp.float32)
    normed, norm_back = jax.vjp(rms_norm, tokens, mixer_gain)
    normed_low = normed.astype(jnp.bfloat16)
    branch_weight = jnp.concatenate([gelu_t, input_t], 0)
    projected = outer(normed_low, branch_weight)
    branch_y = projected[:, :width] + vector_full[0]
    branch_u = projected[:, width:] + vector_full[1]
    rim_u = passed_along(branch_u[local_rows - rim :], "chan", 1)

    def recurrent(u_part, rim_part, taps, cbias, dgate, dbias, igate, ibias, dparam):
        return mixer_block(
            u_part, rim_part, window_segments, taps, cbias, dgate, dbias, igate, ibias, dparam
        )

    (states, factors), recur_back, decay_sum = jax.vjp(
        recurrent,
        branch_u,
        rim_u,
        taps_full,
        vector_full[2],
        dgate_full,
        vector_full[3],
        igate_full,
        vector_full[4],
        vector_full[5],
        has_aux=True,
    )
    state_in = entering(jnp.stack([factors[-1], states[-1]]), "chan", join_carries, False)
    full_states = states + factors * state_in
    gelu_y, gelu_back = jax.vjp(jax.nn.gelu, branch_y)
    mixed_low = (full_states * gelu_y).astype(jnp.bfloat16)
    middle = tokens + jnp.dot(mixed_low, out_full, preferred_element_type=jnp.float32)
    normed2, feed_norm_back = jax.vjp(rms_norm, middle, feed_gain)
    normed2_low = normed2.astype(jnp.bfloat16)
    hidden_width = gate_t.shape[0]
    feed_weight = jnp.concatenate([gate_t, up_t], 0)
    feed_pre = outer(normed2_low, feed_weight)
    hidden, act_back = jax.vjp(activate, feed_pre[:, :hidden_width], feed_pre[:, hidden_width:])
    hidden_low = hidden.astype(jnp.bfloat16)
    block_output = middle + jnp.dot(hidden_low, down_full, preferred_element_type=jnp.float32)
    out_low = cotangent.astype(jnp.bfloat16)
    down_grad = inner(hidden_low, out_low).astype(jnp.bfloat16)
    hidden_grad = outer(out_low, down_full)
    gate_grad, up_grad = act_back(hidden_grad)
    feed_grad_low = jnp.concatenate([gate_grad, up_grad], 1).astype(jnp.bfloat16)
    feed_weight_grad = inner(feed_grad_low, normed2_low).astype(jnp.bfloat16)
    normed2_grad = jnp.dot(feed_grad_low, feed_weight, preferred_element_type=jnp.float32)

    def joined(parts):
        each = [part.reshape(chans, -1, part.shape[1]) for part in parts]
        return jnp.concatenate(each, 1).reshape(-1, parts[0].shape[1])

    feed_sum = summed_over_all(
        joined([feed_weight_grad[:hidden_width], feed_weight_grad[hidden_width:], down_grad])
    )
    middle_norm_grad, feed_gain_part = feed_norm_back(normed2_grad)
    middle_grad = cotangent + middle_norm_grad
    mid_low = middle_grad.astype(jnp.bfloat16)
    out_grad = inner(mixed_low, mid_low).astype(jnp.bfloat16)
    mixed_grad = outer(mid_low, out_full)
    (y_grad,) = gelu_back(mixed_grad * full_states)
    state_grad = mixed_grad * gelu_y
    local_back = jnp.sum(state_grad * factors, 0)
    later_grad = entering(jnp.stack([factors[-1], local_back]), "chan", join_carries, True)
    states_cot = jnp.concatenate([state_grad[:-1], state_grad[-1:] + later_grad[None, :]], 0)
    factors_base = state_grad * state_in
    factors_cot = jnp.concatenate(
        [factors_base[:-1], factors_base[-1:] + (later_grad * state_in)[None, :]], 0
    )
    (
        u_grad,
        rim_grad,
        taps_grad,
        cbias_grad,
        dgate_grad,
        dbias_grad,
        igate_grad,
        ibias_grad,
        dparam_grad,
    ) = recur_back((states_cot, factors_cot))
    incoming = passed_along(rim_grad, "chan", -1)
    u_grad = u_grad + jnp.concatenate(
        [jnp.zeros((local_rows - rim, width), jnp.float32), incoming], 0
    )
    branch_grad_low = jnp.concatenate([y_grad, u_grad], 1).astype(jnp.bfloat16)
    branch_bias_grad = jnp.sum(branch_grad_low, 0, dtype=jnp.float32)
    branch_weight_grad = inner(branch_grad_low, normed_low).astype(jnp.bfloat16)
    normed_grad = jnp.dot(branch_grad_low, branch_weight, preferred_element_type=jnp.float32)
    tokens_norm_grad, mixer_gain_part = norm_back(normed_grad)
    tokens_grad = middle_grad + tokens_norm_grad
    mixer_gain_grad, feed_gain_grad = lax.psum((mixer_gain_part, feed_gain_part), ("rows", "chan"))
    vector_grads = jnp.concatenate(
        [
            jnp.stack(
                [
                    branch_bias_grad[:width],
                    branch_bias_grad[width:],
                    cbias_grad,
                    dbias_grad,
                    ibias_grad,
                    dparam_grad,
                    decay_sum,
                ]
            ),
            taps_grad,
        ]
    )
    share = width // chans
    vector_total = lax.psum(vector_grads, ("rows", "chan"))
    vector_sum = lax.dynamic_slice_in_dim(
        vector_total, lax.axis_index("chan") * share, share, axis=1
    )
    taps_sum = vector_sum[7:]
    branch_sum = summed_over_all(
        joined([branch_weight_grad[:width], branch_weight_grad[width:]])
    )
    out_sum = summed_over_all(out_grad)
    gates_sum = summed_over_all(
        joined([dgate_grad.astype(jnp.bfloat16), igate_grad.astype(jnp.bfloat16)])
    )
    half = branch_sum.shape[0] // 2
    gelu_sum, input_sum = branch_sum[:half].T, branch_sum[half:].T
    half = gates_sum.shape[0] // 2
    dgate_sum, igate_sum = gates_sum[:half], gates_sum[half:]
    third = feed_sum.shape[0] // 3
    gate_sum, up_sum = feed_sum[:third].T, feed_sum[third : 2 * third].T
    down_sum = feed_sum[2 * third :]
    mean_decay = vector_sum[6] / (local_rows * lax.axis_size("rows") * lax.axis_size("chan"))
    return (
        block_output,
        tokens_grad,
        gelu_sum,
        vector_sum[0],
        input_sum,
        vector_sum[1],
        taps_sum,
        vector_sum[2],
        dgate_sum,
        vector_sum[3],
        igate_sum,
        vector_sum[4],
        vector_sum[5],
        out_sum,
        mixer_gain_grad,
        gate_sum,
        up_sum,
        down_sum,
        feed_gain_grad,
        mean_decay,
    )


def solution(mesh):
    return jax.shard_map(
        local,
        mesh=mesh,
        in_specs=(
            P(("rows", "chan"), None),
            P("rows"),
            P(None, "chan"),
            P("chan"),
            P(None, "chan"),
            P("chan"),
            P(None, "chan"),
            P("chan"),
            P("chan", None),
            P("chan"),
            P("chan", None),
            P("chan"),
            P("chan"),
            P("chan", None),
            P(),
            P(None, "chan"),
            P(None, "chan"),
            P("chan", None),
            P(),
            P(("rows", "chan"), None),
        ),
        out_specs=(
            P(("rows", "chan"), None),
            P(("rows", "chan"), None),
            P(None, "chan"),
            P("chan"),
            P(None, "chan"),
            P("chan"),
            P(None, "chan"),
            P("chan"),
            P("chan", None),
            P("chan"),
            P("chan", None),
            P("chan"),
            P("chan"),
            P("chan", None),
            P(),
            P(None, "chan"),
            P(None, "chan"),
            P("chan", None),
            P(),
            P("chan"),
        ),
        check_vma=False,
    )
```

```python
import functools

import jax
import jax.numpy as jnp
from jax import lax
from jax.experimental import pallas as pl
from jax.experimental.pallas import tpu as pltpu
from jax.sharding import PartitionSpec as P

LOW = jnp.bfloat16
WIDE = jnp.float32
RIM = 16
STEP = 16
VMEM_BYTES = 56 * 1024 * 1024
GELU_SLOPE = 0.7978845608028654
GELU_CUBE = 0.044715


def params(**more):
    return pltpu.CompilerParams(vmem_limit_bytes=VMEM_BYTES, **more)


def moved_by(value, axis, steps):
    count = lax.axis_size(axis)
    leading, last = (max(0, -steps), min(count, count - steps))
    return lax.ppermute(value, axis, [(source, source + steps) for source in range(leading, last)])


def swapped(value, axis, bits):
    count = lax.axis_size(axis)
    return lax.ppermute(value, axis, [(source, source ^ bits) for source in range(count)])


def join(earlier, later):
    return jnp.concatenate(
        [earlier[0:1] * later[0:1], later[0:1] * earlier[1:2] + later[1:2]], 0
    )


def entering(value, axis, sign):
    count = lax.axis_size(axis)
    if count > 2:
        near = [moved_by(value, axis, sign * reach) for reach in (1, 2, 3) if reach < count]
        total = value
        for one in near:
            total = join(one, total)
        reach = 4
        while 2 * reach < count:
            total = join(moved_by(total, axis, sign * reach), total)
            reach *= 2
        last = moved_by(total, axis, sign)
        if reach + 1 < count:
            last = join(moved_by(total, axis, sign * (reach + 1)), last)
        return last[1:2]
    return moved_by(value, axis, sign)[1:2]


def rms_norm(values, gain):
    return values * lax.rsqrt(jnp.mean(values * values, axis=-1, keepdims=True) + 1e-06) * gain


def nt(left, right):
    return lax.dot_general(left, right, (((1,), (1,)), ((), ())), preferred_element_type=WIDE)


def tn(left, right):
    return lax.dot_general(left, right, (((0,), (0,)), ((), ())), preferred_element_type=WIDE)


def nn(left, right):
    return lax.dot_general(left, right, (((1,), (0,)), ((), ())), preferred_element_type=WIDE)


def sigmoid(value):
    return 0.5 * jnp.tanh(0.5 * value) + 0.5


def gelu_parts(value):
    square = value * value
    bend = jnp.tanh(GELU_SLOPE * value * (1.0 + GELU_CUBE * square))
    half = 0.5 + 0.5 * bend
    slope = half + 0.5 * GELU_SLOPE * value * (1.0 - bend * bend) * (1.0 + 3.0 * GELU_CUBE * square)
    return value * half, slope


def split_low(value):
    high = value.astype(LOW)
    return high, (value - high.astype(WIDE)).astype(LOW)


def fold(value):
    total = value[0:8]
    for group in range(1, value.shape[0] // 8):
        total = total + value[8 * group : 8 * group + 8]
    return total


def mixer_forward_kernel(
    normed, y_weight, u_weight, gates, vec, mask, y_out, u_out, conv_out, r_out, i_out, h_out, f_out,
    sum_out, high, low, zed,
):
    ext = normed.shape[0]
    width = y_out.shape[1]
    count = (ext - RIM) // STEP
    model = normed.shape[1]
    y_out[...] = nt(normed[RIM:, :], y_weight[...].reshape(width, model)) + vec[0:1, :]
    u_out[...] = nt(normed[...], u_weight[...].reshape(width, model)) + vec[1:2, :]

    def convolve(index, _):
        base = pl.multiple_of(index * STEP, STEP)
        own = pl.ds(base, STEP)
        window = u_out[pl.ds(base + 8, STEP + 8), :]
        flags = mask[pl.ds(base + RIM, STEP), :]
        conv = vec[2:3, :] + vec[6:7, :] * window[8:]
        for shift in (1, 2, 3):
            conv = conv + flags[:, shift : shift + 1] * (
                vec[6 + shift : 7 + shift, :] * window[8 - shift : 8 - shift + STEP]
            )
        conv = conv * flags[:, 4:5]
        conv_out[own, :] = conv
        high[own, :], low[own, :] = split_low(conv)
        return 0

    lax.fori_loop(0, count, convolve, 0)
    zed[...] = nn(high[...], gates[0]) + nn(low[...], gates[0])
    line = lax.broadcasted_iota(jnp.int32, (8, width), 0)

    def advance(index, carry):
        state, factor, total = carry
        own = pl.ds(pl.multiple_of(index * STEP, STEP), STEP)
        going = mask[pl.ds(pl.multiple_of(index * STEP + RIM, STEP), STEP), :][:, 0:1]
        rate = sigmoid(zed[own, 0:width] + vec[3:4, :])
        into = sigmoid(zed[own, width:] + vec[4:5, :])
        decay = jnp.exp(vec[5:6, :] * rate)
        r_out[own, :] = rate
        i_out[own, :] = into
        scale = jnp.where(going == 0.0, 1.0, jnp.sqrt(1.01 - decay * decay))
        inject = conv_out[own, :] * into * scale
        carried = decay * going
        total = total + fold(decay)
        for group in range(STEP // 8):
            part = slice(8 * group, 8 * group + 8)
            mul, add = carried[part], inject[part]
            for reach in (1, 2, 4):
                inside = line >= reach
                add = add + mul * jnp.where(inside, pltpu.roll(add, reach, 0), 0.0)
                mul = mul * jnp.where(inside, pltpu.roll(mul, reach, 0), 1.0)
            here = add + mul * state
            gone = mul * factor
            rows = pl.ds(pl.multiple_of(index * STEP + 8 * group, 8), 8)
            h_out[rows, :] = here
            f_out[rows, :] = gone
            state, factor = here[7:8], gone[7:8]
        return state, factor, total

    zero = jnp.zeros((1, width), WIDE)
    _, _, total = lax.fori_loop(
        0, count, advance, (zero, zero + 1.0, jnp.zeros((8, width), WIDE))
    )
    sum_out[...] = total


def mixer_forward(normed, slab, gates, vec, mask, rows):
    ext, model = normed.shape
    tokens = ext - RIM
    pairs, width = gates.shape[0], gates.shape[1]
    chans = slab.shape[0]
    group = width // rows
    total = pairs * width
    by_lane = lambda length: pl.BlockSpec((length, width), lambda step: (0, step))
    whole = lambda array: pl.BlockSpec(array.shape, lambda step: (0,) * array.ndim)
    flat = jax.ShapeDtypeStruct((tokens, total), WIDE)
    return pl.pallas_call(
        mixer_forward_kernel,
        grid=(pairs,),
        in_specs=[
            whole(normed),
            pl.BlockSpec((group, rows, model), lambda step: (step, 0, 0)),
            pl.BlockSpec((group, rows, model), lambda step: (step, 1, 0)),
            pl.BlockSpec((1, width, 2 * width), lambda step: (step, 0, 0)),
            by_lane(vec.shape[0]),
            whole(mask),
        ],
        out_specs=[
            by_lane(tokens), by_lane(ext), by_lane(tokens), by_lane(tokens), by_lane(tokens),
            by_lane(tokens), by_lane(tokens), by_lane(8),
        ],
        out_shape=[
            flat, jax.ShapeDtypeStruct((ext, total), WIDE), flat, flat, flat, flat, flat,
            jax.ShapeDtypeStruct((8, total), WIDE),
        ],
        scratch_shapes=[
            pltpu.VMEM((tokens, width), LOW),
            pltpu.VMEM((tokens, width), LOW),
            pltpu.VMEM((tokens, 2 * width), WIDE),
        ],
        compiler_params=params(),
        name="mixer_forward",
    )(normed, slab, slab, gates, vec, mask)


def mixer_out_kernel(y, h, f, state, weight, tokens, gain, mixed, middle, normed):
    model = tokens.shape[1]

    def gate(index, _):
        own = pl.ds(pl.multiple_of(index * STEP, STEP), STEP)
        full = h[own, :] + f[own, :] * state[...]
        value = y[own, :]
        bend = jnp.tanh(GELU_SLOPE * value * (1.0 + GELU_CUBE * value * value))
        mixed[own, :] = (full * (value * (0.5 + 0.5 * bend))).astype(LOW)
        return 0

    lax.fori_loop(0, y.shape[0] // STEP, gate, 0)
    total = tokens[...] + nn(mixed[...], weight[...].reshape(-1, model))
    middle[...] = total
    scale = lax.rsqrt(jnp.mean(total * total, axis=-1, keepdims=True) + 1e-06)
    normed[...] = (total * scale * gain[...]).astype(LOW)


def mixer_out(y, h, f, state, slab, rows, row_index, tokens, gain):
    length, model = tokens.shape
    total = y.shape[1]
    chans = slab.shape[0]
    tile = 128 if length % 128 == 0 else length
    row = lambda lanes: pl.BlockSpec((tile, lanes), lambda step: (step, 0))
    return pl.pallas_call(
        mixer_out_kernel,
        grid=(length // tile,),
        in_specs=[
            row(total), row(total), row(total),
            pl.BlockSpec((1, total), lambda step: (0, 0)),
            pl.BlockSpec((chans, rows, model), lambda step: (0, row_index, 0)),
            row(model),
            pl.BlockSpec((1, model), lambda step: (0, 0)),
        ],
        out_specs=[row(total), row(model), row(model)],
        out_shape=[
            jax.ShapeDtypeStruct((length, total), LOW),
            jax.ShapeDtypeStruct((length, model), WIDE),
            jax.ShapeDtypeStruct((length, model), LOW),
        ],
        compiler_params=params(),
        name="mixer_out",
    )(y, h, f, state, slab, tokens, gain)


def spread(place, wide, keep, send, matrix, group, rows):
    part = rows // 4
    if part % 8:
        value = wide[...]
        pieces = [value[begin : begin + part] for begin in range(0, group * rows, part)]
        mine = place[1] * 4 + place[2]
        bit = 1
        while bit < len(pieces):
            turned = (mine & bit) != 0
            pieces = [
                jnp.where(turned, pieces[index ^ bit], pieces[index])
                for index in range(len(pieces))
            ]
            bit *= 2
    for slot in range(group):
        shard = slot ^ place[1]
        for turn in range(4):
            if part % 8:
                value = pieces[4 * slot + turn]
            else:
                begin = pl.multiple_of(shard * rows + (turn ^ place[2]) * part, 8)
                value = wide[pl.ds(begin, part), :]
            (keep, send)[turn & 1][slot, matrix, turn >> 1, :, :] = value.astype(LOW)


def feed_kernel(
    rows, place, normed, cot, w_gate, w_up, w_down, out_in, grad_in, out, grad, keep, send,
    gate_s, up_s, back_s, hidden_l, gate_l, up_l, wide,
):
    model = normed.shape[1]
    width = gate_s.shape[0]
    group = width // rows
    first, second, third = (w[...].reshape(width, model) for w in (w_gate, w_up, w_down))

    @pl.when(pl.program_id(0) == 0)
    def _():
        out[...] = out_in[...]
        grad[...] = grad_in[...]

    gate_s[...] = nt(first, normed[...])
    up_s[...] = nt(second, normed[...])
    back_s[...] = nt(third, cot[...])

    def act(index, _):
        own = pl.ds(pl.multiple_of(index * STEP, STEP), STEP)
        up, back = up_s[own, :], back_s[own, :]
        value, slope = gelu_parts(gate_s[own, :])
        hidden_l[own, :] = (value * up).astype(LOW)
        gate_l[own, :] = (back * up * slope).astype(LOW)
        up_l[own, :] = (back * value).astype(LOW)
        return 0

    lax.fori_loop(0, width // STEP, act, 0)
    out[...] += tn(hidden_l[...], third)
    grad[...] += tn(gate_l[...], first) + tn(up_l[...], second)
    for matrix, (left, right) in enumerate(((gate_l, normed), (up_l, normed), (hidden_l, cot))):
        wide[...] = nn(left[...], right[...])
        spread(place, wide, keep, send, matrix, group, rows)


def feed(place, normed, cot, slab, rows, group, out_in, grad_in, begin, steps):
    length, model = normed.shape
    width = group * rows
    part = rows // 4
    whole = lambda array: pl.BlockSpec(array.shape, lambda step, place: (0,) * array.ndim)
    weight = lambda index: pl.BlockSpec(
        (group, rows, model), lambda step, place: ((step + begin) ^ place[0], index, 0)
    )
    piece = pl.BlockSpec(
        (group, 3, 2, part, model), lambda step, place: (step, 0, 0, 0, 0)
    )
    slots = steps * group
    return pl.pallas_call(
        functools.partial(feed_kernel, rows),
        grid_spec=pltpu.PrefetchScalarGridSpec(
            num_scalar_prefetch=1,
            grid=(steps,),
            in_specs=[
                whole(normed), whole(cot), weight(0), weight(1), weight(2), whole(out_in),
                whole(grad_in),
            ],
            out_specs=[whole(out_in), whole(grad_in), piece, piece],
            scratch_shapes=[pltpu.VMEM((width, length), WIDE)] * 3
            + [pltpu.VMEM((width, length), LOW)] * 3
            + [pltpu.VMEM((width, model), WIDE)],
        ),
        out_shape=[
            jax.ShapeDtypeStruct((length, model), WIDE),
            jax.ShapeDtypeStruct((length, model), WIDE),
            jax.ShapeDtypeStruct((slots, 3, 2, part, model), LOW),
            jax.ShapeDtypeStruct((slots, 3, 2, part, model), LOW),
        ],
        compiler_params=params(),
        name="feed",
    )(place, normed, cot, slab, slab, slab, out_in, grad_in)


def middle_back_kernel(
    middle, grad, cot, gain, weight, y, h, f, state, mid_grad, mid_low, state_grad, y_grad,
    gain_sum, back_sum, bias_sum, mixed_s,
):
    model = middle.shape[1]

    @pl.when(pl.program_id(0) == 0)
    def _():
        gain_sum[...] = jnp.zeros_like(gain_sum)
        back_sum[...] = jnp.zeros_like(back_sum)
        bias_sum[...] = jnp.zeros_like(bias_sum)

    value, error = middle[...], grad[...]
    scale = lax.rsqrt(jnp.mean(value * value, axis=-1, keepdims=True) + 1e-06)
    gained = gain[...] * error
    mean = jnp.mean(gained * value, axis=-1, keepdims=True)
    total = cot[...] + scale * gained - value * (scale * scale * scale * mean)
    gain_sum[...] += fold(error * value * scale)
    mid_grad[...] = total
    mid_low[...] = total.astype(LOW)
    mixed_s[...] = nt(mid_low[...], weight[...].reshape(-1, model))

    def turn(index, carry):
        back, bias = carry
        own = pl.ds(pl.multiple_of(index * STEP, STEP), STEP)
        error = mixed_s[own, :]
        active, slope = gelu_parts(y[own, :])
        gone = f[own, :]
        full = h[own, :] + gone * state[...]
        here = error * active
        state_grad[own, :] = here
        low = (error * full * slope).astype(LOW)
        y_grad[own, :] = low
        return back + fold(here * gone), bias + fold(low.astype(WIDE))

    zero = jnp.zeros(back_sum.shape, WIDE)
    back, bias = lax.fori_loop(0, middle.shape[0] // STEP, turn, (zero, zero))
    back_sum[...] += back
    bias_sum[...] += bias


def middle_back(middle, grad, cot, gain, slab, rows, row_index, y, h, f, state):
    length, model = middle.shape
    total = y.shape[1]
    chans = slab.shape[0]
    tile = 128 if length % 128 == 0 else length
    row = lambda lanes: pl.BlockSpec((tile, lanes), lambda step: (step, 0))
    one = lambda lines, lanes: pl.BlockSpec((lines, lanes), lambda step: (0, 0))
    return pl.pallas_call(
        middle_back_kernel,
        grid=(length // tile,),
        in_specs=[
            row(model), row(model), row(model), one(1, model),
            pl.BlockSpec((chans, rows, model), lambda step: (0, row_index, 0)),
            row(total), row(total), row(total), one(1, total),
        ],
        out_specs=[
            row(model), row(model), row(total), row(total), one(8, model), one(8, total),
            one(8, total),
        ],
        out_shape=[
            jax.ShapeDtypeStruct((length, model), WIDE),
            jax.ShapeDtypeStruct((length, model), LOW),
            jax.ShapeDtypeStruct((length, total), WIDE),
            jax.ShapeDtypeStruct((length, total), LOW),
            jax.ShapeDtypeStruct((8, model), WIDE),
            jax.ShapeDtypeStruct((8, total), WIDE),
            jax.ShapeDtypeStruct((8, total), WIDE),
        ],
        scratch_shapes=[pltpu.VMEM((tile, total), WIDE)],
        compiler_params=params(),
        name="middle_back",
    )(middle, grad, cot, gain, slab, y, h, f, state)


def side_kernel(rows, place, y_grad, mixed, normed, mid, keep, send, wide):
    group = wide.shape[0] // rows
    wide[...] = tn(y_grad[...], normed[RIM:, :])
    spread(place, wide, keep, send, 0, group, rows)
    wide[...] = tn(mixed[...], mid[...])
    spread(place, wide, keep, send, 1, group, rows)


def side_grads(place, y_grad, mixed, normed, mid, rows, width):
    length, total = y_grad.shape
    model = mid.shape[1]
    group, part = width // rows, rows // 4
    whole = lambda array: pl.BlockSpec(array.shape, lambda step, place: (0,) * array.ndim)
    lane = pl.BlockSpec((length, width), lambda step, place: (0, step ^ place[0]))
    piece = pl.BlockSpec((group, 2, 2, part, model), lambda step, place: (step, 0, 0, 0, 0))
    shape = jax.ShapeDtypeStruct((total // rows, 2, 2, part, model), LOW)
    return pl.pallas_call(
        functools.partial(side_kernel, rows),
        grid_spec=pltpu.PrefetchScalarGridSpec(
            num_scalar_prefetch=1,
            grid=(total // width,),
            in_specs=[lane, lane, whole(normed), whole(mid)],
            out_specs=[piece, piece],
            scratch_shapes=[pltpu.VMEM((width, model), WIDE)],
        ),
        out_shape=[shape, shape],
        compiler_params=params(),
        name="side_grads",
    )(place, y_grad, mixed, normed, mid)


def mixer_back_kernel(
    rows, place, state_grad, r_in, i_in, conv_in, h, f, u, y_grad, y_weight, u_weight, gates, vec,
    mask, state, after, normed, keep, send, gate_keep, gate_send, sums, normed_grad,
    conv_s, high, low, conv_h, conv_l, grown, u_low, wide, gate_w,
):
    length, width = state_grad.shape
    ext, model = normed.shape
    group = width // rows
    block = width // 2
    count = length // STEP
    line = lax.broadcasted_iota(jnp.int32, (8, width), 0)

    @pl.when(pl.program_id(0) == 0)
    def _():
        normed_grad[...] = jnp.zeros_like(normed_grad)

    def retreat(index, carry):
        error, rate_sum, into_sum, slope_sum = carry
        base = pl.multiple_of((count - 1 - index) * STEP, STEP)
        own = pl.ds(base, STEP)
        going = mask[pl.ds(base + RIM, STEP), :][:, 0:1]
        rate, into, conv = r_in[own, :], i_in[own, :], conv_in[own, :]
        slope = vec[5:6, :]
        decay = jnp.exp(slope * rate)
        carried = decay * going
        given = state_grad[own, :]
        full = h[own, :] + f[own, :] * state[...]
        ahead = pl.ds(pl.multiple_of(jnp.maximum(base - 8, 0), 8), 8)
        edge = h[ahead, :][7:8] + f[ahead, :][7:8] * state[...]
        edge = jnp.where(base == 0, state[...], edge)
        parts = []
        for part in reversed(range(STEP // 8)):
            place_of = slice(8 * part, 8 * part + 8)
            mul = carried[place_of]
            add = mul * given[place_of]
            for reach in (1, 2, 4):
                inside = line < 8 - reach
                add = add + mul * jnp.where(inside, pltpu.roll(add, 8 - reach, 0), 0.0)
                mul = mul * jnp.where(inside, pltpu.roll(mul, 8 - reach, 0), 1.0)
            here = add + mul * error
            parts.append(given[place_of] + jnp.where(line < 7, pltpu.roll(here, 7, 0), error))
            error = here[0:1]
        grad = jnp.concatenate(parts[::-1], 0)
        befores = []
        for part in range(STEP // 8):
            last = edge if part == 0 else full[8 * part - 1 : 8 * part]
            befores.append(
                jnp.where(line > 0, pltpu.roll(full[8 * part : 8 * part + 8], 1, 0), last)
            )
        before = jnp.concatenate(befores, 0)
        root = lax.rsqrt(1.01 - decay * decay)
        scale = jnp.where(going == 0.0, 1.0, (1.01 - decay * decay) * root)
        through = grad * conv
        into_grad = through * scale
        conv_s[own, :] = grad * into * scale
        decay_grad = going * decay * (grad * before - through * into * decay * root)
        z_rate = decay_grad * slope * rate * (1.0 - rate)
        z_into = into_grad * into * (1.0 - into)
        high[own, 0:width], low[own, 0:width] = split_low(z_rate)
        high[own, width:], low[own, width:] = split_low(z_into)
        conv_h[own, :], conv_l[own, :] = split_low(conv)
        return (
            error,
            rate_sum + fold(z_rate),
            into_sum + fold(z_into),
            slope_sum + fold(decay_grad * rate),
        )

    zero = jnp.zeros((8, width), WIDE)
    _, rate_sum, into_sum, slope_sum = lax.fori_loop(
        0, count, retreat, (after[...], zero, zero, zero)
    )
    conv_s[...] += nt(high[...], gates[0]) + nt(low[...], gates[0])
    gate_full = (
        tn(conv_h[...], high[...]) + tn(conv_l[...], high[...]) + tn(conv_h[...], low[...])
    )
    for half in (0, block):
        rows_of = slice(half, half + block)
        gate_w[rows_of, 0:block] = gate_full[rows_of, half : half + block]
        gate_w[rows_of, block:] = gate_full[rows_of, width + half : width + half + block]
    grown[0:RIM, :] = jnp.zeros((RIM, width), WIDE)
    grown[RIM + length :, :] = jnp.zeros((RIM, width), WIDE)

    def taps(index, carry):
        base = pl.multiple_of(index * STEP, STEP)
        window = u[pl.ds(base + 8, STEP + 8), :]
        flags = mask[pl.ds(base + RIM, STEP), :]
        error = conv_s[pl.ds(base, STEP), :] * flags[:, 4:5]
        grown[pl.ds(base + RIM, STEP), :] = error
        out = [carry[0] + fold(error), carry[1] + fold(error * window[8:])]
        for shift in (1, 2, 3):
            moved = window[8 - shift : 8 - shift + STEP]
            out.append(carry[1 + shift] + fold(flags[:, shift : shift + 1] * error * moved))
        return tuple(out)

    bias_sum, *tap_sums = lax.fori_loop(0, count, taps, (zero,) * 5)

    def spread_back(index, total):
        base = pl.multiple_of(index * STEP, STEP)
        window = grown[pl.ds(base, STEP + 8), :]
        flags = mask[pl.ds(base, STEP + 8), :]
        value = vec[6:7, :] * window[0:STEP]
        for shift in (1, 2, 3):
            masked = flags[:, shift : shift + 1] * window
            value = value + vec[6 + shift : 7 + shift, :] * masked[shift : shift + STEP]
        rounded = value.astype(LOW)
        u_low[pl.ds(base, STEP), :] = rounded
        return total + fold(rounded.astype(WIDE))

    input_sum = lax.fori_loop(0, ext // STEP, spread_back, zero)
    for row, value in enumerate((input_sum, bias_sum, rate_sum, into_sum, slope_sum, *tap_sums)):
        sums[row : row + 1, :] = jnp.sum(value, axis=0, keepdims=True)
    sums[9:16, :] = jnp.zeros((7, width), WIDE)
    wide[...] = tn(u_low[...], normed[...])
    spread(place, wide, keep, send, 0, group, rows)
    spread(place, gate_w, gate_keep, gate_send, 0, group, rows)
    normed_grad[...] += nn(u_low[...], u_weight[...].reshape(width, model))
    normed_grad[RIM:, :] += nn(y_grad[...], y_weight[...].reshape(width, model))


def mixer_back(
    place, state_grad, r, i, conv, h, f, u, y_grad, slab, gates, vec, mask, state, after, normed,
    rows,
):
    length, total = state_grad.shape
    ext, model = normed.shape
    width = gates.shape[1]
    group, part = width // rows, rows // 4
    whole = lambda array: pl.BlockSpec(array.shape, lambda step, place: (0,) * array.ndim)
    lane = lambda lines: pl.BlockSpec((lines, width), lambda step, place: (0, step ^ place[0]))
    weight = lambda index: pl.BlockSpec(
        (group, rows, model), lambda step, place: (step ^ place[0], index, 0)
    )
    piece = lambda lanes: pl.BlockSpec(
        (group, 1, 2, part, lanes), lambda step, place: (step, 0, 0, 0, 0)
    )
    shape = lambda lanes: jax.ShapeDtypeStruct((total // rows, 1, 2, part, lanes), LOW)
    return pl.pallas_call(
        functools.partial(mixer_back_kernel, rows),
        grid_spec=pltpu.PrefetchScalarGridSpec(
            num_scalar_prefetch=1,
            grid=(total // width,),
            in_specs=[
                lane(length), lane(length), lane(length), lane(length), lane(length),
                lane(length), lane(ext), lane(length), weight(0), weight(1),
                pl.BlockSpec((1, width, 2 * width), lambda step, place: (step ^ place[0], 0, 0)),
                lane(vec.shape[0]), whole(mask), lane(1), lane(1), whole(normed),
            ],
            out_specs=[
                piece(model), piece(model), piece(width), piece(width), lane(16),
                pl.BlockSpec((ext, model), lambda step, place: (0, 0)),
            ],
            scratch_shapes=[
                pltpu.VMEM((length, width), WIDE),
                pltpu.VMEM((length, 2 * width), LOW),
                pltpu.VMEM((length, 2 * width), LOW),
                pltpu.VMEM((length, width), LOW),
                pltpu.VMEM((length, width), LOW),
                pltpu.VMEM((ext + RIM, width), WIDE),
                pltpu.VMEM((ext, width), LOW),
                pltpu.VMEM((width, model), WIDE),
                pltpu.VMEM((width, width), WIDE),
            ],
        ),
        out_shape=[
            shape(model), shape(model), shape(width), shape(width),
            jax.ShapeDtypeStruct((16, total), WIDE),
            jax.ShapeDtypeStruct((ext, model), WIDE),
        ],
        compiler_params=params(),
        name="mixer_back",
    )(
        place, state_grad, r, i, conv, h, f, u, y_grad, slab, slab, gates, vec, mask, state, after,
        normed,
    )


def wide_of(value):
    return value.astype(WIDE)


def owned(keep, send, begin):
    slots, matrices, _, part, lanes = keep.shape
    shape = (slots // 2, 2, matrices, 2, part, lanes)
    keep = keep.reshape(shape)
    came = swapped(send, "rows", 1).reshape(shape)
    result = {}
    for parity in (0, 1):
        picked = slice((parity - begin) % 2, None, 2)
        mine, theirs = keep[picked], came[picked]
        if mine.shape[0] == 0:
            continue
        if parity == 0:
            away = (wide_of(mine[:, :, :, 1]) + wide_of(theirs[:, :, :, 1])).astype(LOW)
            back = swapped(away, "rows", 2)
            rest = wide_of(mine[:, :, :, 0]) + wide_of(theirs[:, :, :, 0]) + wide_of(back)
            back = swapped(rest[:, 1].astype(LOW), "chan", 1)
            rest = rest[:, 0] + wide_of(back)
        else:
            away = (wide_of(mine[:, 1]) + wide_of(theirs[:, 1])).astype(LOW)
            back = swapped(away, "chan", 1)
            rest = wide_of(mine[:, 0]) + wide_of(theirs[:, 0]) + wide_of(back)
            back = swapped(rest[:, :, 1].astype(LOW), "rows", 2)
            rest = rest[:, :, 0] + wide_of(back)
        for index in range(rest.shape[0]):
            result[begin + (parity - begin) % 2 + 2 * index] = rest[index]
    return result


def settled(results):
    total = results[0]
    for distance, value in results.items():
        if distance:
            total = total + wide_of(swapped(value.astype(LOW), "chan", 2 * distance))
    total = total.astype(LOW)
    pair = jnp.stack([total, swapped(total, "rows", 1)])
    four = jnp.stack([pair, swapped(pair, "rows", 2)])
    place = lax.axis_index("rows")
    four = jnp.where(place & 1, four[:, ::-1], four)
    four = jnp.where(place & 2, four[::-1], four)
    _, _, matrices, part, lanes = four.shape
    four = four.reshape(4, matrices, part, lanes).transpose(1, 0, 2, 3)
    return four.reshape(matrices, 4 * part, lanes).astype(WIDE)


def summed_everywhere(value):
    for axis in ("rows", "chan"):
        bits = 1
        while bits < lax.axis_size(axis):
            value = value + swapped(value, axis, bits)
            bits *= 2
    return value


def gathered(piece):
    parts = lax.axis_size("rows")
    share = piece.shape[0] // parts
    own = lax.dynamic_slice_in_dim(piece, lax.axis_index("rows") * share, share)
    full = lax.all_gather(own, ("chan", "rows"), axis=0, tiled=True)
    return full.reshape(lax.axis_size("chan"), piece.shape[0], piece.shape[1])


def local(
    tokens, segments, gelu_weight, gelu_bias, input_weight, input_bias, conv_taps, conv_bias,
    decay_gate, decay_bias, input_gate, ingate_bias, decay_param, out_weight, mixer_gain,
    gate_weight, up_weight, down_weight, feed_gain, cotangent,
):
    length, model = tokens.shape
    rim = conv_taps.shape[0] - 1
    chans = lax.axis_size("chan")
    me, row_place = lax.axis_index("chan"), lax.axis_index("rows")
    rows, block = decay_gate.shape
    feed_rows = gate_weight.shape[1]
    total = rows * chans
    width = 2 * block
    group = width // rows
    feed_group = max(1, width // feed_rows)

    padded = jnp.concatenate([jnp.full((rim,), -1, jnp.int32), segments])
    window = lax.dynamic_slice_in_dim(padded, me * length, length + rim)
    own = window[rim:]
    same = [own == window[rim - shift : rim - shift + length] for shift in range(1, rim + 1)]
    mask = jnp.stack([same[0], *same, own != 0] + [same[0]] * (7 - rim - 1), 1).astype(WIDE)
    mask = jnp.pad(mask, ((RIM, RIM), (0, 0)))

    small = jnp.concatenate(
        [
            jnp.stack([gelu_bias, input_bias, conv_bias, decay_bias, ingate_bias, decay_param]),
            conv_taps,
        ]
    )
    gate_rows = 2 * rows * block // model
    slab_rows = -(-(2 * rows + gate_rows + -(-small.size // model)) // 32) * 32
    small_rows = slab_rows - 2 * rows - gate_rows
    packed = jnp.pad(small.reshape(-1), (0, small_rows * model - small.size))
    slab = gathered(
        jnp.concatenate(
            [
                gelu_weight.T,
                input_weight.T,
                jnp.concatenate([decay_gate, input_gate], 1).reshape(gate_rows, model),
                packed.reshape(small_rows, model),
            ]
        )
    )
    late = gathered(jnp.concatenate([gate_weight.T, up_weight.T, down_weight, out_weight]))
    out_index = 3 * feed_rows // rows

    both = slab[:, 2 * rows : 2 * rows + gate_rows].reshape(total, 2 * block)
    both = both.reshape(total // width, 2, block, 2, block)
    none = jnp.zeros(both.shape[:1] + (block, block), LOW)
    gates = jnp.concatenate(
        [
            jnp.concatenate([both[:, 0, :, 0], none, both[:, 0, :, 1], none], 2),
            jnp.concatenate([none, both[:, 1, :, 0], none, both[:, 1, :, 1]], 2),
        ],
        1,
    )
    small_full = slab[:, 2 * rows + gate_rows :].reshape(chans, -1)[:, : small.size]
    small_full = small_full.reshape(chans, small.shape[0], rows).transpose(1, 0, 2)
    small_full = small_full.reshape(small.shape[0], total).astype(WIDE)
    param = small_full[5:6]
    vec = jnp.concatenate(
        [small_full[:5], -8.0 * jax.nn.softplus(param), small_full[6:], jnp.zeros((6, total), WIDE)]
    )

    rim_tokens = moved_by(tokens[length - rim :], "chan", 1)
    extended = jnp.concatenate([jnp.zeros((RIM - rim, model), WIDE), rim_tokens, tokens])
    normed = rms_norm(extended, mixer_gain).astype(LOW)
    y, u, conv, rate, into, state, factor, decay_sum = mixer_forward(
        normed, slab, gates, vec, mask, rows
    )
    carry = entering(jnp.concatenate([factor[-1:], state[-1:]]), "chan", 1)
    mixed, middle, normed2 = mixer_out(
        y, state, factor, carry, late, rows, out_index, tokens, feed_gain[None]
    )
    cot_low = cotangent.astype(LOW)
    low_bits = feed_group - 1
    place = jnp.stack([me // feed_group, me & low_bits, row_place]).astype(jnp.int32)
    steps = chans // feed_group // 2
    block_output, normed2_grad, keep_far, send_far = feed(
        place, normed2, cot_low, late, feed_rows, feed_group, middle,
        jnp.zeros_like(middle), steps, steps,
    )
    far = owned(keep_far, send_far, steps * feed_group // 2)
    block_output, normed2_grad, keep_near, send_near = feed(
        place, normed2, cot_low, late, feed_rows, feed_group, block_output, normed2_grad, 0, steps,
    )
    near = owned(keep_near, send_near, 0)
    feed_sum = settled({**near, **far})

    mid_grad, mid_low, state_grad, y_grad, feed_gain_sum, back_sum, y_sum = middle_back(
        middle, normed2_grad, cotangent, feed_gain[None], late, rows, out_index, y, state, factor,
        carry,
    )
    after = entering(
        jnp.concatenate([factor[-1:], jnp.sum(back_sum, 0, keepdims=True)]), "chan", -1
    )
    place = jnp.stack([me // group, me % group, row_place]).astype(jnp.int32)
    keep, send = side_grads(place, y_grad, mixed, normed, mid_low, rows, width)
    side_sum = settled(owned(keep, send, 0))
    keep, send, gate_keep, gate_send, sums, normed_grad = mixer_back(
        place, state_grad, rate, into, conv, state, factor, u, y_grad, slab, gates, vec, mask,
        carry, after, normed, rows,
    )
    input_sum = settled(owned(keep, send, 0))[0]
    gates_sum = settled(owned(gate_keep, gate_send, 0))[0]
    rim_grad = moved_by(normed_grad[RIM - rim : RIM], "chan", -1)
    error = normed_grad[RIM:] + jnp.concatenate([jnp.zeros((length - rim, model), WIDE), rim_grad])
    scale = lax.rsqrt(jnp.mean(tokens * tokens, axis=-1, keepdims=True) + 1e-06)
    gained = mixer_gain * error
    mean = jnp.mean(gained * tokens, axis=-1, keepdims=True)
    tokens_grad = mid_grad + scale * gained - tokens * (scale * scale * scale * mean)
    mixer_gain_sum = jnp.sum(error * tokens * scale, 0)

    slope_grad = sums[4:5] * (-8.0 * jax.nn.sigmoid(param))
    lines = jnp.concatenate(
        [jnp.sum(y_sum, 0, keepdims=True), sums[:4], slope_grad, sums[5:9],
         jnp.sum(decay_sum, 0, keepdims=True)]
    )
    gains = jnp.stack([mixer_gain_sum, jnp.sum(feed_gain_sum, 0)])
    everything = summed_everywhere(
        jnp.concatenate([lines.reshape(-1, 128), gains.reshape(-1, 128)])
    )
    cut = lines.size // 128
    gains = everything[cut:].reshape(2, model)
    lines = lax.dynamic_slice_in_dim(
        everything[:cut].reshape(lines.shape), me * rows, rows, axis=1
    )
    mean_decay = lines[10] / (length * lax.axis_size("rows") * chans)
    return (
        block_output,
        tokens_grad,
        side_sum[0].T,
        lines[0],
        input_sum.T,
        lines[1],
        lines[6:10],
        lines[2],
        gates_sum[:, :block],
        lines[3],
        gates_sum[:, block:],
        lines[4],
        lines[5],
        side_sum[1],
        gains[0],
        feed_sum[0].T,
        feed_sum[1].T,
        feed_sum[2],
        gains[1],
        mean_decay,
    )


def solution(mesh):
    return jax.shard_map(
        local,
        mesh=mesh,
        in_specs=(
            P(("rows", "chan"), None),
            P("rows"),
            P(None, "chan"),
            P("chan"),
            P(None, "chan"),
            P("chan"),
            P(None, "chan"),
            P("chan"),
            P("chan", None),
            P("chan"),
            P("chan", None),
            P("chan"),
            P("chan"),
            P("chan", None),
            P(),
            P(None, "chan"),
            P(None, "chan"),
            P("chan", None),
            P(),
            P(("rows", "chan"), None),
        ),
        out_specs=(
            P(("rows", "chan"), None),
            P(("rows", "chan"), None),
            P(None, "chan"),
            P("chan"),
            P(None, "chan"),
            P("chan"),
            P(None, "chan"),
            P("chan"),
            P("chan", None),
            P("chan"),
            P("chan", None),
            P("chan"),
            P("chan"),
            P("chan", None),
            P(),
            P(None, "chan"),
            P(None, "chan"),
            P("chan", None),
            P(),
            P("chan"),
        ),
        check_vma=False,
    )
```

```python
import functools

import jax
import jax.numpy as jnp
from jax import lax
from jax.experimental import pallas as pl
from jax.experimental.pallas import tpu as pltpu
from jax.sharding import PartitionSpec as P

LOW = jnp.bfloat16
WIDE = jnp.float32
RIM = 16
STEP = 16
VMEM_BYTES = 56 * 1024 * 1024
GELU_SLOPE = 0.7978845608028654
GELU_CUBE = 0.044715


def params(**more):
    return pltpu.CompilerParams(vmem_limit_bytes=VMEM_BYTES, **more)


def moved_by(value, axis, steps):
    count = lax.axis_size(axis)
    leading, last = (max(0, -steps), min(count, count - steps))
    return lax.ppermute(value, axis, [(source, source + steps) for source in range(leading, last)])


def swapped(value, axis, bits):
    count = lax.axis_size(axis)
    return lax.ppermute(value, axis, [(source, source ^ bits) for source in range(count)])


def join(earlier, later):
    return jnp.concatenate(
        [earlier[0:1] * later[0:1], later[0:1] * earlier[1:2] + later[1:2]], 0
    )


def entering(value, axis, sign):
    count = lax.axis_size(axis)
    if count > 2:
        near = [moved_by(value, axis, sign * reach) for reach in (1, 2, 3) if reach < count]
        total = value
        for one in near:
            total = join(one, total)
        reach = 4
        while 2 * reach < count:
            total = join(moved_by(total, axis, sign * reach), total)
            reach *= 2
        last = moved_by(total, axis, sign)
        if reach + 1 < count:
            last = join(moved_by(total, axis, sign * (reach + 1)), last)
        return last[1:2]
    return moved_by(value, axis, sign)[1:2]


def rms_norm(values, gain):
    return values * lax.rsqrt(jnp.mean(values * values, axis=-1, keepdims=True) + 1e-06) * gain


def nt(left, right):
    return lax.dot_general(left, right, (((1,), (1,)), ((), ())), preferred_element_type=WIDE)


def tn(left, right):
    return lax.dot_general(left, right, (((0,), (0,)), ((), ())), preferred_element_type=WIDE)


def nn(left, right):
    return lax.dot_general(left, right, (((1,), (0,)), ((), ())), preferred_element_type=WIDE)


def sigmoid(value):
    return 0.5 * jnp.tanh(0.5 * value) + 0.5


def gelu_parts(value):
    square = value * value
    bend = jnp.tanh(GELU_SLOPE * value * (1.0 + GELU_CUBE * square))
    half = 0.5 + 0.5 * bend
    slope = half + 0.5 * GELU_SLOPE * value * (1.0 - bend * bend) * (1.0 + 3.0 * GELU_CUBE * square)
    return value * half, slope


def split_low(value):
    high = value.astype(LOW)
    return high, (value - high.astype(WIDE)).astype(LOW)


def loop(count, unroll, body, init):
    while count % unroll:
        unroll -= 1

    def several(index, carry):
        for turn in range(unroll):
            carry = body(index * unroll + turn, carry)
        return carry

    return lax.fori_loop(0, count // unroll, several, init)


def cost(microseconds):
    return pl.CostEstimate(
        flops=int(microseconds * 1.1e9), bytes_accessed=int(microseconds * 3.5e6), transcendentals=0
    )


def fold(value):
    total = value[0:8]
    for group in range(1, value.shape[0] // 8):
        total = total + value[8 * group : 8 * group + 8]
    return total


def mixer_forward_kernel(
    normed, y_weight, u_weight, gates, vec, mask, y_out, u_out, conv_out, r_out, i_out, h_out, f_out,
    sum_out, high, low, zed,
):
    ext = normed.shape[0]
    width = y_out.shape[1]
    count = (ext - RIM) // STEP
    model = normed.shape[1]
    y_out[...] = nt(normed[RIM:, :], y_weight[...].reshape(width, model)) + vec[0:1, :]
    u_out[...] = nt(normed[...], u_weight[...].reshape(width, model)) + vec[1:2, :]

    def convolve(index, _):
        base = pl.multiple_of(index * STEP, STEP)
        own = pl.ds(base, STEP)
        window = u_out[pl.ds(base + 8, STEP + 8), :]
        flags = mask[pl.ds(base + RIM, STEP), :]
        conv = vec[2:3, :] + vec[6:7, :] * window[8:]
        for shift in (1, 2, 3):
            conv = conv + flags[:, shift : shift + 1] * (
                vec[6 + shift : 7 + shift, :] * window[8 - shift : 8 - shift + STEP]
            )
        conv = conv * flags[:, 4:5]
        conv_out[own, :] = conv
        high[own, :], low[own, :] = split_low(conv)
        return 0

    loop(count, 2, convolve, 0)
    zed[...] = nn(high[...], gates[0]) + nn(low[...], gates[0])
    line = lax.broadcasted_iota(jnp.int32, (8, width), 0)

    def advance(index, carry):
        state, factor, total = carry
        own = pl.ds(pl.multiple_of(index * STEP, STEP), STEP)
        going = mask[pl.ds(pl.multiple_of(index * STEP + RIM, STEP), STEP), :][:, 0:1]
        rate = sigmoid(zed[own, 0:width] + vec[3:4, :])
        into = sigmoid(zed[own, width:] + vec[4:5, :])
        decay = jnp.exp(vec[5:6, :] * rate)
        r_out[own, :] = rate
        i_out[own, :] = into
        scale = jnp.where(going == 0.0, 1.0, jnp.sqrt(1.01 - decay * decay))
        inject = conv_out[own, :] * into * scale
        carried = decay * going
        total = total + fold(decay)
        for group in range(STEP // 8):
            part = slice(8 * group, 8 * group + 8)
            mul, add = carried[part], inject[part]
            for reach in (1, 2, 4):
                inside = line >= reach
                add = add + mul * jnp.where(inside, pltpu.roll(add, reach, 0), 0.0)
                mul = mul * jnp.where(inside, pltpu.roll(mul, reach, 0), 1.0)
            here = add + mul * state
            gone = mul * factor
            rows = pl.ds(pl.multiple_of(index * STEP + 8 * group, 8), 8)
            h_out[rows, :] = here
            f_out[rows, :] = gone
            state, factor = here[7:8], gone[7:8]
        return state, factor, total

    zero = jnp.zeros((1, width), WIDE)
    _, _, total = loop(
        count, 2, advance, (zero, zero + 1.0, jnp.zeros((8, width), WIDE))
    )
    sum_out[...] = total


def mixer_forward(normed, slab, gates, vec, mask, rows):
    ext, model = normed.shape
    tokens = ext - RIM
    pairs, width = gates.shape[0], gates.shape[1]
    chans = slab.shape[0]
    group = width // rows
    total = pairs * width
    by_lane = lambda length: pl.BlockSpec((length, width), lambda step: (0, step))
    whole = lambda array: pl.BlockSpec(array.shape, lambda step: (0,) * array.ndim)
    flat = jax.ShapeDtypeStruct((tokens, total), WIDE)
    return pl.pallas_call(
        mixer_forward_kernel,
        grid=(pairs,),
        in_specs=[
            whole(normed),
            pl.BlockSpec((group, rows, model), lambda step: (step, 0, 0)),
            pl.BlockSpec((group, rows, model), lambda step: (step, 1, 0)),
            pl.BlockSpec((1, width, 2 * width), lambda step: (step, 0, 0)),
            by_lane(vec.shape[0]),
            whole(mask),
        ],
        out_specs=[
            by_lane(tokens), by_lane(ext), by_lane(tokens), by_lane(tokens), by_lane(tokens),
            by_lane(tokens), by_lane(tokens), by_lane(8),
        ],
        out_shape=[
            flat, jax.ShapeDtypeStruct((ext, total), WIDE), flat, flat, flat, flat, flat,
            jax.ShapeDtypeStruct((8, total), WIDE),
        ],
        scratch_shapes=[
            pltpu.VMEM((tokens, width), LOW),
            pltpu.VMEM((tokens, width), LOW),
            pltpu.VMEM((tokens, 2 * width), WIDE),
        ],
        compiler_params=params(),
        cost_estimate=cost(30),
        name="mixer_forward",
    )(normed, slab, slab, gates, vec, mask)


def mixer_out_kernel(y, h, f, state, weight, tokens, gain, mixed, middle, normed):
    model = tokens.shape[1]

    def gate(index, _):
        own = pl.ds(pl.multiple_of(index * STEP, STEP), STEP)
        full = h[own, :] + f[own, :] * state[...]
        value = y[own, :]
        bend = jnp.tanh(GELU_SLOPE * value * (1.0 + GELU_CUBE * value * value))
        mixed[own, :] = (full * (value * (0.5 + 0.5 * bend))).astype(LOW)
        return 0

    loop(y.shape[0] // STEP, 2, gate, 0)
    total = tokens[...] + nn(mixed[...], weight[...].reshape(-1, model))
    middle[...] = total
    scale = lax.rsqrt(jnp.mean(total * total, axis=-1, keepdims=True) + 1e-06)
    normed[...] = (total * scale * gain[...]).astype(LOW)


def mixer_out(y, h, f, state, slab, rows, row_index, tokens, gain):
    length, model = tokens.shape
    total = y.shape[1]
    chans = slab.shape[0]
    tile = 128 if length % 128 == 0 else length
    row = lambda lanes: pl.BlockSpec((tile, lanes), lambda step: (step, 0))
    return pl.pallas_call(
        mixer_out_kernel,
        grid=(length // tile,),
        in_specs=[
            row(total), row(total), row(total),
            pl.BlockSpec((1, total), lambda step: (0, 0)),
            pl.BlockSpec((chans, rows, model), lambda step: (0, row_index, 0)),
            row(model),
            pl.BlockSpec((1, model), lambda step: (0, 0)),
        ],
        out_specs=[row(total), row(model), row(model)],
        out_shape=[
            jax.ShapeDtypeStruct((length, total), LOW),
            jax.ShapeDtypeStruct((length, model), WIDE),
            jax.ShapeDtypeStruct((length, model), LOW),
        ],
        compiler_params=params(),
        cost_estimate=cost(9),
        name="mixer_out",
    )(y, h, f, state, slab, tokens, gain)


def spread(place, wide, keep, send, matrix, group, rows, lanes=slice(None)):
    part = rows // 4
    if part % 8:
        value = wide[...]
        pieces = [value[begin : begin + part] for begin in range(0, group * rows, part)]
        mine = place[1] * 4 + place[2]
        bit = 1
        while bit < len(pieces):
            turned = (mine & bit) != 0
            pieces = [
                jnp.where(turned, pieces[index ^ bit], pieces[index])
                for index in range(len(pieces))
            ]
            bit *= 2
    for slot in range(group):
        shard = slot ^ place[1]
        for turn in range(4):
            if part % 8:
                value = pieces[4 * slot + turn]
            else:
                begin = pl.multiple_of(shard * rows + (turn ^ place[2]) * part, 8)
                value = wide[pl.ds(begin, part), :]
            (keep, send)[turn & 1][slot, matrix, turn >> 1, :, lanes] = value.astype(LOW)


def feed_kernel(
    rows, place, normed, cot, w_gate, w_up, w_down, out_in, grad_in, out, grad, keep, send,
    gate_s, up_s, back_s, hidden_l, gate_l, up_l, wide,
):
    model = normed.shape[1]
    width = gate_s.shape[0]
    group = width // rows
    first, second, third = (w[...].reshape(width, model) for w in (w_gate, w_up, w_down))

    @pl.when(pl.program_id(0) == 0)
    def _():
        out[...] = out_in[...]
        grad[...] = grad_in[...]

    gate_s[...] = nt(first, normed[...])
    up_s[...] = nt(second, normed[...])
    back_s[...] = nt(third, cot[...])

    def act(index, _):
        own = pl.ds(pl.multiple_of(index * STEP, STEP), STEP)
        up, back = up_s[own, :], back_s[own, :]
        value, slope = gelu_parts(gate_s[own, :])
        hidden_l[own, :] = (value * up).astype(LOW)
        gate_l[own, :] = (back * up * slope).astype(LOW)
        up_l[own, :] = (back * value).astype(LOW)
        return 0

    loop(width // STEP, 2, act, 0)
    out[...] += tn(hidden_l[...], third)
    grad[...] += tn(gate_l[...], first) + tn(up_l[...], second)
    for matrix, (left, right) in enumerate(((gate_l, normed), (up_l, normed), (hidden_l, cot))):
        wide[...] = nn(left[...], right[...])
        spread(place, wide, keep, send, matrix, group, rows)


def feed(place, normed, cot, slab, rows, group, out_in, grad_in, begin, steps):
    length, model = normed.shape
    width = group * rows
    part = rows // 4
    whole = lambda array: pl.BlockSpec(array.shape, lambda step, place: (0,) * array.ndim)
    weight = lambda index: pl.BlockSpec(
        (group, rows, model), lambda step, place: ((step + begin) ^ place[0], index, 0)
    )
    piece = pl.BlockSpec(
        (group, 3, 2, part, model), lambda step, place: (step, 0, 0, 0, 0)
    )
    slots = steps * group
    return pl.pallas_call(
        functools.partial(feed_kernel, rows),
        grid_spec=pltpu.PrefetchScalarGridSpec(
            num_scalar_prefetch=1,
            grid=(steps,),
            in_specs=[
                whole(normed), whole(cot), weight(0), weight(1), weight(2), whole(out_in),
                whole(grad_in),
            ],
            out_specs=[whole(out_in), whole(grad_in), piece, piece],
            scratch_shapes=[pltpu.VMEM((width, length), WIDE)] * 3
            + [pltpu.VMEM((width, length), LOW)] * 3
            + [pltpu.VMEM((width, model), WIDE)],
        ),
        out_shape=[
            jax.ShapeDtypeStruct((length, model), WIDE),
            jax.ShapeDtypeStruct((length, model), WIDE),
            jax.ShapeDtypeStruct((slots, 3, 2, part, model), LOW),
            jax.ShapeDtypeStruct((slots, 3, 2, part, model), LOW),
        ],
        compiler_params=params(),
        cost_estimate=cost(28),
        name="feed",
    )(place, normed, cot, slab, slab, slab, out_in, grad_in)


def middle_back_kernel(
    middle, grad, cot, gain, weight, y, h, f, state, mid_grad, mid_low, state_grad, y_grad,
    gain_sum, back_sum, bias_sum, mixed_s,
):
    model = middle.shape[1]

    @pl.when(pl.program_id(0) == 0)
    def _():
        gain_sum[...] = jnp.zeros_like(gain_sum)
        back_sum[...] = jnp.zeros_like(back_sum)
        bias_sum[...] = jnp.zeros_like(bias_sum)

    value, error = middle[...], grad[...]
    scale = lax.rsqrt(jnp.mean(value * value, axis=-1, keepdims=True) + 1e-06)
    gained = gain[...] * error
    mean = jnp.mean(gained * value, axis=-1, keepdims=True)
    total = cot[...] + scale * gained - value * (scale * scale * scale * mean)
    gain_sum[...] += fold(error * value * scale)
    mid_grad[...] = total
    mid_low[...] = total.astype(LOW)
    mixed_s[...] = nt(mid_low[...], weight[...].reshape(-1, model))

    def turn(index, carry):
        back, bias = carry
        own = pl.ds(pl.multiple_of(index * STEP, STEP), STEP)
        error = mixed_s[own, :]
        active, slope = gelu_parts(y[own, :])
        gone = f[own, :]
        full = h[own, :] + gone * state[...]
        here = error * active
        state_grad[own, :] = here
        low = (error * full * slope).astype(LOW)
        y_grad[own, :] = low
        return back + fold(here * gone), bias + fold(low.astype(WIDE))

    zero = jnp.zeros(back_sum.shape, WIDE)
    back, bias = loop(middle.shape[0] // STEP, 2, turn, (zero, zero))
    back_sum[...] += back
    bias_sum[...] += bias


def middle_back(middle, grad, cot, gain, slab, rows, row_index, y, h, f, state):
    length, model = middle.shape
    total = y.shape[1]
    chans = slab.shape[0]
    tile = 128 if length % 128 == 0 else length
    row = lambda lanes: pl.BlockSpec((tile, lanes), lambda step: (step, 0))
    one = lambda lines, lanes: pl.BlockSpec((lines, lanes), lambda step: (0, 0))
    return pl.pallas_call(
        middle_back_kernel,
        grid=(length // tile,),
        in_specs=[
            row(model), row(model), row(model), one(1, model),
            pl.BlockSpec((chans, rows, model), lambda step: (0, row_index, 0)),
            row(total), row(total), row(total), one(1, total),
        ],
        out_specs=[
            row(model), row(model), row(total), row(total), one(8, model), one(8, total),
            one(8, total),
        ],
        out_shape=[
            jax.ShapeDtypeStruct((length, model), WIDE),
            jax.ShapeDtypeStruct((length, model), LOW),
            jax.ShapeDtypeStruct((length, total), WIDE),
            jax.ShapeDtypeStruct((length, total), LOW),
            jax.ShapeDtypeStruct((8, model), WIDE),
            jax.ShapeDtypeStruct((8, total), WIDE),
            jax.ShapeDtypeStruct((8, total), WIDE),
        ],
        scratch_shapes=[pltpu.VMEM((tile, total), WIDE)],
        compiler_params=params(),
        cost_estimate=cost(13),
        name="middle_back",
    )(middle, grad, cot, gain, slab, y, h, f, state)


def side_kernel(rows, place, y_grad, mixed, normed, mid, keep, send, wide):
    group = wide.shape[0] // rows
    wide[...] = tn(y_grad[...], normed[RIM:, :])
    spread(place, wide, keep, send, 0, group, rows)
    wide[...] = tn(mixed[...], mid[...])
    spread(place, wide, keep, send, 1, group, rows)


def side_grads(place, y_grad, mixed, normed, mid, rows, width):
    length, total = y_grad.shape
    model = mid.shape[1]
    group, part = width // rows, rows // 4
    whole = lambda array: pl.BlockSpec(array.shape, lambda step, place: (0,) * array.ndim)
    lane = pl.BlockSpec((length, width), lambda step, place: (0, step ^ place[0]))
    piece = pl.BlockSpec((group, 2, 2, part, model), lambda step, place: (step, 0, 0, 0, 0))
    shape = jax.ShapeDtypeStruct((total // rows, 2, 2, part, model), LOW)
    return pl.pallas_call(
        functools.partial(side_kernel, rows),
        grid_spec=pltpu.PrefetchScalarGridSpec(
            num_scalar_prefetch=1,
            grid=(total // width,),
            in_specs=[lane, lane, whole(normed), whole(mid)],
            out_specs=[piece, piece],
            scratch_shapes=[pltpu.VMEM((width, model), WIDE)],
        ),
        out_shape=[shape, shape],
        compiler_params=params(),
        cost_estimate=cost(9),
        name="side_grads",
    )(place, y_grad, mixed, normed, mid)


def mixer_back_kernel(
    rows, place, state_grad, r_in, i_in, conv_in, h, f, u, y_grad, y_weight, u_weight, gates, vec,
    mask, state, after, normed, grad_in, keep, send, sums, normed_grad,
    conv_s, high, low, conv_h, conv_l, grown, u_low, wide, gate_w,
):
    length, width = state_grad.shape
    ext, model = normed.shape
    group = width // rows
    block = width // 2
    count = length // STEP
    line = lax.broadcasted_iota(jnp.int32, (8, width), 0)

    @pl.when(pl.program_id(0) == 0)
    def _():
        normed_grad[...] = grad_in[...]

    def retreat(index, carry):
        error, rate_sum, into_sum, slope_sum = carry
        base = pl.multiple_of((count - 1 - index) * STEP, STEP)
        own = pl.ds(base, STEP)
        going = mask[pl.ds(base + RIM, STEP), :][:, 0:1]
        rate, into, conv = r_in[own, :], i_in[own, :], conv_in[own, :]
        slope = vec[5:6, :]
        decay = jnp.exp(slope * rate)
        carried = decay * going
        given = state_grad[own, :]
        full = h[own, :] + f[own, :] * state[...]
        ahead = pl.ds(pl.multiple_of(jnp.maximum(base - 8, 0), 8), 8)
        edge = h[ahead, :][7:8] + f[ahead, :][7:8] * state[...]
        edge = jnp.where(base == 0, state[...], edge)
        parts = []
        for part in reversed(range(STEP // 8)):
            place_of = slice(8 * part, 8 * part + 8)
            mul = carried[place_of]
            add = mul * given[place_of]
            for reach in (1, 2, 4):
                inside = line < 8 - reach
                add = add + mul * jnp.where(inside, pltpu.roll(add, 8 - reach, 0), 0.0)
                mul = mul * jnp.where(inside, pltpu.roll(mul, 8 - reach, 0), 1.0)
            here = add + mul * error
            parts.append(given[place_of] + jnp.where(line < 7, pltpu.roll(here, 7, 0), error))
            error = here[0:1]
        grad = jnp.concatenate(parts[::-1], 0)
        befores = []
        for part in range(STEP // 8):
            last = edge if part == 0 else full[8 * part - 1 : 8 * part]
            befores.append(
                jnp.where(line > 0, pltpu.roll(full[8 * part : 8 * part + 8], 1, 0), last)
            )
        before = jnp.concatenate(befores, 0)
        root = lax.rsqrt(1.01 - decay * decay)
        scale = jnp.where(going == 0.0, 1.0, (1.01 - decay * decay) * root)
        through = grad * conv
        into_grad = through * scale
        conv_s[own, :] = grad * into * scale
        decay_grad = going * decay * (grad * before - through * into * decay * root)
        z_rate = decay_grad * slope * rate * (1.0 - rate)
        z_into = into_grad * into * (1.0 - into)
        high[own, 0:width], low[own, 0:width] = split_low(z_rate)
        high[own, width:], low[own, width:] = split_low(z_into)
        conv_h[own, :], conv_l[own, :] = split_low(conv)
        return (
            error,
            rate_sum + fold(z_rate),
            into_sum + fold(z_into),
            slope_sum + fold(decay_grad * rate),
        )

    zero = jnp.zeros((8, width), WIDE)
    _, rate_sum, into_sum, slope_sum = loop(
        count, 2, retreat, (after[...], zero, zero, zero)
    )
    conv_s[...] += nt(high[...], gates[0]) + nt(low[...], gates[0])
    gate_full = (
        tn(conv_h[...], high[...]) + tn(conv_l[...], high[...]) + tn(conv_h[...], low[...])
    )
    for half in (0, block):
        rows_of = slice(half, half + block)
        gate_w[rows_of, 0:block] = gate_full[rows_of, half : half + block]
        gate_w[rows_of, block:] = gate_full[rows_of, width + half : width + half + block]
    grown[0:RIM, :] = jnp.zeros((RIM, width), WIDE)
    grown[RIM + length :, :] = jnp.zeros((RIM, width), WIDE)

    def taps(index, carry):
        base = pl.multiple_of(index * STEP, STEP)
        window = u[pl.ds(base + 8, STEP + 8), :]
        flags = mask[pl.ds(base + RIM, STEP), :]
        error = conv_s[pl.ds(base, STEP), :] * flags[:, 4:5]
        grown[pl.ds(base + RIM, STEP), :] = error
        out = [carry[0] + fold(error), carry[1] + fold(error * window[8:])]
        for shift in (1, 2, 3):
            moved = window[8 - shift : 8 - shift + STEP]
            out.append(carry[1 + shift] + fold(flags[:, shift : shift + 1] * error * moved))
        return tuple(out)

    bias_sum, *tap_sums = loop(count, 2, taps, (zero,) * 5)

    def spread_back(index, total):
        base = pl.multiple_of(index * STEP, STEP)
        window = grown[pl.ds(base, STEP + 8), :]
        flags = mask[pl.ds(base, STEP + 8), :]
        value = vec[6:7, :] * window[0:STEP]
        for shift in (1, 2, 3):
            masked = flags[:, shift : shift + 1] * window
            value = value + vec[6 + shift : 7 + shift, :] * masked[shift : shift + STEP]
        rounded = value.astype(LOW)
        u_low[pl.ds(base, STEP), :] = rounded
        return total + fold(rounded.astype(WIDE))

    input_sum = loop(ext // STEP, 3, spread_back, zero)
    for row, value in enumerate((input_sum, bias_sum, rate_sum, into_sum, slope_sum, *tap_sums)):
        sums[0, row : row + 1, :] = jnp.sum(value, axis=0, keepdims=True)
    sums[0, 9:16, :] = jnp.zeros((7, width), WIDE)
    wide[...] = tn(u_low[...], normed[...])
    spread(place, wide, keep, send, 0, group, rows, slice(0, model))
    spread(place, gate_w, keep, send, 0, group, rows, slice(model, model + width))
    normed_grad[...] += nn(u_low[...], u_weight[...].reshape(width, model))
    normed_grad[RIM:, :] += nn(y_grad[...], y_weight[...].reshape(width, model))


def mixer_back(
    place, state_grad, r, i, conv, h, f, u, y_grad, slab, gates, vec, mask, state, after, normed,
    grad_in, rows, begin, steps,
):
    length, total = state_grad.shape
    ext, model = normed.shape
    width = gates.shape[1]
    group, part = width // rows, rows // 4
    pair = lambda step, place: (step + begin) ^ place[0]
    whole = lambda array: pl.BlockSpec(array.shape, lambda step, place: (0,) * array.ndim)
    lane = lambda lines: pl.BlockSpec((lines, width), lambda step, place: (0, pair(step, place)))
    weight = lambda index: pl.BlockSpec(
        (group, rows, model), lambda step, place: (pair(step, place), index, 0)
    )
    lanes = model + width
    piece = pl.BlockSpec((group, 1, 2, part, lanes), lambda step, place: (step, 0, 0, 0, 0))
    shape = jax.ShapeDtypeStruct((steps * group, 1, 2, part, lanes), LOW)
    return pl.pallas_call(
        functools.partial(mixer_back_kernel, rows),
        grid_spec=pltpu.PrefetchScalarGridSpec(
            num_scalar_prefetch=1,
            grid=(steps,),
            in_specs=[
                lane(length), lane(length), lane(length), lane(length), lane(length),
                lane(length), lane(ext), lane(length), weight(0), weight(1),
                pl.BlockSpec(
                    (1, width, 2 * width), lambda step, place: (pair(step, place), 0, 0)
                ),
                lane(vec.shape[0]), whole(mask), lane(1), lane(1), whole(normed), whole(grad_in),
            ],
            out_specs=[
                piece, piece,
                pl.BlockSpec((1, 16, width), lambda step, place: (step, 0, 0)),
                whole(grad_in),
            ],
            scratch_shapes=[
                pltpu.VMEM((length, width), WIDE),
                pltpu.VMEM((length, 2 * width), LOW),
                pltpu.VMEM((length, 2 * width), LOW),
                pltpu.VMEM((length, width), LOW),
                pltpu.VMEM((length, width), LOW),
                pltpu.VMEM((ext + RIM, width), WIDE),
                pltpu.VMEM((ext, width), LOW),
                pltpu.VMEM((width, model), WIDE),
                pltpu.VMEM((width, width), WIDE),
            ],
        ),
        out_shape=[
            shape, shape,
            jax.ShapeDtypeStruct((steps, 16, width), WIDE),
            jax.ShapeDtypeStruct((ext, model), WIDE),
        ],
        compiler_params=params(),
        cost_estimate=cost(13 * steps),
        name="mixer_back",
    )(
        place, state_grad, r, i, conv, h, f, u, y_grad, slab, slab, gates, vec, mask, state, after,
        normed, grad_in,
    )


def wide_of(value):
    return value.astype(WIDE)


class Sums:
    def __init__(self, stages):
        self.stages = stages
        self.moving = next(stages)
        self.result = None

    def step(self):
        try:
            self.moving = self.stages.send(self.moving)
        except StopIteration as end:
            self.moving = []
            self.result = end.value

    def finish(self):
        while self.result is None:
            self.step()
        return self.result


def fence(arrays, *groups):
    arrays, moving = lax.optimization_barrier((arrays, [group.moving for group in groups]))
    for group, came in zip(groups, moving):
        group.moving = came
    return arrays


def owned(keep, send, begin):
    slots, matrices, _, part, lanes = keep.shape
    shape = (slots // 2, 2, matrices, 2, part, lanes)
    keep = keep.reshape(shape)
    (came,) = yield [swapped(send, "rows", 1)]
    came = came.reshape(shape)
    even, odd = slice(begin % 2, None, 2), slice((1 - begin) % 2, None, 2)
    sum_of = lambda where: wide_of(keep[where]) + wide_of(came[where])
    rest, also = yield [
        swapped(sum_of((even, slice(None), slice(None), 1)).astype(LOW), "rows", 2),
        swapped(sum_of((odd, 1)).astype(LOW), "chan", 1),
    ]
    rest = sum_of((even, slice(None), slice(None), 0)) + wide_of(rest)
    also = sum_of((odd, 0)) + wide_of(also)
    came, came_also = yield [
        swapped(rest[:, 1].astype(LOW), "chan", 1),
        swapped(also[:, :, 1].astype(LOW), "rows", 2),
    ]
    rest = rest[:, 0] + wide_of(came)
    also = also[:, :, 0] + wide_of(came_also)
    parts = {}
    for index in range(rest.shape[0]):
        parts[begin + begin % 2 + 2 * index] = rest[index]
    for index in range(also.shape[0]):
        parts[begin + 1 - begin % 2 + 2 * index] = also[index]
    came = yield [
        swapped(value.astype(LOW), "chan", 2 * distance)
        for distance, value in parts.items() if distance
    ]
    values = [wide_of(value) for value in came]
    if 0 in parts:
        values.append(parts[0])
    return functools.reduce(jnp.add, values)


def settled(total):
    total = total.astype(LOW)
    (came,) = yield [swapped(total, "rows", 1)]
    pair = jnp.stack([total, came])
    (came,) = yield [swapped(pair, "rows", 2)]
    four = jnp.stack([pair, came])
    place = lax.axis_index("rows")
    four = jnp.where(place & 1, four[:, ::-1], four)
    four = jnp.where(place & 2, four[::-1], four)
    _, _, matrices, part, lanes = four.shape
    four = four.reshape(4, matrices, part, lanes).transpose(1, 0, 2, 3)
    return four.reshape(matrices, 4 * part, lanes).astype(WIDE)


def summed_everywhere(value):
    for axis in ("rows", "chan"):
        bits = 1
        while bits < lax.axis_size(axis):
            value = value + swapped(value, axis, bits)
            bits *= 2
    return value


def gathered(piece):
    parts = lax.axis_size("rows")
    share = piece.shape[0] // parts
    own = lax.dynamic_slice_in_dim(piece, lax.axis_index("rows") * share, share)
    full = lax.all_gather(own, ("chan", "rows"), axis=0, tiled=True)
    return full.reshape(lax.axis_size("chan"), piece.shape[0], piece.shape[1])


def local(
    tokens, segments, gelu_weight, gelu_bias, input_weight, input_bias, conv_taps, conv_bias,
    decay_gate, decay_bias, input_gate, ingate_bias, decay_param, out_weight, mixer_gain,
    gate_weight, up_weight, down_weight, feed_gain, cotangent,
):
    length, model = tokens.shape
    rim = conv_taps.shape[0] - 1
    chans = lax.axis_size("chan")
    me, row_place = lax.axis_index("chan"), lax.axis_index("rows")
    rows, block = decay_gate.shape
    feed_rows = gate_weight.shape[1]
    total = rows * chans
    width = 2 * block
    group = width // rows
    feed_group = max(1, width // feed_rows)

    padded = jnp.concatenate([jnp.full((rim,), -1, jnp.int32), segments])
    window = lax.dynamic_slice_in_dim(padded, me * length, length + rim)
    own = window[rim:]
    same = [own == window[rim - shift : rim - shift + length] for shift in range(1, rim + 1)]
    mask = jnp.stack([same[0], *same, own != 0] + [same[0]] * (7 - rim - 1), 1).astype(WIDE)
    mask = jnp.pad(mask, ((RIM, RIM), (0, 0)))

    small = jnp.concatenate(
        [
            jnp.stack([gelu_bias, input_bias, conv_bias, decay_bias, ingate_bias, decay_param]),
            conv_taps,
        ]
    )
    gate_rows = 2 * rows * block // model
    slab_rows = -(-(2 * rows + gate_rows + -(-small.size // model)) // 32) * 32
    small_rows = slab_rows - 2 * rows - gate_rows
    packed = jnp.pad(small.reshape(-1), (0, small_rows * model - small.size))
    slab = gathered(
        jnp.concatenate(
            [
                gelu_weight.T,
                input_weight.T,
                jnp.concatenate([decay_gate, input_gate], 1).reshape(gate_rows, model),
                packed.reshape(small_rows, model),
            ]
        )
    )
    late = gathered(jnp.concatenate([gate_weight.T, up_weight.T, down_weight, out_weight]))
    out_index = 3 * feed_rows // rows

    both = slab[:, 2 * rows : 2 * rows + gate_rows].reshape(total, 2 * block)
    both = both.reshape(total // width, 2, block, 2, block)
    none = jnp.zeros(both.shape[:1] + (block, block), LOW)
    gates = jnp.concatenate(
        [
            jnp.concatenate([both[:, 0, :, 0], none, both[:, 0, :, 1], none], 2),
            jnp.concatenate([none, both[:, 1, :, 0], none, both[:, 1, :, 1]], 2),
        ],
        1,
    )
    small_full = slab[:, 2 * rows + gate_rows :].reshape(chans, -1)[:, : small.size]
    small_full = small_full.reshape(chans, small.shape[0], rows).transpose(1, 0, 2)
    small_full = small_full.reshape(small.shape[0], total).astype(WIDE)
    param = small_full[5:6]
    vec = jnp.concatenate(
        [small_full[:5], -8.0 * jax.nn.softplus(param), small_full[6:], jnp.zeros((6, total), WIDE)]
    )

    rim_tokens = moved_by(tokens[length - rim :], "chan", 1)
    extended = jnp.concatenate([jnp.zeros((RIM - rim, model), WIDE), rim_tokens, tokens])
    normed = rms_norm(extended, mixer_gain).astype(LOW)
    y, u, conv, rate, into, state, factor, decay_sum = mixer_forward(
        normed, slab, gates, vec, mask, rows
    )
    carry = entering(jnp.concatenate([factor[-1:], state[-1:]]), "chan", 1)
    mixed, middle, normed2 = mixer_out(
        y, state, factor, carry, late, rows, out_index, tokens, feed_gain[None]
    )
    cot_low = cotangent.astype(LOW)
    low_bits = feed_group - 1
    place = jnp.stack([me // feed_group, me & low_bits, row_place]).astype(jnp.int32)
    steps = chans // feed_group // 2
    block_output, normed2_grad, keep, send = feed(
        place, normed2, cot_low, late, feed_rows, feed_group, middle,
        jnp.zeros_like(middle), steps, steps,
    )
    far = Sums(owned(keep, send, steps * feed_group // 2))
    block_output, normed2_grad, keep, send = feed(
        place, normed2, cot_low, late, feed_rows, feed_group, block_output, normed2_grad, 0, steps,
    )
    near = Sums(owned(keep, send, 0))

    normed2_grad = fence(normed2_grad, far)
    far.step()
    mid_grad, mid_low, state_grad, y_grad, feed_gain_sum, back_sum, y_sum = middle_back(
        middle, normed2_grad, cotangent, feed_gain[None], late, rows, out_index, y, state, factor,
        carry,
    )
    after = entering(
        jnp.concatenate([factor[-1:], jnp.sum(back_sum, 0, keepdims=True)]), "chan", -1
    )
    place = jnp.stack([me // group, me % group, row_place]).astype(jnp.int32)
    y_grad = fence(y_grad, near)
    near.step()
    keep, send = side_grads(place, y_grad, mixed, normed, mid_low, rows, width)
    side = Sums(owned(keep, send, 0))
    after = fence(after, far)
    far.step()
    steps = total // width // 2
    back = lambda after, grad_in, begin: mixer_back(
        place, state_grad, rate, into, conv, state, factor, u, y_grad, slab, gates, vec, mask,
        carry, after, normed, grad_in, rows, begin, steps,
    )
    keep, send, sums_far, normed_grad = back(after, jnp.zeros(normed.shape, WIDE), steps)
    input_far = Sums(owned(keep, send, steps * group // 2))
    normed_grad = fence(normed_grad, near, far, side)
    near.step()
    far.step()
    side.step()
    keep, send, sums_near, normed_grad = back(after, normed_grad, 0)
    input_near = Sums(owned(keep, send, 0))
    sums = jnp.concatenate([sums_near, sums_far])
    moved = jnp.arange(2 * steps) ^ place[0]
    sums = sums[moved].transpose(1, 0, 2).reshape(16, total)
    side.step()
    normed_grad = fence(normed_grad, input_far)
    input_far.step()
    feed_total = near.finish() + far.finish()
    feed_sum = Sums(settled(feed_total)).finish()
    side_sum = Sums(settled(side.finish())).finish()
    input_sum = Sums(settled(input_far.finish() + input_near.finish())).finish()[0]
    input_sum, gates_sum = input_sum[:, :model], input_sum[:, model:]
    rim_grad = moved_by(normed_grad[RIM - rim : RIM], "chan", -1)
    error = normed_grad[RIM:] + jnp.concatenate([jnp.zeros((length - rim, model), WIDE), rim_grad])
    scale = lax.rsqrt(jnp.mean(tokens * tokens, axis=-1, keepdims=True) + 1e-06)
    gained = mixer_gain * error
    mean = jnp.mean(gained * tokens, axis=-1, keepdims=True)
    tokens_grad = mid_grad + scale * gained - tokens * (scale * scale * scale * mean)
    mixer_gain_sum = jnp.sum(error * tokens * scale, 0)

    slope_grad = sums[4:5] * (-8.0 * jax.nn.sigmoid(param))
    lines = jnp.concatenate(
        [jnp.sum(y_sum, 0, keepdims=True), sums[:4], slope_grad, sums[5:9],
         jnp.sum(decay_sum, 0, keepdims=True)]
    )
    gains = jnp.stack([mixer_gain_sum, jnp.sum(feed_gain_sum, 0)])
    everything = summed_everywhere(
        jnp.concatenate([lines.reshape(-1, 128), gains.reshape(-1, 128)])
    )
    cut = lines.size // 128
    gains = everything[cut:].reshape(2, model)
    lines = lax.dynamic_slice_in_dim(
        everything[:cut].reshape(lines.shape), me * rows, rows, axis=1
    )
    mean_decay = lines[10] / (length * lax.axis_size("rows") * chans)
    return (
        block_output,
        tokens_grad,
        side_sum[0].T,
        lines[0],
        input_sum.T,
        lines[1],
        lines[6:10],
        lines[2],
        gates_sum[:, :block],
        lines[3],
        gates_sum[:, block:],
        lines[4],
        lines[5],
        side_sum[1],
        gains[0],
        feed_sum[0].T,
        feed_sum[1].T,
        feed_sum[2],
        gains[1],
        mean_decay,
    )


def solution(mesh):
    return jax.shard_map(
        local,
        mesh=mesh,
        in_specs=(
            P(("rows", "chan"), None),
            P("rows"),
            P(None, "chan"),
            P("chan"),
            P(None, "chan"),
            P("chan"),
            P(None, "chan"),
            P("chan"),
            P("chan", None),
            P("chan"),
            P("chan", None),
            P("chan"),
            P("chan"),
            P("chan", None),
            P(),
            P(None, "chan"),
            P(None, "chan"),
            P("chan", None),
            P(),
            P(("rows", "chan"), None),
        ),
        out_specs=(
            P(("rows", "chan"), None),
            P(("rows", "chan"), None),
            P(None, "chan"),
            P("chan"),
            P(None, "chan"),
            P("chan"),
            P(None, "chan"),
            P("chan"),
            P("chan", None),
            P("chan"),
            P("chan", None),
            P("chan"),
            P("chan"),
            P("chan", None),
            P(),
            P(None, "chan"),
            P(None, "chan"),
            P("chan", None),
            P(),
            P("chan"),
        ),
        check_vma=False,
    )
```

```python
import functools

import jax
import jax.numpy as jnp
from jax import lax
from jax.experimental import pallas as pl
from jax.experimental.pallas import tpu as pltpu
from jax.sharding import PartitionSpec as P

LOW = jnp.bfloat16
WIDE = jnp.float32
RIM = 16
STEP = 16
VMEM_BYTES = 56 * 1024 * 1024
GELU_SLOPE = 0.7978845608028654
GELU_CUBE = 0.044715


def params(**more):
    return pltpu.CompilerParams(vmem_limit_bytes=VMEM_BYTES, **more)


def moved_by(value, axis, steps):
    count = lax.axis_size(axis)
    leading, last = (max(0, -steps), min(count, count - steps))
    return lax.ppermute(value, axis, [(source, source + steps) for source in range(leading, last)])


def swapped(value, axis, bits):
    count = lax.axis_size(axis)
    return lax.ppermute(value, axis, [(source, source ^ bits) for source in range(count)])


def join(earlier, later):
    return jnp.concatenate(
        [earlier[0:1] * later[0:1], later[0:1] * earlier[1:2] + later[1:2]], 0
    )


def entering(value, axis, sign):
    count = lax.axis_size(axis)
    if count > 2:
        near = [moved_by(value, axis, sign * reach) for reach in (1, 2, 3) if reach < count]
        total = value
        for one in near:
            total = join(one, total)
        reach = 4
        while 2 * reach < count:
            total = join(moved_by(total, axis, sign * reach), total)
            reach *= 2
        last = moved_by(total, axis, sign)
        if reach + 1 < count:
            last = join(moved_by(total, axis, sign * (reach + 1)), last)
        return last[1:2]
    return moved_by(value, axis, sign)[1:2]


def rms_norm(values, gain):
    return values * lax.rsqrt(jnp.mean(values * values, axis=-1, keepdims=True) + 1e-06) * gain


def nt(left, right):
    return lax.dot_general(left, right, (((1,), (1,)), ((), ())), preferred_element_type=WIDE)


def tn(left, right):
    return lax.dot_general(left, right, (((0,), (0,)), ((), ())), preferred_element_type=WIDE)


def nn(left, right):
    return lax.dot_general(left, right, (((1,), (0,)), ((), ())), preferred_element_type=WIDE)


def sigmoid(value):
    return 0.5 * jnp.tanh(0.5 * value) + 0.5


def gelu_parts(value):
    square = value * value
    bend = jnp.tanh(GELU_SLOPE * value * (1.0 + GELU_CUBE * square))
    half = 0.5 + 0.5 * bend
    slope = half + 0.5 * GELU_SLOPE * value * (1.0 - bend * bend) * (1.0 + 3.0 * GELU_CUBE * square)
    return value * half, slope


def split_low(value):
    high = value.astype(LOW)
    return high, (value - high.astype(WIDE)).astype(LOW)


def loop(count, unroll, body, init):
    while count % unroll:
        unroll -= 1

    def several(index, carry):
        for turn in range(unroll):
            carry = body(index * unroll + turn, carry)
        return carry

    return lax.fori_loop(0, count // unroll, several, init)


def cost(microseconds):
    return pl.CostEstimate(
        flops=int(microseconds * 1.1e9), bytes_accessed=int(microseconds * 3.5e6), transcendentals=0
    )


def fold(value):
    total = value[0:8]
    for group in range(1, value.shape[0] // 8):
        total = total + value[8 * group : 8 * group + 8]
    return total


def fill_gates(packed, gates, rows, block):
    width = 2 * block

    @pl.when(pl.program_id(0) == 0)
    def _():
        gates[...] = jnp.zeros_like(gates)

    kind = LOW if rows % 32 == 0 else WIDE
    lines = []
    for slot in range(packed.shape[0]):
        value = packed[slot].astype(kind)
        lines += [value[:, 0:width], value[:, 512 : 512 + width]]
    lines = jnp.concatenate(lines, 0).astype(LOW)
    for half in (0, block):
        gates[half : half + block, half : half + block] = lines[half : half + block, 0:block]
        gates[half : half + block, width + half : width + half + block] = lines[
            half : half + block, block:
        ]


def mixer_forward_kernel(
    rows, normed, y_weight, u_weight, packed, vec, mask, y_out, u_out, conv_out, r_out, i_out,
    h_out, f_out, sum_out, high, low, zed, gates,
):
    fill_gates(packed, gates, rows, y_out.shape[1] // 2)
    ext = normed.shape[0]
    width = y_out.shape[1]
    count = (ext - RIM) // STEP
    model = normed.shape[1]
    y_out[...] = nt(normed[RIM:, :], y_weight[...].reshape(width, model)) + vec[0:1, :]
    u_out[...] = nt(normed[...], u_weight[...].reshape(width, model)) + vec[1:2, :]

    def convolve(index, _):
        base = pl.multiple_of(index * STEP, STEP)
        own = pl.ds(base, STEP)
        window = u_out[pl.ds(base + 8, STEP + 8), :]
        flags = mask[pl.ds(base + RIM, STEP), :]
        conv = vec[2:3, :] + vec[6:7, :] * window[8:]
        for shift in (1, 2, 3):
            conv = conv + flags[:, shift : shift + 1] * (
                vec[6 + shift : 7 + shift, :] * window[8 - shift : 8 - shift + STEP]
            )
        conv = conv * flags[:, 4:5]
        conv_out[own, :] = conv
        high[own, :], low[own, :] = split_low(conv)
        return 0

    loop(count, 2, convolve, 0)
    zed[...] = nn(high[...], gates[...]) + nn(low[...], gates[...])
    line = lax.broadcasted_iota(jnp.int32, (8, width), 0)

    def advance(index, carry):
        state, factor, total = carry
        own = pl.ds(pl.multiple_of(index * STEP, STEP), STEP)
        going = mask[pl.ds(pl.multiple_of(index * STEP + RIM, STEP), STEP), :][:, 0:1]
        rate = sigmoid(zed[own, 0:width] + vec[3:4, :])
        into = sigmoid(zed[own, width:] + vec[4:5, :])
        decay = jnp.exp(vec[5:6, :] * rate)
        r_out[own, :] = rate
        i_out[own, :] = into
        scale = jnp.where(going == 0.0, 1.0, jnp.sqrt(1.01 - decay * decay))
        inject = conv_out[own, :] * into * scale
        carried = decay * going
        total = total + fold(decay)
        for group in range(STEP // 8):
            part = slice(8 * group, 8 * group + 8)
            mul, add = carried[part], inject[part]
            for reach in (1, 2, 4):
                inside = line >= reach
                add = add + mul * jnp.where(inside, pltpu.roll(add, reach, 0), 0.0)
                mul = mul * jnp.where(inside, pltpu.roll(mul, reach, 0), 1.0)
            here = add + mul * state
            gone = mul * factor
            rows = pl.ds(pl.multiple_of(index * STEP + 8 * group, 8), 8)
            h_out[rows, :] = here
            f_out[rows, :] = gone
            state, factor = here[7:8], gone[7:8]
        return state, factor, total

    zero = jnp.zeros((1, width), WIDE)
    _, _, total = loop(
        count, 2, advance, (zero, zero + 1.0, jnp.zeros((8, width), WIDE))
    )
    sum_out[...] = total


def mixer_forward(normed, slab, vec, mask, rows, width):
    ext, model = normed.shape
    tokens = ext - RIM
    chans = slab.shape[0]
    group = width // rows
    pairs = chans // group
    total = pairs * width
    by_lane = lambda length: pl.BlockSpec((length, width), lambda step: (0, step))
    whole = lambda array: pl.BlockSpec(array.shape, lambda step: (0,) * array.ndim)
    flat = jax.ShapeDtypeStruct((tokens, total), WIDE)
    return pl.pallas_call(
        functools.partial(mixer_forward_kernel, rows),
        grid=(pairs,),
        in_specs=[
            whole(normed),
            pl.BlockSpec((group, rows, model), lambda step: (step, 0, 0)),
            pl.BlockSpec((group, rows, model), lambda step: (step, 1, 0)),
            pl.BlockSpec((group, rows // 2, model), lambda step: (step, 4, 0)),
            by_lane(vec.shape[0]),
            whole(mask),
        ],
        out_specs=[
            by_lane(tokens), by_lane(ext), by_lane(tokens), by_lane(tokens), by_lane(tokens),
            by_lane(tokens), by_lane(tokens), by_lane(8),
        ],
        out_shape=[
            flat, jax.ShapeDtypeStruct((ext, total), WIDE), flat, flat, flat, flat, flat,
            jax.ShapeDtypeStruct((8, total), WIDE),
        ],
        scratch_shapes=[
            pltpu.VMEM((tokens, width), LOW),
            pltpu.VMEM((tokens, width), LOW),
            pltpu.VMEM((tokens, 2 * width), WIDE),
            pltpu.VMEM((width, 2 * width), LOW),
        ],
        compiler_params=params(),
        cost_estimate=cost(30),
        name="mixer_forward",
    )(normed, slab, slab, slab, vec, mask)


def mixer_out_kernel(y, h, f, state, weight, tokens, gain, mixed, middle, normed):
    model = tokens.shape[1]

    def gate(index, _):
        own = pl.ds(pl.multiple_of(index * STEP, STEP), STEP)
        full = h[own, :] + f[own, :] * state[...]
        value = y[own, :]
        bend = jnp.tanh(GELU_SLOPE * value * (1.0 + GELU_CUBE * value * value))
        mixed[own, :] = (full * (value * (0.5 + 0.5 * bend))).astype(LOW)
        return 0

    loop(y.shape[0] // STEP, 2, gate, 0)
    total = tokens[...] + nn(mixed[...], weight[...].reshape(-1, model))
    middle[...] = total
    scale = lax.rsqrt(jnp.mean(total * total, axis=-1, keepdims=True) + 1e-06)
    normed[...] = (total * scale * gain[...]).astype(LOW)


def mixer_out(y, h, f, state, slab, rows, row_index, tokens, gain):
    length, model = tokens.shape
    total = y.shape[1]
    chans = slab.shape[0]
    tile = 128 if length % 128 == 0 else length
    row = lambda lanes: pl.BlockSpec((tile, lanes), lambda step: (step, 0))
    return pl.pallas_call(
        mixer_out_kernel,
        grid=(length // tile,),
        in_specs=[
            row(total), row(total), row(total),
            pl.BlockSpec((1, total), lambda step: (0, 0)),
            pl.BlockSpec((chans, rows, model), lambda step: (0, row_index, 0)),
            row(model),
            pl.BlockSpec((1, model), lambda step: (0, 0)),
        ],
        out_specs=[row(total), row(model), row(model)],
        out_shape=[
            jax.ShapeDtypeStruct((length, total), LOW),
            jax.ShapeDtypeStruct((length, model), WIDE),
            jax.ShapeDtypeStruct((length, model), LOW),
        ],
        compiler_params=params(),
        cost_estimate=cost(9),
        name="mixer_out",
    )(y, h, f, state, slab, tokens, gain)


def spread(place, wide, keep, send, matrix, group, rows, lanes=slice(None)):
    part = rows // 4
    if part % 8:
        value = wide[...]
        pieces = [value[begin : begin + part] for begin in range(0, group * rows, part)]
        mine = place[1] * 4 + place[2]
        bit = 1
        while bit < len(pieces):
            turned = (mine & bit) != 0
            pieces = [
                jnp.where(turned, pieces[index ^ bit], pieces[index])
                for index in range(len(pieces))
            ]
            bit *= 2
    for slot in range(group):
        shard = slot ^ place[1]
        for turn in range(4):
            if part % 8:
                value = pieces[4 * slot + turn]
            else:
                begin = pl.multiple_of(shard * rows + (turn ^ place[2]) * part, 8)
                value = wide[pl.ds(begin, part), :]
            (keep, send)[turn & 1][slot, matrix, turn >> 1, :, lanes] = value.astype(LOW)


def feed_kernel(
    pairs, normed, cot, out_in, *refs
):
    near, far = refs[:pairs], refs[pairs : 2 * pairs]
    out, grad, keep, send, gate_s, up_s, back_s, hidden_l, gate_l, up_l, held, sems = refs[2 * pairs :]
    model = normed.shape[1]
    width = gate_s.shape[0]
    part = width // 4
    step = pl.program_id(0)

    def copies(index, slot):
        for turn in range(4):
            source = (near, far)[turn // 2][index // 2]
            yield pltpu.make_async_copy(
                source.at[turn % 2, index % 2],
                held.at[slot, :, turn],
                sems.at[slot, turn],
            )

    @pl.when(step == 0)
    def _():
        out[...] = out_in[...]
        grad[...] = jnp.zeros_like(grad)
        for copy in copies(0, 0):
            copy.start()

    for index in range(1, 2 * pairs):

        @pl.when(step + 1 == index)
        def _():
            for copy in copies(index, index % 2):
                copy.start()

    for index in range(2 * pairs):

        @pl.when(step == index)
        def _():
            for copy in copies(index, index % 2):
                copy.wait()

    def weight(matrix):
        if part % 16 == 0:
            return held[step % 2, matrix].reshape(width, model)
        pieces = [held[step % 2, matrix, turn].astype(WIDE) for turn in range(4)]
        return jnp.concatenate(pieces, 0).astype(LOW)

    first, second, third = weight(0), weight(1), weight(2)
    gate_s[...] = nt(first, normed[...])
    up_s[...] = nt(second, normed[...])
    back_s[...] = nt(third, cot[...])

    def act(index, _):
        own = pl.ds(pl.multiple_of(index * STEP, STEP), STEP)
        up, back = up_s[own, :], back_s[own, :]
        value, slope = gelu_parts(gate_s[own, :])
        hidden_l[own, :] = (value * up).astype(LOW)
        gate_l[own, :] = (back * up * slope).astype(LOW)
        up_l[own, :] = (back * value).astype(LOW)
        return 0

    loop(width // STEP, 2, act, 0)
    out[...] += tn(hidden_l[...], third)
    grad[...] += tn(gate_l[...], first) + tn(up_l[...], second)
    for matrix, (left, right) in enumerate(((gate_l, normed), (up_l, normed), (hidden_l, cot))):
        for half, target in enumerate((keep, send)):
            value = nn(left[...][2 * half * part : 2 * (half + 1) * part], right[...]).astype(LOW)
            target[0, matrix, 0] = value[:part]
            target[0, matrix, 1] = value[part:]


def feed(normed, cot, out_in, near, far):
    length, model = normed.shape
    pairs = len(near)
    part = near[0].shape[3]
    width = 4 * part
    whole = lambda array: pl.BlockSpec(array.shape, lambda step: (0,) * array.ndim)
    piece = pl.BlockSpec((1, 3, 2, part, model), lambda step: (step, 0, 0, 0, 0))
    wide = jax.ShapeDtypeStruct((length, model), WIDE)
    grads = jax.ShapeDtypeStruct((2 * pairs, 3, 2, part, model), LOW)
    return pl.pallas_call(
        functools.partial(feed_kernel, pairs),
        grid=(2 * pairs,),
        in_specs=[whole(normed), whole(cot), whole(out_in)]
        + [pl.BlockSpec(memory_space=pl.ANY)] * (2 * pairs),
        out_specs=[whole(out_in), whole(out_in), piece, piece],
        scratch_shapes=[pltpu.VMEM((width, length), WIDE)] * 3
        + [pltpu.VMEM((width, length), LOW)] * 3
        + [pltpu.VMEM((2, 3, 4, part, model), LOW), pltpu.SemaphoreType.DMA((2, 4))],
        out_shape=[wide, wide, grads, grads],
        compiler_params=params(),
        cost_estimate=cost(55),
        name="feed",
    )(normed, cot, out_in, *near, *far)


def middle_back_kernel(
    middle, grad, cot, gain, weight, y, h, f, state, mid_grad, mid_low, state_grad, y_grad,
    gain_sum, back_sum, bias_sum, mixed_s,
):
    model = middle.shape[1]

    @pl.when(pl.program_id(0) == 0)
    def _():
        gain_sum[...] = jnp.zeros_like(gain_sum)
        back_sum[...] = jnp.zeros_like(back_sum)
        bias_sum[...] = jnp.zeros_like(bias_sum)

    value, error = middle[...], grad[...]
    scale = lax.rsqrt(jnp.mean(value * value, axis=-1, keepdims=True) + 1e-06)
    gained = gain[...] * error
    mean = jnp.mean(gained * value, axis=-1, keepdims=True)
    total = cot[...] + scale * gained - value * (scale * scale * scale * mean)
    gain_sum[...] += fold(error * value * scale)
    mid_grad[...] = total
    mid_low[...] = total.astype(LOW)
    mixed_s[...] = nt(mid_low[...], weight[...].reshape(-1, model))

    def turn(index, carry):
        back, bias = carry
        own = pl.ds(pl.multiple_of(index * STEP, STEP), STEP)
        error = mixed_s[own, :]
        active, slope = gelu_parts(y[own, :])
        gone = f[own, :]
        full = h[own, :] + gone * state[...]
        here = error * active
        state_grad[own, :] = here
        low = (error * full * slope).astype(LOW)
        y_grad[own, :] = low
        return back + fold(here * gone), bias + fold(low.astype(WIDE))

    zero = jnp.zeros(back_sum.shape, WIDE)
    back, bias = loop(middle.shape[0] // STEP, 2, turn, (zero, zero))
    back_sum[...] += back
    bias_sum[...] += bias


def middle_back(middle, grad, cot, gain, slab, rows, row_index, y, h, f, state):
    length, model = middle.shape
    total = y.shape[1]
    chans = slab.shape[0]
    tile = 128 if length % 128 == 0 else length
    row = lambda lanes: pl.BlockSpec((tile, lanes), lambda step: (step, 0))
    one = lambda lines, lanes: pl.BlockSpec((lines, lanes), lambda step: (0, 0))
    return pl.pallas_call(
        middle_back_kernel,
        grid=(length // tile,),
        in_specs=[
            row(model), row(model), row(model), one(1, model),
            pl.BlockSpec((chans, rows, model), lambda step: (0, row_index, 0)),
            row(total), row(total), row(total), one(1, total),
        ],
        out_specs=[
            row(model), row(model), row(total), row(total), one(8, model), one(8, total),
            one(8, total),
        ],
        out_shape=[
            jax.ShapeDtypeStruct((length, model), WIDE),
            jax.ShapeDtypeStruct((length, model), LOW),
            jax.ShapeDtypeStruct((length, total), WIDE),
            jax.ShapeDtypeStruct((length, total), LOW),
            jax.ShapeDtypeStruct((8, model), WIDE),
            jax.ShapeDtypeStruct((8, total), WIDE),
            jax.ShapeDtypeStruct((8, total), WIDE),
        ],
        scratch_shapes=[pltpu.VMEM((tile, total), WIDE)],
        compiler_params=params(),
        cost_estimate=cost(13),
        name="middle_back",
    )(middle, grad, cot, gain, slab, y, h, f, state)


def mixer_back_kernel(
    rows, first, place, state_grad, r_in, i_in, conv_in, h, f, u, y_grad, mixed, y_weight, u_weight,
    packed, vec, mask, state, after, normed, mid_low, *refs
):
    if not first:
        grad_in, refs = refs[3], refs[4:]
    (
        keep, send, sums, normed_grad, conv_s, high, low, conv_h, conv_l, grown, u_low, wide,
        gate_w, gates,
    ) = refs
    length, width = state_grad.shape
    ext, model = normed.shape
    group = width // rows
    block = width // 2
    count = length // STEP
    line = lax.broadcasted_iota(jnp.int32, (8, width), 0)

    fill_gates(packed, gates, rows, block)

    @pl.when(pl.program_id(0) == 0)
    def _():
        if first:
            normed_grad[...] = jnp.zeros_like(normed_grad)
        else:
            normed_grad[...] = grad_in[...]

    def retreat(index, carry):
        error, rate_sum, into_sum, slope_sum = carry
        base = pl.multiple_of((count - 1 - index) * STEP, STEP)
        own = pl.ds(base, STEP)
        going = mask[pl.ds(base + RIM, STEP), :][:, 0:1]
        rate, into, conv = r_in[own, :], i_in[own, :], conv_in[own, :]
        slope = vec[5:6, :]
        decay = jnp.exp(slope * rate)
        carried = decay * going
        given = state_grad[own, :]
        full = h[own, :] + f[own, :] * state[...]
        ahead = pl.ds(pl.multiple_of(jnp.maximum(base - 8, 0), 8), 8)
        edge = h[ahead, :][7:8] + f[ahead, :][7:8] * state[...]
        edge = jnp.where(base == 0, state[...], edge)
        parts = []
        for part in reversed(range(STEP // 8)):
            place_of = slice(8 * part, 8 * part + 8)
            mul = carried[place_of]
            add = mul * given[place_of]
            for reach in (1, 2, 4):
                inside = line < 8 - reach
                add = add + mul * jnp.where(inside, pltpu.roll(add, 8 - reach, 0), 0.0)
                mul = mul * jnp.where(inside, pltpu.roll(mul, 8 - reach, 0), 1.0)
            here = add + mul * error
            parts.append(given[place_of] + jnp.where(line < 7, pltpu.roll(here, 7, 0), error))
            error = here[0:1]
        grad = jnp.concatenate(parts[::-1], 0)
        befores = []
        for part in range(STEP // 8):
            last = edge if part == 0 else full[8 * part - 1 : 8 * part]
            befores.append(
                jnp.where(line > 0, pltpu.roll(full[8 * part : 8 * part + 8], 1, 0), last)
            )
        before = jnp.concatenate(befores, 0)
        root = lax.rsqrt(1.01 - decay * decay)
        scale = jnp.where(going == 0.0, 1.0, (1.01 - decay * decay) * root)
        through = grad * conv
        into_grad = through * scale
        conv_s[own, :] = grad * into * scale
        decay_grad = going * decay * (grad * before - through * into * decay * root)
        z_rate = decay_grad * slope * rate * (1.0 - rate)
        z_into = into_grad * into * (1.0 - into)
        high[own, 0:width], low[own, 0:width] = split_low(z_rate)
        high[own, width:], low[own, width:] = split_low(z_into)
        conv_h[own, :], conv_l[own, :] = split_low(conv)
        return (
            error,
            rate_sum + fold(z_rate),
            into_sum + fold(z_into),
            slope_sum + fold(decay_grad * rate),
        )

    zero = jnp.zeros((8, width), WIDE)
    _, rate_sum, into_sum, slope_sum = loop(
        count, 2, retreat, (after[...], zero, zero, zero)
    )
    conv_s[...] += nt(high[...], gates[...]) + nt(low[...], gates[...])
    gate_full = (
        tn(conv_h[...], high[...]) + tn(conv_l[...], high[...]) + tn(conv_h[...], low[...])
    )
    for half in (0, block):
        rows_of = slice(half, half + block)
        gate_w[rows_of, 0:block] = gate_full[rows_of, half : half + block]
        gate_w[rows_of, block:] = gate_full[rows_of, width + half : width + half + block]
    grown[0:RIM, :] = jnp.zeros((RIM, width), WIDE)
    grown[RIM + length :, :] = jnp.zeros((RIM, width), WIDE)

    def taps(index, carry):
        base = pl.multiple_of(index * STEP, STEP)
        window = u[pl.ds(base + 8, STEP + 8), :]
        flags = mask[pl.ds(base + RIM, STEP), :]
        error = conv_s[pl.ds(base, STEP), :] * flags[:, 4:5]
        grown[pl.ds(base + RIM, STEP), :] = error
        out = [carry[0] + fold(error), carry[1] + fold(error * window[8:])]
        for shift in (1, 2, 3):
            moved = window[8 - shift : 8 - shift + STEP]
            out.append(carry[1 + shift] + fold(flags[:, shift : shift + 1] * error * moved))
        return tuple(out)

    bias_sum, *tap_sums = loop(count, 2, taps, (zero,) * 5)

    def spread_back(index, total):
        base = pl.multiple_of(index * STEP, STEP)
        window = grown[pl.ds(base, STEP + 8), :]
        flags = mask[pl.ds(base, STEP + 8), :]
        value = vec[6:7, :] * window[0:STEP]
        for shift in (1, 2, 3):
            masked = flags[:, shift : shift + 1] * window
            value = value + vec[6 + shift : 7 + shift, :] * masked[shift : shift + STEP]
        rounded = value.astype(LOW)
        u_low[pl.ds(base, STEP), :] = rounded
        return total + fold(rounded.astype(WIDE))

    input_sum = loop(ext // STEP, 3, spread_back, zero)
    for row, value in enumerate((input_sum, bias_sum, rate_sum, into_sum, slope_sum, *tap_sums)):
        sums[row : row + 1, :] = jnp.sum(value, axis=0, keepdims=True)
    sums[9:16, :] = jnp.zeros((7, width), WIDE)
    wide[...] = tn(u_low[...], normed[...])
    spread(place, wide, keep, send, 0, group, rows, slice(0, model))
    spread(place, gate_w, keep, send, 0, group, rows, slice(3 * model, 3 * model + width))
    wide[...] = tn(y_grad[...], normed[RIM:, :])
    spread(place, wide, keep, send, 0, group, rows, slice(model, 2 * model))
    wide[...] = tn(mixed[...], mid_low[...])
    spread(place, wide, keep, send, 0, group, rows, slice(2 * model, 3 * model))
    normed_grad[...] += nn(u_low[...], u_weight[...].reshape(width, model))
    normed_grad[RIM:, :] += nn(y_grad[...], y_weight[...].reshape(width, model))


def mixer_back(
    place, state_grad, r, i, conv, h, f, u, y_grad, mixed, slab, vec, mask, state, after, normed,
    mid_low, rows, width, begin, steps, so_far=(),
):
    length, total = state_grad.shape
    ext, model = normed.shape
    group, part = width // rows, rows // 4
    pair = lambda step, place: (step + begin) ^ place[0]
    whole = lambda array: pl.BlockSpec(array.shape, lambda step, place: (0,) * array.ndim)
    lane = lambda lines: pl.BlockSpec((lines, width), lambda step, place: (0, pair(step, place)))
    weight = lambda count, index: pl.BlockSpec(
        (group, count, model), lambda step, place: (pair(step, place), index, 0)
    )
    lanes = 3 * model + width
    piece = pl.BlockSpec((group, 1, 2, part, lanes), lambda step, place: (step + begin, 0, 0, 0, 0))
    shape = jax.ShapeDtypeStruct((total // rows, 1, 2, part, lanes), LOW)
    operands = [
        state_grad, r, i, conv, h, f, u, y_grad, mixed, slab, slab, slab, vec, mask, state, after,
        normed, mid_low,
    ]
    kept = pl.BlockSpec(memory_space=pl.ANY)
    return pl.pallas_call(
        functools.partial(mixer_back_kernel, rows, not so_far),
        grid_spec=pltpu.PrefetchScalarGridSpec(
            num_scalar_prefetch=1,
            grid=(steps,),
            in_specs=[
                lane(length), lane(length), lane(length), lane(length), lane(length),
                lane(length), lane(ext), lane(length), lane(length), weight(rows, 0),
                weight(rows, 1), weight(rows // 2, 4), lane(vec.shape[0]), whole(mask), lane(1),
                lane(1), whole(normed), whole(mid_low),
            ]
            + ([kept, kept, kept, whole(so_far[3])] if so_far else []),
            out_specs=[
                piece, piece, lane(16), pl.BlockSpec((ext, model), lambda step, place: (0, 0)),
            ],
            scratch_shapes=[
                pltpu.VMEM((length, width), WIDE),
                pltpu.VMEM((length, 2 * width), LOW),
                pltpu.VMEM((length, 2 * width), LOW),
                pltpu.VMEM((length, width), LOW),
                pltpu.VMEM((length, width), LOW),
                pltpu.VMEM((ext + RIM, width), WIDE),
                pltpu.VMEM((ext, width), LOW),
                pltpu.VMEM((width, model), WIDE),
                pltpu.VMEM((width, width), WIDE),
                pltpu.VMEM((width, 2 * width), LOW),
            ],
        ),
        out_shape=[
            shape, shape,
            jax.ShapeDtypeStruct((16, total), WIDE),
            jax.ShapeDtypeStruct((ext, model), WIDE),
        ],
        input_output_aliases={len(operands) + 1 + k: k for k in range(3)} if so_far else {},
        compiler_params=params(),
        cost_estimate=cost(15 * steps),
        name="mixer_back",
    )(place, *operands, *so_far)


def wide_of(value):
    return value.astype(WIDE)


class Sums:
    def __init__(self, stages):
        self.stages = stages
        self.moving = next(stages)
        self.result = None

    def step(self):
        try:
            self.moving = self.stages.send(self.moving)
        except StopIteration as end:
            self.moving = []
            self.result = end.value

    def finish(self):
        while self.result is None:
            self.step()
        return self.result


def fence(arrays, *groups):
    arrays, moving = lax.optimization_barrier((arrays, [group.moving for group in groups]))
    for group, came in zip(groups, moving):
        group.moving = came
    return arrays


def owned(keep, send, begin):
    slots, matrices, _, part, lanes = keep.shape
    shape = (slots // 2, 2, matrices, 2, part, lanes)
    keep = keep.reshape(shape)
    (came,) = yield [swapped(send, "rows", 1)]
    came = came.reshape(shape)
    even, odd = slice(begin % 2, None, 2), slice((1 - begin) % 2, None, 2)
    sum_of = lambda where: wide_of(keep[where]) + wide_of(came[where])
    rest, also = yield [
        swapped(sum_of((even, slice(None), slice(None), 1)).astype(LOW), "rows", 2),
        swapped(sum_of((odd, 1)).astype(LOW), "chan", 1),
    ]
    rest = sum_of((even, slice(None), slice(None), 0)) + wide_of(rest)
    also = sum_of((odd, 0)) + wide_of(also)
    came, came_also = yield [
        swapped(rest[:, 1].astype(LOW), "chan", 1),
        swapped(also[:, :, 1].astype(LOW), "rows", 2),
    ]
    rest = rest[:, 0] + wide_of(came)
    also = also[:, :, 0] + wide_of(came_also)
    parts = {}
    for index in range(rest.shape[0]):
        parts[begin + begin % 2 + 2 * index] = rest[index]
    for index in range(also.shape[0]):
        parts[begin + 1 - begin % 2 + 2 * index] = also[index]
    came = yield [
        swapped(value.astype(LOW), "chan", 2 * distance)
        for distance, value in parts.items() if distance
    ]
    values = [wide_of(value) for value in came]
    if 0 in parts:
        values.append(parts[0])
    return functools.reduce(jnp.add, values)


def settled(total):
    total = total.astype(LOW)
    (came,) = yield [swapped(total, "rows", 1)]
    pair = jnp.stack([total, came])
    (came,) = yield [swapped(pair, "rows", 2)]
    four = jnp.stack([pair, came])
    place = lax.axis_index("rows")
    four = jnp.where(place & 1, four[:, ::-1], four)
    four = jnp.where(place & 2, four[::-1], four)
    _, _, matrices, part, lanes = four.shape
    four = four.reshape(4, matrices, part, lanes).transpose(1, 0, 2, 3)
    return four.reshape(matrices, 4 * part, lanes).astype(WIDE)


def summed_everywhere(value):
    for axis in ("rows", "chan"):
        bits = 1
        while bits < lax.axis_size(axis):
            value = value + swapped(value, axis, bits)
            bits *= 2
    return value


def gathered(piece):
    parts = lax.axis_size("rows")
    share = piece.shape[0] // parts
    own = lax.dynamic_slice_in_dim(piece, lax.axis_index("rows") * share, share)
    full = lax.all_gather(own, ("chan", "rows"), axis=0, tiled=True)
    return full.reshape(lax.axis_size("chan"), piece.shape[0], piece.shape[1])


def feed_weights(gate_weight, up_weight, down_weight):
    count = lax.axis_size("chan")
    place = lax.axis_index("rows")
    own = jnp.stack([gate_weight.T, up_weight.T, down_weight])
    own = own.reshape(3, 4, -1, own.shape[2])
    quarter = lambda bits: lax.dynamic_index_in_dim(own, place ^ bits, 1, keepdims=False)
    half = jnp.stack([quarter(0), quarter(2)])
    from_chan = [half if pair < 2 else half[0] for pair in range(1, count // 2)]
    from_chan = [swapped(v, "chan", 2 * k) for k, v in enumerate(from_chan, 1)]
    near = [jnp.stack([v, swapped(v, "chan", 1)], v.ndim - 3) for v in [half] + from_chan]
    near = [v if v.ndim == 5 else jnp.stack([v, swapped(v, "rows", 2)]) for v in near]
    other = jnp.stack([quarter(1), quarter(3)])
    far = [jnp.stack([other, swapped(near[0][:, 1], "rows", 1)], 1)]
    far += [swapped(v, "rows", 1) for v in near[1:]]
    return near, far


def local(
    tokens, segments, gelu_weight, gelu_bias, input_weight, input_bias, conv_taps, conv_bias,
    decay_gate, decay_bias, input_gate, ingate_bias, decay_param, out_weight, mixer_gain,
    gate_weight, up_weight, down_weight, feed_gain, cotangent,
):
    length, model = tokens.shape
    rim = conv_taps.shape[0] - 1
    chans = lax.axis_size("chan")
    me, row_place = lax.axis_index("chan"), lax.axis_index("rows")
    rows, block = decay_gate.shape
    total = rows * chans
    width = 2 * block
    group = width // rows

    padded = jnp.concatenate([jnp.full((rim,), -1, jnp.int32), segments])
    window = lax.dynamic_slice_in_dim(padded, me * length, length + rim)
    own = window[rim:]
    same = [own == window[rim - shift : rim - shift + length] for shift in range(1, rim + 1)]
    mask = jnp.stack([same[0], *same, own != 0] + [same[0]] * (7 - rim - 1), 1).astype(WIDE)
    mask = jnp.pad(mask, ((RIM, RIM), (0, 0)))

    small = jnp.concatenate(
        [
            jnp.stack([gelu_bias, input_bias, conv_bias, decay_bias, ingate_bias, decay_param]),
            conv_taps,
        ]
    )
    gate_rows = rows // 2
    slab_rows = -(-(2 * rows + gate_rows + -(-small.size // model)) // 64) * 64
    small_rows = slab_rows - 2 * rows - gate_rows
    flat = jnp.pad(small.reshape(-1), (0, small_rows * model - small.size))
    both = jnp.concatenate([decay_gate, input_gate], 1)
    both = jnp.pad(both, ((0, 0), (0, model // 2 - 2 * block)))
    slab = gathered(
        jnp.concatenate(
            [
                gelu_weight.T,
                input_weight.T,
                jnp.concatenate([both[:gate_rows], both[gate_rows:]], 1),
                flat.reshape(small_rows, model),
            ]
        )
    )
    late = gathered(out_weight)
    out_index = 0
    near, far = feed_weights(gate_weight, up_weight, down_weight)
    small_full = slab[:, 2 * rows + gate_rows :].reshape(chans, -1)[:, : small.size]
    small_full = small_full.reshape(chans, small.shape[0], rows).transpose(1, 0, 2)
    small_full = small_full.reshape(small.shape[0], total).astype(WIDE)
    param = small_full[5:6]
    vec = jnp.concatenate(
        [small_full[:5], -8.0 * jax.nn.softplus(param), small_full[6:], jnp.zeros((6, total), WIDE)]
    )

    rim_tokens = moved_by(tokens[length - rim :], "chan", 1)
    extended = jnp.concatenate([jnp.zeros((RIM - rim, model), WIDE), rim_tokens, tokens])
    normed = rms_norm(extended, mixer_gain).astype(LOW)
    y, u, conv, rate, into, state, factor, decay_sum = mixer_forward(
        normed, slab, vec, mask, rows, width
    )
    carry = entering(jnp.concatenate([factor[-1:], state[-1:]]), "chan", 1)
    mixed, middle, normed2 = mixer_out(
        y, state, factor, carry, late, rows, out_index, tokens, feed_gain[None]
    )
    cot_low = cotangent.astype(LOW)
    block_output, normed2_grad, keep, send = feed(normed2, cot_low, middle, near, far)
    fed = Sums(owned(keep, send, 0))

    mid_grad, mid_low, state_grad, y_grad, feed_gain_sum, back_sum, y_sum = middle_back(
        middle, normed2_grad, cotangent, feed_gain[None], late, rows, out_index, y, state, factor,
        carry,
    )
    after = entering(
        jnp.concatenate([factor[-1:], jnp.sum(back_sum, 0, keepdims=True)]), "chan", -1
    )
    place = jnp.stack([me // group, me % group, row_place]).astype(jnp.int32)
    after = fence(after, fed)
    fed.step()
    steps = total // width // 2
    back = lambda after, begin, so_far: mixer_back(
        place, state_grad, rate, into, conv, state, factor, u, y_grad, mixed, slab, vec, mask,
        carry, after, normed, mid_low, rows, width, begin, steps, so_far,
    )
    so_far = back(after, steps, ())
    so_far = fence(so_far, fed)
    fed.step()
    keep, send, sums, normed_grad = back(after, 0, so_far)
    rest = Sums(owned(keep, send, 0))
    normed_grad = fence(normed_grad, fed)
    fed.step()
    fed = Sums(settled(fed.finish()))
    rest.step()
    feed_sum = fed.finish()
    rest_sum = Sums(settled(rest.finish())).finish()[0]
    input_sum, gelu_sum, out_sum = (rest_sum[:, k * model : (k + 1) * model] for k in range(3))
    gates_sum = rest_sum[:, 3 * model :]
    rim_grad = moved_by(normed_grad[RIM - rim : RIM], "chan", -1)
    error = normed_grad[RIM:] + jnp.concatenate([jnp.zeros((length - rim, model), WIDE), rim_grad])
    scale = lax.rsqrt(jnp.mean(tokens * tokens, axis=-1, keepdims=True) + 1e-06)
    gained = mixer_gain * error
    mean = jnp.mean(gained * tokens, axis=-1, keepdims=True)
    tokens_grad = mid_grad + scale * gained - tokens * (scale * scale * scale * mean)
    mixer_gain_sum = jnp.sum(error * tokens * scale, 0)

    slope_grad = sums[4:5] * (-8.0 * jax.nn.sigmoid(param))
    lines = jnp.concatenate(
        [jnp.sum(y_sum, 0, keepdims=True), sums[:4], slope_grad, sums[5:9],
         jnp.sum(decay_sum, 0, keepdims=True)]
    )
    gains = jnp.stack([mixer_gain_sum, jnp.sum(feed_gain_sum, 0)])
    everything = summed_everywhere(
        jnp.concatenate([lines.reshape(-1, 128), gains.reshape(-1, 128)])
    )
    cut = lines.size // 128
    gains = everything[cut:].reshape(2, model)
    lines = lax.dynamic_slice_in_dim(
        everything[:cut].reshape(lines.shape), me * rows, rows, axis=1
    )
    mean_decay = lines[10] / (length * lax.axis_size("rows") * chans)
    return (
        block_output,
        tokens_grad,
        gelu_sum.T,
        lines[0],
        input_sum.T,
        lines[1],
        lines[6:10],
        lines[2],
        gates_sum[:, :block],
        lines[3],
        gates_sum[:, block:],
        lines[4],
        lines[5],
        out_sum,
        gains[0],
        feed_sum[0].T,
        feed_sum[1].T,
        feed_sum[2],
        gains[1],
        mean_decay,
    )


def solution(mesh):
    return jax.shard_map(
        local,
        mesh=mesh,
        in_specs=(
            P(("rows", "chan"), None),
            P("rows"),
            P(None, "chan"),
            P("chan"),
            P(None, "chan"),
            P("chan"),
            P(None, "chan"),
            P("chan"),
            P("chan", None),
            P("chan"),
            P("chan", None),
            P("chan"),
            P("chan"),
            P("chan", None),
            P(),
            P(None, "chan"),
            P(None, "chan"),
            P("chan", None),
            P(),
            P(("rows", "chan"), None),
        ),
        out_specs=(
            P(("rows", "chan"), None),
            P(("rows", "chan"), None),
            P(None, "chan"),
            P("chan"),
            P(None, "chan"),
            P("chan"),
            P(None, "chan"),
            P("chan"),
            P("chan", None),
            P("chan"),
            P("chan", None),
            P("chan"),
            P("chan"),
            P("chan", None),
            P(),
            P(None, "chan"),
            P(None, "chan"),
            P("chan", None),
            P(),
            P("chan"),
        ),
        check_vma=False,
    )
```

```python
import functools

import jax
import jax.numpy as jnp
from jax import lax
from jax.experimental import pallas as pl
from jax.experimental.pallas import tpu as pltpu
from jax.sharding import PartitionSpec as P

LOW = jnp.bfloat16
WIDE = jnp.float32
RIM = 16
STEP = 16
VMEM_BYTES = 56 * 1024 * 1024
GELU_SLOPE = 0.7978845608028654
GELU_CUBE = 0.044715


def params(**more):
    return pltpu.CompilerParams(vmem_limit_bytes=VMEM_BYTES, **more)


def moved_by(value, axis, steps):
    count = lax.axis_size(axis)
    leading, last = (max(0, -steps), min(count, count - steps))
    return lax.ppermute(value, axis, [(source, source + steps) for source in range(leading, last)])


def swapped(value, axis, bits):
    count = lax.axis_size(axis)
    return lax.ppermute(value, axis, [(source, source ^ bits) for source in range(count)])


def join(earlier, later):
    return jnp.concatenate(
        [earlier[0:1] * later[0:1], later[0:1] * earlier[1:2] + later[1:2]], 0
    )


def entering(value, axis, sign):
    count = lax.axis_size(axis)
    total = value
    came = yield [(value, axis, sign * reach) for reach in (1, 2, 3) if reach < count]
    for one in came:
        total = join(one, total)
    reach = 4
    while 2 * reach < count:
        (one,) = yield [(total, axis, sign * reach)]
        total = join(one, total)
        reach *= 2
    came = yield [(total, axis, sign * far) for far in (1, reach + 1) if far < count]
    last = came[0]
    for one in came[1:]:
        last = join(one, last)
    return last[1:2]


def rms_norm(values, gain):
    return values * lax.rsqrt(jnp.mean(values * values, axis=-1, keepdims=True) + 1e-06) * gain


def nt(left, right):
    return lax.dot_general(left, right, (((1,), (1,)), ((), ())), preferred_element_type=WIDE)


def tn(left, right):
    return lax.dot_general(left, right, (((0,), (0,)), ((), ())), preferred_element_type=WIDE)


def nn(left, right):
    return lax.dot_general(left, right, (((1,), (0,)), ((), ())), preferred_element_type=WIDE)


def sigmoid(value):
    return 0.5 * jnp.tanh(0.5 * value) + 0.5


def gelu_parts(value):
    square = value * value
    bend = jnp.tanh(GELU_SLOPE * value * (1.0 + GELU_CUBE * square))
    half = 0.5 + 0.5 * bend
    slope = half + 0.5 * GELU_SLOPE * value * (1.0 - bend * bend) * (1.0 + 3.0 * GELU_CUBE * square)
    return value * half, slope


def split_low(value):
    high = value.astype(LOW)
    return high, (value - high.astype(WIDE)).astype(LOW)


def loop(count, unroll, body, init):
    while count % unroll:
        unroll -= 1

    def several(index, carry):
        for turn in range(unroll):
            carry = body(index * unroll + turn, carry)
        return carry

    return lax.fori_loop(0, count // unroll, several, init)


def cost(microseconds):
    return pl.CostEstimate(
        flops=int(microseconds * 1.1e9), bytes_accessed=int(microseconds * 3.5e6), transcendentals=0
    )


def fold(value):
    total = value[0:8]
    for group in range(1, value.shape[0] // 8):
        total = total + value[8 * group : 8 * group + 8]
    return total


def fill_gates(packed, gates, rows, block):
    width = 2 * block

    @pl.when(pl.program_id(0) == 0)
    def _():
        gates[...] = jnp.zeros_like(gates)

    kind = LOW if rows % 32 == 0 else WIDE
    lines = []
    for slot in range(packed.shape[0]):
        value = packed[slot].astype(kind)
        lines += [value[:, 0:width], value[:, 512 : 512 + width]]
    lines = jnp.concatenate(lines, 0).astype(LOW)
    for half in (0, block):
        gates[half : half + block, half : half + block] = lines[half : half + block, 0:block]
        gates[half : half + block, width + half : width + half + block] = lines[
            half : half + block, block:
        ]


def mixer_forward_kernel(
    rows, normed, y_weight, u_weight, packed, vec, mask, y_out, u_out, conv_out, r_out, i_out,
    h_out, f_out, sum_out, high, low, zed, gates,
):
    fill_gates(packed, gates, rows, y_out.shape[1] // 2)
    ext = normed.shape[0]
    width = y_out.shape[1]
    count = (ext - RIM) // STEP
    model = normed.shape[1]
    y_out[...] = nt(normed[RIM:, :], y_weight[...].reshape(width, model)) + vec[0:1, :]
    u_out[...] = nt(normed[...], u_weight[...].reshape(width, model)) + vec[1:2, :]

    def convolve(index, _):
        base = pl.multiple_of(index * STEP, STEP)
        own = pl.ds(base, STEP)
        window = u_out[pl.ds(base + 8, STEP + 8), :]
        flags = mask[pl.ds(base + RIM, STEP), :]
        conv = vec[2:3, :] + vec[6:7, :] * window[8:]
        for shift in (1, 2, 3):
            conv = conv + flags[:, shift : shift + 1] * (
                vec[6 + shift : 7 + shift, :] * window[8 - shift : 8 - shift + STEP]
            )
        conv = conv * flags[:, 4:5]
        conv_out[own, :] = conv
        high[own, :], low[own, :] = split_low(conv)
        return 0

    loop(count, 2, convolve, 0)
    zed[...] = nn(high[...], gates[...]) + nn(low[...], gates[...])
    line = lax.broadcasted_iota(jnp.int32, (8, width), 0)

    def advance(index, carry):
        state, factor, total = carry
        own = pl.ds(pl.multiple_of(index * STEP, STEP), STEP)
        going = mask[pl.ds(pl.multiple_of(index * STEP + RIM, STEP), STEP), :][:, 0:1]
        rate = sigmoid(zed[own, 0:width] + vec[3:4, :])
        into = sigmoid(zed[own, width:] + vec[4:5, :])
        decay = jnp.exp(vec[5:6, :] * rate)
        r_out[own, :] = rate
        i_out[own, :] = into
        scale = jnp.where(going == 0.0, 1.0, jnp.sqrt(1.01 - decay * decay))
        inject = conv_out[own, :] * into * scale
        carried = decay * going
        total = total + fold(decay)
        for group in range(STEP // 8):
            part = slice(8 * group, 8 * group + 8)
            mul, add = carried[part], inject[part]
            for reach in (1, 2, 4):
                inside = line >= reach
                add = add + mul * jnp.where(inside, pltpu.roll(add, reach, 0), 0.0)
                mul = mul * jnp.where(inside, pltpu.roll(mul, reach, 0), 1.0)
            here = add + mul * state
            gone = mul * factor
            rows = pl.ds(pl.multiple_of(index * STEP + 8 * group, 8), 8)
            h_out[rows, :] = here
            f_out[rows, :] = gone
            state, factor = here[7:8], gone[7:8]
        return state, factor, total

    zero = jnp.zeros((1, width), WIDE)
    _, _, total = loop(
        count, 2, advance, (zero, zero + 1.0, jnp.zeros((8, width), WIDE))
    )
    sum_out[...] = total


def mixer_forward(normed, slab, vec, mask, rows, width):
    ext, model = normed.shape
    tokens = ext - RIM
    chans = slab.shape[0]
    group = width // rows
    pairs = chans // group
    total = pairs * width
    by_lane = lambda length: pl.BlockSpec((length, width), lambda step: (0, step))
    whole = lambda array: pl.BlockSpec(array.shape, lambda step: (0,) * array.ndim)
    flat = jax.ShapeDtypeStruct((tokens, total), WIDE)
    return pl.pallas_call(
        functools.partial(mixer_forward_kernel, rows),
        grid=(pairs,),
        in_specs=[
            whole(normed),
            pl.BlockSpec((group, rows, model), lambda step: (step, 0, 0)),
            pl.BlockSpec((group, rows, model), lambda step: (step, 1, 0)),
            pl.BlockSpec((group, rows // 2, model), lambda step: (step, 4, 0)),
            by_lane(vec.shape[0]),
            whole(mask),
        ],
        out_specs=[
            by_lane(tokens), by_lane(ext), by_lane(tokens), by_lane(tokens), by_lane(tokens),
            by_lane(tokens), by_lane(tokens), by_lane(8),
        ],
        out_shape=[
            flat, jax.ShapeDtypeStruct((ext, total), WIDE), flat, flat, flat, flat, flat,
            jax.ShapeDtypeStruct((8, total), WIDE),
        ],
        scratch_shapes=[
            pltpu.VMEM((tokens, width), LOW),
            pltpu.VMEM((tokens, width), LOW),
            pltpu.VMEM((tokens, 2 * width), WIDE),
            pltpu.VMEM((width, 2 * width), LOW),
        ],
        compiler_params=params(),
        cost_estimate=cost(30),
        name="mixer_forward",
    )(normed, slab, slab, slab, vec, mask)


def mixer_out_kernel(y, h, f, state, weight, tokens, gain, mixed, middle, normed):
    model = tokens.shape[1]

    def gate(index, _):
        own = pl.ds(pl.multiple_of(index * STEP, STEP), STEP)
        full = h[own, :] + f[own, :] * state[...]
        value = y[own, :]
        bend = jnp.tanh(GELU_SLOPE * value * (1.0 + GELU_CUBE * value * value))
        mixed[own, :] = (full * (value * (0.5 + 0.5 * bend))).astype(LOW)
        return 0

    loop(y.shape[0] // STEP, 2, gate, 0)
    total = tokens[...] + nn(mixed[...], weight[...].reshape(-1, model))
    middle[...] = total
    scale = lax.rsqrt(jnp.mean(total * total, axis=-1, keepdims=True) + 1e-06)
    normed[...] = (total * scale * gain[...]).astype(LOW)


def mixer_out(y, h, f, state, slab, rows, row_index, tokens, gain):
    length, model = tokens.shape
    total = y.shape[1]
    chans = slab.shape[0]
    tile = 256 if length % 256 == 0 else length
    row = lambda lanes: pl.BlockSpec((tile, lanes), lambda step: (step, 0))
    return pl.pallas_call(
        mixer_out_kernel,
        grid=(length // tile,),
        in_specs=[
            row(total), row(total), row(total),
            pl.BlockSpec((1, total), lambda step: (0, 0)),
            pl.BlockSpec((chans, rows, model), lambda step: (0, row_index, 0)),
            row(model),
            pl.BlockSpec((1, model), lambda step: (0, 0)),
        ],
        out_specs=[row(total), row(model), row(model)],
        out_shape=[
            jax.ShapeDtypeStruct((length, total), LOW),
            jax.ShapeDtypeStruct((length, model), WIDE),
            jax.ShapeDtypeStruct((length, model), LOW),
        ],
        compiler_params=params(),
        cost_estimate=cost(9),
        name="mixer_out",
    )(y, h, f, state, slab, tokens, gain)


def spread(place, wide, keep, send, matrix, group, rows, lanes=slice(None)):
    part = rows // 4
    if part % 8:
        value = wide[...]
        pieces = [value[begin : begin + part] for begin in range(0, group * rows, part)]
        mine = place[1] * 4 + place[2]
        bit = 1
        while bit < len(pieces):
            turned = (mine & bit) != 0
            pieces = [
                jnp.where(turned, pieces[index ^ bit], pieces[index])
                for index in range(len(pieces))
            ]
            bit *= 2
    for slot in range(group):
        shard = slot ^ place[1]
        for turn in range(4):
            if part % 8:
                value = pieces[4 * slot + turn]
            else:
                begin = pl.multiple_of(shard * rows + (turn ^ place[2]) * part, 8)
                value = wide[pl.ds(begin, part), :]
            (keep, send)[turn & 1][slot, matrix, turn >> 1, :, lanes] = value.astype(LOW)


def feed_kernel(
    pairs, normed, cot, out_in, *refs
):
    near, far = refs[:pairs], refs[pairs : 2 * pairs]
    out, grad, keep, send, gate_s, up_s, back_s, hidden_l, gate_l, up_l, held, sems = refs[2 * pairs :]
    half = gate_s.shape[0] // 2
    model = normed.shape[1]
    width = gate_s.shape[0]
    part = width // 4
    step = pl.program_id(0)

    def copies(index, slot):
        for turn in range(4):
            source = (near, far)[turn // 2][index // 2]
            yield pltpu.make_async_copy(
                source.at[turn % 2, index % 2],
                held.at[slot, :, turn],
                sems.at[slot, turn],
            )

    @pl.when(step == 0)
    def _():
        out[...] = out_in[...]
        grad[...] = jnp.zeros_like(grad)
        for copy in copies(0, 0):
            copy.start()

    for index in range(1, 2 * pairs):

        @pl.when(step + 1 == index)
        def _():
            for copy in copies(index, index % 2):
                copy.start()

    for index in range(2 * pairs):

        @pl.when(step == index)
        def _():
            for copy in copies(index, index % 2):
                copy.wait()

    def weight(matrix):
        if part % 16 == 0:
            return held[step % 2, matrix].reshape(width, model)
        pieces = [held[step % 2, matrix, turn].astype(WIDE) for turn in range(4)]
        return jnp.concatenate(pieces, 0).astype(LOW)

    first, second, third = weight(0), weight(1), weight(2)
    gate_s[...] = nt(first, normed[...])
    up_s[...] = nt(second, normed[...])
    back_s[...] = nt(third, cot[...])

    def act(index, _):
        own = pl.ds(pl.multiple_of(index * STEP, STEP), STEP)
        up, back = up_s[own, :], back_s[own, :]
        value, slope = gelu_parts(gate_s[own, :])
        hidden_l[own, :] = (value * up).astype(LOW)
        gate_l[own, :] = (back * up * slope).astype(LOW)
        up_l[own, :] = (back * value).astype(LOW)
        return 0

    loop(width // STEP, 2, act, 0)
    out[...] += tn(hidden_l[...], third)
    grad[...] += tn(gate_l[...], first) + tn(up_l[...], second)
    for matrix, value in enumerate((gate_l, up_l, hidden_l)):
        keep[0, matrix] = value[:half, :]
        send[0, matrix] = value[half:, :]


def feed(normed, cot, out_in, near, far):
    length, model = normed.shape
    pairs = len(near)
    part = near[0].shape[3]
    width = 4 * part
    whole = lambda array: pl.BlockSpec(array.shape, lambda step: (0,) * array.ndim)
    piece = pl.BlockSpec((1, 3, 2 * part, length), lambda step: (step, 0, 0, 0))
    wide = jax.ShapeDtypeStruct((length, model), WIDE)
    grads = jax.ShapeDtypeStruct((2 * pairs, 3, 2 * part, length), LOW)
    return pl.pallas_call(
        functools.partial(feed_kernel, pairs),
        grid=(2 * pairs,),
        in_specs=[whole(normed), whole(cot), whole(out_in)]
        + [pl.BlockSpec(memory_space=pl.ANY)] * (2 * pairs),
        out_specs=[whole(out_in), whole(out_in), piece, piece],
        scratch_shapes=[pltpu.VMEM((width, length), WIDE)] * 3
        + [pltpu.VMEM((width, length), LOW)] * 3
        + [pltpu.VMEM((2, 3, 4, part, model), LOW), pltpu.SemaphoreType.DMA((2, 4))],
        out_shape=[wide, wide, grads, grads],
        compiler_params=params(),
        cost_estimate=cost(34),
        name="feed",
    )(normed, cot, out_in, *near, *far)


def feed_grads_kernel(pairs, mine, theirs, normed, cot, normed_too, cot_too, *outs):
    part = outs[0].shape[2]
    step = pl.program_id(0)
    for matrix in range(3):
        right, right_too = (cot, cot_too) if matrix == 2 else (normed, normed_too)
        value = nn(mine[0, matrix], right[...]) + nn(theirs[0, matrix], right_too[...])
        value = value.astype(LOW)

        @pl.when(step < pairs)
        def _():
            outs[0][0, matrix] = value[:part]
            outs[1][0, matrix] = value[part:]

        for place, out in ((pairs, outs[2]), (pairs + pairs // 2, outs[3])):

            @pl.when((step >= place) & (step < place + pairs // 2))
            def _():
                out[0, matrix, 0] = value[:part]
                out[0, matrix, 1] = value[part:]


def feed_grads(mine, theirs, normed, cot, normed_too, cot_too):
    slots, _, rows, length = mine.shape
    model = normed.shape[1]
    pairs, part = slots // 2, rows // 2
    whole = lambda array: pl.BlockSpec(array.shape, lambda step: (0,) * array.ndim)

    def source(step):
        even = 4 * (step // 2) + step % 2
        odd = step - pairs
        last = odd >= pairs // 2
        odd = 4 * jnp.where(last, odd - pairs // 2, odd) + 2 + last.astype(jnp.int32)
        return jnp.where(step < pairs, even, odd), 0, 0, 0

    clipped = lambda first, count: lambda step: jnp.clip(step - first, 0, count - 1)
    even = clipped(0, pairs)
    spec = lambda place, count: pl.BlockSpec(
        (1, 3, 2, part, model), lambda step: (clipped(place, count)(step), 0, 0, 0, 0)
    )
    flat = pl.BlockSpec((1, 3, part, model), lambda step: (even(step), 0, 0, 0))
    return pl.pallas_call(
        functools.partial(feed_grads_kernel, pairs),
        grid=(slots,),
        in_specs=[pl.BlockSpec((1, 3, rows, length), source)] * 2
        + [whole(normed)] * 4,
        out_specs=[flat, flat, spec(pairs, pairs // 2), spec(pairs + pairs // 2, pairs // 2)],
        out_shape=[jax.ShapeDtypeStruct((pairs, 3, part, model), LOW)] * 2
        + [jax.ShapeDtypeStruct((pairs // 2, 3, 2, part, model), LOW)] * 2,
        compiler_params=params(),
        cost_estimate=cost(17),
        name="feed_grads",
    )(mine, theirs, normed, cot, normed_too, cot_too)


def middle_back_kernel(
    middle, grad, cot, gain, weight, y, h, f, state, mid_grad, mid_low, state_grad, y_grad,
    gain_sum, back_sum, bias_sum, mixed_s,
):
    model = middle.shape[1]

    @pl.when(pl.program_id(0) == 0)
    def _():
        gain_sum[...] = jnp.zeros_like(gain_sum)
        back_sum[...] = jnp.zeros_like(back_sum)
        bias_sum[...] = jnp.zeros_like(bias_sum)

    value, error = middle[...], grad[...]
    scale = lax.rsqrt(jnp.mean(value * value, axis=-1, keepdims=True) + 1e-06)
    gained = gain[...] * error
    mean = jnp.mean(gained * value, axis=-1, keepdims=True)
    total = cot[...] + scale * gained - value * (scale * scale * scale * mean)
    gain_sum[...] += fold(error * value * scale)
    mid_grad[...] = total
    mid_low[...] = total.astype(LOW)
    mixed_s[...] = nt(mid_low[...], weight[...].reshape(-1, model))

    def turn(index, carry):
        back, bias = carry
        own = pl.ds(pl.multiple_of(index * STEP, STEP), STEP)
        error = mixed_s[own, :]
        active, slope = gelu_parts(y[own, :])
        gone = f[own, :]
        full = h[own, :] + gone * state[...]
        here = error * active
        state_grad[own, :] = here
        low = (error * full * slope).astype(LOW)
        y_grad[own, :] = low
        return back + fold(here * gone), bias + fold(low.astype(WIDE))

    zero = jnp.zeros(back_sum.shape, WIDE)
    back, bias = loop(middle.shape[0] // STEP, 2, turn, (zero, zero))
    back_sum[...] += back
    bias_sum[...] += bias


def middle_back(middle, grad, cot, gain, slab, rows, row_index, y, h, f, state):
    length, model = middle.shape
    total = y.shape[1]
    chans = slab.shape[0]
    tile = 256 if length % 256 == 0 else length
    row = lambda lanes: pl.BlockSpec((tile, lanes), lambda step: (step, 0))
    one = lambda lines, lanes: pl.BlockSpec((lines, lanes), lambda step: (0, 0))
    return pl.pallas_call(
        middle_back_kernel,
        grid=(length // tile,),
        in_specs=[
            row(model), row(model), row(model), one(1, model),
            pl.BlockSpec((chans, rows, model), lambda step: (0, row_index, 0)),
            row(total), row(total), row(total), one(1, total),
        ],
        out_specs=[
            row(model), row(model), row(total), row(total), one(8, model), one(8, total),
            one(8, total),
        ],
        out_shape=[
            jax.ShapeDtypeStruct((length, model), WIDE),
            jax.ShapeDtypeStruct((length, model), LOW),
            jax.ShapeDtypeStruct((length, total), WIDE),
            jax.ShapeDtypeStruct((length, total), LOW),
            jax.ShapeDtypeStruct((8, model), WIDE),
            jax.ShapeDtypeStruct((8, total), WIDE),
            jax.ShapeDtypeStruct((8, total), WIDE),
        ],
        scratch_shapes=[pltpu.VMEM((tile, total), WIDE)],
        compiler_params=params(),
        cost_estimate=cost(13),
        name="middle_back",
    )(middle, grad, cot, gain, slab, y, h, f, state)


def mixer_back_kernel(
    rows, first, place, state_grad, r_in, i_in, conv_in, h, f, u, y_grad, mixed, y_weight, u_weight,
    packed, vec, mask, state, after, normed, mid_low, *refs
):
    if not first:
        grad_in, refs = refs[3], refs[4:]
    (
        keep, send, sums, normed_grad, conv_s, high, low, conv_h, conv_l, grown, u_low, wide,
        gate_w, gates,
    ) = refs
    length, width = state_grad.shape
    ext, model = normed.shape
    group = width // rows
    block = width // 2
    count = length // STEP
    line = lax.broadcasted_iota(jnp.int32, (8, width), 0)

    fill_gates(packed, gates, rows, block)

    @pl.when(pl.program_id(0) == 0)
    def _():
        if first:
            normed_grad[...] = jnp.zeros_like(normed_grad)
        else:
            normed_grad[...] = grad_in[...]

    def retreat(index, carry):
        error, rate_sum, into_sum, slope_sum = carry
        base = pl.multiple_of((count - 1 - index) * STEP, STEP)
        own = pl.ds(base, STEP)
        going = mask[pl.ds(base + RIM, STEP), :][:, 0:1]
        rate, into, conv = r_in[own, :], i_in[own, :], conv_in[own, :]
        slope = vec[5:6, :]
        decay = jnp.exp(slope * rate)
        carried = decay * going
        given = state_grad[own, :]
        full = h[own, :] + f[own, :] * state[...]
        ahead = pl.ds(pl.multiple_of(jnp.maximum(base - 8, 0), 8), 8)
        edge = h[ahead, :][7:8] + f[ahead, :][7:8] * state[...]
        edge = jnp.where(base == 0, state[...], edge)
        parts = []
        for part in reversed(range(STEP // 8)):
            place_of = slice(8 * part, 8 * part + 8)
            mul = carried[place_of]
            add = mul * given[place_of]
            for reach in (1, 2, 4):
                inside = line < 8 - reach
                add = add + mul * jnp.where(inside, pltpu.roll(add, 8 - reach, 0), 0.0)
                mul = mul * jnp.where(inside, pltpu.roll(mul, 8 - reach, 0), 1.0)
            here = add + mul * error
            parts.append(given[place_of] + jnp.where(line < 7, pltpu.roll(here, 7, 0), error))
            error = here[0:1]
        grad = jnp.concatenate(parts[::-1], 0)
        befores = []
        for part in range(STEP // 8):
            last = edge if part == 0 else full[8 * part - 1 : 8 * part]
            befores.append(
                jnp.where(line > 0, pltpu.roll(full[8 * part : 8 * part + 8], 1, 0), last)
            )
        before = jnp.concatenate(befores, 0)
        root = lax.rsqrt(1.01 - decay * decay)
        scale = jnp.where(going == 0.0, 1.0, (1.01 - decay * decay) * root)
        through = grad * conv
        into_grad = through * scale
        conv_s[own, :] = grad * into * scale
        decay_grad = going * decay * (grad * before - through * into * decay * root)
        z_rate = decay_grad * slope * rate * (1.0 - rate)
        z_into = into_grad * into * (1.0 - into)
        high[own, 0:width], low[own, 0:width] = split_low(z_rate)
        high[own, width:], low[own, width:] = split_low(z_into)
        conv_h[own, :], conv_l[own, :] = split_low(conv)
        return (
            error,
            rate_sum + fold(z_rate),
            into_sum + fold(z_into),
            slope_sum + fold(decay_grad * rate),
        )

    zero = jnp.zeros((8, width), WIDE)
    _, rate_sum, into_sum, slope_sum = loop(
        count, 2, retreat, (after[...], zero, zero, zero)
    )
    conv_s[...] += nt(high[...], gates[...]) + nt(low[...], gates[...])
    gate_full = (
        tn(conv_h[...], high[...]) + tn(conv_l[...], high[...]) + tn(conv_h[...], low[...])
    )
    for half in (0, block):
        rows_of = slice(half, half + block)
        gate_w[rows_of, 0:block] = gate_full[rows_of, half : half + block]
        gate_w[rows_of, block:] = gate_full[rows_of, width + half : width + half + block]
    grown[0:RIM, :] = jnp.zeros((RIM, width), WIDE)
    grown[RIM + length :, :] = jnp.zeros((RIM, width), WIDE)

    def taps(index, carry):
        base = pl.multiple_of(index * STEP, STEP)
        window = u[pl.ds(base + 8, STEP + 8), :]
        flags = mask[pl.ds(base + RIM, STEP), :]
        error = conv_s[pl.ds(base, STEP), :] * flags[:, 4:5]
        grown[pl.ds(base + RIM, STEP), :] = error
        out = [carry[0] + fold(error), carry[1] + fold(error * window[8:])]
        for shift in (1, 2, 3):
            moved = window[8 - shift : 8 - shift + STEP]
            out.append(carry[1 + shift] + fold(flags[:, shift : shift + 1] * error * moved))
        return tuple(out)

    bias_sum, *tap_sums = loop(count, 2, taps, (zero,) * 5)

    def spread_back(index, total):
        base = pl.multiple_of(index * STEP, STEP)
        window = grown[pl.ds(base, STEP + 8), :]
        flags = mask[pl.ds(base, STEP + 8), :]
        value = vec[6:7, :] * window[0:STEP]
        for shift in (1, 2, 3):
            masked = flags[:, shift : shift + 1] * window
            value = value + vec[6 + shift : 7 + shift, :] * masked[shift : shift + STEP]
        rounded = value.astype(LOW)
        u_low[pl.ds(base, STEP), :] = rounded
        return total + fold(rounded.astype(WIDE))

    input_sum = loop(ext // STEP, 3, spread_back, zero)
    for row, value in enumerate((input_sum, bias_sum, rate_sum, into_sum, slope_sum, *tap_sums)):
        sums[row : row + 1, :] = jnp.sum(value, axis=0, keepdims=True)
    sums[9:16, :] = jnp.zeros((7, width), WIDE)
    wide[...] = tn(u_low[...], normed[...])
    spread(place, wide, keep, send, 0, group, rows, slice(0, model))
    spread(place, gate_w, keep, send, 0, group, rows, slice(3 * model, 3 * model + width))
    wide[...] = tn(y_grad[...], normed[RIM:, :])
    spread(place, wide, keep, send, 0, group, rows, slice(model, 2 * model))
    wide[...] = tn(mixed[...], mid_low[...])
    spread(place, wide, keep, send, 0, group, rows, slice(2 * model, 3 * model))
    normed_grad[...] += nn(u_low[...], u_weight[...].reshape(width, model))
    normed_grad[RIM:, :] += nn(y_grad[...], y_weight[...].reshape(width, model))


def mixer_back(
    place, state_grad, r, i, conv, h, f, u, y_grad, mixed, slab, vec, mask, state, after, normed,
    mid_low, rows, width, begin, steps, so_far=(),
):
    length, total = state_grad.shape
    ext, model = normed.shape
    group, part = width // rows, rows // 4
    pair = lambda step, place: (step + begin) ^ place[0]
    whole = lambda array: pl.BlockSpec(array.shape, lambda step, place: (0,) * array.ndim)
    lane = lambda lines: pl.BlockSpec((lines, width), lambda step, place: (0, pair(step, place)))
    weight = lambda count, index: pl.BlockSpec(
        (group, count, model), lambda step, place: (pair(step, place), index, 0)
    )
    lanes = 3 * model + width
    piece = pl.BlockSpec((group, 1, 2, part, lanes), lambda step, place: (step + begin, 0, 0, 0, 0))
    shape = jax.ShapeDtypeStruct((total // rows, 1, 2, part, lanes), LOW)
    operands = [
        state_grad, r, i, conv, h, f, u, y_grad, mixed, slab, slab, slab, vec, mask, state, after,
        normed, mid_low,
    ]
    kept = pl.BlockSpec(memory_space=pl.ANY)
    return pl.pallas_call(
        functools.partial(mixer_back_kernel, rows, not so_far),
        grid_spec=pltpu.PrefetchScalarGridSpec(
            num_scalar_prefetch=1,
            grid=(steps,),
            in_specs=[
                lane(length), lane(length), lane(length), lane(length), lane(length),
                lane(length), lane(ext), lane(length), lane(length), weight(rows, 0),
                weight(rows, 1), weight(rows // 2, 4), lane(vec.shape[0]), whole(mask), lane(1),
                lane(1), whole(normed), whole(mid_low),
            ]
            + ([kept, kept, kept, whole(so_far[3])] if so_far else []),
            out_specs=[
                piece, piece, lane(16), pl.BlockSpec((ext, model), lambda step, place: (0, 0)),
            ],
            scratch_shapes=[
                pltpu.VMEM((length, width), WIDE),
                pltpu.VMEM((length, 2 * width), LOW),
                pltpu.VMEM((length, 2 * width), LOW),
                pltpu.VMEM((length, width), LOW),
                pltpu.VMEM((length, width), LOW),
                pltpu.VMEM((ext + RIM, width), WIDE),
                pltpu.VMEM((ext, width), LOW),
                pltpu.VMEM((width, model), WIDE),
                pltpu.VMEM((width, width), WIDE),
                pltpu.VMEM((width, 2 * width), LOW),
            ],
        ),
        out_shape=[
            shape, shape,
            jax.ShapeDtypeStruct((16, total), WIDE),
            jax.ShapeDtypeStruct((ext, model), WIDE),
        ],
        input_output_aliases={len(operands) + 1 + k: k for k in range(3)} if so_far else {},
        compiler_params=params(),
        cost_estimate=cost(15 * steps),
        name="mixer_back",
    )(place, *operands, *so_far)


def wide_of(value):
    return value.astype(WIDE)


class Sums:
    def __init__(self, stages, move=swapped):
        self.stages = stages
        self.move = move
        self.result = None
        self.send(next(stages))

    def send(self, transfers):
        self.sent = [value for value, _, _ in transfers]
        self.moving = [self.move(*transfer) for transfer in transfers]

    def step(self):
        try:
            self.send(self.stages.send(self.moving))
        except StopIteration as end:
            self.sent = self.moving = []
            self.result = end.value

    def finish(self):
        while self.result is None:
            self.step()
        return self.result


def fence(arrays, *groups):
    arrays, moving = lax.optimization_barrier((arrays, [group.moving for group in groups]))
    for group, came in zip(groups, moving):
        group.moving = came
    return arrays


def ahead(first, *others):
    moving = [group.moving for group in others]
    moving, _ = lax.optimization_barrier((moving, first.sent))
    for group, came in zip(others, moving):
        group.moving = came


def sent(arrays, *groups):
    arrays, values = lax.optimization_barrier((arrays, [group.sent for group in groups]))
    return arrays


def halved(keep, send):
    slots, matrices, _, part, lanes = keep.shape
    shape = (slots // 4, 2, 2, matrices, 2, part, lanes)
    keep = keep.reshape(shape)
    (came,) = yield [(send, "rows", 1)]
    came = came.reshape(shape)
    both = lambda *where: (wide_of(keep[where]) + wide_of(came[where]))
    every = slice(None)
    near_y = both(every, 0, every, every, 0)
    far_y = both(every, 0, every, every, 1).astype(LOW)
    near_x = both(every, 1, 0)
    far_x = both(every, 1, 1).astype(LOW)
    return (yield from owned(near_y, far_y, near_x, far_x))


def owned(near_y, far_y, near_x, far_x):
    from_y, from_x = yield [(far_y, "rows", 2), (far_x, "chan", 1)]
    rest = lambda place: wide_of(near_y[:, place]) + wide_of(from_y[:, place])
    also = lambda place: wide_of(near_x[:, :, place]) + wide_of(from_x[:, :, place])
    rest_came, also_came = yield [
        (rest(1).astype(LOW), "chan", 1),
        (also(1).astype(LOW), "rows", 2),
    ]
    rest, also = rest(0), also(0)
    parts = {}
    for index in range(rest.shape[0]):
        parts[2 * index] = rest[index] + wide_of(rest_came[index])
        parts[2 * index + 1] = also[index] + wide_of(also_came[index])
    came = yield [
        (value.astype(LOW), "chan", 2 * distance) for distance, value in parts.items() if distance
    ]
    total = parts[0]
    for value in came:
        total = total + wide_of(value)
    return total


def settled(total):
    total = total.astype(LOW)
    (came,) = yield [(total, "rows", 1)]
    pair = jnp.stack([total, came])
    (came,) = yield [(pair, "rows", 2)]
    four = jnp.stack([pair, came])
    place = lax.axis_index("rows")
    four = jnp.where(place & 1, four[:, ::-1], four)
    four = jnp.where(place & 2, four[::-1], four)
    _, _, matrices, part, lanes = four.shape
    four = four.reshape(4, matrices, part, lanes).transpose(1, 0, 2, 3)
    return four.reshape(matrices, 4 * part, lanes).astype(WIDE)


def everywhere(value):
    for axis in ("rows", "chan"):
        bits = 1
        while bits < lax.axis_size(axis):
            (came,) = yield [(value, axis, bits)]
            value = value + came
            bits *= 2
    return value


def gathered(piece):
    parts = lax.axis_size("rows")
    share = piece.shape[0] // parts
    own = lax.dynamic_slice_in_dim(piece, lax.axis_index("rows") * share, share)
    full = lax.all_gather(own, ("chan", "rows"), axis=0, tiled=True)
    return full.reshape(lax.axis_size("chan"), piece.shape[0], piece.shape[1])


def feed_weights(gate_weight, up_weight, down_weight, slab):
    count = lax.axis_size("chan")
    place = lax.axis_index("rows")
    own = jnp.stack([gate_weight.T, up_weight.T, down_weight])
    own = own.reshape(3, 4, -1, own.shape[2])
    quarter = lambda bits: lax.dynamic_index_in_dim(own, place ^ bits, 1, keepdims=False)
    half = jnp.stack([quarter(0), quarter(2)])
    from_chan = [half if pair < 2 else half[0] for pair in range(1, count // 2)]
    from_chan = [swapped(v, "chan", 2 * k) for k, v in enumerate(from_chan, 1)]
    beside = [swapped(half, "chan", 1)]
    from_chan, slab = lax.optimization_barrier((from_chan, slab))
    beside += [swapped(v, "chan", 1) for v in from_chan]
    near = [jnp.stack([v, w], v.ndim - 3) for v, w in zip([half] + from_chan, beside)]
    near = [v if v.ndim == 5 else jnp.stack([v, swapped(v, "rows", 2)]) for v in near]
    other = jnp.stack([quarter(1), quarter(3)])
    far = [jnp.stack([other, swapped(near[0][:, 1], "rows", 1)], 1)]
    far += [swapped(v, "rows", 1) for v in near[1:]]
    return near, far, slab


def local(
    tokens, segments, gelu_weight, gelu_bias, input_weight, input_bias, conv_taps, conv_bias,
    decay_gate, decay_bias, input_gate, ingate_bias, decay_param, out_weight, mixer_gain,
    gate_weight, up_weight, down_weight, feed_gain, cotangent,
):
    length, model = tokens.shape
    rim = conv_taps.shape[0] - 1
    chans = lax.axis_size("chan")
    me, row_place = lax.axis_index("chan"), lax.axis_index("rows")
    rows, block = decay_gate.shape
    total = rows * chans
    width = 2 * block
    group = width // rows

    padded = jnp.concatenate([jnp.full((rim,), -1, jnp.int32), segments])
    window = lax.dynamic_slice_in_dim(padded, me * length, length + rim)
    own = window[rim:]
    same = [own == window[rim - shift : rim - shift + length] for shift in range(1, rim + 1)]
    mask = jnp.stack([same[0], *same, own != 0] + [same[0]] * (7 - rim - 1), 1).astype(WIDE)
    mask = jnp.pad(mask, ((RIM, RIM), (0, 0)))

    small = jnp.concatenate(
        [
            jnp.stack([gelu_bias, input_bias, conv_bias, decay_bias, ingate_bias, decay_param]),
            conv_taps,
        ]
    )
    gate_rows = rows // 2
    slab_rows = -(-(2 * rows + gate_rows + -(-small.size // model)) // 64) * 64
    small_rows = slab_rows - 2 * rows - gate_rows
    flat = jnp.pad(small.reshape(-1), (0, small_rows * model - small.size))
    both = jnp.concatenate([decay_gate, input_gate], 1)
    both = jnp.pad(both, ((0, 0), (0, model // 2 - 2 * block)))
    slab = gathered(
        jnp.concatenate(
            [
                gelu_weight.T,
                input_weight.T,
                jnp.concatenate([both[:gate_rows], both[gate_rows:]], 1),
                flat.reshape(small_rows, model),
            ]
        )
    )
    late = gathered(out_weight)
    out_index = 0
    near, far, slab = feed_weights(gate_weight, up_weight, down_weight, slab)
    small_full = slab[:, 2 * rows + gate_rows :].reshape(chans, -1)[:, : small.size]
    small_full = small_full.reshape(chans, small.shape[0], rows).transpose(1, 0, 2)
    small_full = small_full.reshape(small.shape[0], total).astype(WIDE)
    param = small_full[5:6]
    vec = jnp.concatenate(
        [small_full[:5], -8.0 * jax.nn.softplus(param), small_full[6:], jnp.zeros((6, total), WIDE)]
    )

    rim_tokens = moved_by(tokens[length - rim :], "chan", 1)
    extended = jnp.concatenate([jnp.zeros((RIM - rim, model), WIDE), rim_tokens, tokens])
    normed = rms_norm(extended, mixer_gain).astype(LOW)
    y, u, conv, rate, into, state, factor, decay_sum = mixer_forward(
        normed, slab, vec, mask, rows, width
    )
    carry = Sums(
        entering(jnp.concatenate([factor[-1:], state[-1:]]), "chan", 1), moved_by
    ).finish()
    mixed, middle, normed2 = mixer_out(
        y, state, factor, carry, late, rows, out_index, tokens, feed_gain[None]
    )
    cot_low = cotangent.astype(LOW)
    normed2_too = swapped(normed2, "rows", 1)
    cot_too = swapped(cot_low, "rows", 1)
    block_output, normed2_grad, mine, send = feed(normed2, cot_low, middle, near, far)
    theirs = swapped(send, "rows", 1)

    normed2_grad, normed2_too, cot_too = lax.optimization_barrier(
        (normed2_grad, normed2_too, cot_too)
    )
    mid_grad, mid_low, state_grad, y_grad, feed_gain_sum, back_sum, y_sum = middle_back(
        middle, normed2_grad, cotangent, feed_gain[None], late, rows, out_index, y, state, factor,
        carry,
    )
    after = Sums(
        entering(
            jnp.concatenate([factor[-1:], jnp.sum(back_sum, 0, keepdims=True)]), "chan", -1
        ),
        moved_by,
    )
    mine = sent(mine, after)
    near_y, far_y, near_x, far_x = feed_grads(mine, theirs, normed2, cot_low, normed2_too, cot_too)
    split = lambda value: value.reshape(-1, 2, *value.shape[1:])
    fed = Sums(owned(split(near_y), split(far_y), near_x, far_x))
    ahead(fed, after)
    after = after.finish()
    place = jnp.stack([me // group, me % group, row_place]).astype(jnp.int32)
    so_far = ()
    calls = total // width
    for call in reversed(range(calls)):
        if call == calls // 2 - 1:
            so_far = fence(so_far, fed)
            fed.step()
            so_far = sent(so_far, fed)
        so_far = mixer_back(
            place, state_grad, rate, into, conv, state, factor, u, y_grad, mixed, slab, vec, mask,
            carry, after, normed, mid_low, rows, width, call, 1, so_far,
        )
    keep, send, sums, normed_grad = fence(so_far, fed)
    rest = Sums(halved(keep, send))
    fed.step()
    normed_grad = sent(normed_grad, fed)

    rim_grad = moved_by(normed_grad[RIM - rim : RIM], "chan", -1)
    error = normed_grad[RIM:] + jnp.concatenate([jnp.zeros((length - rim, model), WIDE), rim_grad])
    scale = lax.rsqrt(jnp.mean(tokens * tokens, axis=-1, keepdims=True) + 1e-06)
    gained = mixer_gain * error
    mean = jnp.mean(gained * tokens, axis=-1, keepdims=True)
    tokens_grad = mid_grad + scale * gained - tokens * (scale * scale * scale * mean)
    mixer_gain_sum = jnp.sum(error * tokens * scale, 0)

    slope_grad = sums[4:5] * (-8.0 * jax.nn.sigmoid(param))
    lines = jnp.concatenate(
        [jnp.sum(y_sum, 0, keepdims=True), sums[:4], slope_grad, sums[5:9],
         jnp.sum(decay_sum, 0, keepdims=True)]
    )
    gains = jnp.stack([mixer_gain_sum, jnp.sum(feed_gain_sum, 0)])
    everything = Sums(
        everywhere(jnp.concatenate([lines.reshape(-1, 128), gains.reshape(-1, 128)]))
    )
    rest.step()
    while everything.result is None:
        ahead(rest, everything)
        everything.step()
    everything = everything.result
    rest.moving, everything = lax.optimization_barrier((rest.moving, everything))
    rest.step()
    ahead(rest, fed)
    fed.step()
    fed = Sums(settled(fed.result))
    ahead(fed, rest)
    rest.step()
    ahead(rest, fed)
    fed.step()
    ahead(fed, rest)
    rest.step()
    rest = Sums(settled(rest.result))
    ahead(rest, fed)
    fed.step()
    feed_sum = fed.result
    rest_sum = rest.finish()[0]
    input_sum, gelu_sum, out_sum = (rest_sum[:, k * model : (k + 1) * model] for k in range(3))
    gates_sum = rest_sum[:, 3 * model :]
    cut = lines.size // 128
    gains = everything[cut:].reshape(2, model)
    lines = lax.dynamic_slice_in_dim(
        everything[:cut].reshape(lines.shape), me * rows, rows, axis=1
    )
    mean_decay = lines[10] / (length * lax.axis_size("rows") * chans)
    return (
        block_output,
        tokens_grad,
        gelu_sum.T,
        lines[0],
        input_sum.T,
        lines[1],
        lines[6:10],
        lines[2],
        gates_sum[:, :block],
        lines[3],
        gates_sum[:, block:],
        lines[4],
        lines[5],
        out_sum,
        gains[0],
        feed_sum[0].T,
        feed_sum[1].T,
        feed_sum[2],
        gains[1],
        mean_decay,
    )


def solution(mesh):
    return jax.shard_map(
        local,
        mesh=mesh,
        in_specs=(
            P(("rows", "chan"), None),
            P("rows"),
            P(None, "chan"),
            P("chan"),
            P(None, "chan"),
            P("chan"),
            P(None, "chan"),
            P("chan"),
            P("chan", None),
            P("chan"),
            P("chan", None),
            P("chan"),
            P("chan"),
            P("chan", None),
            P(),
            P(None, "chan"),
            P(None, "chan"),
            P("chan", None),
            P(),
            P(("rows", "chan"), None),
        ),
        out_specs=(
            P(("rows", "chan"), None),
            P(("rows", "chan"), None),
            P(None, "chan"),
            P("chan"),
            P(None, "chan"),
            P("chan"),
            P(None, "chan"),
            P("chan"),
            P("chan", None),
            P("chan"),
            P("chan", None),
            P("chan"),
            P("chan"),
            P("chan", None),
            P(),
            P(None, "chan"),
            P(None, "chan"),
            P("chan", None),
            P(),
            P("chan"),
        ),
        check_vma=False,
    )
```

```python
import functools

import jax
import jax.numpy as jnp
from jax import lax
from jax.experimental import pallas as pl
from jax.experimental.pallas import tpu as pltpu
from jax.sharding import PartitionSpec as P

LOW = jnp.bfloat16
WIDE = jnp.float32
RIM = 16
STEP = 16
VMEM_BYTES = 56 * 1024 * 1024
GELU_SLOPE = 0.7978845608028654
GELU_CUBE = 0.044715


def params(**more):
    return pltpu.CompilerParams(vmem_limit_bytes=VMEM_BYTES, **more)


def moved_by(value, axis, steps):
    count = lax.axis_size(axis)
    leading, last = (max(0, -steps), min(count, count - steps))
    return lax.ppermute(value, axis, [(source, source + steps) for source in range(leading, last)])


def swapped(value, axis, bits):
    count = lax.axis_size(axis)
    return lax.ppermute(value, axis, [(source, source ^ bits) for source in range(count)])


def join(earlier, later):
    return jnp.concatenate(
        [earlier[0:1] * later[0:1], later[0:1] * earlier[1:2] + later[1:2]], 0
    )


def entering(value, axis, sign):
    count = lax.axis_size(axis)
    total = value
    came = yield [(value, axis, sign * reach) for reach in (1, 2, 3) if reach < count]
    for one in came:
        total = join(one, total)
    reach = 4
    while 2 * reach < count:
        (one,) = yield [(total, axis, sign * reach)]
        total = join(one, total)
        reach *= 2
    came = yield [(total, axis, sign * far) for far in (1, reach + 1) if far < count]
    last = came[0]
    for one in came[1:]:
        last = join(one, last)
    return last[1:2]


def rms_norm(values, gain):
    return values * lax.rsqrt(jnp.mean(values * values, axis=-1, keepdims=True) + 1e-06) * gain


def nt(left, right):
    return lax.dot_general(left, right, (((1,), (1,)), ((), ())), preferred_element_type=WIDE)


def tn(left, right):
    return lax.dot_general(left, right, (((0,), (0,)), ((), ())), preferred_element_type=WIDE)


def nn(left, right):
    return lax.dot_general(left, right, (((1,), (0,)), ((), ())), preferred_element_type=WIDE)


def sigmoid(value):
    return 0.5 * jnp.tanh(0.5 * value) + 0.5


def gelu_parts(value):
    square = value * value
    bend = jnp.tanh(GELU_SLOPE * value * (1.0 + GELU_CUBE * square))
    half = 0.5 + 0.5 * bend
    slope = half + 0.5 * GELU_SLOPE * value * (1.0 - bend * bend) * (1.0 + 3.0 * GELU_CUBE * square)
    return value * half, slope


def split_low(value):
    high = value.astype(LOW)
    return high, (value - high.astype(WIDE)).astype(LOW)


def loop(count, unroll, body, init):
    while count % unroll:
        unroll -= 1

    def several(index, carry):
        for turn in range(unroll):
            carry = body(index * unroll + turn, carry)
        return carry

    return lax.fori_loop(0, count // unroll, several, init)


def cost(microseconds):
    return pl.CostEstimate(
        flops=int(microseconds * 1.1e9), bytes_accessed=int(microseconds * 3.5e6), transcendentals=0
    )


def fold(value):
    total = value[0:8]
    for group in range(1, value.shape[0] // 8):
        total = total + value[8 * group : 8 * group + 8]
    return total


def fill_gates(packed, gates, block):
    width = 2 * block
    lines = packed.shape[1] * 3 // 4

    @pl.when(pl.program_id(0) == 0)
    def _():
        gates[...] = jnp.zeros_like(gates)

    parts = []
    for unit in range(packed.shape[0]):
        value = packed[unit].astype(WIDE)[:lines]
        parts += [value[:, 0:width], value[:, 512 : 512 + width]]
    parts = jnp.concatenate(parts, 0).astype(LOW)
    for half in (0, block):
        gates[half : half + block, half : half + block] = parts[half : half + block, 0:block]
        gates[half : half + block, width + half : width + half + block] = parts[
            half : half + block, block:
        ]


def mixer_forward_kernel(
    normed, u_weight, packed, vec, mask, u_out, conv_out, r_out, i_out, h_out, f_out, sum_out,
    high, low, zed, gates,
):
    ext = normed.shape[0]
    width = u_out.shape[1]
    fill_gates(packed, gates, width // 2)
    count = (ext - RIM) // STEP
    u_out[...] = nt(normed[...], u_weight[...]) + vec[1:2, :]

    def convolve(index, _):
        base = pl.multiple_of(index * STEP, STEP)
        own = pl.ds(base, STEP)
        window = u_out[pl.ds(base + 8, STEP + 8), :]
        flags = mask[pl.ds(base + RIM, STEP), :]
        conv = vec[2:3, :] + vec[6:7, :] * window[8:]
        for shift in (1, 2, 3):
            conv = conv + flags[:, shift : shift + 1] * (
                vec[6 + shift : 7 + shift, :] * window[8 - shift : 8 - shift + STEP]
            )
        conv = conv * flags[:, 4:5]
        conv_out[own, :] = conv
        high[own, :], low[own, :] = split_low(conv)
        return 0

    loop(count, 4, convolve, 0)
    zed[...] = nn(high[...], gates[...]) + nn(low[...], gates[...])
    line = lax.broadcasted_iota(jnp.int32, (8, width), 0)

    def advance(index, carry):
        state, factor, total = carry
        own = pl.ds(pl.multiple_of(index * STEP, STEP), STEP)
        going = mask[pl.ds(pl.multiple_of(index * STEP + RIM, STEP), STEP), :][:, 0:1]
        rate = sigmoid(zed[own, 0:width] + vec[3:4, :])
        into = sigmoid(zed[own, width:] + vec[4:5, :])
        decay = jnp.exp(vec[5:6, :] * rate)
        r_out[own, :] = rate
        i_out[own, :] = into
        scale = jnp.where(going == 0.0, 1.0, jnp.sqrt(1.01 - decay * decay))
        inject = conv_out[own, :] * into * scale
        carried = decay * going
        total = total + fold(decay)
        for group in range(STEP // 8):
            part = slice(8 * group, 8 * group + 8)
            mul, add = carried[part], inject[part]
            for reach in (1, 2, 4):
                inside = line >= reach
                add = add + mul * jnp.where(inside, pltpu.roll(add, reach, 0), 0.0)
                mul = mul * jnp.where(inside, pltpu.roll(mul, reach, 0), 1.0)
            here = add + mul * state
            gone = mul * factor
            rows = pl.ds(pl.multiple_of(index * STEP + 8 * group, 8), 8)
            h_out[rows, :] = here
            f_out[rows, :] = gone
            state, factor = here[7:8], gone[7:8]
        return state, factor, total

    zero = jnp.zeros((1, width), WIDE)
    _, _, total = loop(
        count, 4, advance, (zero, zero + 1.0, jnp.zeros((8, width), WIDE))
    )
    sum_out[...] = total


def mixer_forward(normed, u_weight, packed, vec, mask, width):
    ext, model = normed.shape
    tokens = ext - RIM
    total = u_weight.shape[0]
    pairs = total // width
    units = packed.shape[0] // pairs
    by_lane = lambda length: pl.BlockSpec((length, width), lambda step: (0, step))
    whole = lambda array: pl.BlockSpec(array.shape, lambda step: (0,) * array.ndim)
    flat = jax.ShapeDtypeStruct((tokens, total), WIDE)
    return pl.pallas_call(
        mixer_forward_kernel,
        grid=(pairs,),
        in_specs=[
            whole(normed),
            pl.BlockSpec((width, model), lambda step: (step, 0)),
            pl.BlockSpec((units, *packed.shape[1:]), lambda step: (step, 0, 0)),
            by_lane(vec.shape[0]),
            whole(mask),
        ],
        out_specs=[by_lane(ext)] + [by_lane(tokens)] * 5 + [by_lane(8)],
        out_shape=[jax.ShapeDtypeStruct((ext, total), WIDE)] + [flat] * 5
        + [jax.ShapeDtypeStruct((8, total), WIDE)],
        scratch_shapes=[
            pltpu.VMEM((tokens, width), LOW),
            pltpu.VMEM((tokens, width), LOW),
            pltpu.VMEM((tokens, 2 * width), WIDE),
            pltpu.VMEM((width, 2 * width), LOW),
        ],
        compiler_params=params(),
        cost_estimate=cost(26),
        name="mixer_forward",
    )(normed, u_weight, packed, vec, mask)


def gelu_branch_kernel(normed, weight, vec, active_out, slope_out, held):
    held[...] = nt(normed[RIM:, :], weight[...]) + vec[0:1, :]

    def act(index, _):
        own = pl.ds(pl.multiple_of(index * STEP, STEP), STEP)
        active_out[own, :], slope_out[own, :] = gelu_parts(held[own, :])
        return 0

    loop(held.shape[0] // STEP, 4, act, 0)


def gelu_branch(normed, weight, vec, width):
    length, total = normed.shape[0] - RIM, weight.shape[0]
    model = normed.shape[1]
    lane = lambda lines: pl.BlockSpec((lines, width), lambda step: (0, step))
    return pl.pallas_call(
        gelu_branch_kernel,
        grid=(total // width,),
        in_specs=[
            pl.BlockSpec(normed.shape, lambda step: (0, 0)),
            pl.BlockSpec((width, model), lambda step: (step, 0)),
            lane(vec.shape[0]),
        ],
        out_specs=[lane(length), lane(length)],
        out_shape=[jax.ShapeDtypeStruct((length, total), WIDE)] * 2,
        scratch_shapes=[pltpu.VMEM((length, width), WIDE)],
        compiler_params=params(),
        cost_estimate=cost(8),
        name="gelu_branch",
    )(normed, weight, vec)


def mixer_out_kernel(active, h, f, state, weight, tokens, gain, mixed, middle, normed):
    def gate(index, _):
        own = pl.ds(pl.multiple_of(index * STEP, STEP), STEP)
        mixed[own, :] = ((h[own, :] + f[own, :] * state[...]) * active[own, :]).astype(LOW)
        return 0

    loop(active.shape[0] // STEP, 4, gate, 0)
    total = tokens[...] + nn(mixed[...], weight[...])
    middle[...] = total
    scale = lax.rsqrt(jnp.mean(total * total, axis=-1, keepdims=True) + 1e-06)
    normed[...] = (total * scale * gain[...]).astype(LOW)


def mixer_out(active, h, f, state, weight, tokens, gain):
    length, model = tokens.shape
    total = active.shape[1]
    tile = 256 if length % 256 == 0 else length
    row = lambda lanes: pl.BlockSpec((tile, lanes), lambda step: (step, 0))
    one = lambda array: pl.BlockSpec(array.shape, lambda step: (0, 0))
    return pl.pallas_call(
        mixer_out_kernel,
        grid=(length // tile,),
        in_specs=[
            row(total), row(total), row(total), one(state), one(weight), row(model), one(gain),
        ],
        out_specs=[row(total), row(model), row(model)],
        out_shape=[
            jax.ShapeDtypeStruct((length, total), LOW),
            jax.ShapeDtypeStruct((length, model), WIDE),
            jax.ShapeDtypeStruct((length, model), LOW),
        ],
        compiler_params=params(),
        cost_estimate=cost(9),
        name="mixer_out",
    )(active, h, f, state, weight, tokens, gain)


def spread(place, wide, keep, send, matrix, group, rows, lanes=slice(None), count=None):
    part = rows // 4
    if part % 8:
        value = wide[:, 0:count]
        pieces = [value[begin : begin + part] for begin in range(0, group * rows, part)]
        mine = place[1] * 4 + place[2]
        bit = 1
        while bit < len(pieces):
            turned = (mine & bit) != 0
            pieces = [
                jnp.where(turned, pieces[index ^ bit], pieces[index])
                for index in range(len(pieces))
            ]
            bit *= 2
    for slot in range(group):
        shard = slot ^ place[1]
        for turn in range(4):
            if part % 8:
                value = pieces[4 * slot + turn]
            else:
                begin = pl.multiple_of(shard * rows + (turn ^ place[2]) * part, 8)
                value = wide[pl.ds(begin, part), 0:count]
            (keep, send)[turn & 1][slot, matrix, turn >> 1, :, lanes] = value.astype(LOW)


def feed_kernel(
    place, normed, cot, out_in, units, out, grad, keep, send, gate_s, up_s, back_s, hidden_l,
    gate_l, up_l, held, sems,
):
    half = gate_s.shape[0] // 2
    model = normed.shape[1]
    width = gate_s.shape[0]
    part = width // 4
    step = pl.program_id(0)

    def copies(index):
        for turn in range(4):
            unit = (place[0] ^ index) * 4 + (place[1] ^ turn)
            order = (turn % 2) * 2 + turn // 2
            slot = index % 2
            yield pltpu.make_async_copy(
                units.at[unit], held.at[slot, :, order], sems.at[slot, turn]
            )

    @pl.when(step == 0)
    def _():
        out[...] = out_in[...]
        grad[...] = jnp.zeros_like(grad)
        for copy in copies(0):
            copy.start()

    @pl.when(step + 1 < pl.num_programs(0))
    def _():
        for copy in copies(step + 1):
            copy.start()

    for copy in copies(step):
        copy.wait()

    def weight(matrix):
        if part % 16 == 0:
            return held[step % 2, matrix].reshape(width, model)
        pieces = [held[step % 2, matrix, turn].astype(WIDE) for turn in range(4)]
        return jnp.concatenate(pieces, 0).astype(LOW)

    first, second, third = weight(0), weight(1), weight(2)
    for begin in (0, half):
        rows = slice(begin, begin + half)
        gate_s[rows, :] = nt(first[rows], normed[...])
        up_s[rows, :] = nt(second[rows], normed[...])
        back_s[rows, :] = nt(third[rows], cot[...])
    for index in range(width // STEP):
        own = slice(index * STEP, index * STEP + STEP)
        up, back = up_s[own, :], back_s[own, :]
        value, slope = gelu_parts(gate_s[own, :])
        hidden_l[own, :] = (value * up).astype(LOW)
        gate_l[own, :] = (back * up * slope).astype(LOW)
        up_l[own, :] = (back * value).astype(LOW)
    out[...] += tn(hidden_l[...], third)
    grad[...] += tn(gate_l[...], first) + tn(up_l[...], second)
    for matrix, value in enumerate((gate_l, up_l, hidden_l)):
        keep[0, matrix] = value[:half, :]
        send[0, matrix] = value[half:, :]


def feed(place, normed, cot, out_in, units):
    length, model = normed.shape
    part = units.shape[2]
    slots = units.shape[0] // 4
    width = 4 * part
    whole = lambda array: pl.BlockSpec(array.shape, lambda step, place: (0,) * array.ndim)
    piece = pl.BlockSpec((1, 3, 2 * part, length), lambda step, place: (step, 0, 0, 0))
    wide = jax.ShapeDtypeStruct((length, model), WIDE)
    grads = jax.ShapeDtypeStruct((slots, 3, 2 * part, length), LOW)
    return pl.pallas_call(
        feed_kernel,
        grid_spec=pltpu.PrefetchScalarGridSpec(
            num_scalar_prefetch=1,
            grid=(slots,),
            in_specs=[
                whole(normed), whole(cot), whole(out_in), pl.BlockSpec(memory_space=pl.ANY),
            ],
            out_specs=[whole(out_in), whole(out_in), piece, piece],
            scratch_shapes=[pltpu.VMEM((width, length), WIDE)] * 3
            + [pltpu.VMEM((width, length), LOW)] * 3
            + [pltpu.VMEM((2, 3, 4, part, model), LOW), pltpu.SemaphoreType.DMA((2, 4))],
        ),
        out_shape=[wide, wide, grads, grads],
        compiler_params=params(),
        cost_estimate=cost(34),
        name="feed",
    )(place, normed, cot, out_in, units)


def feed_grads_kernel(pairs, mine, theirs, normed, cot, normed_too, cot_too, *outs):
    part = outs[0].shape[2]
    step = pl.program_id(0)
    for matrix in range(3):
        right, right_too = (cot, cot_too) if matrix == 2 else (normed, normed_too)
        value = nn(mine[0, matrix], right[...]) + nn(theirs[0, matrix], right_too[...])
        value = value.astype(LOW)

        @pl.when(step < pairs)
        def _():
            outs[0][0, matrix] = value[:part]
            outs[1][0, matrix] = value[part:]

        for place, out in ((pairs, outs[2]), (pairs + pairs // 2, outs[3])):

            @pl.when((step >= place) & (step < place + pairs // 2))
            def _():
                out[0, matrix, 0] = value[:part]
                out[0, matrix, 1] = value[part:]


def feed_grads(mine, theirs, normed, cot, normed_too, cot_too):
    slots, _, rows, length = mine.shape
    model = normed.shape[1]
    pairs, part = slots // 2, rows // 2
    whole = lambda array: pl.BlockSpec(array.shape, lambda step: (0,) * array.ndim)

    def source(step):
        even = 4 * (step // 2) + step % 2
        odd = step - pairs
        last = odd >= pairs // 2
        odd = 4 * jnp.where(last, odd - pairs // 2, odd) + 2 + last.astype(jnp.int32)
        return jnp.where(step < pairs, even, odd), 0, 0, 0

    clipped = lambda first, count: lambda step: jnp.clip(step - first, 0, count - 1)
    even = clipped(0, pairs)
    spec = lambda place, count: pl.BlockSpec(
        (1, 3, 2, part, model), lambda step: (clipped(place, count)(step), 0, 0, 0, 0)
    )
    flat = pl.BlockSpec((1, 3, part, model), lambda step: (even(step), 0, 0, 0))
    return pl.pallas_call(
        functools.partial(feed_grads_kernel, pairs),
        grid=(slots,),
        in_specs=[pl.BlockSpec((1, 3, rows, length), source)] * 2
        + [whole(normed)] * 4,
        out_specs=[flat, flat, spec(pairs, pairs // 2), spec(pairs + pairs // 2, pairs // 2)],
        out_shape=[jax.ShapeDtypeStruct((pairs, 3, part, model), LOW)] * 2
        + [jax.ShapeDtypeStruct((pairs // 2, 3, 2, part, model), LOW)] * 2,
        compiler_params=params(),
        cost_estimate=cost(17),
        name="feed_grads",
    )(mine, theirs, normed, cot, normed_too, cot_too)


def middle_back_kernel(
    middle, grad, cot, gain, weight, active_in, slope_in, h, f, state, mid_grad, mid_low, state_grad, y_grad,
    gain_sum, back_sum, bias_sum, mixed_s,
):
    @pl.when(pl.program_id(0) == 0)
    def _():
        gain_sum[...] = jnp.zeros_like(gain_sum)
        back_sum[...] = jnp.zeros_like(back_sum)
        bias_sum[...] = jnp.zeros_like(bias_sum)

    value, error = middle[...], grad[...]
    scale = lax.rsqrt(jnp.mean(value * value, axis=-1, keepdims=True) + 1e-06)
    gained = gain[...] * error
    mean = jnp.mean(gained * value, axis=-1, keepdims=True)
    total = cot[...] + scale * gained - value * (scale * scale * scale * mean)
    gain_sum[...] += fold(error * value * scale)
    mid_grad[...] = total
    mid_low[...] = total.astype(LOW)
    mixed_s[...] = nt(mid_low[...], weight[...])

    def turn(index, carry):
        back, bias = carry
        own = pl.ds(pl.multiple_of(index * STEP, STEP), STEP)
        error = mixed_s[own, :]
        active, slope = active_in[own, :], slope_in[own, :]
        gone = f[own, :]
        full = h[own, :] + gone * state[...]
        here = error * active
        state_grad[own, :] = here
        low = (error * full * slope).astype(LOW)
        y_grad[own, :] = low
        return back + fold(here * gone), bias + fold(low.astype(WIDE))

    zero = jnp.zeros(back_sum.shape, WIDE)
    back, bias = loop(middle.shape[0] // STEP, 4, turn, (zero, zero))
    back_sum[...] += back
    bias_sum[...] += bias


def middle_back(middle, grad, cot, gain, weight, active, slope, h, f, state):
    length, model = middle.shape
    total = active.shape[1]
    tile = 256 if length % 256 == 0 else length
    row = lambda lanes: pl.BlockSpec((tile, lanes), lambda step: (step, 0))
    one = lambda lines, lanes: pl.BlockSpec((lines, lanes), lambda step: (0, 0))
    return pl.pallas_call(
        middle_back_kernel,
        grid=(length // tile,),
        in_specs=[
            row(model), row(model), row(model), one(1, model),
            one(total, model), row(total), row(total), row(total), row(total), one(1, total),
        ],
        out_specs=[
            row(model), row(model), row(total), row(total), one(8, model), one(8, total),
            one(8, total),
        ],
        out_shape=[
            jax.ShapeDtypeStruct((length, model), WIDE),
            jax.ShapeDtypeStruct((length, model), LOW),
            jax.ShapeDtypeStruct((length, total), WIDE),
            jax.ShapeDtypeStruct((length, total), LOW),
            jax.ShapeDtypeStruct((8, model), WIDE),
            jax.ShapeDtypeStruct((8, total), WIDE),
            jax.ShapeDtypeStruct((8, total), WIDE),
        ],
        scratch_shapes=[pltpu.VMEM((tile, total), WIDE)],
        compiler_params=params(),
        cost_estimate=cost(13),
        name="middle_back",
    )(middle, grad, cot, gain, weight, active, slope, h, f, state)


def mixer_back_kernel(
    rows, first, place, state_grad, r_in, i_in, conv_in, h, f, u, y_grad, mixed, y_weight, u_weight,
    packed, vec, mask, state, after, normed, mid_low, y_sum, decay_sum, *refs
):
    if not first:
        grad_in, refs = refs[2], refs[3:]
    (
        keep, send, normed_grad, conv_s, high, low, conv_h, conv_l, grown, u_low, wide, gate_w,
        gates, sums,
    ) = refs
    length, width = state_grad.shape
    ext, model = normed.shape
    group = width // rows
    block = width // 2
    count = length // STEP
    line = lax.broadcasted_iota(jnp.int32, (8, width), 0)

    fill_gates(packed, gates, block)

    @pl.when(pl.program_id(0) == 0)
    def _():
        if first:
            normed_grad[...] = jnp.zeros_like(normed_grad)
        else:
            normed_grad[...] = grad_in[...]

    def retreat(index, carry):
        error, rate_sum, into_sum, slope_sum = carry
        base = pl.multiple_of((count - 1 - index) * STEP, STEP)
        own = pl.ds(base, STEP)
        going = mask[pl.ds(base + RIM, STEP), :][:, 0:1]
        rate, into, conv = r_in[own, :], i_in[own, :], conv_in[own, :]
        slope = vec[5:6, :]
        decay = jnp.exp(slope * rate)
        carried = decay * going
        given = state_grad[own, :]
        full = h[own, :] + f[own, :] * state[...]
        ahead = pl.ds(pl.multiple_of(jnp.maximum(base - 8, 0), 8), 8)
        edge = h[ahead, :][7:8] + f[ahead, :][7:8] * state[...]
        edge = jnp.where(base == 0, state[...], edge)
        parts = []
        for part in reversed(range(STEP // 8)):
            place_of = slice(8 * part, 8 * part + 8)
            mul = carried[place_of]
            add = mul * given[place_of]
            for reach in (1, 2, 4):
                inside = line < 8 - reach
                add = add + mul * jnp.where(inside, pltpu.roll(add, 8 - reach, 0), 0.0)
                mul = mul * jnp.where(inside, pltpu.roll(mul, 8 - reach, 0), 1.0)
            here = add + mul * error
            parts.append(given[place_of] + jnp.where(line < 7, pltpu.roll(here, 7, 0), error))
            error = here[0:1]
        grad = jnp.concatenate(parts[::-1], 0)
        befores = []
        for part in range(STEP // 8):
            last = edge if part == 0 else full[8 * part - 1 : 8 * part]
            befores.append(
                jnp.where(line > 0, pltpu.roll(full[8 * part : 8 * part + 8], 1, 0), last)
            )
        before = jnp.concatenate(befores, 0)
        root = lax.rsqrt(1.01 - decay * decay)
        scale = jnp.where(going == 0.0, 1.0, (1.01 - decay * decay) * root)
        through = grad * conv
        into_grad = through * scale
        conv_s[own, :] = grad * into * scale
        decay_grad = going * decay * (grad * before - through * into * decay * root)
        z_rate = decay_grad * slope * rate * (1.0 - rate)
        z_into = into_grad * into * (1.0 - into)
        high[own, 0:width], low[own, 0:width] = split_low(z_rate)
        high[own, width:], low[own, width:] = split_low(z_into)
        conv_h[own, :], conv_l[own, :] = split_low(conv)
        return (
            error,
            rate_sum + fold(z_rate),
            into_sum + fold(z_into),
            slope_sum + fold(decay_grad * rate),
        )

    zero = jnp.zeros((8, width), WIDE)
    _, rate_sum, into_sum, slope_sum = loop(
        count, 4, retreat, (after[...], zero, zero, zero)
    )
    conv_s[...] += nt(high[...], gates[...]) + nt(low[...], gates[...])
    gate_full = (
        tn(conv_h[...], high[...]) + tn(conv_l[...], high[...]) + tn(conv_h[...], low[...])
    )
    for half in (0, block):
        rows_of = slice(half, half + block)
        gate_w[rows_of, 0:block] = gate_full[rows_of, half : half + block]
        gate_w[rows_of, block:] = gate_full[rows_of, width + half : width + half + block]
    grown[0:RIM, :] = jnp.zeros((RIM, width), WIDE)
    grown[RIM + length :, :] = jnp.zeros((RIM, width), WIDE)

    def taps(index, carry):
        base = pl.multiple_of(index * STEP, STEP)
        window = u[pl.ds(base + 8, STEP + 8), :]
        flags = mask[pl.ds(base + RIM, STEP), :]
        error = conv_s[pl.ds(base, STEP), :] * flags[:, 4:5]
        grown[pl.ds(base + RIM, STEP), :] = error
        out = [carry[0] + fold(error), carry[1] + fold(error * window[8:])]
        for shift in (1, 2, 3):
            moved = window[8 - shift : 8 - shift + STEP]
            out.append(carry[1 + shift] + fold(flags[:, shift : shift + 1] * error * moved))
        return tuple(out)

    bias_sum, *tap_sums = loop(count, 4, taps, (zero,) * 5)

    def spread_back(index, total):
        base = pl.multiple_of(index * STEP, STEP)
        window = grown[pl.ds(base, STEP + 8), :]
        flags = mask[pl.ds(base, STEP + 8), :]
        value = vec[6:7, :] * window[0:STEP]
        for shift in (1, 2, 3):
            masked = flags[:, shift : shift + 1] * window
            value = value + vec[6 + shift : 7 + shift, :] * masked[shift : shift + STEP]
        rounded = value.astype(LOW)
        u_low[pl.ds(base, STEP), :] = rounded
        return total + fold(rounded.astype(WIDE))

    input_sum = loop(ext // STEP, 3, spread_back, zero)
    sums[...] = jnp.zeros_like(sums)
    slope_sum = slope_sum * vec[10:11, :]
    values = (y_sum[...], input_sum, *tap_sums, bias_sum, rate_sum, into_sum, slope_sum, decay_sum[...])
    for row, value in enumerate(values):
        sums[row : row + 1, :] = jnp.sum(value, axis=0, keepdims=True)
    wide[:, 0:128] = jnp.transpose(sums[...])
    spread(place, wide, keep, send, 0, group, rows, slice(3 * model + width, None), 128)
    wide[...] = tn(u_low[...], normed[...])
    spread(place, wide, keep, send, 0, group, rows, slice(0, model))
    spread(place, gate_w, keep, send, 0, group, rows, slice(3 * model, 3 * model + width))
    wide[...] = tn(y_grad[...], normed[RIM:, :])
    spread(place, wide, keep, send, 0, group, rows, slice(model, 2 * model))
    wide[...] = tn(mixed[...], mid_low[...])
    spread(place, wide, keep, send, 0, group, rows, slice(2 * model, 3 * model))
    normed_grad[...] += nn(u_low[...], u_weight[...])
    normed_grad[RIM:, :] += nn(y_grad[...], y_weight[...])


def mixer_back(
    place, state_grad, r, i, conv, h, f, u, y_grad, mixed, y_weight, u_weight, packed, vec, mask,
    state, after, normed, mid_low, y_sum, decay_sum, rows, width, begin, steps, so_far=(),
):
    length, total = state_grad.shape
    ext, model = normed.shape
    group, part = width // rows, rows // 4
    pair = lambda step, place: (step + begin) ^ place[0]
    whole = lambda array: pl.BlockSpec(array.shape, lambda step, place: (0,) * array.ndim)
    lane = lambda lines: pl.BlockSpec((lines, width), lambda step, place: (0, pair(step, place)))
    weight = pl.BlockSpec((width, model), lambda step, place: (pair(step, place), 0))
    units = packed.shape[0] * width // total
    lanes = 3 * model + width + 128
    piece = pl.BlockSpec((group, 1, 2, part, lanes), lambda step, place: (step + begin, 0, 0, 0, 0))
    shape = jax.ShapeDtypeStruct((total // rows, 1, 2, part, lanes), LOW)
    operands = [
        state_grad, r, i, conv, h, f, u, y_grad, mixed, y_weight, u_weight, packed, vec, mask,
        state, after, normed, mid_low, y_sum, decay_sum,
    ]
    kept = pl.BlockSpec(memory_space=pl.ANY)
    return pl.pallas_call(
        functools.partial(mixer_back_kernel, rows, not so_far),
        grid_spec=pltpu.PrefetchScalarGridSpec(
            num_scalar_prefetch=1,
            grid=(steps,),
            in_specs=[
                lane(length), lane(length), lane(length), lane(length), lane(length),
                lane(length), lane(ext), lane(length), lane(length), weight, weight,
                pl.BlockSpec(
                    (units, *packed.shape[1:]), lambda step, place: (pair(step, place), 0, 0)
                ),
                lane(vec.shape[0]), whole(mask), lane(1),
                lane(1), whole(normed), whole(mid_low), lane(8), lane(8),
            ]
            + ([kept, kept, whole(so_far[2])] if so_far else []),
            out_specs=[
                piece, piece, pl.BlockSpec((ext, model), lambda step, place: (0, 0)),
            ],
            scratch_shapes=[
                pltpu.VMEM((length, width), WIDE),
                pltpu.VMEM((length, 2 * width), LOW),
                pltpu.VMEM((length, 2 * width), LOW),
                pltpu.VMEM((length, width), LOW),
                pltpu.VMEM((length, width), LOW),
                pltpu.VMEM((ext + RIM, width), WIDE),
                pltpu.VMEM((ext, width), LOW),
                pltpu.VMEM((width, model), WIDE),
                pltpu.VMEM((width, width), WIDE),
                pltpu.VMEM((width, 2 * width), LOW),
                pltpu.VMEM((128, width), WIDE),
            ],
        ),
        out_shape=[shape, shape, jax.ShapeDtypeStruct((ext, model), WIDE)],
        input_output_aliases={len(operands) + 1 + k: k for k in range(2)} if so_far else {},
        compiler_params=params(),
        cost_estimate=cost(15 * steps),
        name="mixer_back",
    )(place, *operands, *so_far)


def wide_of(value):
    return value.astype(WIDE)


def pin_kernel(source, target):
    del source, target


class Clock:
    def __init__(self):
        self.time = jnp.zeros((8, 128), WIDE)

    def tick(self, values):
        values, self.time = lax.optimization_barrier((values, self.time))
        return values

    def pin(self):
        self.time = pl.pallas_call(
            pin_kernel,
            in_specs=[pl.BlockSpec(memory_space=pl.ANY)],
            out_specs=pl.BlockSpec(memory_space=pl.ANY),
            out_shape=jax.ShapeDtypeStruct(self.time.shape, WIDE),
            input_output_aliases={0: 0},
            cost_estimate=cost(5000),
            name="pin",
        )(self.time)


class Sums:
    def __init__(self, clock, stages, move=swapped, pin=False, start=True):
        self.clock = clock
        self.stages = stages
        self.move = move
        self.result = self.moving = None
        if start:
            self.begin(pin)

    def begin(self, pin=False):
        self.send(next(self.stages), pin)

    def send(self, transfers, pin):
        values = self.clock.tick([transfer[0] for transfer in transfers])
        self.moving = [
            self.move(value, *transfer[1:]) for value, transfer in zip(values, transfers)
        ]
        if pin:
            self.clock.pin()

    def step(self, pin=False):
        try:
            transfers = self.stages.send(self.clock.tick(self.moving))
        except StopIteration as end:
            self.result = end.value
        else:
            self.send(transfers, pin)

    def finish(self):
        while self.result is None:
            self.step()
        return self.result


def halved(keep, send):
    slots, matrices, _, part, lanes = keep.shape
    shape = (slots // 4, 2, 2, matrices, 2, part, lanes)
    keep = keep.reshape(shape)
    (came,) = yield [(send, "rows", 1)]
    came = came.reshape(shape)
    both = lambda *where: (wide_of(keep[where]) + wide_of(came[where]))
    every = slice(None)
    near_y = lambda place: both(every, 0, place, every, 0)
    far_y = both(every, 0, every, every, 1).astype(LOW)
    near_x = lambda place: both(every, 1, 0, every, place)
    far_x = both(every, 1, 1).astype(LOW)
    return (yield from owned(near_y, far_y, near_x, far_x))


def owned(near_y, far_y, near_x, far_x):
    from_y, from_x = yield [(far_y, "rows", 2), (far_x, "chan", 1)]
    rest = lambda place: wide_of(near_y(place)) + wide_of(from_y[:, place])
    also = lambda place: wide_of(near_x(place)) + wide_of(from_x[:, :, place])
    rest_came, also_came = yield [
        (rest(1).astype(LOW), "chan", 1),
        (also(1).astype(LOW), "rows", 2),
    ]
    rest, also = rest(0), also(0)
    parts = {}
    for index in range(rest.shape[0]):
        parts[2 * index] = rest[index] + wide_of(rest_came[index])
        parts[2 * index + 1] = also[index] + wide_of(also_came[index])
    came = yield [
        (value.astype(LOW), "chan", 2 * distance) for distance, value in parts.items() if distance
    ]
    total = parts[0]
    for value in came:
        total = total + wide_of(value)
    return total


def settled(total):
    total = total.astype(LOW)
    (came,) = yield [(total, "rows", 2)]
    pair = jnp.stack([total, came])
    (came,) = yield [(pair, "rows", 1)]
    return pair, came


def ordered(pair, came):
    four = jnp.stack([pair, came], 1)
    place = lax.axis_index("rows")
    four = jnp.where(place & 1, four[:, ::-1], four)
    four = jnp.where(place & 2, four[::-1], four)
    _, _, matrices, part, lanes = four.shape
    four = four.reshape(4, matrices, part, lanes).transpose(1, 0, 2, 3)
    return four.reshape(matrices, 4 * part, lanes).astype(WIDE)


def finish_kernel(place, pair, came, gate, up, down):
    def rows_of(matrix):
        parts = []
        for quarter in range(4):
            turn = quarter ^ place[1]
            own, other = (ref[turn // 2, matrix].astype(WIDE) for ref in (pair, came))
            parts.append(jnp.where(turn % 2 == 0, own, other))
        return jnp.concatenate(parts, 0)

    gate[...] = jnp.transpose(rows_of(0))
    up[...] = jnp.transpose(rows_of(1))
    down[...] = rows_of(2)


def finish(place, pair, came):
    _, _, part, model = pair.shape
    tall = jax.ShapeDtypeStruct((model, 4 * part), WIDE)
    vmem = pl.BlockSpec(memory_space=pltpu.VMEM)
    return pl.pallas_call(
        finish_kernel,
        grid_spec=pltpu.PrefetchScalarGridSpec(
            num_scalar_prefetch=1, grid=(1,), in_specs=[vmem] * 2, out_specs=[vmem] * 3
        ),
        out_shape=[tall, tall, jax.ShapeDtypeStruct((4 * part, model), WIDE)],
        compiler_params=params(),
        cost_estimate=cost(4),
        name="finish",
    )(place, pair, came)


def everywhere(value):
    for axis in ("rows", "chan"):
        bits = 1
        while bits < lax.axis_size(axis):
            (came,) = yield [(value, axis, bits)]
            value = value + came
            bits *= 2
    return value


def gathered(piece):
    parts = lax.axis_size("rows")
    share = piece.shape[0] // parts
    own = lax.dynamic_slice_in_dim(piece, lax.axis_index("rows") * share, share)
    full = lax.all_gather(own, ("chan", "rows"), axis=0, tiled=True)
    return full.reshape(lax.axis_size("chan"), piece.shape[0], piece.shape[1])


def pack_kernel(table, count, *refs):
    sources, outs, sems = refs[:count], refs[count:-1], refs[-1]
    copies = [
        pltpu.make_async_copy(
            sources[source].at[begin : begin + size],
            outs[out].at[at : at + size],
            sems.at[index],
        )
        for index, (out, at, source, begin, size) in enumerate(table)
    ]
    for copy in copies:
        copy.start()
    for copy in copies:
        copy.wait()


def pack(*lists):
    sources, table, shapes = [], [], []
    for out, pieces in enumerate(lists):
        at = 0
        for array, begin, size in pieces:
            known = [index for index, one in enumerate(sources) if one is array]
            if not known:
                known = [len(sources)]
                sources.append(array)
            table.append((out, at, known[0], begin, size))
            at += size
        shapes.append(jax.ShapeDtypeStruct((at, *pieces[0][0].shape[1:]), pieces[0][0].dtype))
    return pl.pallas_call(
        functools.partial(pack_kernel, table, len(sources)),
        in_specs=[pl.BlockSpec(memory_space=pl.ANY)] * len(sources),
        out_specs=[pl.BlockSpec(memory_space=pltpu.VMEM)] * len(shapes),
        scratch_shapes=[pltpu.SemaphoreType.DMA((len(table),))],
        out_shape=shapes,
        compiler_params=params(),
        cost_estimate=cost(0.01),
        name="pack",
    )(*sources)


def spread_units(units):
    pairs = range(2, lax.axis_size("chan") // 2)
    count = len(pairs)
    behind, *came = yield [(units[:2], "chan", 2)] + [
        (units[:1], "chan", 2 * pair) for pair in pairs
    ]
    singles = [(value, 0, 1) for value in came]
    (turned,) = pack([(units, 0, 1), (behind, 0, 2), *singles])
    (corners,) = yield [(turned, "chan", 1)]
    near, away = pack(
        [(behind, 0, 2), (corners, 1, 2)], [(corners, 0, 1), *singles, (corners, 3, count)]
    )
    over, near_too = yield [(away, "rows", 2), (near, "rows", 1)]
    size = 2 * count + 1
    (away,) = pack([(away, 0, size), (over, 0, size)])
    (away_too,) = yield [(away, "rows", 1)]
    return units, near, near_too, away, away_too


def unit_source(pair, side, turn, count):
    upper, other = turn // 2, turn % 2
    if pair == 0 and side == 0:
        return 0, 2 * other + upper
    if pair == 1:
        return 1 + other, 2 * side + upper
    if pair == 0:
        return 3 + other, upper * (2 * count + 1)
    return 3 + other, upper * (2 * count + 1) + 1 + side * count + pair - 2


def assemble_kernel(cuts, pairs, place, *refs):
    sources, outs, sems = refs[:5], refs[5:-1], refs[-1]
    copies = []
    for pair in range(pairs):
        for side in range(2):
            for turn in range(4):
                array, index = unit_source(pair, side, turn, pairs - 2)
                unit = ((2 * pair + side) ^ place[0]) * 4 + (turn ^ place[1])
                for (begin, end), out in zip(cuts, outs):
                    copies.append(
                        pltpu.make_async_copy(
                            sources[array].at[index, begin:end],
                            out.at[unit],
                            sems.at[len(copies)],
                        )
                    )
    for copy in copies:
        copy.start()
    for copy in copies:
        copy.wait()


def assembled(place, sources, cuts):
    pairs = lax.axis_size("chan") // 2
    model = sources[0].shape[2]
    anywhere = pl.BlockSpec(memory_space=pl.ANY)
    return pl.pallas_call(
        functools.partial(assemble_kernel, cuts, pairs),
        grid_spec=pltpu.PrefetchScalarGridSpec(
            num_scalar_prefetch=1,
            grid=(1,),
            in_specs=[anywhere] * 5,
            out_specs=[pl.BlockSpec(memory_space=pltpu.VMEM)] * len(cuts),
            scratch_shapes=[pltpu.SemaphoreType.DMA((8 * pairs * len(cuts),))],
        ),
        out_shape=[
            jax.ShapeDtypeStruct((8 * pairs, end - begin, model), LOW) for begin, end in cuts
        ],
        compiler_params=params(),
        cost_estimate=cost(5),
        name="assemble",
    )(place, *sources)


def local(
    tokens, segments, gelu_weight, gelu_bias, input_weight, input_bias, conv_taps, conv_bias,
    decay_gate, decay_bias, input_gate, ingate_bias, decay_param, out_weight, mixer_gain,
    gate_weight, up_weight, down_weight, feed_gain, cotangent,
):
    length, model = tokens.shape
    rim = conv_taps.shape[0] - 1
    chans = lax.axis_size("chan")
    me, row_place = lax.axis_index("chan"), lax.axis_index("rows")
    rows, block = decay_gate.shape
    total = rows * chans
    width = 2 * block
    group = width // rows

    padded = jnp.concatenate([jnp.full((rim,), -1, jnp.int32), segments])
    window = lax.dynamic_slice_in_dim(padded, me * length, length + rim)
    own = window[rim:]
    same = [own == window[rim - shift : rim - shift + length] for shift in range(1, rim + 1)]
    mask = jnp.stack([same[0], *same, own != 0] + [same[0]] * (7 - rim - 1), 1).astype(WIDE)
    mask = jnp.pad(mask, ((RIM, RIM), (0, 0)))

    small = jnp.concatenate(
        [
            jnp.stack([gelu_bias, input_bias, conv_bias, decay_bias, ingate_bias, decay_param]),
            conv_taps,
        ]
    )
    unit_rows = block // 4
    count = rows // unit_rows
    lines = unit_rows // 2
    place = jnp.stack([me, row_place]).astype(jnp.int32)
    clock = Clock()

    part = gate_weight.shape[1] // 4
    own_columns = lambda weight: lax.dynamic_slice_in_dim(weight, row_place * part, part, 1).T
    own_unit = jnp.stack(
        [
            own_columns(gate_weight),
            own_columns(up_weight),
            lax.dynamic_slice_in_dim(down_weight, row_place * part, part),
        ]
    )
    both = jnp.concatenate([decay_gate, input_gate], 1)
    both = jnp.pad(both, ((0, 0), (0, model // 2 - 2 * block)))
    both = both.reshape(count, 2, lines, model // 2).swapaxes(1, 2).reshape(count, lines, model)
    flat = small.reshape(small.shape[0], count, unit_rows).swapaxes(0, 1).reshape(count, 1, -1)
    flat = jnp.pad(flat, ((0, 0), (0, lines // 3 - 1), (0, model - flat.shape[2])))
    by_unit = lambda weight: weight.reshape(count, unit_rows, model)
    first = jnp.concatenate([by_unit(input_weight.T), both, flat], 1)
    second = jnp.concatenate([by_unit(gelu_weight.T), by_unit(out_weight)], 1)
    first_cuts = ((0, unit_rows), (unit_rows, first.shape[1]))
    second_cuts = ((0, unit_rows), (unit_rows, 2 * unit_rows))
    cot_low = cotangent.astype(LOW)
    if count == 4:
        quarters = lambda units: jnp.stack(
            [
                lax.dynamic_index_in_dim(units, row_place ^ bits, keepdims=False)
                for bits in (0, 2, 1, 3)
            ]
        )
        own_unit = clock.tick(own_unit)
        first = Sums(clock, spread_units(quarters(first)), pin=True)
        second = Sums(clock, spread_units(quarters(second)), start=False)
        first.step(pin=True)
        first.step()
        second.begin(pin=True)
        first.step(pin=True)
        first.step()
        second.step(pin=True)
        u_weight, packed = clock.tick(assembled(place, first.result, first_cuts))
    else:
        cut = lambda units, cuts: [
            gathered(units.reshape(-1, model))[:, begin:end] for begin, end in cuts
        ]
        u_weight, packed = cut(first, first_cuts)
        y_weight, o_weight = cut(second, second_cuts)
        y_weight, o_weight = (w.reshape(total, model) for w in (y_weight, o_weight))
    feed_units = lax.all_gather(own_unit[None], ("chan", "rows"), axis=0, tiled=True)
    u_weight = u_weight.reshape(total, model)
    small_full = packed[:, lines, : small.shape[0] * unit_rows]
    small_full = small_full.reshape(-1, small.shape[0], unit_rows).swapaxes(0, 1)
    small_full = small_full.reshape(small.shape[0], total).astype(WIDE)
    param = small_full[5:6]
    line = lax.broadcasted_iota(jnp.int32, (16, total), 0)
    vec = jnp.pad(small_full, ((0, 6), (0, 0)))
    vec = jnp.where(line == 5, -8.0 * jax.nn.softplus(param), vec)
    vec = jnp.where(line == 10, -8.0 * jax.nn.sigmoid(param), vec)

    rim_tokens = moved_by(tokens[length - rim :], "chan", 1)
    extended = jnp.concatenate([jnp.zeros((RIM - rim, model), WIDE), rim_tokens, tokens])
    normed = rms_norm(extended, mixer_gain).astype(LOW)
    normed, u_weight = clock.tick((normed, u_weight))
    u, conv, rate, into, state, factor, decay_sum = clock.tick(
        mixer_forward(normed, u_weight, packed, vec, mask, width)
    )
    carry = Sums(
        clock, entering(jnp.concatenate([factor[-1:], state[-1:]]), "chan", 1), moved_by
    )
    if count == 4:
        second.step()
        carry.step()
        second.step()
        second.step()
        y_weight, o_weight = clock.tick(assembled(place, second.result, second_cuts))
        y_weight, o_weight = (w.reshape(total, model) for w in (y_weight, o_weight))
    active, slope = clock.tick(gelu_branch(normed, y_weight, vec, width))
    carry = clock.tick(carry.finish())
    cot_too = swapped(cot_low, "rows", 1)
    mixed, middle, normed2 = clock.tick(
        mixer_out(active, state, factor, carry, o_weight, tokens, feed_gain[None])
    )
    cot_too = clock.tick(cot_too)
    normed2_too = swapped(normed2, "rows", 1)
    feed_units = clock.tick(feed_units)
    block_output, normed2_grad, mine, send = clock.tick(
        feed(place, normed2, cot_low, middle, feed_units)
    )
    theirs = swapped(send, "rows", 1)

    mid_grad, mid_low, state_grad, y_grad, feed_gain_sum, back_sum, y_sum = clock.tick(
        middle_back(
            middle, normed2_grad, cotangent, feed_gain[None], o_weight, active, slope, state,
            factor, carry,
        )
    )
    after = Sums(
        clock,
        entering(
            jnp.concatenate([factor[-1:], jnp.sum(back_sum, 0, keepdims=True)]), "chan", -1
        ),
        moved_by,
    )
    theirs, normed2_too = clock.tick((theirs, normed2_too))
    near_y, far_y, near_x, far_x = clock.tick(
        feed_grads(mine, theirs, normed2, cot_low, normed2_too, cot_too)
    )
    split = lambda value: value.reshape(-1, 2, *value.shape[1:])
    fed = Sums(
        clock,
        owned(
            lambda place: split(near_y)[:, place],
            split(far_y),
            lambda place: near_x[:, :, place],
            far_x,
        ),
    )
    after = clock.tick(after.finish())
    place = jnp.stack([me // group, me % group, row_place]).astype(jnp.int32)
    pairs = total // width
    back = lambda after, begin, steps, so_far: clock.tick(
        mixer_back(
            place, state_grad, rate, into, conv, state, factor, u, y_grad, mixed, y_weight, u_weight,
            packed, vec, mask, carry, after, normed, mid_low, y_sum, decay_sum, rows, width, begin, steps, so_far,
        )
    )
    so_far = back(after, 1, pairs - 1, ())
    fed.step()
    so_far = clock.tick(so_far)
    keep, send, normed_grad = back(after, 0, 1, so_far)
    rest = Sums(clock, halved(keep, send))
    fed.step(pin=True)
    rest.step(pin=True)
    rim_grad = clock.tick(moved_by(clock.tick(normed_grad[RIM - rim : RIM]), "chan", -1))
    error = normed_grad[RIM:] + jnp.concatenate([jnp.zeros((length - rim, model), WIDE), rim_grad])
    scale = lax.rsqrt(jnp.mean(tokens * tokens, axis=-1, keepdims=True) + 1e-06)
    gained = mixer_gain * error
    mean = jnp.mean(gained * tokens, axis=-1, keepdims=True)
    tokens_grad = clock.tick(mid_grad + scale * gained - tokens * (scale * scale * scale * mean))
    mixer_gain_sum = jnp.sum(error * tokens * scale, 0)

    gains = Sums(clock, everywhere(jnp.stack([mixer_gain_sum, jnp.sum(feed_gain_sum, 0)])))
    gains.moving = clock.tick(gains.moving)
    rest.step(pin=True)
    rest.step(pin=True)
    fed.step()
    fed = Sums(clock, settled(fed.result))
    gains.step()
    gains.step()
    fed.step()
    gains.step()
    rest.step()
    rest = Sums(clock, settled(rest.result))
    gains.step()
    fed.step()
    feed_sum = clock.tick(finish(jnp.stack([me, row_place]).astype(jnp.int32), *fed.result))
    rest.step()
    gains = gains.finish()
    rest_sum = ordered(*rest.finish())[0]
    gains = gains + clock.time[:1, :1]
    input_sum, gelu_sum, out_sum = (rest_sum[:, k * model : (k + 1) * model] for k in range(3))
    gates_sum = rest_sum[:, 3 * model : 3 * model + width]
    lines = rest_sum[:, 3 * model + width : 3 * model + width + 11].T
    mean_decay = lines[10] / (length * lax.axis_size("rows") * chans)
    return (
        block_output,
        tokens_grad,
        gelu_sum.T,
        lines[0],
        input_sum.T,
        lines[1],
        lines[2:6],
        lines[6],
        gates_sum[:, :block],
        lines[7],
        gates_sum[:, block:],
        lines[8],
        lines[9],
        out_sum,
        gains[0],
        feed_sum[0],
        feed_sum[1],
        feed_sum[2],
        gains[1],
        mean_decay,
    )


def solution(mesh):
    return jax.shard_map(
        local,
        mesh=mesh,
        in_specs=(
            P(("rows", "chan"), None),
            P("rows"),
            P(None, "chan"),
            P("chan"),
            P(None, "chan"),
            P("chan"),
            P(None, "chan"),
            P("chan"),
            P("chan", None),
            P("chan"),
            P("chan", None),
            P("chan"),
            P("chan"),
            P("chan", None),
            P(),
            P(None, "chan"),
            P(None, "chan"),
            P("chan", None),
            P(),
            P(("rows", "chan"), None),
        ),
        out_specs=(
            P(("rows", "chan"), None),
            P(("rows", "chan"), None),
            P(None, "chan"),
            P("chan"),
            P(None, "chan"),
            P("chan"),
            P(None, "chan"),
            P("chan"),
            P("chan", None),
            P("chan"),
            P("chan", None),
            P("chan"),
            P("chan"),
            P("chan", None),
            P(),
            P(None, "chan"),
            P(None, "chan"),
            P("chan", None),
            P(),
            P("chan"),
        ),
        check_vma=False,
    )
```

```python
import functools

import jax
import jax.numpy as jnp
from jax import lax
from jax.experimental import pallas as pl
from jax.experimental.pallas import tpu as pltpu
from jax.sharding import PartitionSpec as P

LOW = jnp.bfloat16
WIDE = jnp.float32
RIM = 16
STEP = 16
VMEM_BYTES = 56 * 1024 * 1024
GELU_SLOPE = 0.7978845608028654
GELU_CUBE = 0.044715


def params(**more):
    return pltpu.CompilerParams(vmem_limit_bytes=VMEM_BYTES, **more)


def moved_by(value, axis, steps):
    count = lax.axis_size(axis)
    leading, last = (max(0, -steps), min(count, count - steps))
    return lax.ppermute(value, axis, [(source, source + steps) for source in range(leading, last)])


def swapped(value, axis, bits):
    count = lax.axis_size(axis)
    return lax.ppermute(value, axis, [(source, source ^ bits) for source in range(count)])


def join(earlier, later):
    return jnp.concatenate(
        [earlier[0:1] * later[0:1], later[0:1] * earlier[1:2] + later[1:2]], 0
    )


def entering(value, axis, sign):
    count = lax.axis_size(axis)
    total = value
    came = yield [(value, axis, sign * reach) for reach in (1, 2, 3) if reach < count]
    for one in came:
        total = join(one, total)
    reach = 4
    while 2 * reach < count:
        (one,) = yield [(total, axis, sign * reach)]
        total = join(one, total)
        reach *= 2
    came = yield [(total, axis, sign * far) for far in (1, reach + 1) if far < count]
    last = came[0]
    for one in came[1:]:
        last = join(one, last)
    return last[1:2]


def rms_norm(values, gain):
    return values * lax.rsqrt(jnp.mean(values * values, axis=-1, keepdims=True) + 1e-06) * gain


def nt(left, right):
    return lax.dot_general(left, right, (((1,), (1,)), ((), ())), preferred_element_type=WIDE)


def tn(left, right):
    return lax.dot_general(left, right, (((0,), (0,)), ((), ())), preferred_element_type=WIDE)


def nn(left, right):
    return lax.dot_general(left, right, (((1,), (0,)), ((), ())), preferred_element_type=WIDE)


def sigmoid(value):
    return 0.5 * jnp.tanh(0.5 * value) + 0.5


def gelu_parts(value):
    square = value * value
    bend = jnp.tanh(GELU_SLOPE * value * (1.0 + GELU_CUBE * square))
    half = 0.5 + 0.5 * bend
    slope = half + 0.5 * GELU_SLOPE * value * (1.0 - bend * bend) * (1.0 + 3.0 * GELU_CUBE * square)
    return value * half, slope


def split_low(value):
    high = value.astype(LOW)
    return high, (value - high.astype(WIDE)).astype(LOW)


def loop(count, unroll, body, init):
    while count % unroll:
        unroll -= 1

    def several(index, carry):
        for turn in range(unroll):
            carry = body(index * unroll + turn, carry)
        return carry

    return lax.fori_loop(0, count // unroll, several, init)


def cost(microseconds):
    return pl.CostEstimate(
        flops=int(microseconds * 1.1e9), bytes_accessed=int(microseconds * 3.5e6), transcendentals=0
    )


def fold(value):
    total = value[0:8]
    for group in range(1, value.shape[0] // 8):
        total = total + value[8 * group : 8 * group + 8]
    return total


def fill_gates(packed, gates, block):
    width = 2 * block
    lines = packed.shape[1] * 3 // 4

    @pl.when(pl.program_id(0) == 0)
    def _():
        gates[...] = jnp.zeros_like(gates)

    parts = []
    for unit in range(packed.shape[0]):
        value = packed[unit].astype(WIDE)[:lines]
        parts += [value[:, 0:width], value[:, 512 : 512 + width]]
    parts = jnp.concatenate(parts, 0).astype(LOW)
    for half in (0, block):
        gates[half : half + block, half : half + block] = parts[half : half + block, 0:block]
        gates[half : half + block, width + half : width + half + block] = parts[
            half : half + block, block:
        ]


def mixer_forward_kernel(
    normed, u_weight, packed, vec, mask, u_out, conv_out, r_out, i_out, h_out, f_out, sum_out,
    high, low, zed, gates,
):
    ext = normed.shape[0]
    width = u_out.shape[1]
    fill_gates(packed, gates, width // 2)
    count = (ext - RIM) // STEP
    u_out[...] = nt(normed[...], u_weight[...]) + vec[1:2, :]

    def convolve(index, _):
        base = pl.multiple_of(index * STEP, STEP)
        own = pl.ds(base, STEP)
        window = u_out[pl.ds(base + 8, STEP + 8), :]
        flags = mask[pl.ds(base + RIM, STEP), :]
        conv = vec[2:3, :] + vec[6:7, :] * window[8:]
        for shift in (1, 2, 3):
            conv = conv + flags[:, shift : shift + 1] * (
                vec[6 + shift : 7 + shift, :] * window[8 - shift : 8 - shift + STEP]
            )
        conv = conv * flags[:, 4:5]
        conv_out[own, :] = conv
        high[own, :], low[own, :] = split_low(conv)
        return 0

    loop(count, 4, convolve, 0)
    zed[...] = nn(high[...], gates[...]) + nn(low[...], gates[...])
    line = lax.broadcasted_iota(jnp.int32, (8, width), 0)

    def advance(index, carry):
        state, factor, total = carry
        own = pl.ds(pl.multiple_of(index * STEP, STEP), STEP)
        going = mask[pl.ds(pl.multiple_of(index * STEP + RIM, STEP), STEP), :][:, 0:1]
        rate = sigmoid(zed[own, 0:width] + vec[3:4, :])
        into = sigmoid(zed[own, width:] + vec[4:5, :])
        decay = jnp.exp(vec[5:6, :] * rate)
        r_out[own, :] = rate
        i_out[own, :] = into
        scale = jnp.where(going == 0.0, 1.0, jnp.sqrt(1.01 - decay * decay))
        inject = conv_out[own, :] * into * scale
        carried = decay * going
        total = total + fold(decay)
        for group in range(STEP // 8):
            part = slice(8 * group, 8 * group + 8)
            mul, add = carried[part], inject[part]
            for reach in (1, 2, 4):
                inside = line >= reach
                add = add + mul * jnp.where(inside, pltpu.roll(add, reach, 0), 0.0)
                mul = mul * jnp.where(inside, pltpu.roll(mul, reach, 0), 1.0)
            here = add + mul * state
            gone = mul * factor
            rows = pl.ds(pl.multiple_of(index * STEP + 8 * group, 8), 8)
            h_out[rows, :] = here
            f_out[rows, :] = gone
            state, factor = here[7:8], gone[7:8]
        return state, factor, total

    zero = jnp.zeros((1, width), WIDE)
    _, _, total = loop(
        count, 4, advance, (zero, zero + 1.0, jnp.zeros((8, width), WIDE))
    )
    sum_out[...] = total


def mixer_forward(normed, u_weight, packed, vec, mask, width):
    ext, model = normed.shape
    tokens = ext - RIM
    total = u_weight.shape[0]
    pairs = total // width
    units = packed.shape[0] // pairs
    by_lane = lambda length: pl.BlockSpec((length, width), lambda step: (0, step))
    whole = lambda array: pl.BlockSpec(array.shape, lambda step: (0,) * array.ndim)
    flat = jax.ShapeDtypeStruct((tokens, total), WIDE)
    return pl.pallas_call(
        mixer_forward_kernel,
        grid=(pairs,),
        in_specs=[
            whole(normed),
            pl.BlockSpec((width, model), lambda step: (step, 0)),
            pl.BlockSpec((units, *packed.shape[1:]), lambda step: (step, 0, 0)),
            by_lane(vec.shape[0]),
            whole(mask),
        ],
        out_specs=[by_lane(ext)] + [by_lane(tokens)] * 5 + [by_lane(8)],
        out_shape=[jax.ShapeDtypeStruct((ext, total), WIDE)] + [flat] * 5
        + [jax.ShapeDtypeStruct((8, total), WIDE)],
        scratch_shapes=[
            pltpu.VMEM((tokens, width), LOW),
            pltpu.VMEM((tokens, width), LOW),
            pltpu.VMEM((tokens, 2 * width), WIDE),
            pltpu.VMEM((width, 2 * width), LOW),
        ],
        compiler_params=params(),
        cost_estimate=cost(26),
        name="mixer_forward",
    )(normed, u_weight, packed, vec, mask)


def gelu_branch_kernel(normed, weight, vec, active_out, slope_out, held):
    held[...] = nt(normed[RIM:, :], weight[...]) + vec[0:1, :]

    def act(index, _):
        own = pl.ds(pl.multiple_of(index * STEP, STEP), STEP)
        active_out[own, :], slope_out[own, :] = gelu_parts(held[own, :])
        return 0

    loop(held.shape[0] // STEP, 4, act, 0)


def gelu_branch(normed, weight, vec, width):
    length, total = normed.shape[0] - RIM, weight.shape[0]
    model = normed.shape[1]
    lane = lambda lines: pl.BlockSpec((lines, width), lambda step: (0, step))
    return pl.pallas_call(
        gelu_branch_kernel,
        grid=(total // width,),
        in_specs=[
            pl.BlockSpec(normed.shape, lambda step: (0, 0)),
            pl.BlockSpec((width, model), lambda step: (step, 0)),
            lane(vec.shape[0]),
        ],
        out_specs=[lane(length), lane(length)],
        out_shape=[jax.ShapeDtypeStruct((length, total), WIDE)] * 2,
        scratch_shapes=[pltpu.VMEM((length, width), WIDE)],
        compiler_params=params(),
        cost_estimate=cost(8),
        name="gelu_branch",
    )(normed, weight, vec)


def mixer_out_kernel(active, h, f, state, weight, tokens, gain, mixed, middle, normed):
    def gate(index, _):
        own = pl.ds(pl.multiple_of(index * STEP, STEP), STEP)
        mixed[own, :] = ((h[own, :] + f[own, :] * state[...]) * active[own, :]).astype(LOW)
        return 0

    loop(active.shape[0] // STEP, 4, gate, 0)
    total = tokens[...] + nn(mixed[...], weight[...])
    middle[...] = total
    scale = lax.rsqrt(jnp.mean(total * total, axis=-1, keepdims=True) + 1e-06)
    normed[...] = (total * scale * gain[...]).astype(LOW)


def mixer_out(active, h, f, state, weight, tokens, gain):
    length, model = tokens.shape
    total = active.shape[1]
    tile = 256 if length % 256 == 0 else length
    row = lambda lanes: pl.BlockSpec((tile, lanes), lambda step: (step, 0))
    one = lambda array: pl.BlockSpec(array.shape, lambda step: (0, 0))
    return pl.pallas_call(
        mixer_out_kernel,
        grid=(length // tile,),
        in_specs=[
            row(total), row(total), row(total), one(state), one(weight), row(model), one(gain),
        ],
        out_specs=[row(total), row(model), row(model)],
        out_shape=[
            jax.ShapeDtypeStruct((length, total), LOW),
            jax.ShapeDtypeStruct((length, model), WIDE),
            jax.ShapeDtypeStruct((length, model), LOW),
        ],
        compiler_params=params(),
        cost_estimate=cost(9),
        name="mixer_out",
    )(active, h, f, state, weight, tokens, gain)


def spread(place, wide, keep, send, matrix, group, rows, lanes=slice(None), count=None):
    part = rows // 4
    if part % 8:
        value = wide[:, 0:count]
        pieces = [value[begin : begin + part] for begin in range(0, group * rows, part)]
        mine = place[1] * 4 + place[2]
        bit = 1
        while bit < len(pieces):
            turned = (mine & bit) != 0
            pieces = [
                jnp.where(turned, pieces[index ^ bit], pieces[index])
                for index in range(len(pieces))
            ]
            bit *= 2
    for slot in range(group):
        shard = slot ^ place[1]
        for turn in range(4):
            if part % 8:
                value = pieces[4 * slot + turn]
            else:
                begin = pl.multiple_of(shard * rows + (turn ^ place[2]) * part, 8)
                value = wide[pl.ds(begin, part), 0:count]
            (keep, send)[turn & 1][slot, matrix, turn >> 1, :, lanes] = value.astype(LOW)


def feed_kernel(
    place, normed, cot, out_in, units, out, grad, keep, send, gate_s, up_s, back_s, hidden_l,
    gate_l, up_l, held, sems,
):
    half = gate_s.shape[0] // 2
    model = normed.shape[1]
    width = gate_s.shape[0]
    part = width // 4
    step = pl.program_id(0)

    def copies(index):
        for turn in range(4):
            unit = (place[0] ^ index) * 4 + (place[1] ^ turn)
            order = (turn % 2) * 2 + turn // 2
            slot = index % 2
            yield pltpu.make_async_copy(
                units.at[unit], held.at[slot, :, order], sems.at[slot, turn]
            )

    @pl.when(step == 0)
    def _():
        out[...] = out_in[...]
        grad[...] = jnp.zeros_like(grad)
        for copy in copies(0):
            copy.start()

    @pl.when(step + 1 < pl.num_programs(0))
    def _():
        for copy in copies(step + 1):
            copy.start()

    for copy in copies(step):
        copy.wait()

    def weight(matrix):
        if part % 16 == 0:
            return held[step % 2, matrix].reshape(width, model)
        pieces = [held[step % 2, matrix, turn].astype(WIDE) for turn in range(4)]
        return jnp.concatenate(pieces, 0).astype(LOW)

    first, second, third = weight(0), weight(1), weight(2)
    gate_s[...] = nt(first, normed[...])
    up_s[...] = nt(second, normed[...])
    back_s[...] = nt(third, cot[...])

    def act(index, _):
        own = pl.ds(pl.multiple_of(index * STEP, STEP), STEP)
        up, back = up_s[own, :], back_s[own, :]
        value, slope = gelu_parts(gate_s[own, :])
        hidden_l[own, :] = (value * up).astype(LOW)
        gate_l[own, :] = (back * up * slope).astype(LOW)
        up_l[own, :] = (back * value).astype(LOW)
        return 0

    loop(width // STEP, 4, act, 0)
    out[...] += tn(hidden_l[...], third)
    grad[...] += tn(gate_l[...], first) + tn(up_l[...], second)
    for matrix, value in enumerate((gate_l, up_l, hidden_l)):
        keep[0, matrix] = value[:half, :]
        send[0, matrix] = value[half:, :]


def feed(place, normed, cot, out_in, units):
    length, model = normed.shape
    part = units.shape[2]
    slots = units.shape[0] // 4
    width = 4 * part
    whole = lambda array: pl.BlockSpec(array.shape, lambda step, place: (0,) * array.ndim)
    piece = pl.BlockSpec((1, 3, 2 * part, length), lambda step, place: (step, 0, 0, 0))
    wide = jax.ShapeDtypeStruct((length, model), WIDE)
    grads = jax.ShapeDtypeStruct((slots, 3, 2 * part, length), LOW)
    return pl.pallas_call(
        feed_kernel,
        grid_spec=pltpu.PrefetchScalarGridSpec(
            num_scalar_prefetch=1,
            grid=(slots,),
            in_specs=[
                whole(normed), whole(cot), whole(out_in), pl.BlockSpec(memory_space=pl.ANY),
            ],
            out_specs=[whole(out_in), whole(out_in), piece, piece],
            scratch_shapes=[pltpu.VMEM((width, length), WIDE)] * 3
            + [pltpu.VMEM((width, length), LOW)] * 3
            + [pltpu.VMEM((2, 3, 4, part, model), LOW), pltpu.SemaphoreType.DMA((2, 4))],
        ),
        out_shape=[wide, wide, grads, grads],
        compiler_params=params(),
        cost_estimate=cost(34),
        name="feed",
    )(place, normed, cot, out_in, units)


def feed_grads_kernel(pairs, mine, theirs, normed, cot, normed_too, cot_too, *outs):
    part = outs[0].shape[2]
    step = pl.program_id(0)
    for matrix in range(3):
        right, right_too = (cot, cot_too) if matrix == 2 else (normed, normed_too)
        value = nn(mine[0, matrix], right[...]) + nn(theirs[0, matrix], right_too[...])
        value = value.astype(LOW)

        @pl.when(step < pairs)
        def _():
            outs[0][0, matrix] = value[:part]
            outs[1][0, matrix] = value[part:]

        for place, out in ((pairs, outs[2]), (pairs + pairs // 2, outs[3])):

            @pl.when((step >= place) & (step < place + pairs // 2))
            def _():
                out[0, matrix, 0] = value[:part]
                out[0, matrix, 1] = value[part:]


def feed_grads(mine, theirs, normed, cot, normed_too, cot_too):
    slots, _, rows, length = mine.shape
    model = normed.shape[1]
    pairs, part = slots // 2, rows // 2
    whole = lambda array: pl.BlockSpec(array.shape, lambda step: (0,) * array.ndim)

    def source(step):
        even = 4 * (step // 2) + step % 2
        odd = step - pairs
        last = odd >= pairs // 2
        odd = 4 * jnp.where(last, odd - pairs // 2, odd) + 2 + last.astype(jnp.int32)
        return jnp.where(step < pairs, even, odd), 0, 0, 0

    clipped = lambda first, count: lambda step: jnp.clip(step - first, 0, count - 1)
    even = clipped(0, pairs)
    spec = lambda place, count: pl.BlockSpec(
        (1, 3, 2, part, model), lambda step: (clipped(place, count)(step), 0, 0, 0, 0)
    )
    flat = pl.BlockSpec((1, 3, part, model), lambda step: (even(step), 0, 0, 0))
    return pl.pallas_call(
        functools.partial(feed_grads_kernel, pairs),
        grid=(slots,),
        in_specs=[pl.BlockSpec((1, 3, rows, length), source)] * 2
        + [whole(normed)] * 4,
        out_specs=[flat, flat, spec(pairs, pairs // 2), spec(pairs + pairs // 2, pairs // 2)],
        out_shape=[jax.ShapeDtypeStruct((pairs, 3, part, model), LOW)] * 2
        + [jax.ShapeDtypeStruct((pairs // 2, 3, 2, part, model), LOW)] * 2,
        compiler_params=params(),
        cost_estimate=cost(17),
        name="feed_grads",
    )(mine, theirs, normed, cot, normed_too, cot_too)


def middle_back_kernel(
    middle, grad, cot, gain, weight, active_in, slope_in, h, f, state, mid_grad, mid_low, state_grad, y_grad,
    gain_sum, back_sum, bias_sum, mixed_s,
):
    @pl.when(pl.program_id(0) == 0)
    def _():
        gain_sum[...] = jnp.zeros_like(gain_sum)
        back_sum[...] = jnp.zeros_like(back_sum)
        bias_sum[...] = jnp.zeros_like(bias_sum)

    value, error = middle[...], grad[...]
    scale = lax.rsqrt(jnp.mean(value * value, axis=-1, keepdims=True) + 1e-06)
    gained = gain[...] * error
    mean = jnp.mean(gained * value, axis=-1, keepdims=True)
    total = cot[...] + scale * gained - value * (scale * scale * scale * mean)
    gain_sum[...] += fold(error * value * scale)
    mid_grad[...] = total
    mid_low[...] = total.astype(LOW)
    mixed_s[...] = nt(mid_low[...], weight[...])

    def turn(index, carry):
        back, bias = carry
        own = pl.ds(pl.multiple_of(index * STEP, STEP), STEP)
        error = mixed_s[own, :]
        active, slope = active_in[own, :], slope_in[own, :]
        gone = f[own, :]
        full = h[own, :] + gone * state[...]
        here = error * active
        state_grad[own, :] = here
        low = (error * full * slope).astype(LOW)
        y_grad[own, :] = low
        return back + fold(here * gone), bias + fold(low.astype(WIDE))

    zero = jnp.zeros(back_sum.shape, WIDE)
    back, bias = loop(middle.shape[0] // STEP, 4, turn, (zero, zero))
    back_sum[...] += back
    bias_sum[...] += bias


def middle_back(middle, grad, cot, gain, weight, active, slope, h, f, state):
    length, model = middle.shape
    total = active.shape[1]
    tile = 256 if length % 256 == 0 else length
    row = lambda lanes: pl.BlockSpec((tile, lanes), lambda step: (step, 0))
    one = lambda lines, lanes: pl.BlockSpec((lines, lanes), lambda step: (0, 0))
    return pl.pallas_call(
        middle_back_kernel,
        grid=(length // tile,),
        in_specs=[
            row(model), row(model), row(model), one(1, model),
            one(total, model), row(total), row(total), row(total), row(total), one(1, total),
        ],
        out_specs=[
            row(model), row(model), row(total), row(total), one(8, model), one(8, total),
            one(8, total),
        ],
        out_shape=[
            jax.ShapeDtypeStruct((length, model), WIDE),
            jax.ShapeDtypeStruct((length, model), LOW),
            jax.ShapeDtypeStruct((length, total), WIDE),
            jax.ShapeDtypeStruct((length, total), LOW),
            jax.ShapeDtypeStruct((8, model), WIDE),
            jax.ShapeDtypeStruct((8, total), WIDE),
            jax.ShapeDtypeStruct((8, total), WIDE),
        ],
        scratch_shapes=[pltpu.VMEM((tile, total), WIDE)],
        compiler_params=params(),
        cost_estimate=cost(13),
        name="middle_back",
    )(middle, grad, cot, gain, weight, active, slope, h, f, state)


def mixer_back_kernel(
    rows, first, place, state_grad, r_in, i_in, conv_in, h, f, u, y_grad, mixed, y_weight, u_weight,
    packed, vec, mask, state, after, normed, mid_low, y_sum, decay_sum, *refs
):
    if not first:
        grad_in, refs = refs[2], refs[3:]
    (
        keep, send, normed_grad, conv_s, high, low, conv_h, conv_l, grown, u_low, wide, gate_w,
        gates, sums,
    ) = refs
    length, width = state_grad.shape
    ext, model = normed.shape
    group = width // rows
    block = width // 2
    count = length // STEP
    line = lax.broadcasted_iota(jnp.int32, (8, width), 0)

    fill_gates(packed, gates, block)

    @pl.when(pl.program_id(0) == 0)
    def _():
        if first:
            normed_grad[...] = jnp.zeros_like(normed_grad)
        else:
            normed_grad[...] = grad_in[...]

    def retreat(index, carry):
        error, rate_sum, into_sum, slope_sum = carry
        base = pl.multiple_of((count - 1 - index) * STEP, STEP)
        own = pl.ds(base, STEP)
        going = mask[pl.ds(base + RIM, STEP), :][:, 0:1]
        rate, into, conv = r_in[own, :], i_in[own, :], conv_in[own, :]
        slope = vec[5:6, :]
        decay = jnp.exp(slope * rate)
        carried = decay * going
        given = state_grad[own, :]
        full = h[own, :] + f[own, :] * state[...]
        ahead = pl.ds(pl.multiple_of(jnp.maximum(base - 8, 0), 8), 8)
        edge = h[ahead, :][7:8] + f[ahead, :][7:8] * state[...]
        edge = jnp.where(base == 0, state[...], edge)
        parts = []
        for part in reversed(range(STEP // 8)):
            place_of = slice(8 * part, 8 * part + 8)
            mul = carried[place_of]
            add = mul * given[place_of]
            for reach in (1, 2, 4):
                inside = line < 8 - reach
                add = add + mul * jnp.where(inside, pltpu.roll(add, 8 - reach, 0), 0.0)
                mul = mul * jnp.where(inside, pltpu.roll(mul, 8 - reach, 0), 1.0)
            here = add + mul * error
            parts.append(given[place_of] + jnp.where(line < 7, pltpu.roll(here, 7, 0), error))
            error = here[0:1]
        grad = jnp.concatenate(parts[::-1], 0)
        befores = []
        for part in range(STEP // 8):
            last = edge if part == 0 else full[8 * part - 1 : 8 * part]
            befores.append(
                jnp.where(line > 0, pltpu.roll(full[8 * part : 8 * part + 8], 1, 0), last)
            )
        before = jnp.concatenate(befores, 0)
        root = lax.rsqrt(1.01 - decay * decay)
        scale = jnp.where(going == 0.0, 1.0, (1.01 - decay * decay) * root)
        through = grad * conv
        into_grad = through * scale
        conv_s[own, :] = grad * into * scale
        decay_grad = going * decay * (grad * before - through * into * decay * root)
        z_rate = decay_grad * slope * rate * (1.0 - rate)
        z_into = into_grad * into * (1.0 - into)
        high[own, 0:width], low[own, 0:width] = split_low(z_rate)
        high[own, width:], low[own, width:] = split_low(z_into)
        conv_h[own, :], conv_l[own, :] = split_low(conv)
        return (
            error,
            rate_sum + fold(z_rate),
            into_sum + fold(z_into),
            slope_sum + fold(decay_grad * rate),
        )

    zero = jnp.zeros((8, width), WIDE)
    _, rate_sum, into_sum, slope_sum = loop(
        count, 4, retreat, (after[...], zero, zero, zero)
    )
    conv_s[...] += nt(high[...], gates[...]) + nt(low[...], gates[...])
    gate_full = (
        tn(conv_h[...], high[...]) + tn(conv_l[...], high[...]) + tn(conv_h[...], low[...])
    )
    for half in (0, block):
        rows_of = slice(half, half + block)
        gate_w[rows_of, 0:block] = gate_full[rows_of, half : half + block]
        gate_w[rows_of, block:] = gate_full[rows_of, width + half : width + half + block]
    grown[0:RIM, :] = jnp.zeros((RIM, width), WIDE)
    grown[RIM + length :, :] = jnp.zeros((RIM, width), WIDE)

    def taps(index, carry):
        base = pl.multiple_of(index * STEP, STEP)
        window = u[pl.ds(base + 8, STEP + 8), :]
        flags = mask[pl.ds(base + RIM, STEP), :]
        error = conv_s[pl.ds(base, STEP), :] * flags[:, 4:5]
        grown[pl.ds(base + RIM, STEP), :] = error
        out = [carry[0] + fold(error), carry[1] + fold(error * window[8:])]
        for shift in (1, 2, 3):
            moved = window[8 - shift : 8 - shift + STEP]
            out.append(carry[1 + shift] + fold(flags[:, shift : shift + 1] * error * moved))
        return tuple(out)

    bias_sum, *tap_sums = loop(count, 4, taps, (zero,) * 5)

    def spread_back(index, total):
        base = pl.multiple_of(index * STEP, STEP)
        window = grown[pl.ds(base, STEP + 8), :]
        flags = mask[pl.ds(base, STEP + 8), :]
        value = vec[6:7, :] * window[0:STEP]
        for shift in (1, 2, 3):
            masked = flags[:, shift : shift + 1] * window
            value = value + vec[6 + shift : 7 + shift, :] * masked[shift : shift + STEP]
        rounded = value.astype(LOW)
        u_low[pl.ds(base, STEP), :] = rounded
        return total + fold(rounded.astype(WIDE))

    input_sum = loop(ext // STEP, 3, spread_back, zero)
    sums[...] = jnp.zeros_like(sums)
    slope_sum = slope_sum * vec[10:11, :]
    values = (y_sum[...], input_sum, *tap_sums, bias_sum, rate_sum, into_sum, slope_sum, decay_sum[...])
    for row, value in enumerate(values):
        sums[row : row + 1, :] = jnp.sum(value, axis=0, keepdims=True)
    wide[:, 0:128] = jnp.transpose(sums[...])
    spread(place, wide, keep, send, 0, group, rows, slice(3 * model + width, None), 128)
    wide[...] = tn(u_low[...], normed[...])
    spread(place, wide, keep, send, 0, group, rows, slice(0, model))
    spread(place, gate_w, keep, send, 0, group, rows, slice(3 * model, 3 * model + width))
    wide[...] = tn(y_grad[...], normed[RIM:, :])
    spread(place, wide, keep, send, 0, group, rows, slice(model, 2 * model))
    wide[...] = tn(mixed[...], mid_low[...])
    spread(place, wide, keep, send, 0, group, rows, slice(2 * model, 3 * model))
    normed_grad[...] += nn(u_low[...], u_weight[...])
    normed_grad[RIM:, :] += nn(y_grad[...], y_weight[...])


def mixer_back(
    place, state_grad, r, i, conv, h, f, u, y_grad, mixed, y_weight, u_weight, packed, vec, mask,
    state, after, normed, mid_low, y_sum, decay_sum, rows, width, begin, steps, so_far=(),
):
    length, total = state_grad.shape
    ext, model = normed.shape
    group, part = width // rows, rows // 4
    pair = lambda step, place: (step + begin) ^ place[0]
    whole = lambda array: pl.BlockSpec(array.shape, lambda step, place: (0,) * array.ndim)
    lane = lambda lines: pl.BlockSpec((lines, width), lambda step, place: (0, pair(step, place)))
    weight = pl.BlockSpec((width, model), lambda step, place: (pair(step, place), 0))
    units = packed.shape[0] * width // total
    lanes = 3 * model + width + 128
    piece = pl.BlockSpec((group, 1, 2, part, lanes), lambda step, place: (step + begin, 0, 0, 0, 0))
    shape = jax.ShapeDtypeStruct((total // rows, 1, 2, part, lanes), LOW)
    operands = [
        state_grad, r, i, conv, h, f, u, y_grad, mixed, y_weight, u_weight, packed, vec, mask,
        state, after, normed, mid_low, y_sum, decay_sum,
    ]
    kept = pl.BlockSpec(memory_space=pl.ANY)
    return pl.pallas_call(
        functools.partial(mixer_back_kernel, rows, not so_far),
        grid_spec=pltpu.PrefetchScalarGridSpec(
            num_scalar_prefetch=1,
            grid=(steps,),
            in_specs=[
                lane(length), lane(length), lane(length), lane(length), lane(length),
                lane(length), lane(ext), lane(length), lane(length), weight, weight,
                pl.BlockSpec(
                    (units, *packed.shape[1:]), lambda step, place: (pair(step, place), 0, 0)
                ),
                lane(vec.shape[0]), whole(mask), lane(1),
                lane(1), whole(normed), whole(mid_low), lane(8), lane(8),
            ]
            + ([kept, kept, whole(so_far[2])] if so_far else []),
            out_specs=[
                piece, piece, pl.BlockSpec((ext, model), lambda step, place: (0, 0)),
            ],
            scratch_shapes=[
                pltpu.VMEM((length, width), WIDE),
                pltpu.VMEM((length, 2 * width), LOW),
                pltpu.VMEM((length, 2 * width), LOW),
                pltpu.VMEM((length, width), LOW),
                pltpu.VMEM((length, width), LOW),
                pltpu.VMEM((ext + RIM, width), WIDE),
                pltpu.VMEM((ext, width), LOW),
                pltpu.VMEM((width, model), WIDE),
                pltpu.VMEM((width, width), WIDE),
                pltpu.VMEM((width, 2 * width), LOW),
                pltpu.VMEM((128, width), WIDE),
            ],
        ),
        out_shape=[shape, shape, jax.ShapeDtypeStruct((ext, model), WIDE)],
        input_output_aliases={len(operands) + 1 + k: k for k in range(2)} if so_far else {},
        compiler_params=params(),
        cost_estimate=cost(15 * steps),
        name="mixer_back",
    )(place, *operands, *so_far)


def wide_of(value):
    return value.astype(WIDE)


def pin_kernel(source, target):
    del source, target


class Clock:
    def __init__(self):
        self.time = jnp.zeros((8, 128), WIDE)

    def tick(self, values):
        values, self.time = lax.optimization_barrier((values, self.time))
        return values

    def pin(self):
        self.time = pl.pallas_call(
            pin_kernel,
            in_specs=[pl.BlockSpec(memory_space=pl.ANY)],
            out_specs=pl.BlockSpec(memory_space=pl.ANY),
            out_shape=jax.ShapeDtypeStruct(self.time.shape, WIDE),
            input_output_aliases={0: 0},
            cost_estimate=cost(5000),
            name="pin",
        )(self.time)


class Sums:
    def __init__(self, clock, stages, move=swapped, pin=False, start=True):
        self.clock = clock
        self.stages = stages
        self.move = move
        self.result = self.moving = None
        if start:
            self.begin(pin)

    def begin(self, pin=False):
        self.send(next(self.stages), pin)

    def send(self, transfers, pin):
        values = self.clock.tick([transfer[0] for transfer in transfers])
        self.moving = [
            self.move(value, *transfer[1:]) for value, transfer in zip(values, transfers)
        ]
        if pin:
            self.clock.pin()

    def step(self, pin=False):
        try:
            transfers = self.stages.send(self.clock.tick(self.moving))
        except StopIteration as end:
            self.result = end.value
        else:
            self.send(transfers, pin)

    def finish(self):
        while self.result is None:
            self.step()
        return self.result


def lockstep(clock, *groups):
    begun = [group for group in groups if group.moving is not None]
    arrived = clock.tick([group.moving for group in begun])
    transfers = []
    for group in groups:
        if group.moving is None:
            transfers.append(next(group.stages))
        else:
            transfers.append(group.stages.send(arrived[begun.index(group)]))
    values = clock.tick([[transfer[0] for transfer in one] for one in transfers])
    for group, one, own in zip(groups, transfers, values):
        group.moving = [group.move(value, *transfer[1:]) for value, transfer in zip(own, one)]


def halved(keep, send):
    slots, matrices, _, part, lanes = keep.shape
    shape = (slots // 4, 2, 2, matrices, 2, part, lanes)
    keep = keep.reshape(shape)
    (came,) = yield [(send, "rows", 1)]
    came = came.reshape(shape)
    both = lambda *where: (wide_of(keep[where]) + wide_of(came[where]))
    every = slice(None)
    near_y = lambda place: both(every, 0, place, every, 0)
    far_y = both(every, 0, every, every, 1).astype(LOW)
    near_x = lambda place: both(every, 1, 0, every, place)
    far_x = both(every, 1, 1).astype(LOW)
    return (yield from owned(near_y, far_y, near_x, far_x))


def owned(near_y, far_y, near_x, far_x):
    from_y, from_x = yield [(far_y, "rows", 2), (far_x, "chan", 1)]
    rest = lambda place: wide_of(near_y(place)) + wide_of(from_y[:, place])
    also = lambda place: wide_of(near_x(place)) + wide_of(from_x[:, :, place])
    rest_came, also_came = yield [
        (rest(1).astype(LOW), "chan", 1),
        (also(1).astype(LOW), "rows", 2),
    ]
    rest, also = rest(0), also(0)
    parts = {}
    for index in range(rest.shape[0]):
        parts[2 * index] = rest[index] + wide_of(rest_came[index])
        parts[2 * index + 1] = also[index] + wide_of(also_came[index])
    came = yield [
        (value.astype(LOW), "chan", 2 * distance) for distance, value in parts.items() if distance
    ]
    total = parts[0]
    for value in came:
        total = total + wide_of(value)
    return total


def settled(total):
    total = total.astype(LOW)
    (came,) = yield [(total, "rows", 2)]
    pair = jnp.stack([total, came])
    (came,) = yield [(pair, "rows", 1)]
    return pair, came


def ordered(pair, came):
    four = jnp.stack([pair, came], 1)
    place = lax.axis_index("rows")
    four = jnp.where(place & 1, four[:, ::-1], four)
    four = jnp.where(place & 2, four[::-1], four)
    _, _, matrices, part, lanes = four.shape
    four = four.reshape(4, matrices, part, lanes).transpose(1, 0, 2, 3)
    return four.reshape(matrices, 4 * part, lanes).astype(WIDE)


def finish_kernel(place, pair, came, gate, up, down):
    def rows_of(matrix):
        parts = []
        for quarter in range(4):
            turn = quarter ^ place[1]
            own, other = (ref[turn // 2, matrix].astype(WIDE) for ref in (pair, came))
            parts.append(jnp.where(turn % 2 == 0, own, other))
        return jnp.concatenate(parts, 0)

    gate[...] = jnp.transpose(rows_of(0))
    up[...] = jnp.transpose(rows_of(1))
    down[...] = rows_of(2)


def finish(place, pair, came):
    _, _, part, model = pair.shape
    tall = jax.ShapeDtypeStruct((model, 4 * part), WIDE)
    vmem = pl.BlockSpec(memory_space=pltpu.VMEM)
    return pl.pallas_call(
        finish_kernel,
        grid_spec=pltpu.PrefetchScalarGridSpec(
            num_scalar_prefetch=1, grid=(1,), in_specs=[vmem] * 2, out_specs=[vmem] * 3
        ),
        out_shape=[tall, tall, jax.ShapeDtypeStruct((4 * part, model), WIDE)],
        compiler_params=params(),
        cost_estimate=cost(4),
        name="finish",
    )(place, pair, came)


def everywhere(value):
    for axis in ("rows", "chan"):
        bits = 1
        while bits < lax.axis_size(axis):
            (came,) = yield [(value, axis, bits)]
            value = value + came
            bits *= 2
    return value


def gathered(piece):
    parts = lax.axis_size("rows")
    share = piece.shape[0] // parts
    own = lax.dynamic_slice_in_dim(piece, lax.axis_index("rows") * share, share)
    full = lax.all_gather(own, ("chan", "rows"), axis=0, tiled=True)
    return full.reshape(lax.axis_size("chan"), piece.shape[0], piece.shape[1])


def pack_kernel(table, count, *refs):
    sources, outs, sems = refs[:count], refs[count:-1], refs[-1]
    copies = [
        pltpu.make_async_copy(
            sources[source].at[begin : begin + size],
            outs[out].at[at : at + size],
            sems.at[index],
        )
        for index, (out, at, source, begin, size) in enumerate(table)
    ]
    for copy in copies:
        copy.start()
    for copy in copies:
        copy.wait()


def pack(*lists):
    sources, table, shapes = [], [], []
    for out, pieces in enumerate(lists):
        at = 0
        for array, begin, size in pieces:
            known = [index for index, one in enumerate(sources) if one is array]
            if not known:
                known = [len(sources)]
                sources.append(array)
            table.append((out, at, known[0], begin, size))
            at += size
        shapes.append(jax.ShapeDtypeStruct((at, *pieces[0][0].shape[1:]), pieces[0][0].dtype))
    return pl.pallas_call(
        functools.partial(pack_kernel, table, len(sources)),
        in_specs=[pl.BlockSpec(memory_space=pl.ANY)] * len(sources),
        out_specs=[pl.BlockSpec(memory_space=pltpu.VMEM)] * len(shapes),
        scratch_shapes=[pltpu.SemaphoreType.DMA((len(table),))],
        out_shape=shapes,
        compiler_params=params(),
        cost_estimate=cost(0.01),
        name="pack",
    )(*sources)


def spread_units(units):
    pairs = range(2, lax.axis_size("chan") // 2)
    count = len(pairs)
    behind, *came = yield [(units[:2], "chan", 2)] + [
        (units[:1], "chan", 2 * pair) for pair in pairs
    ]
    singles = [(value, 0, 1) for value in came]
    (turned,) = pack([(units, 0, 1), (behind, 0, 2), *singles])
    (corners,) = yield [(turned, "chan", 1)]
    near, away = pack(
        [(behind, 0, 2), (corners, 1, 2)], [(corners, 0, 1), *singles, (corners, 3, count)]
    )
    over, near_too = yield [(away, "rows", 2), (near, "rows", 1)]
    size = 2 * count + 1
    (away,) = pack([(away, 0, size), (over, 0, size)])
    (away_too,) = yield [(away, "rows", 1)]
    return units, near, near_too, away, away_too


def unit_source(pair, side, turn, count):
    upper, other = turn // 2, turn % 2
    if pair == 0 and side == 0:
        return 0, 2 * other + upper
    if pair == 1:
        return 1 + other, 2 * side + upper
    if pair == 0:
        return 3 + other, upper * (2 * count + 1)
    return 3 + other, upper * (2 * count + 1) + 1 + side * count + pair - 2


def assemble_kernel(cuts, pairs, place, *refs):
    sources, outs, sems = refs[:5], refs[5:-1], refs[-1]
    copies = []
    for pair in range(pairs):
        for side in range(2):
            for turn in range(4):
                array, index = unit_source(pair, side, turn, pairs - 2)
                unit = ((2 * pair + side) ^ place[0]) * 4 + (turn ^ place[1])
                for (begin, end), out in zip(cuts, outs):
                    copies.append(
                        pltpu.make_async_copy(
                            sources[array].at[index, begin:end],
                            out.at[unit],
                            sems.at[len(copies)],
                        )
                    )
    for copy in copies:
        copy.start()
    for copy in copies:
        copy.wait()


def assembled(place, sources, cuts):
    pairs = lax.axis_size("chan") // 2
    model = sources[0].shape[2]
    anywhere = pl.BlockSpec(memory_space=pl.ANY)
    return pl.pallas_call(
        functools.partial(assemble_kernel, cuts, pairs),
        grid_spec=pltpu.PrefetchScalarGridSpec(
            num_scalar_prefetch=1,
            grid=(1,),
            in_specs=[anywhere] * 5,
            out_specs=[pl.BlockSpec(memory_space=pltpu.VMEM)] * len(cuts),
            scratch_shapes=[pltpu.SemaphoreType.DMA((8 * pairs * len(cuts),))],
        ),
        out_shape=[
            jax.ShapeDtypeStruct((8 * pairs, end - begin, model), LOW) for begin, end in cuts
        ],
        compiler_params=params(),
        cost_estimate=cost(5),
        name="assemble",
    )(place, *sources)


def local(
    tokens, segments, gelu_weight, gelu_bias, input_weight, input_bias, conv_taps, conv_bias,
    decay_gate, decay_bias, input_gate, ingate_bias, decay_param, out_weight, mixer_gain,
    gate_weight, up_weight, down_weight, feed_gain, cotangent,
):
    length, model = tokens.shape
    rim = conv_taps.shape[0] - 1
    chans = lax.axis_size("chan")
    me, row_place = lax.axis_index("chan"), lax.axis_index("rows")
    rows, block = decay_gate.shape
    total = rows * chans
    width = 2 * block
    group = width // rows

    padded = jnp.concatenate([jnp.full((rim,), -1, jnp.int32), segments])
    window = lax.dynamic_slice_in_dim(padded, me * length, length + rim)
    own = window[rim:]
    same = [own == window[rim - shift : rim - shift + length] for shift in range(1, rim + 1)]
    mask = jnp.stack([same[0], *same, own != 0] + [same[0]] * (7 - rim - 1), 1).astype(WIDE)
    mask = jnp.pad(mask, ((RIM, RIM), (0, 0)))

    small = jnp.concatenate(
        [
            jnp.stack([gelu_bias, input_bias, conv_bias, decay_bias, ingate_bias, decay_param]),
            conv_taps,
        ]
    )
    unit_rows = block // 4
    count = rows // unit_rows
    lines = unit_rows // 2
    place = jnp.stack([me, row_place]).astype(jnp.int32)
    clock = Clock()

    part = gate_weight.shape[1] // 4
    own_columns = lambda weight: lax.dynamic_slice_in_dim(weight, row_place * part, part, 1).T
    own_unit = jnp.stack(
        [
            own_columns(gate_weight),
            own_columns(up_weight),
            lax.dynamic_slice_in_dim(down_weight, row_place * part, part),
        ]
    )
    both = jnp.concatenate([decay_gate, input_gate], 1)
    both = jnp.pad(both, ((0, 0), (0, model // 2 - 2 * block)))
    both = both.reshape(count, 2, lines, model // 2).swapaxes(1, 2).reshape(count, lines, model)
    flat = small.reshape(small.shape[0], count, unit_rows).swapaxes(0, 1).reshape(count, 1, -1)
    flat = jnp.pad(flat, ((0, 0), (0, lines // 3 - 1), (0, model - flat.shape[2])))
    by_unit = lambda weight: weight.reshape(count, unit_rows, model)
    first = jnp.concatenate([by_unit(input_weight.T), both, flat], 1)
    second = jnp.concatenate([by_unit(gelu_weight.T), by_unit(out_weight)], 1)
    first_cuts = ((0, unit_rows), (unit_rows, first.shape[1]))
    second_cuts = ((0, unit_rows), (unit_rows, 2 * unit_rows))
    cot_low = cotangent.astype(LOW)
    if count == 4:
        quarters = lambda units: jnp.stack(
            [
                lax.dynamic_index_in_dim(units, row_place ^ bits, keepdims=False)
                for bits in (0, 2, 1, 3)
            ]
        )
        own_unit = clock.tick(own_unit)
        first = Sums(clock, spread_units(quarters(first)), pin=True)
        second = Sums(clock, spread_units(quarters(second)), start=False)
        for _ in range(3):
            lockstep(clock, first, second)
            clock.pin()
        first.step()
        u_weight, packed = clock.tick(assembled(place, first.result, first_cuts))
    else:
        cut = lambda units, cuts: [
            gathered(units.reshape(-1, model))[:, begin:end] for begin, end in cuts
        ]
        u_weight, packed = cut(first, first_cuts)
        y_weight, o_weight = cut(second, second_cuts)
        y_weight, o_weight = (w.reshape(total, model) for w in (y_weight, o_weight))
    feed_units = lax.all_gather(own_unit[None], ("chan", "rows"), axis=0, tiled=True)
    u_weight = u_weight.reshape(total, model)
    small_full = packed[:, lines, : small.shape[0] * unit_rows]
    small_full = small_full.reshape(-1, small.shape[0], unit_rows).swapaxes(0, 1)
    small_full = small_full.reshape(small.shape[0], total).astype(WIDE)
    param = small_full[5:6]
    line = lax.broadcasted_iota(jnp.int32, (16, total), 0)
    vec = jnp.pad(small_full, ((0, 6), (0, 0)))
    vec = jnp.where(line == 5, -8.0 * jax.nn.softplus(param), vec)
    vec = jnp.where(line == 10, -8.0 * jax.nn.sigmoid(param), vec)

    rim_tokens = moved_by(tokens[length - rim :], "chan", 1)
    extended = jnp.concatenate([jnp.zeros((RIM - rim, model), WIDE), rim_tokens, tokens])
    normed = rms_norm(extended, mixer_gain).astype(LOW)
    normed, u_weight = clock.tick((normed, u_weight))
    u, conv, rate, into, state, factor, decay_sum = clock.tick(
        mixer_forward(normed, u_weight, packed, vec, mask, width)
    )
    carry = Sums(
        clock, entering(jnp.concatenate([factor[-1:], state[-1:]]), "chan", 1), moved_by
    )
    if count == 4:
        second.step()
        carry.step()
        second.step()
        y_weight, o_weight = clock.tick(assembled(place, second.result, second_cuts))
        y_weight, o_weight = (w.reshape(total, model) for w in (y_weight, o_weight))
    active, slope = clock.tick(gelu_branch(normed, y_weight, vec, width))
    carry = clock.tick(carry.finish())
    cot_too = swapped(cot_low, "rows", 1)
    mixed, middle, normed2 = clock.tick(
        mixer_out(active, state, factor, carry, o_weight, tokens, feed_gain[None])
    )
    cot_too = clock.tick(cot_too)
    normed2_too = swapped(normed2, "rows", 1)
    feed_units = clock.tick(feed_units)
    block_output, normed2_grad, mine, send = clock.tick(
        feed(place, normed2, cot_low, middle, feed_units)
    )
    theirs = swapped(send, "rows", 1)

    mid_grad, mid_low, state_grad, y_grad, feed_gain_sum, back_sum, y_sum = clock.tick(
        middle_back(
            middle, normed2_grad, cotangent, feed_gain[None], o_weight, active, slope, state,
            factor, carry,
        )
    )
    after = Sums(
        clock,
        entering(
            jnp.concatenate([factor[-1:], jnp.sum(back_sum, 0, keepdims=True)]), "chan", -1
        ),
        moved_by,
    )
    theirs, normed2_too = clock.tick((theirs, normed2_too))
    near_y, far_y, near_x, far_x = clock.tick(
        feed_grads(mine, theirs, normed2, cot_low, normed2_too, cot_too)
    )
    split = lambda value: value.reshape(-1, 2, *value.shape[1:])
    fed = Sums(
        clock,
        owned(
            lambda place: split(near_y)[:, place],
            split(far_y),
            lambda place: near_x[:, :, place],
            far_x,
        ),
    )
    after = clock.tick(after.finish())
    place = jnp.stack([me // group, me % group, row_place]).astype(jnp.int32)
    pairs = total // width
    back = lambda after, begin, steps, so_far: clock.tick(
        mixer_back(
            place, state_grad, rate, into, conv, state, factor, u, y_grad, mixed, y_weight, u_weight,
            packed, vec, mask, carry, after, normed, mid_low, y_sum, decay_sum, rows, width, begin, steps, so_far,
        )
    )
    so_far = back(after, 1, pairs - 1, ())
    fed.step()
    so_far = clock.tick(so_far)
    keep, send, normed_grad = back(after, 0, 1, so_far)
    fed.moving = clock.tick(fed.moving)
    rest = Sums(clock, halved(keep, send))
    rim_grad = moved_by(clock.tick(normed_grad[RIM - rim : RIM]), "chan", -1)
    rim_grad = clock.tick(rim_grad)
    error = normed_grad[RIM:] + jnp.concatenate([jnp.zeros((length - rim, model), WIDE), rim_grad])
    scale = lax.rsqrt(jnp.mean(tokens * tokens, axis=-1, keepdims=True) + 1e-06)
    gained = mixer_gain * error
    mean = jnp.mean(gained * tokens, axis=-1, keepdims=True)
    tokens_grad = clock.tick(mid_grad + scale * gained - tokens * (scale * scale * scale * mean))
    mixer_gain_sum = jnp.sum(error * tokens * scale, 0)

    gains = Sums(clock, everywhere(jnp.stack([mixer_gain_sum, jnp.sum(feed_gain_sum, 0)])))
    rest.step()
    gains.moving = clock.tick(gains.moving)
    fed.step(pin=True)
    rest.step(pin=True)
    rest.step(pin=True)
    fed.step()
    fed = Sums(clock, settled(fed.result))
    gains.step()
    gains.step()
    fed.step()
    gains.step()
    rest.step()
    rest = Sums(clock, settled(rest.result))
    gains.step()
    fed.step()
    feed_sum = clock.tick(finish(jnp.stack([me, row_place]).astype(jnp.int32), *fed.result))
    rest.step()
    gains = gains.finish()
    rest_sum = ordered(*rest.finish())[0]
    gains = gains + clock.time[:1, :1]
    input_sum, gelu_sum, out_sum = (rest_sum[:, k * model : (k + 1) * model] for k in range(3))
    gates_sum = rest_sum[:, 3 * model : 3 * model + width]
    lines = rest_sum[:, 3 * model + width : 3 * model + width + 11].T
    mean_decay = lines[10] / (length * lax.axis_size("rows") * chans)
    return (
        block_output,
        tokens_grad,
        gelu_sum.T,
        lines[0],
        input_sum.T,
        lines[1],
        lines[2:6],
        lines[6],
        gates_sum[:, :block],
        lines[7],
        gates_sum[:, block:],
        lines[8],
        lines[9],
        out_sum,
        gains[0],
        feed_sum[0],
        feed_sum[1],
        feed_sum[2],
        gains[1],
        mean_decay,
    )


def solution(mesh):
    return jax.shard_map(
        local,
        mesh=mesh,
        in_specs=(
            P(("rows", "chan"), None),
            P("rows"),
            P(None, "chan"),
            P("chan"),
            P(None, "chan"),
            P("chan"),
            P(None, "chan"),
            P("chan"),
            P("chan", None),
            P("chan"),
            P("chan", None),
            P("chan"),
            P("chan"),
            P("chan", None),
            P(),
            P(None, "chan"),
            P(None, "chan"),
            P("chan", None),
            P(),
            P(("rows", "chan"), None),
        ),
        out_specs=(
            P(("rows", "chan"), None),
            P(("rows", "chan"), None),
            P(None, "chan"),
            P("chan"),
            P(None, "chan"),
            P("chan"),
            P(None, "chan"),
            P("chan"),
            P("chan", None),
            P("chan"),
            P("chan", None),
            P("chan"),
            P("chan"),
            P("chan", None),
            P(),
            P(None, "chan"),
            P(None, "chan"),
            P("chan", None),
            P(),
            P("chan"),
        ),
        check_vma=False,
    )
```

```python
import functools

import jax
import jax.numpy as jnp
from jax import lax
from jax.experimental import pallas as pl
from jax.experimental.pallas import tpu as pltpu
from jax.sharding import PartitionSpec as P

LOW = jnp.bfloat16
WIDE = jnp.float32
RIM = 16
STEP = 16
VMEM_BYTES = 56 * 1024 * 1024
GELU_SLOPE = 0.7978845608028654
GELU_CUBE = 0.044715


def params(**more):
    return pltpu.CompilerParams(vmem_limit_bytes=VMEM_BYTES, **more)


def moved_by(value, axis, steps):
    count = lax.axis_size(axis)
    leading, last = (max(0, -steps), min(count, count - steps))
    return lax.ppermute(value, axis, [(source, source + steps) for source in range(leading, last)])


def swapped(value, axis, bits):
    count = lax.axis_size(axis)
    return lax.ppermute(value, axis, [(source, source ^ bits) for source in range(count)])


def join(earlier, later):
    return jnp.concatenate(
        [earlier[0:1] * later[0:1], later[0:1] * earlier[1:2] + later[1:2]], 0
    )


def entering(value, axis, sign):
    count = lax.axis_size(axis)
    if count in (4, 8):
        (partner,) = yield [(value, axis, 1, swapped)]
        later = (lax.axis_index(axis) & 1) == (1 if sign > 0 else 0)
        both = join(jnp.where(later, partner, value), jnp.where(later, value, partner))
        came = yield [(both, axis, 2 * sign * reach) for reach in range(1, count // 2)]
        total = came[-1]
        for one in came[-2::-1]:
            total = join(total, one)
        return jnp.where(later, join(total, partner)[1:2], total[1:2])
    total = value
    came = yield [(value, axis, sign * reach) for reach in (1, 2, 3) if reach < count]
    for one in came:
        total = join(one, total)
    reach = 4
    while 2 * reach < count:
        (one,) = yield [(total, axis, sign * reach)]
        total = join(one, total)
        reach *= 2
    came = yield [(total, axis, sign * far) for far in (1, reach + 1) if far < count]
    last = came[0]
    for one in came[1:]:
        last = join(one, last)
    return last[1:2]


def rms_norm(values, gain):
    return values * lax.rsqrt(jnp.mean(values * values, axis=-1, keepdims=True) + 1e-06) * gain


def nt(left, right):
    return lax.dot_general(left, right, (((1,), (1,)), ((), ())), preferred_element_type=WIDE)


def tn(left, right):
    return lax.dot_general(left, right, (((0,), (0,)), ((), ())), preferred_element_type=WIDE)


def nn(left, right):
    return lax.dot_general(left, right, (((1,), (0,)), ((), ())), preferred_element_type=WIDE)


def sigmoid(value):
    return 0.5 * jnp.tanh(0.5 * value) + 0.5


def gelu_parts(value):
    square = value * value
    bend = jnp.tanh(GELU_SLOPE * value * (1.0 + GELU_CUBE * square))
    half = 0.5 + 0.5 * bend
    slope = half + 0.5 * GELU_SLOPE * value * (1.0 - bend * bend) * (1.0 + 3.0 * GELU_CUBE * square)
    return value * half, slope


def loop(count, unroll, body, init):
    while count % unroll:
        unroll -= 1

    def several(index, carry):
        for turn in range(unroll):
            carry = body(index * unroll + turn, carry)
        return carry

    return lax.fori_loop(0, count // unroll, several, init)


def cost(microseconds):
    return pl.CostEstimate(
        flops=int(microseconds * 1.1e9), bytes_accessed=int(microseconds * 3.5e6), transcendentals=0
    )


def fold(value):
    total = value[0:8]
    for group in range(1, value.shape[0] // 8):
        total = total + value[8 * group : 8 * group + 8]
    return total


def fill_gates(packed, gates, block):
    width = 2 * block
    lines = packed.shape[1] * 3 // 4

    @pl.when(pl.program_id(0) == 0)
    def _():
        gates[...] = jnp.zeros_like(gates)

    parts = []
    for unit in range(packed.shape[0]):
        value = packed[unit].astype(WIDE)[:lines]
        parts += [value[:, 0:width], value[:, 512 : 512 + width]]
    parts = jnp.concatenate(parts, 0).astype(LOW)
    for half in (0, block):
        gates[half : half + block, half : half + block] = parts[half : half + block, 0:block]
        gates[half : half + block, width + half : width + half + block] = parts[
            half : half + block, block:
        ]


def mixer_forward_kernel(
    normed, u_weight, packed, vec, mask, u_out, conv_out, r_out, i_out, h_out, f_out, sum_out,
    low, zed, gates,
):
    ext = normed.shape[0]
    width = u_out.shape[1]
    fill_gates(packed, gates, width // 2)
    count = (ext - RIM) // STEP
    u_out[...] = nt(normed[...], u_weight[...]) + vec[1:2, :]

    def convolve(index, _):
        base = pl.multiple_of(index * STEP, STEP)
        own = pl.ds(base, STEP)
        window = u_out[pl.ds(base + 8, STEP + 8), :]
        flags = mask[pl.ds(base + RIM, STEP), :]
        conv = vec[2:3, :] + vec[6:7, :] * window[8:]
        for shift in (1, 2, 3):
            conv = conv + flags[:, shift : shift + 1] * (
                vec[6 + shift : 7 + shift, :] * window[8 - shift : 8 - shift + STEP]
            )
        conv = conv * flags[:, 4:5]
        conv_out[own, :] = conv
        low[own, :] = conv.astype(LOW)
        return 0

    loop(count, 4, convolve, 0)
    zed[...] = nn(low[...], gates[...])
    line = lax.broadcasted_iota(jnp.int32, (8, width), 0)

    def advance(index, carry):
        state, factor, total = carry
        own = pl.ds(pl.multiple_of(index * STEP, STEP), STEP)
        going = mask[pl.ds(pl.multiple_of(index * STEP + RIM, STEP), STEP), :][:, 0:1]
        rate = sigmoid(zed[own, 0:width] + vec[3:4, :])
        into = sigmoid(zed[own, width:] + vec[4:5, :])
        decay = jnp.exp(vec[5:6, :] * rate)
        r_out[own, :] = rate
        i_out[own, :] = into
        scale = jnp.where(going == 0.0, 1.0, jnp.sqrt(1.01 - decay * decay))
        inject = conv_out[own, :] * into * scale
        carried = decay * going
        total = total + fold(decay)
        for group in range(STEP // 8):
            part = slice(8 * group, 8 * group + 8)
            mul, add = carried[part], inject[part]
            for reach in (1, 2, 4):
                inside = line >= reach
                add = add + mul * jnp.where(inside, pltpu.roll(add, reach, 0), 0.0)
                mul = mul * jnp.where(inside, pltpu.roll(mul, reach, 0), 1.0)
            here = add + mul * state
            gone = mul * factor
            rows = pl.ds(pl.multiple_of(index * STEP + 8 * group, 8), 8)
            h_out[rows, :] = here
            f_out[rows, :] = gone
            state, factor = here[7:8], gone[7:8]
        return state, factor, total

    zero = jnp.zeros((1, width), WIDE)
    _, _, total = loop(
        count, 4, advance, (zero, zero + 1.0, jnp.zeros((8, width), WIDE))
    )
    sum_out[...] = total


def mixer_forward(normed, u_weight, packed, vec, mask, width):
    ext, model = normed.shape
    tokens = ext - RIM
    total = u_weight.shape[0]
    pairs = total // width
    units = packed.shape[0] // pairs
    by_lane = lambda length: pl.BlockSpec((length, width), lambda step: (0, step))
    whole = lambda array: pl.BlockSpec(array.shape, lambda step: (0,) * array.ndim)
    flat = jax.ShapeDtypeStruct((tokens, total), WIDE)
    return pl.pallas_call(
        mixer_forward_kernel,
        grid=(pairs,),
        in_specs=[
            whole(normed),
            pl.BlockSpec((width, model), lambda step: (step, 0)),
            pl.BlockSpec((units, *packed.shape[1:]), lambda step: (step, 0, 0)),
            by_lane(vec.shape[0]),
            whole(mask),
        ],
        out_specs=[by_lane(ext)] + [by_lane(tokens)] * 5 + [by_lane(8)],
        out_shape=[jax.ShapeDtypeStruct((ext, total), WIDE)] + [flat] * 5
        + [jax.ShapeDtypeStruct((8, total), WIDE)],
        scratch_shapes=[
            pltpu.VMEM((tokens, width), LOW),
            pltpu.VMEM((tokens, 2 * width), WIDE),
            pltpu.VMEM((width, 2 * width), LOW),
        ],
        compiler_params=params(),
        cost_estimate=cost(26),
        name="mixer_forward",
    )(normed, u_weight, packed, vec, mask)


def gelu_branch_kernel(normed, weight, vec, active_out, slope_out, held):
    held[...] = nt(normed[RIM:, :], weight[...]) + vec[0:1, :]

    def act(index, _):
        own = pl.ds(pl.multiple_of(index * STEP, STEP), STEP)
        active_out[own, :], slope_out[own, :] = gelu_parts(held[own, :])
        return 0

    loop(held.shape[0] // STEP, 4, act, 0)


def gelu_branch(normed, weight, vec, width):
    length, total = normed.shape[0] - RIM, weight.shape[0]
    model = normed.shape[1]
    lane = lambda lines: pl.BlockSpec((lines, width), lambda step: (0, step))
    return pl.pallas_call(
        gelu_branch_kernel,
        grid=(total // width,),
        in_specs=[
            pl.BlockSpec(normed.shape, lambda step: (0, 0)),
            pl.BlockSpec((width, model), lambda step: (step, 0)),
            lane(vec.shape[0]),
        ],
        out_specs=[lane(length), lane(length)],
        out_shape=[jax.ShapeDtypeStruct((length, total), WIDE)] * 2,
        scratch_shapes=[pltpu.VMEM((length, width), WIDE)],
        compiler_params=params(),
        cost_estimate=cost(8),
        name="gelu_branch",
    )(normed, weight, vec)


def mixer_out_kernel(active, h, f, state, weight, tokens, gain, mixed, middle, normed):
    def gate(index, _):
        own = pl.ds(pl.multiple_of(index * STEP, STEP), STEP)
        mixed[own, :] = ((h[own, :] + f[own, :] * state[...]) * active[own, :]).astype(LOW)
        return 0

    loop(active.shape[0] // STEP, 4, gate, 0)
    total = tokens[...] + nn(mixed[...], weight[...])
    middle[...] = total
    scale = lax.rsqrt(jnp.mean(total * total, axis=-1, keepdims=True) + 1e-06)
    normed[...] = (total * scale * gain[...]).astype(LOW)


def mixer_out(active, h, f, state, weight, tokens, gain):
    length, model = tokens.shape
    total = active.shape[1]
    tile = 256 if length % 256 == 0 else length
    row = lambda lanes: pl.BlockSpec((tile, lanes), lambda step: (step, 0))
    one = lambda array: pl.BlockSpec(array.shape, lambda step: (0, 0))
    return pl.pallas_call(
        mixer_out_kernel,
        grid=(length // tile,),
        in_specs=[
            row(total), row(total), row(total), one(state), one(weight), row(model), one(gain),
        ],
        out_specs=[row(total), row(model), row(model)],
        out_shape=[
            jax.ShapeDtypeStruct((length, total), LOW),
            jax.ShapeDtypeStruct((length, model), WIDE),
            jax.ShapeDtypeStruct((length, model), LOW),
        ],
        compiler_params=params(),
        cost_estimate=cost(9),
        name="mixer_out",
    )(active, h, f, state, weight, tokens, gain)


def spread(place, wide, keep, send, matrix, group, rows, lanes=slice(None), count=None):
    part = rows // 4
    if part % 8:
        value = wide[:, 0:count]
        pieces = [value[begin : begin + part] for begin in range(0, group * rows, part)]
        mine = place[1] * 4 + place[2]
        bit = 1
        while bit < len(pieces):
            turned = (mine & bit) != 0
            pieces = [
                jnp.where(turned, pieces[index ^ bit], pieces[index])
                for index in range(len(pieces))
            ]
            bit *= 2
    for slot in range(group):
        shard = slot ^ place[1]
        for turn in range(4):
            if part % 8:
                value = pieces[4 * slot + turn]
            else:
                begin = pl.multiple_of(shard * rows + (turn ^ place[2]) * part, 8)
                value = wide[pl.ds(begin, part), 0:count]
            (keep, send)[turn & 1][slot, matrix, turn >> 1, :, lanes] = value.astype(LOW)


def feed_kernel(
    place, normed, cot, out_in, units, out, grad, keep, send, gate_s, up_s, back_s, hidden_l,
    gate_l, up_l, held, sems, turned, cot_turned,
):
    half = gate_s.shape[0] // 2
    model = normed.shape[1]
    width = gate_s.shape[0]
    part = width // 4
    step = pl.program_id(0)

    def copies(index):
        for turn in range(4):
            unit = (place[0] ^ index) * 4 + (place[1] ^ turn)
            order = (turn % 2) * 2 + turn // 2
            slot = index % 2
            yield pltpu.make_async_copy(
                units.at[unit], held.at[slot, :, order], sems.at[slot, turn]
            )

    @pl.when(step == 0)
    def _():
        out[...] = out_in[...]
        grad[...] = jnp.zeros_like(grad)
        turned[...] = jnp.transpose(normed[...])
        cot_turned[...] = jnp.transpose(cot[...])
        for copy in copies(0):
            copy.start()

    @pl.when(step + 1 < pl.num_programs(0))
    def _():
        for copy in copies(step + 1):
            copy.start()

    for copy in copies(step):
        copy.wait()

    def weight(matrix):
        if part % 16 == 0:
            return held[step % 2, matrix].reshape(width, model)
        pieces = [held[step % 2, matrix, turn].astype(WIDE) for turn in range(4)]
        return jnp.concatenate(pieces, 0).astype(LOW)

    first, second, third = weight(0), weight(1), weight(2)
    gate_s[...] = nn(first, turned[...])
    up_s[...] = nn(second, turned[...])
    back_s[...] = nn(third, cot_turned[...])

    def act(index, _):
        own = pl.ds(pl.multiple_of(index * STEP, STEP), STEP)
        up, back = up_s[own, :], back_s[own, :]
        value, slope = gelu_parts(gate_s[own, :])
        hidden_l[own, :] = (value * up).astype(LOW)
        gate_l[own, :] = (back * up * slope).astype(LOW)
        up_l[own, :] = (back * value).astype(LOW)
        return 0

    loop(width // STEP, 4, act, 0)
    out[...] += tn(hidden_l[...], third)
    grad[...] += tn(gate_l[...], first) + tn(up_l[...], second)
    for matrix, value in enumerate((gate_l, up_l, hidden_l)):
        keep[0, matrix] = value[:half, :]
        send[0, matrix] = value[half:, :]


def feed(place, normed, cot, out_in, units):
    length, model = normed.shape
    part = units.shape[2]
    slots = units.shape[0] // 4
    width = 4 * part
    whole = lambda array: pl.BlockSpec(array.shape, lambda step, place: (0,) * array.ndim)
    piece = pl.BlockSpec((1, 3, 2 * part, length), lambda step, place: (step, 0, 0, 0))
    wide = jax.ShapeDtypeStruct((length, model), WIDE)
    grads = jax.ShapeDtypeStruct((slots, 3, 2 * part, length), LOW)
    return pl.pallas_call(
        feed_kernel,
        grid_spec=pltpu.PrefetchScalarGridSpec(
            num_scalar_prefetch=1,
            grid=(slots,),
            in_specs=[
                whole(normed), whole(cot), whole(out_in), pl.BlockSpec(memory_space=pl.ANY),
            ],
            out_specs=[whole(out_in), whole(out_in), piece, piece],
            scratch_shapes=[pltpu.VMEM((width, length), WIDE)] * 3
            + [pltpu.VMEM((width, length), LOW)] * 3
            + [pltpu.VMEM((2, 3, 4, part, model), LOW), pltpu.SemaphoreType.DMA((2, 4))]
            + [pltpu.VMEM((model, length), LOW)] * 2,
        ),
        out_shape=[wide, wide, grads, grads],
        compiler_params=params(),
        cost_estimate=cost(34),
        name="feed",
    )(place, normed, cot, out_in, units)


def feed_grads_kernel(pairs, mine, theirs, normed, cot, normed_too, cot_too, *outs):
    part = outs[0].shape[2]
    step = pl.program_id(0)
    for matrix in range(3):
        right, right_too = (cot, cot_too) if matrix == 2 else (normed, normed_too)
        value = nn(mine[0, matrix], right[...]) + nn(theirs[0, matrix], right_too[...])
        value = value.astype(LOW)

        @pl.when(step < pairs)
        def _():
            outs[0][0, matrix] = value[:part]
            outs[1][0, matrix] = value[part:]

        for place, out in ((pairs, outs[2]), (pairs + pairs // 2, outs[3])):

            @pl.when((step >= place) & (step < place + pairs // 2))
            def _():
                out[0, matrix, 0] = value[:part]
                out[0, matrix, 1] = value[part:]


def feed_grads(mine, theirs, normed, cot, normed_too, cot_too):
    slots, _, rows, length = mine.shape
    model = normed.shape[1]
    pairs, part = slots // 2, rows // 2
    whole = lambda array: pl.BlockSpec(array.shape, lambda step: (0,) * array.ndim)

    def source(step):
        even = 4 * (step // 2) + step % 2
        odd = step - pairs
        last = odd >= pairs // 2
        odd = 4 * jnp.where(last, odd - pairs // 2, odd) + 2 + last.astype(jnp.int32)
        return jnp.where(step < pairs, even, odd), 0, 0, 0

    clipped = lambda first, count: lambda step: jnp.clip(step - first, 0, count - 1)
    even = clipped(0, pairs)
    spec = lambda place, count: pl.BlockSpec(
        (1, 3, 2, part, model), lambda step: (clipped(place, count)(step), 0, 0, 0, 0)
    )
    flat = pl.BlockSpec((1, 3, part, model), lambda step: (even(step), 0, 0, 0))
    return pl.pallas_call(
        functools.partial(feed_grads_kernel, pairs),
        grid=(slots,),
        in_specs=[pl.BlockSpec((1, 3, rows, length), source)] * 2
        + [whole(normed)] * 4,
        out_specs=[flat, flat, spec(pairs, pairs // 2), spec(pairs + pairs // 2, pairs // 2)],
        out_shape=[jax.ShapeDtypeStruct((pairs, 3, part, model), LOW)] * 2
        + [jax.ShapeDtypeStruct((pairs // 2, 3, 2, part, model), LOW)] * 2,
        compiler_params=params(),
        cost_estimate=cost(17),
        name="feed_grads",
    )(mine, theirs, normed, cot, normed_too, cot_too)


def middle_back_kernel(
    middle, grad, cot, gain, weight, active_in, slope_in, h, f, state, mid_grad, mid_low, state_grad, y_grad,
    gain_sum, back_sum, bias_sum, mixed_s,
):
    @pl.when(pl.program_id(0) == 0)
    def _():
        gain_sum[...] = jnp.zeros_like(gain_sum)
        back_sum[...] = jnp.zeros_like(back_sum)
        bias_sum[...] = jnp.zeros_like(bias_sum)

    value, error = middle[...], grad[...]
    scale = lax.rsqrt(jnp.mean(value * value, axis=-1, keepdims=True) + 1e-06)
    gained = gain[...] * error
    mean = jnp.mean(gained * value, axis=-1, keepdims=True)
    total = cot[...] + scale * gained - value * (scale * scale * scale * mean)
    gain_sum[...] += fold(error * value * scale)
    mid_grad[...] = total
    mid_low[...] = total.astype(LOW)
    mixed_s[...] = nt(mid_low[...], weight[...])

    def turn(index, carry):
        back, bias = carry
        own = pl.ds(pl.multiple_of(index * STEP, STEP), STEP)
        error = mixed_s[own, :]
        active, slope = active_in[own, :], slope_in[own, :]
        gone = f[own, :]
        full = h[own, :] + gone * state[...]
        here = error * active
        state_grad[own, :] = here
        low = (error * full * slope).astype(LOW)
        y_grad[own, :] = low
        return back + fold(here * gone), bias + fold(low.astype(WIDE))

    zero = jnp.zeros(back_sum.shape, WIDE)
    back, bias = loop(middle.shape[0] // STEP, 4, turn, (zero, zero))
    back_sum[...] += back
    bias_sum[...] += bias


def middle_back(middle, grad, cot, gain, weight, active, slope, h, f, state):
    length, model = middle.shape
    total = active.shape[1]
    tile = 256 if length % 256 == 0 else length
    row = lambda lanes: pl.BlockSpec((tile, lanes), lambda step: (step, 0))
    one = lambda lines, lanes: pl.BlockSpec((lines, lanes), lambda step: (0, 0))
    return pl.pallas_call(
        middle_back_kernel,
        grid=(length // tile,),
        in_specs=[
            row(model), row(model), row(model), one(1, model),
            one(total, model), row(total), row(total), row(total), row(total), one(1, total),
        ],
        out_specs=[
            row(model), row(model), row(total), row(total), one(8, model), one(8, total),
            one(8, total),
        ],
        out_shape=[
            jax.ShapeDtypeStruct((length, model), WIDE),
            jax.ShapeDtypeStruct((length, model), LOW),
            jax.ShapeDtypeStruct((length, total), WIDE),
            jax.ShapeDtypeStruct((length, total), LOW),
            jax.ShapeDtypeStruct((8, model), WIDE),
            jax.ShapeDtypeStruct((8, total), WIDE),
            jax.ShapeDtypeStruct((8, total), WIDE),
        ],
        scratch_shapes=[pltpu.VMEM((tile, total), WIDE)],
        compiler_params=params(),
        cost_estimate=cost(13),
        name="middle_back",
    )(middle, grad, cot, gain, weight, active, slope, h, f, state)


def mixer_back_kernel(
    rows, first, place, state_grad, r_in, i_in, conv_in, h, f, u, y_grad, mixed, y_weight, u_weight,
    packed, vec, mask, state, after, normed, mid_low, y_sum, decay_sum, *refs
):
    if not first:
        grad_in, refs = refs[2], refs[3:]
    (
        keep, send, normed_grad, conv_s, low, conv_l, grown, u_low, wide, gate_w, gates, sums,
    ) = refs
    length, width = state_grad.shape
    ext, model = normed.shape
    group = width // rows
    block = width // 2
    count = length // STEP
    line = lax.broadcasted_iota(jnp.int32, (8, width), 0)

    fill_gates(packed, gates, block)

    @pl.when(pl.program_id(0) == 0)
    def _():
        if first:
            normed_grad[...] = jnp.zeros_like(normed_grad)
        else:
            normed_grad[...] = grad_in[...]

    def retreat(index, carry):
        error, rate_sum, into_sum, slope_sum = carry
        base = pl.multiple_of((count - 1 - index) * STEP, STEP)
        own = pl.ds(base, STEP)
        going = mask[pl.ds(base + RIM, STEP), :][:, 0:1]
        rate, into, conv = r_in[own, :], i_in[own, :], conv_in[own, :]
        slope = vec[5:6, :]
        decay = jnp.exp(slope * rate)
        carried = decay * going
        given = state_grad[own, :]
        full = h[own, :] + f[own, :] * state[...]
        ahead = pl.ds(pl.multiple_of(jnp.maximum(base - 8, 0), 8), 8)
        edge = h[ahead, :][7:8] + f[ahead, :][7:8] * state[...]
        edge = jnp.where(base == 0, state[...], edge)
        parts = []
        for part in reversed(range(STEP // 8)):
            place_of = slice(8 * part, 8 * part + 8)
            mul = carried[place_of]
            add = mul * given[place_of]
            for reach in (1, 2, 4):
                inside = line < 8 - reach
                add = add + mul * jnp.where(inside, pltpu.roll(add, 8 - reach, 0), 0.0)
                mul = mul * jnp.where(inside, pltpu.roll(mul, 8 - reach, 0), 1.0)
            here = add + mul * error
            parts.append(given[place_of] + jnp.where(line < 7, pltpu.roll(here, 7, 0), error))
            error = here[0:1]
        grad = jnp.concatenate(parts[::-1], 0)
        befores = []
        for part in range(STEP // 8):
            last = edge if part == 0 else full[8 * part - 1 : 8 * part]
            befores.append(
                jnp.where(line > 0, pltpu.roll(full[8 * part : 8 * part + 8], 1, 0), last)
            )
        before = jnp.concatenate(befores, 0)
        root = lax.rsqrt(1.01 - decay * decay)
        scale = jnp.where(going == 0.0, 1.0, (1.01 - decay * decay) * root)
        through = grad * conv
        into_grad = through * scale
        conv_s[own, :] = grad * into * scale
        decay_grad = going * decay * (grad * before - through * into * decay * root)
        z_rate = decay_grad * slope * rate * (1.0 - rate)
        z_into = into_grad * into * (1.0 - into)
        low[own, 0:width] = z_rate.astype(LOW)
        low[own, width:] = z_into.astype(LOW)
        conv_l[own, :] = conv.astype(LOW)
        return (
            error,
            rate_sum + fold(z_rate),
            into_sum + fold(z_into),
            slope_sum + fold(decay_grad * rate),
        )

    zero = jnp.zeros((8, width), WIDE)
    _, rate_sum, into_sum, slope_sum = loop(
        count, 4, retreat, (after[...], zero, zero, zero)
    )
    conv_s[...] += nt(low[...], gates[...])
    gate_full = tn(conv_l[...], low[...])
    for half in (0, block):
        rows_of = slice(half, half + block)
        gate_w[rows_of, 0:block] = gate_full[rows_of, half : half + block]
        gate_w[rows_of, block:] = gate_full[rows_of, width + half : width + half + block]
    grown[0:RIM, :] = jnp.zeros((RIM, width), WIDE)
    grown[RIM + length :, :] = jnp.zeros((RIM, width), WIDE)

    def taps(index, carry):
        base = pl.multiple_of(index * STEP, STEP)
        window = u[pl.ds(base + 8, STEP + 8), :]
        flags = mask[pl.ds(base + RIM, STEP), :]
        error = conv_s[pl.ds(base, STEP), :] * flags[:, 4:5]
        grown[pl.ds(base + RIM, STEP), :] = error
        out = [carry[0] + fold(error), carry[1] + fold(error * window[8:])]
        for shift in (1, 2, 3):
            moved = window[8 - shift : 8 - shift + STEP]
            out.append(carry[1 + shift] + fold(flags[:, shift : shift + 1] * error * moved))
        return tuple(out)

    bias_sum, *tap_sums = loop(count, 4, taps, (zero,) * 5)

    def spread_back(index, total):
        base = pl.multiple_of(index * STEP, STEP)
        window = grown[pl.ds(base, STEP + 8), :]
        flags = mask[pl.ds(base, STEP + 8), :]
        value = vec[6:7, :] * window[0:STEP]
        for shift in (1, 2, 3):
            masked = flags[:, shift : shift + 1] * window
            value = value + vec[6 + shift : 7 + shift, :] * masked[shift : shift + STEP]
        rounded = value.astype(LOW)
        u_low[pl.ds(base, STEP), :] = rounded
        return total + fold(rounded.astype(WIDE))

    input_sum = loop(ext // STEP, 3, spread_back, zero)
    sums[...] = jnp.zeros_like(sums)
    slope_sum = slope_sum * vec[10:11, :]
    values = (y_sum[...], input_sum, *tap_sums, bias_sum, rate_sum, into_sum, slope_sum, decay_sum[...])
    for row, value in enumerate(values):
        sums[row : row + 1, :] = jnp.sum(value, axis=0, keepdims=True)
    wide[:, 0:128] = jnp.transpose(sums[...])
    spread(place, wide, keep, send, 0, group, rows, slice(3 * model + width, None), 128)
    wide[...] = tn(u_low[...], normed[...])
    spread(place, wide, keep, send, 0, group, rows, slice(0, model))
    spread(place, gate_w, keep, send, 0, group, rows, slice(3 * model, 3 * model + width))
    wide[...] = tn(y_grad[...], normed[RIM:, :])
    spread(place, wide, keep, send, 0, group, rows, slice(model, 2 * model))
    wide[...] = tn(mixed[...], mid_low[...])
    spread(place, wide, keep, send, 0, group, rows, slice(2 * model, 3 * model))
    normed_grad[...] += nn(u_low[...], u_weight[...])
    normed_grad[RIM:, :] += nn(y_grad[...], y_weight[...])


def mixer_back(
    place, state_grad, r, i, conv, h, f, u, y_grad, mixed, y_weight, u_weight, packed, vec, mask,
    state, after, normed, mid_low, y_sum, decay_sum, rows, width, begin, steps, so_far=(),
):
    length, total = state_grad.shape
    ext, model = normed.shape
    group, part = width // rows, rows // 4
    pair = lambda step, place: (step + begin) ^ place[0]
    whole = lambda array: pl.BlockSpec(array.shape, lambda step, place: (0,) * array.ndim)
    lane = lambda lines: pl.BlockSpec((lines, width), lambda step, place: (0, pair(step, place)))
    weight = pl.BlockSpec((width, model), lambda step, place: (pair(step, place), 0))
    units = packed.shape[0] * width // total
    lanes = 3 * model + width + 128
    piece = pl.BlockSpec((group, 1, 2, part, lanes), lambda step, place: (step + begin, 0, 0, 0, 0))
    shape = jax.ShapeDtypeStruct((total // rows, 1, 2, part, lanes), LOW)
    operands = [
        state_grad, r, i, conv, h, f, u, y_grad, mixed, y_weight, u_weight, packed, vec, mask,
        state, after, normed, mid_low, y_sum, decay_sum,
    ]
    kept = pl.BlockSpec(memory_space=pl.ANY)
    return pl.pallas_call(
        functools.partial(mixer_back_kernel, rows, not so_far),
        grid_spec=pltpu.PrefetchScalarGridSpec(
            num_scalar_prefetch=1,
            grid=(steps,),
            in_specs=[
                lane(length), lane(length), lane(length), lane(length), lane(length),
                lane(length), lane(ext), lane(length), lane(length), weight, weight,
                pl.BlockSpec(
                    (units, *packed.shape[1:]), lambda step, place: (pair(step, place), 0, 0)
                ),
                lane(vec.shape[0]), whole(mask), lane(1),
                lane(1), whole(normed), whole(mid_low), lane(8), lane(8),
            ]
            + ([kept, kept, whole(so_far[2])] if so_far else []),
            out_specs=[
                piece, piece, pl.BlockSpec((ext, model), lambda step, place: (0, 0)),
            ],
            scratch_shapes=[
                pltpu.VMEM((length, width), WIDE),
                pltpu.VMEM((length, 2 * width), LOW),
                pltpu.VMEM((length, width), LOW),
                pltpu.VMEM((ext + RIM, width), WIDE),
                pltpu.VMEM((ext, width), LOW),
                pltpu.VMEM((width, model), WIDE),
                pltpu.VMEM((width, width), WIDE),
                pltpu.VMEM((width, 2 * width), LOW),
                pltpu.VMEM((128, width), WIDE),
            ],
        ),
        out_shape=[shape, shape, jax.ShapeDtypeStruct((ext, model), WIDE)],
        input_output_aliases={len(operands) + 1 + k: k for k in range(2)} if so_far else {},
        compiler_params=params(),
        cost_estimate=cost(15 * steps),
        name="mixer_back",
    )(place, *operands, *so_far)


def wide_of(value):
    return value.astype(WIDE)


def pin_kernel(source, target):
    del source, target


class Clock:
    def __init__(self):
        self.time = jnp.zeros((8, 128), WIDE)

    def tick(self, values):
        values, self.time = lax.optimization_barrier((values, self.time))
        return values

    def pin(self):
        self.time = pl.pallas_call(
            pin_kernel,
            in_specs=[pl.BlockSpec(memory_space=pl.ANY)],
            out_specs=pl.BlockSpec(memory_space=pl.ANY),
            out_shape=jax.ShapeDtypeStruct(self.time.shape, WIDE),
            input_output_aliases={0: 0},
            cost_estimate=cost(5000),
            name="pin",
        )(self.time)


class Sums:
    def __init__(self, clock, stages, move=swapped, pin=False, start=True):
        self.clock = clock
        self.stages = stages
        self.move = move
        self.result = self.moving = None
        if start:
            self.begin(pin)

    def begin(self, pin=False):
        self.send(next(self.stages), pin)

    def send(self, transfers, pin):
        meanwhile = transfers.pop() if callable(transfers[-1]) else None
        values = self.clock.tick([transfer[0] for transfer in transfers])
        self.moving = [
            (transfer[3] if len(transfer) > 3 else self.move)(value, *transfer[1:3])
            for value, transfer in zip(values, transfers)
        ]
        if pin:
            self.clock.pin()
        if meanwhile:
            meanwhile()

    def step(self, pin=False):
        try:
            transfers = self.stages.send(self.clock.tick(self.moving))
        except StopIteration as end:
            self.result = end.value
        else:
            self.send(transfers, pin)

    def finish(self):
        while self.result is None:
            self.step()
        return self.result


def lockstep(clock, *groups):
    begun = [group for group in groups if group.moving is not None]
    arrived = clock.tick([group.moving for group in begun])
    transfers = []
    for group in groups:
        if group.moving is None:
            transfers.append(next(group.stages))
        else:
            transfers.append(group.stages.send(arrived[begun.index(group)]))
    values = clock.tick([[transfer[0] for transfer in one] for one in transfers])
    for group, one, own in zip(groups, transfers, values):
        group.moving = [group.move(value, *transfer[1:]) for value, transfer in zip(own, one)]


def halved(clock, keep, send):
    slots, matrices, _, part, lanes = keep.shape
    shape = (slots // 4, 2, 2, matrices, 2, part, lanes)
    keep = keep.reshape(shape)
    (came,) = yield [(send, "rows", 1)]
    came = came.reshape(shape)
    every = slice(None)
    near = {}

    def both(one, other, *where):
        return wide_of(one[where]) + wide_of(other[where])

    def meanwhile():
        one, other = clock.tick((keep, came))
        near["y"] = both(one, other, every, 0, every, every, 0)
        near["x"] = both(one, other, every, 1, 0)
        near.update(clock.tick(dict(near)))

    return (
        yield from owned(
            lambda place: near["y"][:, place],
            both(keep, came, every, 0, every, every, 1).astype(LOW),
            lambda place: near["x"][:, :, place],
            both(keep, came, every, 1, 1).astype(LOW),
            meanwhile,
        )
    )


def owned(near_y, far_y, near_x, far_x, meanwhile=None):
    from_y, from_x = yield [(far_y, "rows", 2), (far_x, "chan", 1)] + (
        [meanwhile] if meanwhile else []
    )
    rest = lambda place: wide_of(near_y(place)) + wide_of(from_y[:, place])
    also = lambda place: wide_of(near_x(place)) + wide_of(from_x[:, :, place])
    rest_came, also_came = yield [
        (rest(1).astype(LOW), "chan", 1),
        (also(1).astype(LOW), "rows", 2),
    ]
    rest, also = rest(0), also(0)
    parts = {}
    for index in range(rest.shape[0]):
        parts[2 * index] = rest[index] + wide_of(rest_came[index])
        parts[2 * index + 1] = also[index] + wide_of(also_came[index])
    came = yield [
        (value.astype(LOW), "chan", 2 * distance) for distance, value in parts.items() if distance
    ]
    total = parts[0]
    for value in came:
        total = total + wide_of(value)
    return total


def settled(total):
    total = total.astype(LOW)
    (came,) = yield [(total, "rows", 2)]
    pair = jnp.stack([total, came])
    (came,) = yield [(pair, "rows", 1)]
    return pair, came


def ordered(pair, came):
    four = jnp.stack([pair, came], 1)
    place = lax.axis_index("rows")
    four = jnp.where(place & 1, four[:, ::-1], four)
    four = jnp.where(place & 2, four[::-1], four)
    _, _, matrices, part, lanes = four.shape
    four = four.reshape(4, matrices, part, lanes).transpose(1, 0, 2, 3)
    return four.reshape(matrices, 4 * part, lanes).astype(WIDE)


def finish_kernel(place, pair, came, gate, up, down):
    def rows_of(matrix):
        parts = []
        for quarter in range(4):
            turn = quarter ^ place[1]
            own, other = (ref[turn // 2, matrix].astype(WIDE) for ref in (pair, came))
            parts.append(jnp.where(turn % 2 == 0, own, other))
        return jnp.concatenate(parts, 0)

    gate[...] = jnp.transpose(rows_of(0))
    up[...] = jnp.transpose(rows_of(1))
    down[...] = rows_of(2)


def finish(place, pair, came):
    _, _, part, model = pair.shape
    tall = jax.ShapeDtypeStruct((model, 4 * part), WIDE)
    vmem = pl.BlockSpec(memory_space=pltpu.VMEM)
    return pl.pallas_call(
        finish_kernel,
        grid_spec=pltpu.PrefetchScalarGridSpec(
            num_scalar_prefetch=1, grid=(1,), in_specs=[vmem] * 2, out_specs=[vmem] * 3
        ),
        out_shape=[tall, tall, jax.ShapeDtypeStruct((4 * part, model), WIDE)],
        compiler_params=params(),
        cost_estimate=cost(4),
        name="finish",
    )(place, pair, came)


def everywhere(value):
    for axis in ("rows", "chan"):
        bits = 1
        while bits < lax.axis_size(axis):
            (came,) = yield [(value, axis, bits)]
            value = value + came
            bits *= 2
    return value


def gathered(piece):
    parts = lax.axis_size("rows")
    share = piece.shape[0] // parts
    own = lax.dynamic_slice_in_dim(piece, lax.axis_index("rows") * share, share)
    full = lax.all_gather(own, ("chan", "rows"), axis=0, tiled=True)
    return full.reshape(lax.axis_size("chan"), piece.shape[0], piece.shape[1])


def pack_kernel(table, count, *refs):
    sources, outs, sems = refs[:count], refs[count:-1], refs[-1]
    copies = [
        pltpu.make_async_copy(
            sources[source].at[begin : begin + size],
            outs[out].at[at : at + size],
            sems.at[index],
        )
        for index, (out, at, source, begin, size) in enumerate(table)
    ]
    for copy in copies:
        copy.start()
    for copy in copies:
        copy.wait()


def pack(*lists):
    sources, table, shapes = [], [], []
    for out, pieces in enumerate(lists):
        at = 0
        for array, begin, size in pieces:
            known = [index for index, one in enumerate(sources) if one is array]
            if not known:
                known = [len(sources)]
                sources.append(array)
            table.append((out, at, known[0], begin, size))
            at += size
        shapes.append(jax.ShapeDtypeStruct((at, *pieces[0][0].shape[1:]), pieces[0][0].dtype))
    return pl.pallas_call(
        functools.partial(pack_kernel, table, len(sources)),
        in_specs=[pl.BlockSpec(memory_space=pl.ANY)] * len(sources),
        out_specs=[pl.BlockSpec(memory_space=pltpu.VMEM)] * len(shapes),
        scratch_shapes=[pltpu.SemaphoreType.DMA((len(table),))],
        out_shape=shapes,
        compiler_params=params(),
        cost_estimate=cost(0.01),
        name="pack",
    )(*sources)


def spread_units(units):
    pairs = range(2, lax.axis_size("chan") // 2)
    count = len(pairs)
    behind, *came = yield [(units[:2], "chan", 2)] + [
        (units[:1], "chan", 2 * pair) for pair in pairs
    ]
    singles = [(value, 0, 1) for value in came]
    (turned,) = pack([(units, 0, 1), (behind, 0, 2), *singles])
    (corners,) = yield [(turned, "chan", 1)]
    near, away = pack(
        [(behind, 0, 2), (corners, 1, 2)], [(corners, 0, 1), *singles, (corners, 3, count)]
    )
    over, near_too = yield [(away, "rows", 2), (near, "rows", 1)]
    size = 2 * count + 1
    (away,) = pack([(away, 0, size), (over, 0, size)])
    (away_too,) = yield [(away, "rows", 1)]
    return units, near, near_too, away, away_too


def unit_source(pair, side, turn, count):
    upper, other = turn // 2, turn % 2
    if pair == 0 and side == 0:
        return 0, 2 * other + upper
    if pair == 1:
        return 1 + other, 2 * side + upper
    if pair == 0:
        return 3 + other, upper * (2 * count + 1)
    return 3 + other, upper * (2 * count + 1) + 1 + side * count + pair - 2


def assemble_kernel(cuts, pairs, place, *refs):
    sources, outs, sems = refs[:5], refs[5:-1], refs[-1]
    copies = []
    for pair in range(pairs):
        for side in range(2):
            for turn in range(4):
                array, index = unit_source(pair, side, turn, pairs - 2)
                unit = ((2 * pair + side) ^ place[0]) * 4 + (turn ^ place[1])
                for (begin, end), out in zip(cuts, outs):
                    copies.append(
                        pltpu.make_async_copy(
                            sources[array].at[index, begin:end],
                            out.at[unit],
                            sems.at[len(copies)],
                        )
                    )
    for copy in copies:
        copy.start()
    for copy in copies:
        copy.wait()


def assembled(place, sources, cuts):
    pairs = lax.axis_size("chan") // 2
    model = sources[0].shape[2]
    anywhere = pl.BlockSpec(memory_space=pl.ANY)
    return pl.pallas_call(
        functools.partial(assemble_kernel, cuts, pairs),
        grid_spec=pltpu.PrefetchScalarGridSpec(
            num_scalar_prefetch=1,
            grid=(1,),
            in_specs=[anywhere] * 5,
            out_specs=[pl.BlockSpec(memory_space=pltpu.VMEM)] * len(cuts),
            scratch_shapes=[pltpu.SemaphoreType.DMA((8 * pairs * len(cuts),))],
        ),
        out_shape=[
            jax.ShapeDtypeStruct((8 * pairs, end - begin, model), LOW) for begin, end in cuts
        ],
        compiler_params=params(),
        cost_estimate=cost(5),
        name="assemble",
    )(place, *sources)


def local(
    tokens, segments, gelu_weight, gelu_bias, input_weight, input_bias, conv_taps, conv_bias,
    decay_gate, decay_bias, input_gate, ingate_bias, decay_param, out_weight, mixer_gain,
    gate_weight, up_weight, down_weight, feed_gain, cotangent,
):
    length, model = tokens.shape
    rim = conv_taps.shape[0] - 1
    chans = lax.axis_size("chan")
    me, row_place = lax.axis_index("chan"), lax.axis_index("rows")
    rows, block = decay_gate.shape
    total = rows * chans
    width = 2 * block
    group = width // rows

    padded = jnp.concatenate([jnp.full((rim,), -1, jnp.int32), segments])
    window = lax.dynamic_slice_in_dim(padded, me * length, length + rim)
    own = window[rim:]
    same = [own == window[rim - shift : rim - shift + length] for shift in range(1, rim + 1)]
    mask = jnp.stack([same[0], *same, own != 0] + [same[0]] * (7 - rim - 1), 1).astype(WIDE)
    mask = jnp.pad(mask, ((RIM, RIM), (0, 0)))

    small = jnp.concatenate(
        [
            jnp.stack([gelu_bias, input_bias, conv_bias, decay_bias, ingate_bias, decay_param]),
            conv_taps,
        ]
    )
    unit_rows = block // 4
    count = rows // unit_rows
    lines = unit_rows // 2
    place = jnp.stack([me, row_place]).astype(jnp.int32)
    clock = Clock()

    part = gate_weight.shape[1] // 4
    own_columns = lambda weight: lax.dynamic_slice_in_dim(weight, row_place * part, part, 1).T
    own_unit = jnp.stack(
        [
            own_columns(gate_weight),
            own_columns(up_weight),
            lax.dynamic_slice_in_dim(down_weight, row_place * part, part),
        ]
    )
    both = jnp.concatenate([decay_gate, input_gate], 1)
    both = jnp.pad(both, ((0, 0), (0, model // 2 - 2 * block)))
    both = both.reshape(count, 2, lines, model // 2).swapaxes(1, 2).reshape(count, lines, model)
    flat = small.reshape(small.shape[0], count, unit_rows).swapaxes(0, 1).reshape(count, 1, -1)
    flat = jnp.pad(flat, ((0, 0), (0, lines // 3 - 1), (0, model - flat.shape[2])))
    by_unit = lambda weight: weight.reshape(count, unit_rows, model)
    first = jnp.concatenate([by_unit(input_weight.T), both, flat], 1)
    second = jnp.concatenate([by_unit(gelu_weight.T), by_unit(out_weight)], 1)
    first_cuts = ((0, unit_rows), (unit_rows, first.shape[1]))
    second_cuts = ((0, unit_rows), (unit_rows, 2 * unit_rows))
    cot_low = cotangent.astype(LOW)
    if count == 4:
        quarters = lambda units: jnp.stack(
            [
                lax.dynamic_index_in_dim(units, row_place ^ bits, keepdims=False)
                for bits in (0, 2, 1, 3)
            ]
        )
        own_unit = clock.tick(own_unit)
        first = Sums(clock, spread_units(quarters(first)), pin=True)
        second = Sums(clock, spread_units(quarters(second)), start=False)
        for _ in range(3):
            lockstep(clock, first, second)
            clock.pin()
        first.step()
        u_weight, packed = clock.tick(assembled(place, first.result, first_cuts))
    else:
        cut = lambda units, cuts: [
            gathered(units.reshape(-1, model))[:, begin:end] for begin, end in cuts
        ]
        u_weight, packed = cut(first, first_cuts)
        y_weight, o_weight = cut(second, second_cuts)
        y_weight, o_weight = (w.reshape(total, model) for w in (y_weight, o_weight))
    feed_units = lax.all_gather(own_unit[None], ("chan", "rows"), axis=0, tiled=True)
    u_weight = u_weight.reshape(total, model)
    small_full = packed[:, lines, : small.shape[0] * unit_rows]
    small_full = small_full.reshape(-1, small.shape[0], unit_rows).swapaxes(0, 1)
    small_full = small_full.reshape(small.shape[0], total).astype(WIDE)
    param = small_full[5:6]
    line = lax.broadcasted_iota(jnp.int32, (16, total), 0)
    vec = jnp.pad(small_full, ((0, 6), (0, 0)))
    vec = jnp.where(line == 5, -8.0 * jax.nn.softplus(param), vec)
    vec = jnp.where(line == 10, -8.0 * jax.nn.sigmoid(param), vec)

    rim_tokens = moved_by(tokens[length - rim :], "chan", 1)
    extended = jnp.concatenate([jnp.zeros((RIM - rim, model), WIDE), rim_tokens, tokens])
    normed = rms_norm(extended, mixer_gain).astype(LOW)
    normed, u_weight = clock.tick((normed, u_weight))
    u, conv, rate, into, state, factor, decay_sum = clock.tick(
        mixer_forward(normed, u_weight, packed, vec, mask, width)
    )
    carry = Sums(
        clock, entering(jnp.concatenate([factor[-1:], state[-1:]]), "chan", 1), moved_by
    )
    if count == 4:
        second.step()
        carry.step()
        second.step()
        y_weight, o_weight = clock.tick(assembled(place, second.result, second_cuts))
        y_weight, o_weight = (w.reshape(total, model) for w in (y_weight, o_weight))
    active, slope = clock.tick(gelu_branch(normed, y_weight, vec, width))
    carry = clock.tick(carry.finish())
    cot_too = swapped(cot_low, "rows", 1)
    mixed, middle, normed2 = clock.tick(
        mixer_out(active, state, factor, carry, o_weight, tokens, feed_gain[None])
    )
    cot_too = clock.tick(cot_too)
    normed2_too = swapped(normed2, "rows", 1)
    feed_units = clock.tick(feed_units)
    block_output, normed2_grad, mine, send = clock.tick(
        feed(place, normed2, cot_low, middle, feed_units)
    )
    theirs = swapped(send, "rows", 1)

    mid_grad, mid_low, state_grad, y_grad, feed_gain_sum, back_sum, y_sum = clock.tick(
        middle_back(
            middle, normed2_grad, cotangent, feed_gain[None], o_weight, active, slope, state,
            factor, carry,
        )
    )
    after = Sums(
        clock,
        entering(
            jnp.concatenate([factor[-1:], jnp.sum(back_sum, 0, keepdims=True)]), "chan", -1
        ),
        moved_by,
    )
    theirs, normed2_too = clock.tick((theirs, normed2_too))
    near_y, far_y, near_x, far_x = clock.tick(
        feed_grads(mine, theirs, normed2, cot_low, normed2_too, cot_too)
    )
    split = lambda value: value.reshape(-1, 2, *value.shape[1:])
    fed = Sums(
        clock,
        owned(
            lambda place: split(near_y)[:, place],
            split(far_y),
            lambda place: near_x[:, :, place],
            far_x,
        ),
    )
    after = clock.tick(after.finish())
    place = jnp.stack([me // group, me % group, row_place]).astype(jnp.int32)
    pairs = total // width
    back = lambda after, begin, steps, so_far: clock.tick(
        mixer_back(
            place, state_grad, rate, into, conv, state, factor, u, y_grad, mixed, y_weight, u_weight,
            packed, vec, mask, carry, after, normed, mid_low, y_sum, decay_sum, rows, width, begin, steps, so_far,
        )
    )
    so_far = back(after, 1, pairs - 1, ())
    fed.step()
    so_far = clock.tick(so_far)
    keep, send, normed_grad = back(after, 0, 1, so_far)
    fed.moving = clock.tick(fed.moving)
    rest = Sums(clock, halved(clock, keep, send))
    rim_grad = moved_by(clock.tick(normed_grad[RIM - rim : RIM]), "chan", -1)
    rim_grad = clock.tick(rim_grad)
    error = normed_grad[RIM:] + jnp.concatenate([jnp.zeros((length - rim, model), WIDE), rim_grad])
    scale = lax.rsqrt(jnp.mean(tokens * tokens, axis=-1, keepdims=True) + 1e-06)
    gained = mixer_gain * error
    mean = jnp.mean(gained * tokens, axis=-1, keepdims=True)
    tokens_grad = clock.tick(mid_grad + scale * gained - tokens * (scale * scale * scale * mean))
    mixer_gain_sum = jnp.sum(error * tokens * scale, 0)

    gains = Sums(clock, everywhere(jnp.stack([mixer_gain_sum, jnp.sum(feed_gain_sum, 0)])))
    gains.step()
    rest.step(pin=True)
    fed.step()
    gains.moving = clock.tick(gains.moving)
    rest.step(pin=True)
    rest.step(pin=True)
    fed.step()
    fed = Sums(clock, settled(fed.result))
    gains.step()
    fed.step()
    gains.step()
    rest.step()
    rest = Sums(clock, settled(rest.result))
    gains.step()
    fed.step()
    feed_sum = clock.tick(finish(jnp.stack([me, row_place]).astype(jnp.int32), *fed.result))
    rest.step()
    gains = gains.finish()
    rest_sum = ordered(*rest.finish())[0]
    gains = gains + clock.time[:1, :1]
    input_sum, gelu_sum, out_sum = (rest_sum[:, k * model : (k + 1) * model] for k in range(3))
    gates_sum = rest_sum[:, 3 * model : 3 * model + width]
    lines = rest_sum[:, 3 * model + width : 3 * model + width + 11].T
    mean_decay = lines[10] / (length * lax.axis_size("rows") * chans)
    return (
        block_output,
        tokens_grad,
        gelu_sum.T,
        lines[0],
        input_sum.T,
        lines[1],
        lines[2:6],
        lines[6],
        gates_sum[:, :block],
        lines[7],
        gates_sum[:, block:],
        lines[8],
        lines[9],
        out_sum,
        gains[0],
        feed_sum[0],
        feed_sum[1],
        feed_sum[2],
        gains[1],
        mean_decay,
    )


def solution(mesh):
    return jax.shard_map(
        local,
        mesh=mesh,
        in_specs=(
            P(("rows", "chan"), None),
            P("rows"),
            P(None, "chan"),
            P("chan"),
            P(None, "chan"),
            P("chan"),
            P(None, "chan"),
            P("chan"),
            P("chan", None),
            P("chan"),
            P("chan", None),
            P("chan"),
            P("chan"),
            P("chan", None),
            P(),
            P(None, "chan"),
            P(None, "chan"),
            P("chan", None),
            P(),
            P(("rows", "chan"), None),
        ),
        out_specs=(
            P(("rows", "chan"), None),
            P(("rows", "chan"), None),
            P(None, "chan"),
            P("chan"),
            P(None, "chan"),
            P("chan"),
            P(None, "chan"),
            P("chan"),
            P("chan", None),
            P("chan"),
            P("chan", None),
            P("chan"),
            P("chan"),
            P("chan", None),
            P(),
            P(None, "chan"),
            P(None, "chan"),
            P("chan", None),
            P(),
            P("chan"),
        ),
        check_vma=False,
    )
```

```python
import functools

import jax
import jax.numpy as jnp
from jax import lax
from jax.experimental import pallas as pl
from jax.experimental.pallas import tpu as pltpu
from jax.sharding import PartitionSpec as P

LOW = jnp.bfloat16
WIDE = jnp.float32
RIM = 16
STEP = 16
VMEM_BYTES = 56 * 1024 * 1024
GELU_SLOPE = 0.7978845608028654
GELU_CUBE = 0.044715


def params(**more):
    return pltpu.CompilerParams(vmem_limit_bytes=VMEM_BYTES, **more)


def moved_by(value, axis, steps):
    count = lax.axis_size(axis)
    leading, last = (max(0, -steps), min(count, count - steps))
    return lax.ppermute(value, axis, [(source, source + steps) for source in range(leading, last)])


def swapped(value, axis, bits):
    count = lax.axis_size(axis)
    return lax.ppermute(value, axis, [(source, source ^ bits) for source in range(count)])


def join(earlier, later):
    return jnp.concatenate(
        [earlier[0:1] * later[0:1], later[0:1] * earlier[1:2] + later[1:2]], 0
    )


def entering(value, axis, sign):
    count = lax.axis_size(axis)
    if count in (4, 8):
        (partner,) = yield [(value, axis, 1, swapped)]
        later = (lax.axis_index(axis) & 1) == (1 if sign > 0 else 0)
        both = join(jnp.where(later, partner, value), jnp.where(later, value, partner))
        came = yield [(both, axis, 2 * sign * reach) for reach in range(1, count // 2)]
        total = came[-1]
        for one in came[-2::-1]:
            total = join(total, one)
        return jnp.where(later, join(total, partner)[1:2], total[1:2])
    total = value
    came = yield [(value, axis, sign * reach) for reach in (1, 2, 3) if reach < count]
    for one in came:
        total = join(one, total)
    reach = 4
    while 2 * reach < count:
        (one,) = yield [(total, axis, sign * reach)]
        total = join(one, total)
        reach *= 2
    came = yield [(total, axis, sign * far) for far in (1, reach + 1) if far < count]
    last = came[0]
    for one in came[1:]:
        last = join(one, last)
    return last[1:2]


def rms_norm(values, gain):
    return values * lax.rsqrt(jnp.mean(values * values, axis=-1, keepdims=True) + 1e-06) * gain


def nt(left, right):
    return lax.dot_general(left, right, (((1,), (1,)), ((), ())), preferred_element_type=WIDE)


def tn(left, right):
    return lax.dot_general(left, right, (((0,), (0,)), ((), ())), preferred_element_type=WIDE)


def nn(left, right):
    return lax.dot_general(left, right, (((1,), (0,)), ((), ())), preferred_element_type=WIDE)


def sigmoid(value):
    return 0.5 * jnp.tanh(0.5 * value) + 0.5


def gelu_parts(value):
    square = value * value
    bend = jnp.tanh(GELU_SLOPE * value * (1.0 + GELU_CUBE * square))
    half = 0.5 + 0.5 * bend
    slope = half + 0.5 * GELU_SLOPE * value * (1.0 - bend * bend) * (1.0 + 3.0 * GELU_CUBE * square)
    return value * half, slope


def loop(count, unroll, body, init):
    while count % unroll:
        unroll -= 1

    def several(index, carry):
        for turn in range(unroll):
            carry = body(index * unroll + turn, carry)
        return carry

    return lax.fori_loop(0, count // unroll, several, init)


def cost(microseconds):
    return pl.CostEstimate(
        flops=int(microseconds * 1.1e7), bytes_accessed=int(microseconds * 3.5e4), transcendentals=0
    )


def fold(value):
    total = value[0:8]
    for group in range(1, value.shape[0] // 8):
        total = total + value[8 * group : 8 * group + 8]
    return total


def fill_gates(packed, gates, block):
    width = 2 * block
    lines = packed.shape[1] * 3 // 4

    @pl.when(pl.program_id(0) == 0)
    def _():
        gates[...] = jnp.zeros_like(gates)

    parts = []
    for unit in range(packed.shape[0]):
        value = packed[unit].astype(WIDE)[:lines]
        parts += [value[:, 0:width], value[:, 512 : 512 + width]]
    parts = jnp.concatenate(parts, 0).astype(LOW)
    for half in (0, block):
        gates[half : half + block, half : half + block] = parts[half : half + block, 0:block]
        gates[half : half + block, width + half : width + half + block] = parts[
            half : half + block, block:
        ]


def mixer_forward_kernel(
    normed, u_weight, packed, vec, mask, u_out, conv_out, r_out, i_out, h_out, f_out, sum_out,
    low, zed, gates,
):
    ext = normed.shape[0]
    width = u_out.shape[1]
    fill_gates(packed, gates, width // 2)
    count = (ext - RIM) // STEP
    u_out[...] = nt(normed[...], u_weight[...]) + vec[1:2, :]

    def convolve(index, _):
        base = pl.multiple_of(index * STEP, STEP)
        own = pl.ds(base, STEP)
        window = u_out[pl.ds(base + 8, STEP + 8), :]
        flags = mask[pl.ds(base + RIM, STEP), :]
        conv = vec[2:3, :] + vec[6:7, :] * window[8:]
        for shift in (1, 2, 3):
            conv = conv + flags[:, shift : shift + 1] * (
                vec[6 + shift : 7 + shift, :] * window[8 - shift : 8 - shift + STEP]
            )
        conv = conv * flags[:, 4:5]
        conv_out[own, :] = conv
        low[own, :] = conv.astype(LOW)
        return 0

    loop(count, 4, convolve, 0)
    zed[...] = nn(low[...], gates[...])
    line = lax.broadcasted_iota(jnp.int32, (8, width), 0)

    def advance(index, carry):
        state, factor, total = carry
        own = pl.ds(pl.multiple_of(index * STEP, STEP), STEP)
        going = mask[pl.ds(pl.multiple_of(index * STEP + RIM, STEP), STEP), :][:, 0:1]
        rate = sigmoid(zed[own, 0:width] + vec[3:4, :])
        into = sigmoid(zed[own, width:] + vec[4:5, :])
        decay = jnp.exp(vec[5:6, :] * rate)
        r_out[own, :] = rate
        i_out[own, :] = into
        scale = jnp.where(going == 0.0, 1.0, jnp.sqrt(1.01 - decay * decay))
        inject = conv_out[own, :] * into * scale
        carried = decay * going
        total = total + fold(decay)
        for group in range(STEP // 8):
            part = slice(8 * group, 8 * group + 8)
            mul, add = carried[part], inject[part]
            for reach in (1, 2, 4):
                inside = line >= reach
                add = add + mul * jnp.where(inside, pltpu.roll(add, reach, 0), 0.0)
                mul = mul * jnp.where(inside, pltpu.roll(mul, reach, 0), 1.0)
            here = add + mul * state
            gone = mul * factor
            rows = pl.ds(pl.multiple_of(index * STEP + 8 * group, 8), 8)
            h_out[rows, :] = here
            f_out[rows, :] = gone
            state, factor = here[7:8], gone[7:8]
        return state, factor, total

    zero = jnp.zeros((1, width), WIDE)
    _, _, total = loop(
        count, 4, advance, (zero, zero + 1.0, jnp.zeros((8, width), WIDE))
    )
    sum_out[...] = total


def mixer_forward(normed, u_weight, packed, vec, mask, width):
    ext, model = normed.shape
    tokens = ext - RIM
    total = u_weight.shape[0]
    pairs = total // width
    units = packed.shape[0] // pairs
    by_lane = lambda length: pl.BlockSpec((length, width), lambda step: (0, step))
    whole = lambda array: pl.BlockSpec(array.shape, lambda step: (0,) * array.ndim)
    flat = jax.ShapeDtypeStruct((tokens, total), WIDE)
    return pl.pallas_call(
        mixer_forward_kernel,
        grid=(pairs,),
        in_specs=[
            whole(normed),
            pl.BlockSpec((width, model), lambda step: (step, 0)),
            pl.BlockSpec((units, *packed.shape[1:]), lambda step: (step, 0, 0)),
            by_lane(vec.shape[0]),
            whole(mask),
        ],
        out_specs=[by_lane(ext)] + [by_lane(tokens)] * 5 + [by_lane(8)],
        out_shape=[jax.ShapeDtypeStruct((ext, total), WIDE)] + [flat] * 5
        + [jax.ShapeDtypeStruct((8, total), WIDE)],
        scratch_shapes=[
            pltpu.VMEM((tokens, width), LOW),
            pltpu.VMEM((tokens, 2 * width), WIDE),
            pltpu.VMEM((width, 2 * width), LOW),
        ],
        compiler_params=params(),
        cost_estimate=cost(26),
        name="mixer_forward",
    )(normed, u_weight, packed, vec, mask)


def gelu_branch_kernel(normed, weight, vec, active_out, slope_out, held):
    held[...] = nt(normed[RIM:, :], weight[...]) + vec[0:1, :]

    def act(index, _):
        own = pl.ds(pl.multiple_of(index * STEP, STEP), STEP)
        active_out[own, :], slope_out[own, :] = gelu_parts(held[own, :])
        return 0

    loop(held.shape[0] // STEP, 4, act, 0)


def gelu_branch(normed, weight, vec, width):
    length, total = normed.shape[0] - RIM, weight.shape[0]
    model = normed.shape[1]
    lane = lambda lines: pl.BlockSpec((lines, width), lambda step: (0, step))
    return pl.pallas_call(
        gelu_branch_kernel,
        grid=(total // width,),
        in_specs=[
            pl.BlockSpec(normed.shape, lambda step: (0, 0)),
            pl.BlockSpec((width, model), lambda step: (step, 0)),
            lane(vec.shape[0]),
        ],
        out_specs=[lane(length), lane(length)],
        out_shape=[jax.ShapeDtypeStruct((length, total), WIDE)] * 2,
        scratch_shapes=[pltpu.VMEM((length, width), WIDE)],
        compiler_params=params(),
        cost_estimate=cost(8),
        name="gelu_branch",
    )(normed, weight, vec)


def mixer_out_kernel(active, h, f, state, weight, tokens, gain, mixed, middle, normed):
    def gate(index, _):
        own = pl.ds(pl.multiple_of(index * STEP, STEP), STEP)
        mixed[own, :] = ((h[own, :] + f[own, :] * state[...]) * active[own, :]).astype(LOW)
        return 0

    loop(active.shape[0] // STEP, 4, gate, 0)
    total = tokens[...] + nn(mixed[...], weight[...])
    middle[...] = total
    scale = lax.rsqrt(jnp.mean(total * total, axis=-1, keepdims=True) + 1e-06)
    normed[...] = (total * scale * gain[...]).astype(LOW)


def mixer_out(active, h, f, state, weight, tokens, gain):
    length, model = tokens.shape
    total = active.shape[1]
    tile = 256 if length % 256 == 0 else length
    row = lambda lanes: pl.BlockSpec((tile, lanes), lambda step: (step, 0))
    one = lambda array: pl.BlockSpec(array.shape, lambda step: (0, 0))
    return pl.pallas_call(
        mixer_out_kernel,
        grid=(length // tile,),
        in_specs=[
            row(total), row(total), row(total), one(state), one(weight), row(model), one(gain),
        ],
        out_specs=[row(total), row(model), row(model)],
        out_shape=[
            jax.ShapeDtypeStruct((length, total), LOW),
            jax.ShapeDtypeStruct((length, model), WIDE),
            jax.ShapeDtypeStruct((length, model), LOW),
        ],
        compiler_params=params(),
        cost_estimate=cost(9),
        name="mixer_out",
    )(active, h, f, state, weight, tokens, gain)


def spread(place, wide, keep, send, matrix, group, rows, lanes=slice(None), count=None):
    part = rows // 4
    if part % 8:
        value = wide[:, 0:count]
        pieces = [value[begin : begin + part] for begin in range(0, group * rows, part)]
        mine = place[1] * 4 + place[2]
        bit = 1
        while bit < len(pieces):
            turned = (mine & bit) != 0
            pieces = [
                jnp.where(turned, pieces[index ^ bit], pieces[index])
                for index in range(len(pieces))
            ]
            bit *= 2
    for slot in range(group):
        shard = slot ^ place[1]
        for turn in range(4):
            if part % 8:
                value = pieces[4 * slot + turn]
            else:
                begin = pl.multiple_of(shard * rows + (turn ^ place[2]) * part, 8)
                value = wide[pl.ds(begin, part), 0:count]
            (keep, send)[turn & 1][slot, matrix, turn >> 1, :, lanes] = value.astype(LOW)


def feed_kernel(
    group, place, normed, cot, out_in, units, out, grad, keep, send, gate_s, up_s, back_s, hidden_l,
    both_l, held, sems, turned, cot_turned,
):
    model = normed.shape[1]
    width = gate_s.shape[0]
    rows = width // group
    part, half = rows // 4, rows // 2
    step = pl.program_id(0)

    def copies(index):
        for member in range(group):
            for turn in range(4):
                unit = (place[0] ^ (group * index + member)) * 4 + (place[1] ^ turn)
                order = 4 * member + (turn % 2) * 2 + turn // 2
                slot = index % 2
                yield pltpu.make_async_copy(
                    units.at[unit], held.at[slot, :, order], sems.at[slot, 4 * member + turn]
                )

    @pl.when(step == 0)
    def _():
        for copy in copies(0):
            copy.start()
        out[...] = out_in[...]
        grad[...] = jnp.zeros_like(grad)
        turned[...] = jnp.transpose(normed[...])
        cot_turned[...] = jnp.transpose(cot[...])

    @pl.when(step + 1 < pl.num_programs(0))
    def _():
        for copy in copies(step + 1):
            copy.start()

    for copy in copies(step):
        copy.wait()

    def weight(begin, end):
        if part % 16 == 0:
            return held[step % 2, begin:end].reshape((end - begin) * width, model)
        pieces = [
            held[step % 2, matrix, order].astype(WIDE)
            for matrix in range(begin, end)
            for order in range(4 * group)
        ]
        return jnp.concatenate(pieces, 0).astype(LOW)

    first, third = weight(0, 2), weight(2, 3)
    gate_s[...] = nn(first[:width], turned[...])
    up_s[...] = nn(first[width:], turned[...])
    back_s[...] = nn(third, cot_turned[...])

    def act(index, _):
        base = pl.multiple_of(index * STEP, STEP)
        own = pl.ds(base, STEP)
        up, back = up_s[own, :], back_s[own, :]
        value, slope = gelu_parts(gate_s[own, :])
        hidden_l[own, :] = (value * up).astype(LOW)
        both_l[own, :] = (back * up * slope).astype(LOW)
        both_l[pl.ds(base + width, STEP), :] = (back * value).astype(LOW)
        return 0

    loop(width // STEP, 4, act, 0)
    out[...] += tn(hidden_l[...], third)
    grad[...] += tn(both_l[...], first)
    for member in range(group):
        for matrix, (value, offset) in enumerate(((both_l, 0), (both_l, width), (hidden_l, 0))):
            begin = offset + member * rows
            keep[member, matrix] = value[begin : begin + half, :]
            send[member, matrix] = value[begin + half : begin + rows, :]


def feed(place, normed, cot, out_in, units):
    length, model = normed.shape
    part = units.shape[2]
    slots = units.shape[0] // 4
    group = 2
    width = 4 * part * group
    whole = lambda array: pl.BlockSpec(array.shape, lambda step, place: (0,) * array.ndim)
    piece = pl.BlockSpec((group, 3, 2 * part, length), lambda step, place: (step, 0, 0, 0))
    wide = jax.ShapeDtypeStruct((length, model), WIDE)
    grads = jax.ShapeDtypeStruct((slots, 3, 2 * part, length), LOW)
    return pl.pallas_call(
        functools.partial(feed_kernel, group),
        grid_spec=pltpu.PrefetchScalarGridSpec(
            num_scalar_prefetch=1,
            grid=(slots // group,),
            in_specs=[
                whole(normed), whole(cot), whole(out_in), pl.BlockSpec(memory_space=pl.ANY),
            ],
            out_specs=[whole(out_in), whole(out_in), piece, piece],
            scratch_shapes=[pltpu.VMEM((width, length), WIDE)] * 3
            + [pltpu.VMEM((width, length), LOW), pltpu.VMEM((2 * width, length), LOW)]
            + [pltpu.VMEM((2, 3, 4 * group, part, model), LOW)]
            + [pltpu.SemaphoreType.DMA((2, 4 * group))]
            + [pltpu.VMEM((model, length), LOW)] * 2,
        ),
        out_shape=[wide, wide, grads, grads],
        compiler_params=params(),
        cost_estimate=cost(34),
        name="feed",
    )(place, normed, cot, out_in, units)


def feed_grads_kernel(parity, count, mine, theirs, normed, cot, normed_too, cot_too, near, far):
    part = mine.shape[2] // 2
    step = pl.program_id(0)
    for matrix in range(3):
        right, right_too = (cot, cot_too) if matrix == 2 else (normed, normed_too)
        value = nn(mine[0, matrix], right[...]) + nn(theirs[0, matrix], right_too[...])
        value = value.astype(LOW)
        if parity == 0:
            near[0, matrix] = value[:part]
            far[0, matrix] = value[part:]
            continue
        for place, out in ((0, near), (count // 2, far)):

            @pl.when((step >= place) & (step < place + count // 2))
            def _():
                out[0, matrix, 0] = value[:part]
                out[0, matrix, 1] = value[part:]


def feed_grads(parity, mine, theirs, normed, cot, normed_too, cot_too):
    slots, _, rows, length = mine.shape
    model = normed.shape[1]
    count, part = slots // 2, rows // 2
    whole = lambda array: pl.BlockSpec(array.shape, lambda step: (0,) * array.ndim)

    def source(step):
        if parity == 0:
            return 4 * (step // 2) + step % 2, 0, 0, 0
        last = (step >= count // 2).astype(jnp.int32)
        return 4 * (step - last * (count // 2)) + 2 + last, 0, 0, 0

    if parity == 0:
        specs = [pl.BlockSpec((1, 3, part, model), lambda step: (step, 0, 0, 0))] * 2
        shape = jax.ShapeDtypeStruct((count, 3, part, model), LOW)
    else:
        clipped = lambda first: lambda step: (jnp.clip(step - first, 0, count // 2 - 1), 0, 0, 0, 0)
        specs = [
            pl.BlockSpec((1, 3, 2, part, model), clipped(first)) for first in (0, count // 2)
        ]
        shape = jax.ShapeDtypeStruct((count // 2, 3, 2, part, model), LOW)
    return pl.pallas_call(
        functools.partial(feed_grads_kernel, parity, count),
        grid=(count,),
        in_specs=[pl.BlockSpec((1, 3, rows, length), source)] * 2 + [whole(normed)] * 4,
        out_specs=specs,
        out_shape=[shape, shape],
        compiler_params=params(),
        cost_estimate=cost(2000),
        name="feed_grads",
    )(mine, theirs, normed, cot, normed_too, cot_too)


def middle_back_kernel(
    middle, grad, cot, gain, weight, active_in, slope_in, h, f, state, mid_grad, mid_low, state_grad, y_grad,
    gain_sum, back_sum, bias_sum, mixed_s,
):
    @pl.when(pl.program_id(0) == 0)
    def _():
        gain_sum[...] = jnp.zeros_like(gain_sum)
        back_sum[...] = jnp.zeros_like(back_sum)
        bias_sum[...] = jnp.zeros_like(bias_sum)

    value, error = middle[...], grad[...]
    scale = lax.rsqrt(jnp.mean(value * value, axis=-1, keepdims=True) + 1e-06)
    gained = gain[...] * error
    mean = jnp.mean(gained * value, axis=-1, keepdims=True)
    total = cot[...] + scale * gained - value * (scale * scale * scale * mean)
    gain_sum[...] += fold(error * value * scale)
    mid_grad[...] = total
    mid_low[...] = total.astype(LOW)
    mixed_s[...] = nt(mid_low[...], weight[...])

    def turn(index, carry):
        back, bias = carry
        own = pl.ds(pl.multiple_of(index * STEP, STEP), STEP)
        error = mixed_s[own, :]
        active, slope = active_in[own, :], slope_in[own, :]
        gone = f[own, :]
        full = h[own, :] + gone * state[...]
        here = error * active
        state_grad[own, :] = here
        low = (error * full * slope).astype(LOW)
        y_grad[own, :] = low
        return back + fold(here * gone), bias + fold(low.astype(WIDE))

    zero = jnp.zeros(back_sum.shape, WIDE)
    back, bias = loop(middle.shape[0] // STEP, 4, turn, (zero, zero))
    back_sum[...] += back
    bias_sum[...] += bias


def middle_back(middle, grad, cot, gain, weight, active, slope, h, f, state):
    length, model = middle.shape
    total = active.shape[1]
    tile = 256 if length % 256 == 0 else length
    row = lambda lanes: pl.BlockSpec((tile, lanes), lambda step: (step, 0))
    one = lambda lines, lanes: pl.BlockSpec((lines, lanes), lambda step: (0, 0))
    return pl.pallas_call(
        middle_back_kernel,
        grid=(length // tile,),
        in_specs=[
            row(model), row(model), row(model), one(1, model),
            one(total, model), row(total), row(total), row(total), row(total), one(1, total),
        ],
        out_specs=[
            row(model), row(model), row(total), row(total), one(8, model), one(8, total),
            one(8, total),
        ],
        out_shape=[
            jax.ShapeDtypeStruct((length, model), WIDE),
            jax.ShapeDtypeStruct((length, model), LOW),
            jax.ShapeDtypeStruct((length, total), WIDE),
            jax.ShapeDtypeStruct((length, total), LOW),
            jax.ShapeDtypeStruct((8, model), WIDE),
            jax.ShapeDtypeStruct((8, total), WIDE),
            jax.ShapeDtypeStruct((8, total), WIDE),
        ],
        scratch_shapes=[pltpu.VMEM((tile, total), WIDE)],
        compiler_params=params(),
        cost_estimate=cost(13),
        name="middle_back",
    )(middle, grad, cot, gain, weight, active, slope, h, f, state)


def mixer_back_kernel(
    rows, first, place, state_grad, r_in, i_in, conv_in, h, f, u, y_grad, mixed, y_weight, u_weight,
    packed, vec, mask, state, after, normed, mid_low, y_sum, decay_sum, *refs
):
    if not first:
        grad_in, refs = refs[2], refs[3:]
    (
        keep, send, normed_grad, conv_s, low, conv_l, grown, u_low, wide, gate_w, gates, sums,
    ) = refs
    length, width = state_grad.shape
    ext, model = normed.shape
    group = width // rows
    block = width // 2
    count = length // STEP
    line = lax.broadcasted_iota(jnp.int32, (8, width), 0)

    fill_gates(packed, gates, block)

    @pl.when(pl.program_id(0) == 0)
    def _():
        if first:
            normed_grad[...] = jnp.zeros_like(normed_grad)
        else:
            normed_grad[...] = grad_in[...]

    def retreat(index, carry):
        error, rate_sum, into_sum, slope_sum = carry
        base = pl.multiple_of((count - 1 - index) * STEP, STEP)
        own = pl.ds(base, STEP)
        going = mask[pl.ds(base + RIM, STEP), :][:, 0:1]
        rate, into, conv = r_in[own, :], i_in[own, :], conv_in[own, :]
        slope = vec[5:6, :]
        decay = jnp.exp(slope * rate)
        carried = decay * going
        given = state_grad[own, :]
        full = h[own, :] + f[own, :] * state[...]
        ahead = pl.ds(pl.multiple_of(jnp.maximum(base - 8, 0), 8), 8)
        edge = h[ahead, :][7:8] + f[ahead, :][7:8] * state[...]
        edge = jnp.where(base == 0, state[...], edge)
        parts = []
        for part in reversed(range(STEP // 8)):
            place_of = slice(8 * part, 8 * part + 8)
            mul = carried[place_of]
            add = mul * given[place_of]
            for reach in (1, 2, 4):
                inside = line < 8 - reach
                add = add + mul * jnp.where(inside, pltpu.roll(add, 8 - reach, 0), 0.0)
                mul = mul * jnp.where(inside, pltpu.roll(mul, 8 - reach, 0), 1.0)
            here = add + mul * error
            parts.append(given[place_of] + jnp.where(line < 7, pltpu.roll(here, 7, 0), error))
            error = here[0:1]
        grad = jnp.concatenate(parts[::-1], 0)
        befores = []
        for part in range(STEP // 8):
            last = edge if part == 0 else full[8 * part - 1 : 8 * part]
            befores.append(
                jnp.where(line > 0, pltpu.roll(full[8 * part : 8 * part + 8], 1, 0), last)
            )
        before = jnp.concatenate(befores, 0)
        root = lax.rsqrt(1.01 - decay * decay)
        scale = jnp.where(going == 0.0, 1.0, (1.01 - decay * decay) * root)
        through = grad * conv
        into_grad = through * scale
        conv_s[own, :] = grad * into * scale
        decay_grad = going * decay * (grad * before - through * into * decay * root)
        z_rate = decay_grad * slope * rate * (1.0 - rate)
        z_into = into_grad * into * (1.0 - into)
        low[own, 0:width] = z_rate.astype(LOW)
        low[own, width:] = z_into.astype(LOW)
        conv_l[own, :] = conv.astype(LOW)
        return (
            error,
            rate_sum + fold(z_rate),
            into_sum + fold(z_into),
            slope_sum + fold(decay_grad * rate),
        )

    zero = jnp.zeros((8, width), WIDE)
    _, rate_sum, into_sum, slope_sum = loop(
        count, 4, retreat, (after[...], zero, zero, zero)
    )
    conv_s[...] += nt(low[...], gates[...])
    gate_full = tn(conv_l[...], low[...])
    for half in (0, block):
        rows_of = slice(half, half + block)
        gate_w[rows_of, 0:block] = gate_full[rows_of, half : half + block]
        gate_w[rows_of, block:] = gate_full[rows_of, width + half : width + half + block]
    grown[0:RIM, :] = jnp.zeros((RIM, width), WIDE)
    grown[RIM + length :, :] = jnp.zeros((RIM, width), WIDE)

    def taps(index, carry):
        base = pl.multiple_of(index * STEP, STEP)
        window = u[pl.ds(base + 8, STEP + 8), :]
        flags = mask[pl.ds(base + RIM, STEP), :]
        error = conv_s[pl.ds(base, STEP), :] * flags[:, 4:5]
        grown[pl.ds(base + RIM, STEP), :] = error
        out = [carry[0] + fold(error), carry[1] + fold(error * window[8:])]
        for shift in (1, 2, 3):
            moved = window[8 - shift : 8 - shift + STEP]
            out.append(carry[1 + shift] + fold(flags[:, shift : shift + 1] * error * moved))
        return tuple(out)

    bias_sum, *tap_sums = loop(count, 4, taps, (zero,) * 5)

    def spread_back(index, total):
        base = pl.multiple_of(index * STEP, STEP)
        window = grown[pl.ds(base, STEP + 8), :]
        flags = mask[pl.ds(base, STEP + 8), :]
        value = vec[6:7, :] * window[0:STEP]
        for shift in (1, 2, 3):
            masked = flags[:, shift : shift + 1] * window
            value = value + vec[6 + shift : 7 + shift, :] * masked[shift : shift + STEP]
        rounded = value.astype(LOW)
        u_low[pl.ds(base, STEP), :] = rounded
        return total + fold(rounded.astype(WIDE))

    input_sum = loop(ext // STEP, 3, spread_back, zero)
    sums[...] = jnp.zeros_like(sums)
    slope_sum = slope_sum * vec[10:11, :]
    values = (y_sum[...], input_sum, *tap_sums, bias_sum, rate_sum, into_sum, slope_sum, decay_sum[...])
    for row, value in enumerate(values):
        sums[row : row + 1, :] = jnp.sum(value, axis=0, keepdims=True)
    wide[:, 0:128] = jnp.transpose(sums[...])
    spread(place, wide, keep, send, 0, group, rows, slice(3 * model + width, None), 128)
    wide[...] = tn(u_low[...], normed[...])
    spread(place, wide, keep, send, 0, group, rows, slice(0, model))
    spread(place, gate_w, keep, send, 0, group, rows, slice(3 * model, 3 * model + width))
    wide[...] = tn(y_grad[...], normed[RIM:, :])
    spread(place, wide, keep, send, 0, group, rows, slice(model, 2 * model))
    wide[...] = tn(mixed[...], mid_low[...])
    spread(place, wide, keep, send, 0, group, rows, slice(2 * model, 3 * model))
    normed_grad[...] += nn(u_low[...], u_weight[...])
    normed_grad[RIM:, :] += nn(y_grad[...], y_weight[...])


def mixer_back(
    place, state_grad, r, i, conv, h, f, u, y_grad, mixed, y_weight, u_weight, packed, vec, mask,
    state, after, normed, mid_low, y_sum, decay_sum, rows, width, begin, steps, so_far=(),
):
    length, total = state_grad.shape
    ext, model = normed.shape
    group, part = width // rows, rows // 4
    pair = lambda step, place: (step + begin) ^ place[0]
    whole = lambda array: pl.BlockSpec(array.shape, lambda step, place: (0,) * array.ndim)
    lane = lambda lines: pl.BlockSpec((lines, width), lambda step, place: (0, pair(step, place)))
    weight = pl.BlockSpec((width, model), lambda step, place: (pair(step, place), 0))
    units = packed.shape[0] * width // total
    lanes = 3 * model + width + 128
    piece = pl.BlockSpec((group, 1, 2, part, lanes), lambda step, place: (step + begin, 0, 0, 0, 0))
    shape = jax.ShapeDtypeStruct((total // rows, 1, 2, part, lanes), LOW)
    operands = [
        state_grad, r, i, conv, h, f, u, y_grad, mixed, y_weight, u_weight, packed, vec, mask,
        state, after, normed, mid_low, y_sum, decay_sum,
    ]
    kept = pl.BlockSpec(memory_space=pl.ANY)
    return pl.pallas_call(
        functools.partial(mixer_back_kernel, rows, not so_far),
        grid_spec=pltpu.PrefetchScalarGridSpec(
            num_scalar_prefetch=1,
            grid=(steps,),
            in_specs=[
                lane(length), lane(length), lane(length), lane(length), lane(length),
                lane(length), lane(ext), lane(length), lane(length), weight, weight,
                pl.BlockSpec(
                    (units, *packed.shape[1:]), lambda step, place: (pair(step, place), 0, 0)
                ),
                lane(vec.shape[0]), whole(mask), lane(1),
                lane(1), whole(normed), whole(mid_low), lane(8), lane(8),
            ]
            + ([kept, kept, whole(so_far[2])] if so_far else []),
            out_specs=[
                piece, piece, pl.BlockSpec((ext, model), lambda step, place: (0, 0)),
            ],
            scratch_shapes=[
                pltpu.VMEM((length, width), WIDE),
                pltpu.VMEM((length, 2 * width), LOW),
                pltpu.VMEM((length, width), LOW),
                pltpu.VMEM((ext + RIM, width), WIDE),
                pltpu.VMEM((ext, width), LOW),
                pltpu.VMEM((width, model), WIDE),
                pltpu.VMEM((width, width), WIDE),
                pltpu.VMEM((width, 2 * width), LOW),
                pltpu.VMEM((128, width), WIDE),
            ],
        ),
        out_shape=[shape, shape, jax.ShapeDtypeStruct((ext, model), WIDE)],
        input_output_aliases={len(operands) + 1 + k: k for k in range(2)} if so_far else {},
        compiler_params=params(),
        cost_estimate=cost(15 * steps),
        name="mixer_back",
    )(place, *operands, *so_far)


def wide_of(value):
    return value.astype(WIDE)


def pin_kernel(source, target):
    del source, target


class Clock:
    def __init__(self):
        self.time = jnp.zeros((8, 128), WIDE)

    def tick(self, values):
        values, self.time = lax.optimization_barrier((values, self.time))
        return values

    def pin(self):
        self.time = pl.pallas_call(
            pin_kernel,
            in_specs=[pl.BlockSpec(memory_space=pl.ANY)],
            out_specs=pl.BlockSpec(memory_space=pl.ANY),
            out_shape=jax.ShapeDtypeStruct(self.time.shape, WIDE),
            input_output_aliases={0: 0},
            cost_estimate=cost(5000),
            name="pin",
        )(self.time)


class Sums:
    def __init__(self, clock, stages, move=swapped, pin=False, start=True):
        self.clock = clock
        self.stages = stages
        self.move = move
        self.result = self.moving = None
        if start:
            self.begin(pin)

    def begin(self, pin=False):
        self.send(next(self.stages), pin)

    def send(self, transfers, pin):
        meanwhile = transfers.pop() if callable(transfers[-1]) else None
        values = self.clock.tick([transfer[0] for transfer in transfers])
        self.moving = [
            (transfer[3] if len(transfer) > 3 else self.move)(value, *transfer[1:3])
            for value, transfer in zip(values, transfers)
        ]
        if meanwhile:
            meanwhile()

    def step(self, pin=False):
        try:
            transfers = self.stages.send(self.clock.tick(self.moving))
        except StopIteration as end:
            self.result = end.value
        else:
            self.send(transfers, pin)

    def finish(self):
        while self.result is None:
            self.step()
        return self.result


def lockstep(clock, *groups):
    begun = [group for group in groups if group.moving is not None]
    arrived = clock.tick([group.moving for group in begun])
    transfers = []
    for group in groups:
        if group.moving is None:
            transfers.append(next(group.stages))
        else:
            transfers.append(group.stages.send(arrived[begun.index(group)]))
    values = clock.tick([[transfer[0] for transfer in one] for one in transfers])
    for group, one, own in zip(groups, transfers, values):
        group.moving = [group.move(value, *transfer[1:]) for value, transfer in zip(own, one)]


def halved(clock, keep, send):
    slots, matrices, _, part, lanes = keep.shape
    shape = (slots // 4, 2, 2, matrices, 2, part, lanes)
    keep = keep.reshape(shape)
    (came,) = yield [(send, "rows", 1)]
    came = came.reshape(shape)
    every = slice(None)
    near = {}

    def both(one, other, *where):
        return wide_of(one[where]) + wide_of(other[where])

    def meanwhile():
        one, other = clock.tick((keep, came))
        near["y"] = both(one, other, every, 0, every, every, 0)
        near["x"] = both(one, other, every, 1, 0)
        near.update(clock.tick(dict(near)))

    return (
        yield from owned(
            lambda place: near["y"][:, place],
            both(keep, came, every, 0, every, every, 1).astype(LOW),
            lambda place: near["x"][:, :, place],
            both(keep, came, every, 1, 1).astype(LOW),
            meanwhile,
        )
    )


def owned(near_y, far_y, near_x, far_x, meanwhile=None):
    from_y, from_x = yield [(far_y, "rows", 2), (far_x, "chan", 1)] + (
        [meanwhile] if meanwhile else []
    )
    rest = lambda place: wide_of(near_y(place)) + wide_of(from_y[:, place])
    also = lambda place: wide_of(near_x(place)) + wide_of(from_x[:, :, place])
    rest_came, also_came = yield [
        (rest(1).astype(LOW), "chan", 1),
        (also(1).astype(LOW), "rows", 2),
    ]
    rest, also = rest(0), also(0)
    parts = {}
    for index in range(rest.shape[0]):
        parts[2 * index] = rest[index] + wide_of(rest_came[index])
        parts[2 * index + 1] = also[index] + wide_of(also_came[index])
    came = yield [
        (value.astype(LOW), "chan", 2 * distance) for distance, value in parts.items() if distance
    ]
    total = parts[0]
    for value in came:
        total = total + wide_of(value)
    return total


def settled(total):
    total = total.astype(LOW)
    (came,) = yield [(total, "rows", 2)]
    pair = jnp.stack([total, came])
    (came,) = yield [(pair, "rows", 1)]
    return pair, came


def ordered(pair, came):
    four = jnp.stack([pair, came], 1)
    place = lax.axis_index("rows")
    four = jnp.where(place & 1, four[:, ::-1], four)
    four = jnp.where(place & 2, four[::-1], four)
    _, _, matrices, part, lanes = four.shape
    four = four.reshape(4, matrices, part, lanes).transpose(1, 0, 2, 3)
    return four.reshape(matrices, 4 * part, lanes).astype(WIDE)


def finish_rest_kernel(place, pair, came, into, gelu, out, gates, lines):
    part, model = pair.shape[2], into.shape[1]
    lanes = gates.shape[1]
    for quarter in range(4):
        turn = quarter ^ place[1]
        own, other = (ref[turn // 2, 0].astype(WIDE) for ref in (pair, came))
        value = jnp.where(turn % 2 == 0, own, other)
        rows = slice(quarter * part, quarter * part + part)
        into[rows, :] = value[:, 0:model]
        gelu[rows, :] = value[:, model : 2 * model]
        out[rows, :] = value[:, 2 * model : 3 * model]
        gates[rows, :] = value[:, 3 * model : 3 * model + lanes]
        lines[rows, :] = value[:, 3 * model + lanes :]


def finish_rest(place, pair, came, model, width):
    rows = 4 * pair.shape[2]
    vmem = pl.BlockSpec(memory_space=pltpu.VMEM)
    shape = lambda lanes: jax.ShapeDtypeStruct((rows, lanes), WIDE)
    return pl.pallas_call(
        finish_rest_kernel,
        grid_spec=pltpu.PrefetchScalarGridSpec(
            num_scalar_prefetch=1, grid=(1,), in_specs=[vmem] * 2, out_specs=[vmem] * 5
        ),
        out_shape=[shape(model)] * 3 + [shape(width), shape(128)],
        compiler_params=params(),
        cost_estimate=cost(3),
        name="finish_rest",
    )(place, pair, came)


def finish_kernel(place, pair, came, gate, up, down):
    def rows_of(matrix):
        parts = []
        for quarter in range(4):
            turn = quarter ^ place[1]
            own, other = (ref[turn // 2, matrix].astype(WIDE) for ref in (pair, came))
            parts.append(jnp.where(turn % 2 == 0, own, other))
        return jnp.concatenate(parts, 0)

    gate[...] = jnp.transpose(rows_of(0))
    up[...] = jnp.transpose(rows_of(1))
    down[...] = rows_of(2)


def finish(place, pair, came):
    _, _, part, model = pair.shape
    tall = jax.ShapeDtypeStruct((model, 4 * part), WIDE)
    vmem = pl.BlockSpec(memory_space=pltpu.VMEM)
    return pl.pallas_call(
        finish_kernel,
        grid_spec=pltpu.PrefetchScalarGridSpec(
            num_scalar_prefetch=1, grid=(1,), in_specs=[vmem] * 2, out_specs=[vmem] * 3
        ),
        out_shape=[tall, tall, jax.ShapeDtypeStruct((4 * part, model), WIDE)],
        compiler_params=params(),
        cost_estimate=cost(4),
        name="finish",
    )(place, pair, came)


def everywhere(value):
    for axis in ("rows", "chan"):
        bits = 1
        while bits < lax.axis_size(axis):
            (came,) = yield [(value, axis, bits)]
            value = value + came
            bits *= 2
    return value


def gathered(piece):
    parts = lax.axis_size("rows")
    share = piece.shape[0] // parts
    own = lax.dynamic_slice_in_dim(piece, lax.axis_index("rows") * share, share)
    full = lax.all_gather(own, ("chan", "rows"), axis=0, tiled=True)
    return full.reshape(lax.axis_size("chan"), piece.shape[0], piece.shape[1])


def pack_kernel(table, count, *refs):
    sources, outs, sems = refs[:count], refs[count:-1], refs[-1]
    copies = [
        pltpu.make_async_copy(
            sources[source].at[begin : begin + size],
            outs[out].at[at : at + size],
            sems.at[index],
        )
        for index, (out, at, source, begin, size) in enumerate(table)
    ]
    for copy in copies:
        copy.start()
    for copy in copies:
        copy.wait()


def pack(*lists):
    sources, table, shapes = [], [], []
    for out, pieces in enumerate(lists):
        at = 0
        for array, begin, size in pieces:
            known = [index for index, one in enumerate(sources) if one is array]
            if not known:
                known = [len(sources)]
                sources.append(array)
            table.append((out, at, known[0], begin, size))
            at += size
        shapes.append(jax.ShapeDtypeStruct((at, *pieces[0][0].shape[1:]), pieces[0][0].dtype))
    return pl.pallas_call(
        functools.partial(pack_kernel, table, len(sources)),
        in_specs=[pl.BlockSpec(memory_space=pl.ANY)] * len(sources),
        out_specs=[pl.BlockSpec(memory_space=pltpu.VMEM)] * len(shapes),
        scratch_shapes=[pltpu.SemaphoreType.DMA((len(table),))],
        out_shape=shapes,
        compiler_params=params(),
        cost_estimate=cost(0.01),
        name="pack",
    )(*sources)


def spread_units(units):
    pairs = range(2, lax.axis_size("chan") // 2)
    count = len(pairs)
    behind, *came = yield [(units[:2], "chan", 2)] + [
        (units[:1], "chan", 2 * pair) for pair in pairs
    ]
    singles = [(value, 0, 1) for value in came]
    (turned,) = pack([(units, 0, 1), (behind, 0, 2), *singles])
    (corners,) = yield [(turned, "chan", 1)]
    near, away = pack(
        [(behind, 0, 2), (corners, 1, 2)], [(corners, 0, 1), *singles, (corners, 3, count)]
    )
    over, near_too = yield [(away, "rows", 2), (near, "rows", 1)]
    size = 2 * count + 1
    (away,) = pack([(away, 0, size), (over, 0, size)])
    (away_too,) = yield [(away, "rows", 1)]
    return units, near, near_too, away, away_too


def unit_source(pair, side, turn, count):
    upper, other = turn // 2, turn % 2
    if pair == 0 and side == 0:
        return 0, 2 * other + upper
    if pair == 1:
        return 1 + other, 2 * side + upper
    if pair == 0:
        return 3 + other, upper * (2 * count + 1)
    return 3 + other, upper * (2 * count + 1) + 1 + side * count + pair - 2


def assemble_kernel(cuts, pairs, place, *refs):
    sources, outs, sems = refs[:5], refs[5:-1], refs[-1]
    copies = []
    for pair in range(pairs):
        for side in range(2):
            for turn in range(4):
                array, index = unit_source(pair, side, turn, pairs - 2)
                unit = ((2 * pair + side) ^ place[0]) * 4 + (turn ^ place[1])
                for (begin, end), out in zip(cuts, outs):
                    copies.append(
                        pltpu.make_async_copy(
                            sources[array].at[index, begin:end],
                            out.at[unit],
                            sems.at[len(copies)],
                        )
                    )
    for copy in copies:
        copy.start()
    for copy in copies:
        copy.wait()


def assembled(place, sources, cuts):
    pairs = lax.axis_size("chan") // 2
    model = sources[0].shape[2]
    anywhere = pl.BlockSpec(memory_space=pl.ANY)
    return pl.pallas_call(
        functools.partial(assemble_kernel, cuts, pairs),
        grid_spec=pltpu.PrefetchScalarGridSpec(
            num_scalar_prefetch=1,
            grid=(1,),
            in_specs=[anywhere] * 5,
            out_specs=[pl.BlockSpec(memory_space=pltpu.VMEM)] * len(cuts),
            scratch_shapes=[pltpu.SemaphoreType.DMA((8 * pairs * len(cuts),))],
        ),
        out_shape=[
            jax.ShapeDtypeStruct((8 * pairs, end - begin, model), LOW) for begin, end in cuts
        ],
        compiler_params=params(),
        cost_estimate=cost(5),
        name="assemble",
    )(place, *sources)


def local(
    tokens, segments, gelu_weight, gelu_bias, input_weight, input_bias, conv_taps, conv_bias,
    decay_gate, decay_bias, input_gate, ingate_bias, decay_param, out_weight, mixer_gain,
    gate_weight, up_weight, down_weight, feed_gain, cotangent,
):
    length, model = tokens.shape
    rim = conv_taps.shape[0] - 1
    chans = lax.axis_size("chan")
    me, row_place = lax.axis_index("chan"), lax.axis_index("rows")
    rows, block = decay_gate.shape
    total = rows * chans
    width = 2 * block
    group = width // rows

    padded = jnp.concatenate([jnp.full((rim,), -1, jnp.int32), segments])
    window = lax.dynamic_slice_in_dim(padded, me * length, length + rim)
    own = window[rim:]
    same = [own == window[rim - shift : rim - shift + length] for shift in range(1, rim + 1)]
    mask = jnp.stack([same[0], *same, own != 0] + [same[0]] * (7 - rim - 1), 1).astype(WIDE)
    mask = jnp.pad(mask, ((RIM, RIM), (0, 0)))

    small = jnp.concatenate(
        [
            jnp.stack([gelu_bias, input_bias, conv_bias, decay_bias, ingate_bias, decay_param]),
            conv_taps,
        ]
    )
    unit_rows = block // 4
    count = rows // unit_rows
    lines = unit_rows // 2
    place = jnp.stack([me, row_place]).astype(jnp.int32)
    clock = Clock()

    part = gate_weight.shape[1] // 4
    own_columns = lambda weight: lax.dynamic_slice_in_dim(weight, row_place * part, part, 1).T
    own_unit = jnp.stack(
        [
            own_columns(gate_weight),
            own_columns(up_weight),
            lax.dynamic_slice_in_dim(down_weight, row_place * part, part),
        ]
    )
    both = jnp.concatenate([decay_gate, input_gate], 1)
    both = jnp.pad(both, ((0, 0), (0, model // 2 - 2 * block)))
    both = both.reshape(count, 2, lines, model // 2).swapaxes(1, 2).reshape(count, lines, model)
    flat = small.reshape(small.shape[0], count, unit_rows).swapaxes(0, 1).reshape(count, 1, -1)
    flat = jnp.pad(flat, ((0, 0), (0, lines // 3 - 1), (0, model - flat.shape[2])))
    by_unit = lambda weight: weight.reshape(count, unit_rows, model)
    first = jnp.concatenate([by_unit(input_weight.T), both, flat], 1)
    second = jnp.concatenate([by_unit(gelu_weight.T), by_unit(out_weight)], 1)
    first_cuts = ((0, unit_rows), (unit_rows, first.shape[1]))
    second_cuts = ((0, unit_rows), (unit_rows, 2 * unit_rows))
    cot_low = cotangent.astype(LOW)
    rim_tokens = moved_by(tokens[length - rim :], "chan", 1)
    extended = jnp.concatenate([jnp.zeros((RIM - rim, model), WIDE), rim_tokens, tokens])
    if count == 4:
        quarters = lambda units: jnp.stack(
            [
                lax.dynamic_index_in_dim(units, row_place ^ bits, keepdims=False)
                for bits in (0, 2, 1, 3)
            ]
        )
        own_unit = clock.tick(own_unit)
        first = Sums(clock, spread_units(quarters(first)), pin=True)
        second = Sums(clock, spread_units(quarters(second)), start=False)
        lockstep(clock, first, second)
        normed = clock.tick(rms_norm(clock.tick(extended), mixer_gain).astype(LOW))
        lockstep(clock, first, second)
        lockstep(clock, first, second)
        first.step()
        u_weight, packed = clock.tick(assembled(place, first.result, first_cuts))
    else:
        cut = lambda units, cuts: [
            gathered(units.reshape(-1, model))[:, begin:end] for begin, end in cuts
        ]
        normed = rms_norm(extended, mixer_gain).astype(LOW)
        u_weight, packed = cut(first, first_cuts)
        y_weight, o_weight = cut(second, second_cuts)
        y_weight, o_weight = (w.reshape(total, model) for w in (y_weight, o_weight))
    feed_units = lax.all_gather(own_unit[None], ("chan", "rows"), axis=0, tiled=True)
    u_weight = u_weight.reshape(total, model)
    small_full = packed[:, lines, : small.shape[0] * unit_rows]
    small_full = small_full.reshape(-1, small.shape[0], unit_rows).swapaxes(0, 1)
    small_full = small_full.reshape(small.shape[0], total).astype(WIDE)
    param = small_full[5:6]
    line = lax.broadcasted_iota(jnp.int32, (16, total), 0)
    vec = jnp.pad(small_full, ((0, 6), (0, 0)))
    vec = jnp.where(line == 5, -8.0 * jax.nn.softplus(param), vec)
    vec = jnp.where(line == 10, -8.0 * jax.nn.sigmoid(param), vec)

    u, conv, rate, into, state, factor, decay_sum = clock.tick(
        mixer_forward(normed, u_weight, packed, vec, mask, width)
    )
    carry = Sums(
        clock, entering(jnp.concatenate([factor[-1:], state[-1:]]), "chan", 1), moved_by
    )
    if count == 4:
        second.step()
        carry.step()
        second.step()
        y_weight, o_weight = clock.tick(assembled(place, second.result, second_cuts))
        y_weight, o_weight = (w.reshape(total, model) for w in (y_weight, o_weight))
    active, slope = clock.tick(gelu_branch(normed, y_weight, vec, width))
    carry = clock.tick(carry.finish())
    cot_too = swapped(cot_low, "rows", 1)
    mixed, middle, normed2 = clock.tick(
        mixer_out(active, state, factor, carry, o_weight, tokens, feed_gain[None])
    )
    cot_too = clock.tick(cot_too)
    normed2_too = swapped(normed2, "rows", 1)
    feed_units = clock.tick(feed_units)
    block_output, normed2_grad, mine, send = clock.tick(
        feed(place, normed2, cot_low, middle, feed_units)
    )
    theirs = swapped(send, "rows", 1)

    mid_grad, mid_low, state_grad, y_grad, feed_gain_sum, back_sum, y_sum = clock.tick(
        middle_back(
            middle, normed2_grad, cotangent, feed_gain[None], o_weight, active, slope, state,
            factor, carry,
        )
    )
    after = Sums(
        clock,
        entering(
            jnp.concatenate([factor[-1:], jnp.sum(back_sum, 0, keepdims=True)]), "chan", -1
        ),
        moved_by,
    )
    theirs, normed2_too = clock.tick((theirs, normed2_too))
    operands = (mine, theirs, normed2, cot_low, normed2_too, cot_too)
    near_y, far_y = clock.tick(feed_grads(0, *operands))
    split = lambda value: value.reshape(-1, 2, *value.shape[1:])
    moving = [swapped(split(far_y), "rows", 2)]
    after.step()
    near_x, far_x = clock.tick(feed_grads(1, *operands))
    moving.append(swapped(far_x, "chan", 1))
    stages = owned(
        lambda place: split(near_y)[:, place], far_y, lambda place: near_x[:, :, place], far_x
    )
    next(stages)
    fed = Sums(clock, stages, start=False)
    fed.moving = moving
    after = clock.tick(after.finish())
    place = jnp.stack([me // group, me % group, row_place]).astype(jnp.int32)
    pairs = total // width
    back = lambda after, begin, steps, so_far: clock.tick(
        mixer_back(
            place, state_grad, rate, into, conv, state, factor, u, y_grad, mixed, y_weight, u_weight,
            packed, vec, mask, carry, after, normed, mid_low, y_sum, decay_sum, rows, width, begin, steps, so_far,
        )
    )
    so_far = back(after, 1, pairs - 1, ())
    fed.step()
    so_far = clock.tick(so_far)
    keep, send, normed_grad = back(after, 0, 1, so_far)
    fed.moving = clock.tick(fed.moving)
    rest = Sums(clock, halved(clock, keep, send))
    rim_grad = moved_by(clock.tick(normed_grad[RIM - rim : RIM]), "chan", -1)
    rim_grad = clock.tick(rim_grad)
    error = normed_grad[RIM:] + jnp.concatenate([jnp.zeros((length - rim, model), WIDE), rim_grad])
    scale = lax.rsqrt(jnp.mean(tokens * tokens, axis=-1, keepdims=True) + 1e-06)
    gained = mixer_gain * error
    mean = jnp.mean(gained * tokens, axis=-1, keepdims=True)
    tokens_grad = clock.tick(mid_grad + scale * gained - tokens * (scale * scale * scale * mean))
    mixer_gain_sum = jnp.sum(error * tokens * scale, 0)

    gains = Sums(clock, everywhere(jnp.stack([mixer_gain_sum, jnp.sum(feed_gain_sum, 0)])))
    gains.step()
    rest.step(pin=True)
    fed.step()
    gains.moving = clock.tick(gains.moving)
    rest.step(pin=True)
    rest.step(pin=True)
    fed.step()
    fed = Sums(clock, settled(fed.result))
    gains.step()
    fed.step()
    gains.step()
    rest.step()
    rest = Sums(clock, settled(rest.result))
    gains.step()
    fed.step()
    feed_sum = clock.tick(finish(jnp.stack([me, row_place]).astype(jnp.int32), *fed.result))
    rest.step()
    gains = gains.finish()
    pair, came = rest.finish()
    gains = gains + clock.time[:1, :1]
    if pair.shape[2] % 8:
        whole = ordered(pair, came)[0]
        input_sum, gelu_sum, out_sum = (whole[:, k * model : (k + 1) * model] for k in range(3))
        gates_sum, lines = whole[:, 3 * model : 3 * model + width], whole[:, 3 * model + width :]
    else:
        input_sum, gelu_sum, out_sum, gates_sum, lines = finish_rest(
            jnp.stack([me, row_place]).astype(jnp.int32), pair, came, model, width
        )
    lines = lines[:, :11].T
    mean_decay = lines[10] / (length * lax.axis_size("rows") * chans)
    return (
        block_output,
        tokens_grad,
        gelu_sum.T,
        lines[0],
        input_sum.T,
        lines[1],
        lines[2:6],
        lines[6],
        gates_sum[:, :block],
        lines[7],
        gates_sum[:, block:],
        lines[8],
        lines[9],
        out_sum,
        gains[0],
        feed_sum[0],
        feed_sum[1],
        feed_sum[2],
        gains[1],
        mean_decay,
    )


def solution(mesh):
    return jax.shard_map(
        local,
        mesh=mesh,
        in_specs=(
            P(("rows", "chan"), None),
            P("rows"),
            P(None, "chan"),
            P("chan"),
            P(None, "chan"),
            P("chan"),
            P(None, "chan"),
            P("chan"),
            P("chan", None),
            P("chan"),
            P("chan", None),
            P("chan"),
            P("chan"),
            P("chan", None),
            P(),
            P(None, "chan"),
            P(None, "chan"),
            P("chan", None),
            P(),
            P(("rows", "chan"), None),
        ),
        out_specs=(
            P(("rows", "chan"), None),
            P(("rows", "chan"), None),
            P(None, "chan"),
            P("chan"),
            P(None, "chan"),
            P("chan"),
            P(None, "chan"),
            P("chan"),
            P("chan", None),
            P("chan"),
            P("chan", None),
            P("chan"),
            P("chan"),
            P("chan", None),
            P(),
            P(None, "chan"),
            P(None, "chan"),
            P("chan", None),
            P(),
            P("chan"),
        ),
        check_vma=False,
    )
```

```python
import functools

import jax
import jax.numpy as jnp
from jax import lax
from jax.experimental import pallas as pl
from jax.experimental.pallas import tpu as pltpu
from jax.sharding import PartitionSpec as P

LOW = jnp.bfloat16
WIDE = jnp.float32
RIM = 16
STEP = 16
VMEM_BYTES = 56 * 1024 * 1024
GELU_SLOPE = 0.7978845608028654
GELU_CUBE = 0.044715


def params(**more):
    return pltpu.CompilerParams(vmem_limit_bytes=VMEM_BYTES, **more)


def moved_by(value, axis, steps):
    count = lax.axis_size(axis)
    leading, last = (max(0, -steps), min(count, count - steps))
    return lax.ppermute(value, axis, [(source, source + steps) for source in range(leading, last)])


def swapped(value, axis, bits):
    count = lax.axis_size(axis)
    return lax.ppermute(value, axis, [(source, source ^ bits) for source in range(count)])


def join(earlier, later):
    return jnp.concatenate(
        [earlier[0:1] * later[0:1], later[0:1] * earlier[1:2] + later[1:2]], 0
    )


def entering(value, axis, sign):
    count = lax.axis_size(axis)
    if count in (4, 8):
        (partner,) = yield [(value, axis, 1, swapped)]
        later = (lax.axis_index(axis) & 1) == (1 if sign > 0 else 0)
        both = join(jnp.where(later, partner, value), jnp.where(later, value, partner))
        came = yield [(both, axis, 2 * sign * reach) for reach in range(1, count // 2)]
        total = came[-1]
        for one in came[-2::-1]:
            total = join(total, one)
        return jnp.where(later, join(total, partner)[1:2], total[1:2])
    total = value
    came = yield [(value, axis, sign * reach) for reach in (1, 2, 3) if reach < count]
    for one in came:
        total = join(one, total)
    reach = 4
    while 2 * reach < count:
        (one,) = yield [(total, axis, sign * reach)]
        total = join(one, total)
        reach *= 2
    came = yield [(total, axis, sign * far) for far in (1, reach + 1) if far < count]
    last = came[0]
    for one in came[1:]:
        last = join(one, last)
    return last[1:2]


def rms_norm(values, gain):
    return values * lax.rsqrt(jnp.mean(values * values, axis=-1, keepdims=True) + 1e-06) * gain


def nt(left, right):
    return lax.dot_general(left, right, (((1,), (1,)), ((), ())), preferred_element_type=WIDE)


def tn(left, right):
    return lax.dot_general(left, right, (((0,), (0,)), ((), ())), preferred_element_type=WIDE)


def nn(left, right):
    return lax.dot_general(left, right, (((1,), (0,)), ((), ())), preferred_element_type=WIDE)


def sigmoid(value):
    return 0.5 * jnp.tanh(0.5 * value) + 0.5


def gelu_parts(value):
    square = value * value
    bend = jnp.tanh(GELU_SLOPE * value * (1.0 + GELU_CUBE * square))
    half = 0.5 + 0.5 * bend
    slope = half + 0.5 * GELU_SLOPE * value * (1.0 - bend * bend) * (1.0 + 3.0 * GELU_CUBE * square)
    return value * half, slope


def loop(count, unroll, body, init):
    while count % unroll:
        unroll -= 1

    def several(index, carry):
        for turn in range(unroll):
            carry = body(index * unroll + turn, carry)
        return carry

    return lax.fori_loop(0, count // unroll, several, init)


def cost(microseconds):
    return pl.CostEstimate(
        flops=int(microseconds * 1.1e7), bytes_accessed=int(microseconds * 3.5e4), transcendentals=0
    )


def fold(value):
    total = value[0:8]
    for group in range(1, value.shape[0] // 8):
        total = total + value[8 * group : 8 * group + 8]
    return total


def fill_gates(packed, gates, block):
    width = 2 * block
    lines = packed.shape[1] * 3 // 4

    @pl.when(pl.program_id(0) == 0)
    def _():
        gates[...] = jnp.zeros_like(gates)

    parts = []
    for unit in range(packed.shape[0]):
        value = packed[unit].astype(WIDE)[:lines]
        parts += [value[:, 0:width], value[:, 512 : 512 + width]]
    parts = jnp.concatenate(parts, 0).astype(LOW)
    for half in (0, block):
        gates[half : half + block, half : half + block] = parts[half : half + block, 0:block]
        gates[half : half + block, width + half : width + half + block] = parts[
            half : half + block, block:
        ]


def mixer_forward_kernel(
    normed, u_weight, packed, vec, mask, u_out, conv_out, r_out, i_out, h_out, f_out, sum_out,
    low, zed, gates,
):
    ext = normed.shape[0]
    width = u_out.shape[1]
    fill_gates(packed, gates, width // 2)
    count = (ext - RIM) // STEP
    u_out[...] = nt(normed[...], u_weight[...]) + vec[1:2, :]

    def convolve(index, _):
        base = pl.multiple_of(index * STEP, STEP)
        own = pl.ds(base, STEP)
        window = u_out[pl.ds(base + 8, STEP + 8), :]
        flags = mask[pl.ds(base + RIM, STEP), :]
        conv = vec[2:3, :] + vec[6:7, :] * window[8:]
        for shift in (1, 2, 3):
            conv = conv + flags[:, shift : shift + 1] * (
                vec[6 + shift : 7 + shift, :] * window[8 - shift : 8 - shift + STEP]
            )
        conv = conv * flags[:, 4:5]
        conv_out[own, :] = conv
        low[own, :] = conv.astype(LOW)
        return 0

    loop(count, 4, convolve, 0)
    zed[...] = nn(low[...], gates[...])
    line = lax.broadcasted_iota(jnp.int32, (8, width), 0)

    def advance(index, carry):
        state, factor, total = carry
        own = pl.ds(pl.multiple_of(index * STEP, STEP), STEP)
        going = mask[pl.ds(pl.multiple_of(index * STEP + RIM, STEP), STEP), :][:, 0:1]
        rate = sigmoid(zed[own, 0:width] + vec[3:4, :])
        into = sigmoid(zed[own, width:] + vec[4:5, :])
        decay = jnp.exp(vec[5:6, :] * rate)
        r_out[own, :] = rate
        i_out[own, :] = into
        scale = jnp.where(going == 0.0, 1.0, jnp.sqrt(1.01 - decay * decay))
        inject = conv_out[own, :] * into * scale
        carried = decay * going
        total = total + fold(decay)
        for group in range(STEP // 8):
            part = slice(8 * group, 8 * group + 8)
            mul, add = carried[part], inject[part]
            for reach in (1, 2, 4):
                inside = line >= reach
                add = add + mul * jnp.where(inside, pltpu.roll(add, reach, 0), 0.0)
                mul = mul * jnp.where(inside, pltpu.roll(mul, reach, 0), 1.0)
            here = add + mul * state
            gone = mul * factor
            rows = pl.ds(pl.multiple_of(index * STEP + 8 * group, 8), 8)
            h_out[rows, :] = here
            f_out[rows, :] = gone
            state, factor = here[7:8], gone[7:8]
        return state, factor, total

    zero = jnp.zeros((1, width), WIDE)
    _, _, total = loop(
        count, 4, advance, (zero, zero + 1.0, jnp.zeros((8, width), WIDE))
    )
    sum_out[...] = total


def mixer_forward(normed, u_weight, packed, vec, mask, width):
    ext, model = normed.shape
    tokens = ext - RIM
    total = u_weight.shape[0]
    pairs = total // width
    units = packed.shape[0] // pairs
    by_lane = lambda length: pl.BlockSpec((length, width), lambda step: (0, step))
    whole = lambda array: pl.BlockSpec(array.shape, lambda step: (0,) * array.ndim)
    flat = jax.ShapeDtypeStruct((tokens, total), WIDE)
    return pl.pallas_call(
        mixer_forward_kernel,
        grid=(pairs,),
        in_specs=[
            whole(normed),
            pl.BlockSpec((width, model), lambda step: (step, 0)),
            pl.BlockSpec((units, *packed.shape[1:]), lambda step: (step, 0, 0)),
            by_lane(vec.shape[0]),
            whole(mask),
        ],
        out_specs=[by_lane(ext)] + [by_lane(tokens)] * 5 + [by_lane(8)],
        out_shape=[jax.ShapeDtypeStruct((ext, total), WIDE)] + [flat] * 5
        + [jax.ShapeDtypeStruct((8, total), WIDE)],
        scratch_shapes=[
            pltpu.VMEM((tokens, width), LOW),
            pltpu.VMEM((tokens, 2 * width), WIDE),
            pltpu.VMEM((width, 2 * width), LOW),
        ],
        compiler_params=params(),
        cost_estimate=cost(26),
        name="mixer_forward",
    )(normed, u_weight, packed, vec, mask)


def gelu_branch_kernel(normed, weight, vec, active_out, slope_out, held):
    held[...] = nt(normed[RIM:, :], weight[...]) + vec[0:1, :]

    def act(index, _):
        own = pl.ds(pl.multiple_of(index * STEP, STEP), STEP)
        active_out[own, :], slope_out[own, :] = gelu_parts(held[own, :])
        return 0

    loop(held.shape[0] // STEP, 4, act, 0)


def gelu_branch(normed, weight, vec, width):
    length, total = normed.shape[0] - RIM, weight.shape[0]
    model = normed.shape[1]
    lane = lambda lines: pl.BlockSpec((lines, width), lambda step: (0, step))
    return pl.pallas_call(
        gelu_branch_kernel,
        grid=(total // width,),
        in_specs=[
            pl.BlockSpec(normed.shape, lambda step: (0, 0)),
            pl.BlockSpec((width, model), lambda step: (step, 0)),
            lane(vec.shape[0]),
        ],
        out_specs=[lane(length), lane(length)],
        out_shape=[jax.ShapeDtypeStruct((length, total), WIDE)] * 2,
        scratch_shapes=[pltpu.VMEM((length, width), WIDE)],
        compiler_params=params(),
        cost_estimate=cost(8),
        name="gelu_branch",
    )(normed, weight, vec)


def mixer_out_kernel(active, h, f, state, weight, tokens, gain, mixed, middle, normed):
    def gate(index, _):
        own = pl.ds(pl.multiple_of(index * STEP, STEP), STEP)
        mixed[own, :] = ((h[own, :] + f[own, :] * state[...]) * active[own, :]).astype(LOW)
        return 0

    loop(active.shape[0] // STEP, 4, gate, 0)
    total = tokens[...] + nn(mixed[...], weight[...])
    middle[...] = total
    scale = lax.rsqrt(jnp.mean(total * total, axis=-1, keepdims=True) + 1e-06)
    normed[...] = (total * scale * gain[...]).astype(LOW)


def mixer_out(active, h, f, state, weight, tokens, gain):
    length, model = tokens.shape
    total = active.shape[1]
    tile = 256 if length % 256 == 0 else length
    row = lambda lanes: pl.BlockSpec((tile, lanes), lambda step: (step, 0))
    one = lambda array: pl.BlockSpec(array.shape, lambda step: (0, 0))
    return pl.pallas_call(
        mixer_out_kernel,
        grid=(length // tile,),
        in_specs=[
            row(total), row(total), row(total), one(state), one(weight), row(model), one(gain),
        ],
        out_specs=[row(total), row(model), row(model)],
        out_shape=[
            jax.ShapeDtypeStruct((length, total), LOW),
            jax.ShapeDtypeStruct((length, model), WIDE),
            jax.ShapeDtypeStruct((length, model), LOW),
        ],
        compiler_params=params(),
        cost_estimate=cost(9),
        name="mixer_out",
    )(active, h, f, state, weight, tokens, gain)


def spread(place, wide, keep, send, matrix, group, rows, lanes=slice(None), count=None):
    part = rows // 4
    if part % 8:
        value = wide[:, 0:count]
        pieces = [value[begin : begin + part] for begin in range(0, group * rows, part)]
        mine = place[1] * 4 + place[2]
        bit = 1
        while bit < len(pieces):
            turned = (mine & bit) != 0
            pieces = [
                jnp.where(turned, pieces[index ^ bit], pieces[index])
                for index in range(len(pieces))
            ]
            bit *= 2
    for slot in range(group):
        shard = slot ^ place[1]
        for turn in range(4):
            if part % 8:
                value = pieces[4 * slot + turn]
            else:
                begin = pl.multiple_of(shard * rows + (turn ^ place[2]) * part, 8)
                value = wide[pl.ds(begin, part), 0:count]
            (keep, send)[turn & 1][slot, matrix, turn >> 1, :, lanes] = value.astype(LOW)


def feed_kernel(
    group, place, normed, cot, out_in, units, out, grad, keep, send, gate_s, up_s, back_s, hidden_l,
    both_l, held, sems, turned, cot_turned,
):
    model = normed.shape[1]
    width = gate_s.shape[0]
    rows = width // group
    part, half = rows // 4, rows // 2
    step = pl.program_id(0)

    def copies(index):
        for member in range(group):
            for turn in range(4):
                unit = (place[0] ^ (group * index + member)) * 4 + (place[1] ^ turn)
                order = 4 * member + (turn % 2) * 2 + turn // 2
                slot = index % 2
                yield pltpu.make_async_copy(
                    units.at[unit], held.at[slot, :, order], sems.at[slot, 4 * member + turn]
                )

    @pl.when(step == 0)
    def _():
        for copy in copies(0):
            copy.start()
        out[...] = out_in[...]
        grad[...] = jnp.zeros_like(grad)
        turned[...] = jnp.transpose(normed[...])
        cot_turned[...] = jnp.transpose(cot[...])

    @pl.when(step + 1 < pl.num_programs(0))
    def _():
        for copy in copies(step + 1):
            copy.start()

    for copy in copies(step):
        copy.wait()

    def weight(begin, end):
        if part % 16 == 0:
            return held[step % 2, begin:end].reshape((end - begin) * width, model)
        pieces = [
            held[step % 2, matrix, order].astype(WIDE)
            for matrix in range(begin, end)
            for order in range(4 * group)
        ]
        return jnp.concatenate(pieces, 0).astype(LOW)

    first, third = weight(0, 2), weight(2, 3)
    gate_s[...] = nn(first[:width], turned[...])
    up_s[...] = nn(first[width:], turned[...])
    back_s[...] = nn(third, cot_turned[...])

    def act(index, _):
        base = pl.multiple_of(index * STEP, STEP)
        own = pl.ds(base, STEP)
        up, back = up_s[own, :], back_s[own, :]
        value, slope = gelu_parts(gate_s[own, :])
        hidden_l[own, :] = (value * up).astype(LOW)
        both_l[own, :] = (back * up * slope).astype(LOW)
        both_l[pl.ds(base + width, STEP), :] = (back * value).astype(LOW)
        return 0

    loop(width // STEP, 4, act, 0)
    out[...] += tn(hidden_l[...], third)
    grad[...] += tn(both_l[...], first)
    for member in range(group):
        for matrix, (value, offset) in enumerate(((both_l, 0), (both_l, width), (hidden_l, 0))):
            begin = offset + member * rows
            keep[member, matrix] = value[begin : begin + half, :]
            send[member, matrix] = value[begin + half : begin + rows, :]


def feed(place, normed, cot, out_in, units):
    length, model = normed.shape
    part = units.shape[2]
    slots = units.shape[0] // 4
    group = 2
    width = 4 * part * group
    whole = lambda array: pl.BlockSpec(array.shape, lambda step, place: (0,) * array.ndim)
    piece = pl.BlockSpec((group, 3, 2 * part, length), lambda step, place: (step, 0, 0, 0))
    wide = jax.ShapeDtypeStruct((length, model), WIDE)
    grads = jax.ShapeDtypeStruct((slots, 3, 2 * part, length), LOW)
    return pl.pallas_call(
        functools.partial(feed_kernel, group),
        grid_spec=pltpu.PrefetchScalarGridSpec(
            num_scalar_prefetch=1,
            grid=(slots // group,),
            in_specs=[
                whole(normed), whole(cot), whole(out_in), pl.BlockSpec(memory_space=pl.ANY),
            ],
            out_specs=[whole(out_in), whole(out_in), piece, piece],
            scratch_shapes=[pltpu.VMEM((width, length), WIDE)] * 3
            + [pltpu.VMEM((width, length), LOW), pltpu.VMEM((2 * width, length), LOW)]
            + [pltpu.VMEM((2, 3, 4 * group, part, model), LOW)]
            + [pltpu.SemaphoreType.DMA((2, 4 * group))]
            + [pltpu.VMEM((model, length), LOW)] * 2,
        ),
        out_shape=[wide, wide, grads, grads],
        compiler_params=params(),
        cost_estimate=cost(34),
        name="feed",
    )(place, normed, cot, out_in, units)


def feed_grads_kernel(parity, count, mine, theirs, normed, cot, normed_too, cot_too, near, far):
    part = mine.shape[2] // 2
    step = pl.program_id(0)
    for matrix in range(3):
        right, right_too = (cot, cot_too) if matrix == 2 else (normed, normed_too)
        value = nn(mine[0, matrix], right[...]) + nn(theirs[0, matrix], right_too[...])
        value = value.astype(LOW)
        if parity == 0:
            near[0, matrix] = value[:part]
            far[0, matrix] = value[part:]
            continue
        for place, out in ((0, near), (count // 2, far)):

            @pl.when((step >= place) & (step < place + count // 2))
            def _():
                out[0, matrix, 0] = value[:part]
                out[0, matrix, 1] = value[part:]


def feed_grads(parity, mine, theirs, normed, cot, normed_too, cot_too):
    slots, _, rows, length = mine.shape
    model = normed.shape[1]
    count, part = slots // 2, rows // 2
    whole = lambda array: pl.BlockSpec(array.shape, lambda step: (0,) * array.ndim)

    def source(step):
        if parity == 0:
            return 4 * (step // 2) + step % 2, 0, 0, 0
        last = (step >= count // 2).astype(jnp.int32)
        return 4 * (step - last * (count // 2)) + 2 + last, 0, 0, 0

    if parity == 0:
        specs = [pl.BlockSpec((1, 3, part, model), lambda step: (step, 0, 0, 0))] * 2
        shape = jax.ShapeDtypeStruct((count, 3, part, model), LOW)
    else:
        clipped = lambda first: lambda step: (jnp.clip(step - first, 0, count // 2 - 1), 0, 0, 0, 0)
        specs = [
            pl.BlockSpec((1, 3, 2, part, model), clipped(first)) for first in (0, count // 2)
        ]
        shape = jax.ShapeDtypeStruct((count // 2, 3, 2, part, model), LOW)
    return pl.pallas_call(
        functools.partial(feed_grads_kernel, parity, count),
        grid=(count,),
        in_specs=[pl.BlockSpec((1, 3, rows, length), source)] * 2 + [whole(normed)] * 4,
        out_specs=specs,
        out_shape=[shape, shape],
        compiler_params=params(),
        cost_estimate=cost(2000),
        name="feed_grads",
    )(mine, theirs, normed, cot, normed_too, cot_too)


def middle_back_kernel(
    middle, grad, cot, gain, weight, active_in, slope_in, h, f, state, mid_grad, mid_low, state_grad, y_grad,
    gain_sum, back_sum, bias_sum, mixed_s,
):
    @pl.when(pl.program_id(0) == 0)
    def _():
        gain_sum[...] = jnp.zeros_like(gain_sum)
        back_sum[...] = jnp.zeros_like(back_sum)
        bias_sum[...] = jnp.zeros_like(bias_sum)

    value, error = middle[...], grad[...]
    scale = lax.rsqrt(jnp.mean(value * value, axis=-1, keepdims=True) + 1e-06)
    gained = gain[...] * error
    mean = jnp.mean(gained * value, axis=-1, keepdims=True)
    total = cot[...] + scale * gained - value * (scale * scale * scale * mean)
    gain_sum[...] += fold(error * value * scale)
    mid_grad[...] = total
    mid_low[...] = total.astype(LOW)
    mixed_s[...] = nt(mid_low[...], weight[...])

    def turn(index, carry):
        back, bias = carry
        own = pl.ds(pl.multiple_of(index * STEP, STEP), STEP)
        error = mixed_s[own, :]
        active, slope = active_in[own, :], slope_in[own, :]
        gone = f[own, :]
        full = h[own, :] + gone * state[...]
        here = error * active
        state_grad[own, :] = here
        low = (error * full * slope).astype(LOW)
        y_grad[own, :] = low
        return back + fold(here * gone), bias + fold(low.astype(WIDE))

    zero = jnp.zeros(back_sum.shape, WIDE)
    back, bias = loop(middle.shape[0] // STEP, 4, turn, (zero, zero))
    back_sum[...] += back
    bias_sum[...] += bias


def middle_back(middle, grad, cot, gain, weight, active, slope, h, f, state):
    length, model = middle.shape
    total = active.shape[1]
    tile = 256 if length % 256 == 0 else length
    row = lambda lanes: pl.BlockSpec((tile, lanes), lambda step: (step, 0))
    one = lambda lines, lanes: pl.BlockSpec((lines, lanes), lambda step: (0, 0))
    return pl.pallas_call(
        middle_back_kernel,
        grid=(length // tile,),
        in_specs=[
            row(model), row(model), row(model), one(1, model),
            one(total, model), row(total), row(total), row(total), row(total), one(1, total),
        ],
        out_specs=[
            row(model), row(model), row(total), row(total), one(8, model), one(8, total),
            one(8, total),
        ],
        out_shape=[
            jax.ShapeDtypeStruct((length, model), WIDE),
            jax.ShapeDtypeStruct((length, model), LOW),
            jax.ShapeDtypeStruct((length, total), WIDE),
            jax.ShapeDtypeStruct((length, total), LOW),
            jax.ShapeDtypeStruct((8, model), WIDE),
            jax.ShapeDtypeStruct((8, total), WIDE),
            jax.ShapeDtypeStruct((8, total), WIDE),
        ],
        scratch_shapes=[pltpu.VMEM((tile, total), WIDE)],
        compiler_params=params(),
        cost_estimate=cost(13),
        name="middle_back",
    )(middle, grad, cot, gain, weight, active, slope, h, f, state)


def mixer_back_kernel(
    rows, first, place, state_grad, r_in, i_in, conv_in, h, f, u, y_grad, mixed, y_weight, u_weight,
    packed, vec, mask, state, after, normed, mid_low, y_sum, decay_sum, *refs
):
    if not first:
        grad_in, refs = refs[2], refs[3:]
    (
        keep, send, normed_grad, conv_s, low, conv_l, grown, u_low, wide, gate_w, gates, sums,
    ) = refs
    length, width = state_grad.shape
    ext, model = normed.shape
    group = width // rows
    block = width // 2
    count = length // STEP
    line = lax.broadcasted_iota(jnp.int32, (8, width), 0)

    fill_gates(packed, gates, block)

    @pl.when(pl.program_id(0) == 0)
    def _():
        if first:
            normed_grad[...] = jnp.zeros_like(normed_grad)
        else:
            normed_grad[...] = grad_in[...]

    def retreat(index, carry):
        error, rate_sum, into_sum, slope_sum = carry
        base = pl.multiple_of((count - 1 - index) * STEP, STEP)
        own = pl.ds(base, STEP)
        going = mask[pl.ds(base + RIM, STEP), :][:, 0:1]
        rate, into, conv = r_in[own, :], i_in[own, :], conv_in[own, :]
        slope = vec[5:6, :]
        decay = jnp.exp(slope * rate)
        carried = decay * going
        given = state_grad[own, :]
        full = h[own, :] + f[own, :] * state[...]
        ahead = pl.ds(pl.multiple_of(jnp.maximum(base - 8, 0), 8), 8)
        edge = h[ahead, :][7:8] + f[ahead, :][7:8] * state[...]
        edge = jnp.where(base == 0, state[...], edge)
        parts = []
        for part in reversed(range(STEP // 8)):
            place_of = slice(8 * part, 8 * part + 8)
            mul = carried[place_of]
            add = mul * given[place_of]
            for reach in (1, 2, 4):
                inside = line < 8 - reach
                add = add + mul * jnp.where(inside, pltpu.roll(add, 8 - reach, 0), 0.0)
                mul = mul * jnp.where(inside, pltpu.roll(mul, 8 - reach, 0), 1.0)
            here = add + mul * error
            parts.append(given[place_of] + jnp.where(line < 7, pltpu.roll(here, 7, 0), error))
            error = here[0:1]
        grad = jnp.concatenate(parts[::-1], 0)
        befores = []
        for part in range(STEP // 8):
            last = edge if part == 0 else full[8 * part - 1 : 8 * part]
            befores.append(
                jnp.where(line > 0, pltpu.roll(full[8 * part : 8 * part + 8], 1, 0), last)
            )
        before = jnp.concatenate(befores, 0)
        root = lax.rsqrt(1.01 - decay * decay)
        scale = jnp.where(going == 0.0, 1.0, (1.01 - decay * decay) * root)
        through = grad * conv
        into_grad = through * scale
        conv_s[own, :] = grad * into * scale
        decay_grad = going * decay * (grad * before - through * into * decay * root)
        z_rate = decay_grad * slope * rate * (1.0 - rate)
        z_into = into_grad * into * (1.0 - into)
        low[own, 0:width] = z_rate.astype(LOW)
        low[own, width:] = z_into.astype(LOW)
        conv_l[own, :] = conv.astype(LOW)
        return (
            error,
            rate_sum + fold(z_rate),
            into_sum + fold(z_into),
            slope_sum + fold(decay_grad * rate),
        )

    zero = jnp.zeros((8, width), WIDE)
    _, rate_sum, into_sum, slope_sum = loop(
        count, 4, retreat, (after[...], zero, zero, zero)
    )
    conv_s[...] += nt(low[...], gates[...])
    gate_full = tn(conv_l[...], low[...])
    for half in (0, block):
        rows_of = slice(half, half + block)
        gate_w[rows_of, 0:block] = gate_full[rows_of, half : half + block]
        gate_w[rows_of, block:] = gate_full[rows_of, width + half : width + half + block]
    grown[0:RIM, :] = jnp.zeros((RIM, width), WIDE)
    grown[RIM + length :, :] = jnp.zeros((RIM, width), WIDE)

    def taps(index, carry):
        base = pl.multiple_of(index * STEP, STEP)
        window = u[pl.ds(base + 8, STEP + 8), :]
        flags = mask[pl.ds(base + RIM, STEP), :]
        error = conv_s[pl.ds(base, STEP), :] * flags[:, 4:5]
        grown[pl.ds(base + RIM, STEP), :] = error
        out = [carry[0] + fold(error), carry[1] + fold(error * window[8:])]
        for shift in (1, 2, 3):
            moved = window[8 - shift : 8 - shift + STEP]
            out.append(carry[1 + shift] + fold(flags[:, shift : shift + 1] * error * moved))
        return tuple(out)

    bias_sum, *tap_sums = loop(count, 4, taps, (zero,) * 5)

    def spread_back(index, total):
        base = pl.multiple_of(index * STEP, STEP)
        window = grown[pl.ds(base, STEP + 8), :]
        flags = mask[pl.ds(base, STEP + 8), :]
        value = vec[6:7, :] * window[0:STEP]
        for shift in (1, 2, 3):
            masked = flags[:, shift : shift + 1] * window
            value = value + vec[6 + shift : 7 + shift, :] * masked[shift : shift + STEP]
        rounded = value.astype(LOW)
        u_low[pl.ds(base, STEP), :] = rounded
        return total + fold(rounded.astype(WIDE))

    input_sum = loop(ext // STEP, 3, spread_back, zero)
    sums[...] = jnp.zeros_like(sums)
    slope_sum = slope_sum * vec[10:11, :]
    values = (y_sum[...], input_sum, *tap_sums, bias_sum, rate_sum, into_sum, slope_sum, decay_sum[...])
    for row, value in enumerate(values):
        sums[row : row + 1, :] = jnp.sum(value, axis=0, keepdims=True)
    wide[:, 0:128] = jnp.transpose(sums[...])
    spread(place, wide, keep, send, 0, group, rows, slice(3 * model + width, None), 128)
    wide[...] = tn(u_low[...], normed[...])
    spread(place, wide, keep, send, 0, group, rows, slice(0, model))
    spread(place, gate_w, keep, send, 0, group, rows, slice(3 * model, 3 * model + width))
    wide[...] = tn(y_grad[...], normed[RIM:, :])
    spread(place, wide, keep, send, 0, group, rows, slice(model, 2 * model))
    wide[...] = tn(mixed[...], mid_low[...])
    spread(place, wide, keep, send, 0, group, rows, slice(2 * model, 3 * model))
    normed_grad[...] += nn(u_low[...], u_weight[...])
    normed_grad[RIM:, :] += nn(y_grad[...], y_weight[...])


def mixer_back(
    place, state_grad, r, i, conv, h, f, u, y_grad, mixed, y_weight, u_weight, packed, vec, mask,
    state, after, normed, mid_low, y_sum, decay_sum, rows, width, begin, steps, so_far=(),
):
    length, total = state_grad.shape
    ext, model = normed.shape
    group, part = width // rows, rows // 4
    pair = lambda step, place: (step + begin) ^ place[0]
    whole = lambda array: pl.BlockSpec(array.shape, lambda step, place: (0,) * array.ndim)
    lane = lambda lines: pl.BlockSpec((lines, width), lambda step, place: (0, pair(step, place)))
    weight = pl.BlockSpec((width, model), lambda step, place: (pair(step, place), 0))
    units = packed.shape[0] * width // total
    lanes = 3 * model + width + 128
    piece = pl.BlockSpec((group, 1, 2, part, lanes), lambda step, place: (step + begin, 0, 0, 0, 0))
    shape = jax.ShapeDtypeStruct((total // rows, 1, 2, part, lanes), LOW)
    operands = [
        state_grad, r, i, conv, h, f, u, y_grad, mixed, y_weight, u_weight, packed, vec, mask,
        state, after, normed, mid_low, y_sum, decay_sum,
    ]
    kept = pl.BlockSpec(memory_space=pl.ANY)
    return pl.pallas_call(
        functools.partial(mixer_back_kernel, rows, not so_far),
        grid_spec=pltpu.PrefetchScalarGridSpec(
            num_scalar_prefetch=1,
            grid=(steps,),
            in_specs=[
                lane(length), lane(length), lane(length), lane(length), lane(length),
                lane(length), lane(ext), lane(length), lane(length), weight, weight,
                pl.BlockSpec(
                    (units, *packed.shape[1:]), lambda step, place: (pair(step, place), 0, 0)
                ),
                lane(vec.shape[0]), whole(mask), lane(1),
                lane(1), whole(normed), whole(mid_low), lane(8), lane(8),
            ]
            + ([kept, kept, whole(so_far[2])] if so_far else []),
            out_specs=[
                piece, piece, pl.BlockSpec((ext, model), lambda step, place: (0, 0)),
            ],
            scratch_shapes=[
                pltpu.VMEM((length, width), WIDE),
                pltpu.VMEM((length, 2 * width), LOW),
                pltpu.VMEM((length, width), LOW),
                pltpu.VMEM((ext + RIM, width), WIDE),
                pltpu.VMEM((ext, width), LOW),
                pltpu.VMEM((width, model), WIDE),
                pltpu.VMEM((width, width), WIDE),
                pltpu.VMEM((width, 2 * width), LOW),
                pltpu.VMEM((128, width), WIDE),
            ],
        ),
        out_shape=[shape, shape, jax.ShapeDtypeStruct((ext, model), WIDE)],
        input_output_aliases={len(operands) + 1 + k: k for k in range(2)} if so_far else {},
        compiler_params=params(),
        cost_estimate=cost(15 * steps),
        name="mixer_back",
    )(place, *operands, *so_far)


def wide_of(value):
    return value.astype(WIDE)


def pin_kernel(source, target):
    del source, target


class Clock:
    def __init__(self):
        self.time = jnp.zeros((8, 128), WIDE)

    def tick(self, values):
        values, self.time = lax.optimization_barrier((values, self.time))
        return values

    def pin(self):
        self.time = pl.pallas_call(
            pin_kernel,
            in_specs=[pl.BlockSpec(memory_space=pl.ANY)],
            out_specs=pl.BlockSpec(memory_space=pl.ANY),
            out_shape=jax.ShapeDtypeStruct(self.time.shape, WIDE),
            input_output_aliases={0: 0},
            cost_estimate=cost(5000),
            name="pin",
        )(self.time)


class Sums:
    def __init__(self, clock, stages, move=swapped, pin=False, start=True):
        self.clock = clock
        self.stages = stages
        self.move = move
        self.result = self.moving = None
        if start:
            self.begin(pin)

    def begin(self, pin=False):
        self.send(next(self.stages), pin)

    def send(self, transfers, pin):
        meanwhile = transfers.pop() if callable(transfers[-1]) else None
        values = self.clock.tick([transfer[0] for transfer in transfers])
        self.moving = [
            (transfer[3] if len(transfer) > 3 else self.move)(value, *transfer[1:3])
            for value, transfer in zip(values, transfers)
        ]
        if pin:
            self.clock.pin()
        if meanwhile:
            meanwhile()

    def step(self, pin=False):
        try:
            transfers = self.stages.send(self.clock.tick(self.moving))
        except StopIteration as end:
            self.result = end.value
        else:
            self.send(transfers, pin)

    def finish(self):
        while self.result is None:
            self.step()
        return self.result


def lockstep(clock, *groups):
    begun = [group for group in groups if group.moving is not None]
    arrived = clock.tick([group.moving for group in begun])
    transfers = []
    for group in groups:
        if group.moving is None:
            transfers.append(next(group.stages))
        else:
            transfers.append(group.stages.send(arrived[begun.index(group)]))
    values = clock.tick([[transfer[0] for transfer in one] for one in transfers])
    for group, one, own in zip(groups, transfers, values):
        group.moving = [group.move(value, *transfer[1:]) for value, transfer in zip(own, one)]


def halved(clock, keep, send):
    slots, matrices, _, part, lanes = keep.shape
    shape = (slots // 4, 2, 2, matrices, 2, part, lanes)
    keep = keep.reshape(shape)
    (came,) = yield [(send, "rows", 1)]
    came = came.reshape(shape)
    every = slice(None)
    near = {}

    def both(one, other, *where):
        return wide_of(one[where]) + wide_of(other[where])

    def meanwhile():
        one, other = clock.tick((keep, came))
        near["y"] = both(one, other, every, 0, every, every, 0)
        near["x"] = both(one, other, every, 1, 0)
        near.update(clock.tick(dict(near)))

    return (
        yield from owned(
            lambda place: near["y"][:, place],
            both(keep, came, every, 0, every, every, 1).astype(LOW),
            lambda place: near["x"][:, :, place],
            both(keep, came, every, 1, 1).astype(LOW),
            meanwhile,
        )
    )


def owned(near_y, far_y, near_x, far_x, meanwhile=None):
    from_y, from_x = yield [(far_y, "rows", 2), (far_x, "chan", 1)] + (
        [meanwhile] if meanwhile else []
    )
    rest = lambda place: wide_of(near_y(place)) + wide_of(from_y[:, place])
    also = lambda place: wide_of(near_x(place)) + wide_of(from_x[:, :, place])
    rest_came, also_came = yield [
        (rest(1).astype(LOW), "chan", 1),
        (also(1).astype(LOW), "rows", 2),
    ]
    rest, also = rest(0), also(0)
    parts = {}
    for index in range(rest.shape[0]):
        parts[2 * index] = rest[index] + wide_of(rest_came[index])
        parts[2 * index + 1] = also[index] + wide_of(also_came[index])
    came = yield [
        (value.astype(LOW), "chan", 2 * distance) for distance, value in parts.items() if distance
    ]
    total = parts[0]
    for value in came:
        total = total + wide_of(value)
    return total


def settled(total):
    total = total.astype(LOW)
    (came,) = yield [(total, "rows", 2)]
    pair = jnp.stack([total, came])
    (came,) = yield [(pair, "rows", 1)]
    return pair, came


def ordered(pair, came):
    four = jnp.stack([pair, came], 1)
    place = lax.axis_index("rows")
    four = jnp.where(place & 1, four[:, ::-1], four)
    four = jnp.where(place & 2, four[::-1], four)
    _, _, matrices, part, lanes = four.shape
    four = four.reshape(4, matrices, part, lanes).transpose(1, 0, 2, 3)
    return four.reshape(matrices, 4 * part, lanes).astype(WIDE)


def finish_rest_kernel(place, pair, came, into, gelu, out, gates, lines):
    part, model = pair.shape[2], into.shape[1]
    lanes = gates.shape[1]
    for quarter in range(4):
        turn = quarter ^ place[1]
        own, other = (ref[turn // 2, 0].astype(WIDE) for ref in (pair, came))
        value = jnp.where(turn % 2 == 0, own, other)
        rows = slice(quarter * part, quarter * part + part)
        into[rows, :] = value[:, 0:model]
        gelu[rows, :] = value[:, model : 2 * model]
        out[rows, :] = value[:, 2 * model : 3 * model]
        gates[rows, :] = value[:, 3 * model : 3 * model + lanes]
        lines[rows, :] = value[:, 3 * model + lanes :]


def finish_rest(place, pair, came, model, width):
    rows = 4 * pair.shape[2]
    vmem = pl.BlockSpec(memory_space=pltpu.VMEM)
    shape = lambda lanes: jax.ShapeDtypeStruct((rows, lanes), WIDE)
    return pl.pallas_call(
        finish_rest_kernel,
        grid_spec=pltpu.PrefetchScalarGridSpec(
            num_scalar_prefetch=1, grid=(1,), in_specs=[vmem] * 2, out_specs=[vmem] * 5
        ),
        out_shape=[shape(model)] * 3 + [shape(width), shape(128)],
        compiler_params=params(),
        cost_estimate=cost(3),
        name="finish_rest",
    )(place, pair, came)


def finish_kernel(place, pair, came, gate, up, down):
    def rows_of(matrix):
        parts = []
        for quarter in range(4):
            turn = quarter ^ place[1]
            own, other = (ref[turn // 2, matrix].astype(WIDE) for ref in (pair, came))
            parts.append(jnp.where(turn % 2 == 0, own, other))
        return jnp.concatenate(parts, 0)

    gate[...] = jnp.transpose(rows_of(0))
    up[...] = jnp.transpose(rows_of(1))
    down[...] = rows_of(2)


def finish(place, pair, came):
    _, _, part, model = pair.shape
    tall = jax.ShapeDtypeStruct((model, 4 * part), WIDE)
    vmem = pl.BlockSpec(memory_space=pltpu.VMEM)
    return pl.pallas_call(
        finish_kernel,
        grid_spec=pltpu.PrefetchScalarGridSpec(
            num_scalar_prefetch=1, grid=(1,), in_specs=[vmem] * 2, out_specs=[vmem] * 3
        ),
        out_shape=[tall, tall, jax.ShapeDtypeStruct((4 * part, model), WIDE)],
        compiler_params=params(),
        cost_estimate=cost(4),
        name="finish",
    )(place, pair, came)


def everywhere(value):
    for axis in ("rows", "chan"):
        bits = 1
        while bits < lax.axis_size(axis):
            (came,) = yield [(value, axis, bits)]
            value = value + came
            bits *= 2
    return value


def gathered(piece):
    parts = lax.axis_size("rows")
    share = piece.shape[0] // parts
    own = lax.dynamic_slice_in_dim(piece, lax.axis_index("rows") * share, share)
    full = lax.all_gather(own, ("chan", "rows"), axis=0, tiled=True)
    return full.reshape(lax.axis_size("chan"), piece.shape[0], piece.shape[1])


def pack_kernel(table, count, *refs):
    sources, outs, sems = refs[:count], refs[count:-1], refs[-1]
    copies = [
        pltpu.make_async_copy(
            sources[source].at[begin : begin + size],
            outs[out].at[at : at + size],
            sems.at[index],
        )
        for index, (out, at, source, begin, size) in enumerate(table)
    ]
    for copy in copies:
        copy.start()
    for copy in copies:
        copy.wait()


def pack(*lists):
    sources, table, shapes = [], [], []
    for out, pieces in enumerate(lists):
        at = 0
        for array, begin, size in pieces:
            known = [index for index, one in enumerate(sources) if one is array]
            if not known:
                known = [len(sources)]
                sources.append(array)
            table.append((out, at, known[0], begin, size))
            at += size
        shapes.append(jax.ShapeDtypeStruct((at, *pieces[0][0].shape[1:]), pieces[0][0].dtype))
    return pl.pallas_call(
        functools.partial(pack_kernel, table, len(sources)),
        in_specs=[pl.BlockSpec(memory_space=pl.ANY)] * len(sources),
        out_specs=[pl.BlockSpec(memory_space=pltpu.VMEM)] * len(shapes),
        scratch_shapes=[pltpu.SemaphoreType.DMA((len(table),))],
        out_shape=shapes,
        compiler_params=params(),
        cost_estimate=cost(0.01),
        name="pack",
    )(*sources)


def spread_units(units):
    pairs = range(2, lax.axis_size("chan") // 2)
    count = len(pairs)
    behind, *came = yield [(units[:2], "chan", 2)] + [
        (units[:1], "chan", 2 * pair) for pair in pairs
    ]
    singles = [(value, 0, 1) for value in came]
    (turned,) = pack([(units, 0, 1), (behind, 0, 2), *singles])
    (corners,) = yield [(turned, "chan", 1)]
    near, away = pack(
        [(behind, 0, 2), (corners, 1, 2)], [(corners, 0, 1), *singles, (corners, 3, count)]
    )
    over, near_too = yield [(away, "rows", 2), (near, "rows", 1)]
    size = 2 * count + 1
    (away,) = pack([(away, 0, size), (over, 0, size)])
    (away_too,) = yield [(away, "rows", 1)]
    return units, near, near_too, away, away_too


def unit_source(pair, side, turn, count):
    upper, other = turn // 2, turn % 2
    if pair == 0 and side == 0:
        return 0, 2 * other + upper
    if pair == 1:
        return 1 + other, 2 * side + upper
    if pair == 0:
        return 3 + other, upper * (2 * count + 1)
    return 3 + other, upper * (2 * count + 1) + 1 + side * count + pair - 2


def assemble_kernel(cuts, pairs, place, *refs):
    sources, outs, sems = refs[:5], refs[5:-1], refs[-1]
    copies = []
    for pair in range(pairs):
        for side in range(2):
            for turn in range(4):
                array, index = unit_source(pair, side, turn, pairs - 2)
                unit = ((2 * pair + side) ^ place[0]) * 4 + (turn ^ place[1])
                for (begin, end), out in zip(cuts, outs):
                    copies.append(
                        pltpu.make_async_copy(
                            sources[array].at[index, begin:end],
                            out.at[unit],
                            sems.at[len(copies)],
                        )
                    )
    for copy in copies:
        copy.start()
    for copy in copies:
        copy.wait()


def assembled(place, sources, cuts):
    pairs = lax.axis_size("chan") // 2
    model = sources[0].shape[2]
    anywhere = pl.BlockSpec(memory_space=pl.ANY)
    return pl.pallas_call(
        functools.partial(assemble_kernel, cuts, pairs),
        grid_spec=pltpu.PrefetchScalarGridSpec(
            num_scalar_prefetch=1,
            grid=(1,),
            in_specs=[anywhere] * 5,
            out_specs=[pl.BlockSpec(memory_space=pltpu.VMEM)] * len(cuts),
            scratch_shapes=[pltpu.SemaphoreType.DMA((8 * pairs * len(cuts),))],
        ),
        out_shape=[
            jax.ShapeDtypeStruct((8 * pairs, end - begin, model), LOW) for begin, end in cuts
        ],
        compiler_params=params(),
        cost_estimate=cost(5),
        name="assemble",
    )(place, *sources)


def local(
    tokens, segments, gelu_weight, gelu_bias, input_weight, input_bias, conv_taps, conv_bias,
    decay_gate, decay_bias, input_gate, ingate_bias, decay_param, out_weight, mixer_gain,
    gate_weight, up_weight, down_weight, feed_gain, cotangent,
):
    length, model = tokens.shape
    rim = conv_taps.shape[0] - 1
    chans = lax.axis_size("chan")
    me, row_place = lax.axis_index("chan"), lax.axis_index("rows")
    rows, block = decay_gate.shape
    total = rows * chans
    width = 2 * block
    group = width // rows

    padded = jnp.concatenate([jnp.full((rim,), -1, jnp.int32), segments])
    window = lax.dynamic_slice_in_dim(padded, me * length, length + rim)
    own = window[rim:]
    same = [own == window[rim - shift : rim - shift + length] for shift in range(1, rim + 1)]
    mask = jnp.stack([same[0], *same, own != 0] + [same[0]] * (7 - rim - 1), 1).astype(WIDE)
    mask = jnp.pad(mask, ((RIM, RIM), (0, 0)))

    small = jnp.concatenate(
        [
            jnp.stack([gelu_bias, input_bias, conv_bias, decay_bias, ingate_bias, decay_param]),
            conv_taps,
        ]
    )
    unit_rows = block // 4
    count = rows // unit_rows
    lines = unit_rows // 2
    place = jnp.stack([me, row_place]).astype(jnp.int32)
    clock = Clock()

    part = gate_weight.shape[1] // 4
    own_columns = lambda weight: lax.dynamic_slice_in_dim(weight, row_place * part, part, 1).T
    own_unit = jnp.stack(
        [
            own_columns(gate_weight),
            own_columns(up_weight),
            lax.dynamic_slice_in_dim(down_weight, row_place * part, part),
        ]
    )
    both = jnp.concatenate([decay_gate, input_gate], 1)
    both = jnp.pad(both, ((0, 0), (0, model // 2 - 2 * block)))
    both = both.reshape(count, 2, lines, model // 2).swapaxes(1, 2).reshape(count, lines, model)
    flat = small.reshape(small.shape[0], count, unit_rows).swapaxes(0, 1).reshape(count, 1, -1)
    flat = jnp.pad(flat, ((0, 0), (0, lines // 3 - 1), (0, model - flat.shape[2])))
    by_unit = lambda weight: weight.reshape(count, unit_rows, model)
    first = jnp.concatenate([by_unit(input_weight.T), both, flat], 1)
    second = jnp.concatenate([by_unit(gelu_weight.T), by_unit(out_weight)], 1)
    first_cuts = ((0, unit_rows), (unit_rows, first.shape[1]))
    second_cuts = ((0, unit_rows), (unit_rows, 2 * unit_rows))
    cot_low = cotangent.astype(LOW)
    rim_tokens = moved_by(tokens[length - rim :], "chan", 1)
    extended = jnp.concatenate([jnp.zeros((RIM - rim, model), WIDE), rim_tokens, tokens])
    if count == 4:
        quarters = lambda units: jnp.stack(
            [
                lax.dynamic_index_in_dim(units, row_place ^ bits, keepdims=False)
                for bits in (0, 2, 1, 3)
            ]
        )
        own_unit = clock.tick(own_unit)
        first = Sums(clock, spread_units(quarters(first)))
        second = Sums(clock, spread_units(quarters(second)), start=False)
        lockstep(clock, first, second)
        normed = clock.tick(rms_norm(clock.tick(extended), mixer_gain).astype(LOW))
        lockstep(clock, first, second)
        lockstep(clock, first, second)
        first.step()
        u_weight, packed = clock.tick(assembled(place, first.result, first_cuts))
    else:
        cut = lambda units, cuts: [
            gathered(units.reshape(-1, model))[:, begin:end] for begin, end in cuts
        ]
        normed = rms_norm(extended, mixer_gain).astype(LOW)
        u_weight, packed = cut(first, first_cuts)
        y_weight, o_weight = cut(second, second_cuts)
        y_weight, o_weight = (w.reshape(total, model) for w in (y_weight, o_weight))
    feed_units = lax.all_gather(own_unit[None], ("chan", "rows"), axis=0, tiled=True)
    u_weight = u_weight.reshape(total, model)
    small_full = packed[:, lines, : small.shape[0] * unit_rows]
    small_full = small_full.reshape(-1, small.shape[0], unit_rows).swapaxes(0, 1)
    small_full = small_full.reshape(small.shape[0], total).astype(WIDE)
    param = small_full[5:6]
    line = lax.broadcasted_iota(jnp.int32, (16, total), 0)
    vec = jnp.pad(small_full, ((0, 6), (0, 0)))
    vec = jnp.where(line == 5, -8.0 * jax.nn.softplus(param), vec)
    vec = jnp.where(line == 10, -8.0 * jax.nn.sigmoid(param), vec)

    u, conv, rate, into, state, factor, decay_sum = clock.tick(
        mixer_forward(normed, u_weight, packed, vec, mask, width)
    )
    carry = Sums(
        clock, entering(jnp.concatenate([factor[-1:], state[-1:]]), "chan", 1), moved_by
    )
    if count == 4:
        second.step()
        carry.step()
        second.step()
        y_weight, o_weight = clock.tick(assembled(place, second.result, second_cuts))
        y_weight, o_weight = (w.reshape(total, model) for w in (y_weight, o_weight))
    active, slope = clock.tick(gelu_branch(normed, y_weight, vec, width))
    carry = clock.tick(carry.finish())
    cot_too = swapped(cot_low, "rows", 1)
    mixed, middle, normed2 = clock.tick(
        mixer_out(active, state, factor, carry, o_weight, tokens, feed_gain[None])
    )
    cot_too = clock.tick(cot_too)
    normed2_too = swapped(normed2, "rows", 1)
    feed_units = clock.tick(feed_units)
    block_output, normed2_grad, mine, send = clock.tick(
        feed(place, normed2, cot_low, middle, feed_units)
    )
    theirs = swapped(send, "rows", 1)

    mid_grad, mid_low, state_grad, y_grad, feed_gain_sum, back_sum, y_sum = clock.tick(
        middle_back(
            middle, normed2_grad, cotangent, feed_gain[None], o_weight, active, slope, state,
            factor, carry,
        )
    )
    after = Sums(
        clock,
        entering(
            jnp.concatenate([factor[-1:], jnp.sum(back_sum, 0, keepdims=True)]), "chan", -1
        ),
        moved_by,
    )
    theirs, normed2_too = clock.tick((theirs, normed2_too))
    operands = (mine, theirs, normed2, cot_low, normed2_too, cot_too)
    near_y, far_y = clock.tick(feed_grads(0, *operands))
    split = lambda value: value.reshape(-1, 2, *value.shape[1:])
    moving = [swapped(split(far_y), "rows", 2)]
    after.step()
    near_x, far_x = clock.tick(feed_grads(1, *operands))
    moving.append(swapped(far_x, "chan", 1))
    stages = owned(
        lambda place: split(near_y)[:, place], far_y, lambda place: near_x[:, :, place], far_x
    )
    next(stages)
    fed = Sums(clock, stages, start=False)
    fed.moving = moving
    after = clock.tick(after.finish())
    place = jnp.stack([me // group, me % group, row_place]).astype(jnp.int32)
    pairs = total // width
    back = lambda after, begin, steps, so_far: clock.tick(
        mixer_back(
            place, state_grad, rate, into, conv, state, factor, u, y_grad, mixed, y_weight, u_weight,
            packed, vec, mask, carry, after, normed, mid_low, y_sum, decay_sum, rows, width, begin, steps, so_far,
        )
    )
    so_far = back(after, 1, pairs - 1, ())
    fed.step()
    so_far = clock.tick(so_far)
    keep, send, normed_grad = back(after, 0, 1, so_far)
    fed.moving = clock.tick(fed.moving)
    rest = Sums(clock, halved(clock, keep, send))
    rim_grad = moved_by(clock.tick(normed_grad[RIM - rim : RIM]), "chan", -1)
    rim_grad = clock.tick(rim_grad)
    error = normed_grad[RIM:] + jnp.concatenate([jnp.zeros((length - rim, model), WIDE), rim_grad])
    scale = lax.rsqrt(jnp.mean(tokens * tokens, axis=-1, keepdims=True) + 1e-06)
    gained = mixer_gain * error
    mean = jnp.mean(gained * tokens, axis=-1, keepdims=True)
    tokens_grad = clock.tick(mid_grad + scale * gained - tokens * (scale * scale * scale * mean))
    mixer_gain_sum = jnp.sum(error * tokens * scale, 0)

    gains = Sums(clock, everywhere(jnp.stack([mixer_gain_sum, jnp.sum(feed_gain_sum, 0)])))
    gains.step()
    rest.step(pin=True)
    fed.step()
    gains.moving = clock.tick(gains.moving)
    rest.step(pin=True)
    rest.step(pin=True)
    gains.step()
    gains.step()
    fed.step()
    fed = Sums(clock, settled(fed.result))
    gains.step()
    fed.step()
    gains = gains.finish()
    rest.step()
    rest = Sums(clock, settled(rest.result))
    fed.step()
    feed_sum = clock.tick(finish(jnp.stack([me, row_place]).astype(jnp.int32), *fed.result))
    pair, came = rest.finish()
    gains = gains + clock.time[:1, :1]
    if pair.shape[2] % 8:
        whole = ordered(pair, came)[0]
        input_sum, gelu_sum, out_sum = (whole[:, k * model : (k + 1) * model] for k in range(3))
        gates_sum, lines = whole[:, 3 * model : 3 * model + width], whole[:, 3 * model + width :]
    else:
        input_sum, gelu_sum, out_sum, gates_sum, lines = finish_rest(
            jnp.stack([me, row_place]).astype(jnp.int32), pair, came, model, width
        )
    lines = lines[:, :11].T
    mean_decay = lines[10] / (length * lax.axis_size("rows") * chans)
    return (
        block_output,
        tokens_grad,
        gelu_sum.T,
        lines[0],
        input_sum.T,
        lines[1],
        lines[2:6],
        lines[6],
        gates_sum[:, :block],
        lines[7],
        gates_sum[:, block:],
        lines[8],
        lines[9],
        out_sum,
        gains[0],
        feed_sum[0],
        feed_sum[1],
        feed_sum[2],
        gains[1],
        mean_decay,
    )


def solution(mesh):
    return jax.shard_map(
        local,
        mesh=mesh,
        in_specs=(
            P(("rows", "chan"), None),
            P("rows"),
            P(None, "chan"),
            P("chan"),
            P(None, "chan"),
            P("chan"),
            P(None, "chan"),
            P("chan"),
            P("chan", None),
            P("chan"),
            P("chan", None),
            P("chan"),
            P("chan"),
            P("chan", None),
            P(),
            P(None, "chan"),
            P(None, "chan"),
            P("chan", None),
            P(),
            P(("rows", "chan"), None),
        ),
        out_specs=(
            P(("rows", "chan"), None),
            P(("rows", "chan"), None),
            P(None, "chan"),
            P("chan"),
            P(None, "chan"),
            P("chan"),
            P(None, "chan"),
            P("chan"),
            P("chan", None),
            P("chan"),
            P("chan", None),
            P("chan"),
            P("chan"),
            P("chan", None),
            P(),
            P(None, "chan"),
            P(None, "chan"),
            P("chan", None),
            P(),
            P("chan"),
        ),
        check_vma=False,
    )
```

```python
import functools

import jax
import jax.numpy as jnp
from jax import lax
from jax.experimental import pallas as pl
from jax.experimental.pallas import tpu as pltpu
from jax.sharding import PartitionSpec as P

LOW = jnp.bfloat16
WIDE = jnp.float32
RIM = 16
STEP = 16
VMEM_BYTES = 56 * 1024 * 1024
GELU_SLOPE = 0.7978845608028654
GELU_CUBE = 0.044715


def params(**more):
    return pltpu.CompilerParams(vmem_limit_bytes=VMEM_BYTES, **more)


def moved_by(value, axis, steps):
    count = lax.axis_size(axis)
    leading, last = (max(0, -steps), min(count, count - steps))
    return lax.ppermute(value, axis, [(source, source + steps) for source in range(leading, last)])


def swapped(value, axis, bits):
    count = lax.axis_size(axis)
    return lax.ppermute(value, axis, [(source, source ^ bits) for source in range(count)])


def join(earlier, later):
    return jnp.concatenate(
        [earlier[0:1] * later[0:1], later[0:1] * earlier[1:2] + later[1:2]], 0
    )


def entering(value, axis, sign):
    count = lax.axis_size(axis)
    if count in (4, 8):
        (partner,) = yield [(value, axis, 1, swapped)]
        later = (lax.axis_index(axis) & 1) == (1 if sign > 0 else 0)
        both = join(jnp.where(later, partner, value), jnp.where(later, value, partner))
        came = yield [(both, axis, 2 * sign * reach) for reach in range(1, count // 2)]
        total = came[-1]
        for one in came[-2::-1]:
            total = join(total, one)
        return jnp.where(later, join(total, partner)[1:2], total[1:2])
    total = value
    came = yield [(value, axis, sign * reach) for reach in (1, 2, 3) if reach < count]
    for one in came:
        total = join(one, total)
    reach = 4
    while 2 * reach < count:
        (one,) = yield [(total, axis, sign * reach)]
        total = join(one, total)
        reach *= 2
    came = yield [(total, axis, sign * far) for far in (1, reach + 1) if far < count]
    last = came[0]
    for one in came[1:]:
        last = join(one, last)
    return last[1:2]


def rms_norm(values, gain):
    return values * lax.rsqrt(jnp.mean(values * values, axis=-1, keepdims=True) + 1e-06) * gain


def nt(left, right):
    return lax.dot_general(left, right, (((1,), (1,)), ((), ())), preferred_element_type=WIDE)


def tn(left, right):
    return lax.dot_general(left, right, (((0,), (0,)), ((), ())), preferred_element_type=WIDE)


def nn(left, right):
    return lax.dot_general(left, right, (((1,), (0,)), ((), ())), preferred_element_type=WIDE)


def sigmoid(value):
    return 0.5 * jnp.tanh(0.5 * value) + 0.5


def gelu_parts(value):
    square = value * value
    bend = jnp.tanh(GELU_SLOPE * value * (1.0 + GELU_CUBE * square))
    half = 0.5 + 0.5 * bend
    slope = half + 0.5 * GELU_SLOPE * value * (1.0 - bend * bend) * (1.0 + 3.0 * GELU_CUBE * square)
    return value * half, slope


def loop(count, unroll, body, init):
    while count % unroll:
        unroll -= 1

    def several(index, carry):
        for turn in range(unroll):
            carry = body(index * unroll + turn, carry)
        return carry

    return lax.fori_loop(0, count // unroll, several, init)


def cost(microseconds):
    return pl.CostEstimate(
        flops=int(microseconds * 1.1e7), bytes_accessed=int(microseconds * 3.5e4), transcendentals=0
    )


def fold(value):
    total = value[0:8]
    for group in range(1, value.shape[0] // 8):
        total = total + value[8 * group : 8 * group + 8]
    return total


def fill_gates(packed, gates, block):
    width = 2 * block
    lines = packed.shape[1] * 3 // 4

    @pl.when(pl.program_id(0) == 0)
    def _():
        gates[...] = jnp.zeros_like(gates)

    parts = []
    for unit in range(packed.shape[0]):
        value = packed[unit].astype(WIDE)[:lines]
        parts += [value[:, 0:width], value[:, 512 : 512 + width]]
    parts = jnp.concatenate(parts, 0).astype(LOW)
    for half in (0, block):
        gates[half : half + block, half : half + block] = parts[half : half + block, 0:block]
        gates[half : half + block, width + half : width + half + block] = parts[
            half : half + block, block:
        ]


def mixer_forward_kernel(
    normed, u_weight, packed, vec, mask, u_out, conv_out, r_out, i_out, h_out, f_out, sum_out,
    low, zed, gates,
):
    ext = normed.shape[0]
    width = u_out.shape[1]
    fill_gates(packed, gates, width // 2)
    count = (ext - RIM) // STEP
    u_out[...] = nt(normed[...], u_weight[...]) + vec[1:2, :]

    def convolve(index, _):
        base = pl.multiple_of(index * STEP, STEP)
        own = pl.ds(base, STEP)
        window = u_out[pl.ds(base + 8, STEP + 8), :]
        flags = mask[pl.ds(base + RIM, STEP), :]
        conv = vec[2:3, :] + vec[6:7, :] * window[8:]
        for shift in (1, 2, 3):
            conv = conv + flags[:, shift : shift + 1] * (
                vec[6 + shift : 7 + shift, :] * window[8 - shift : 8 - shift + STEP]
            )
        conv = conv * flags[:, 4:5]
        conv_out[own, :] = conv
        low[own, :] = conv.astype(LOW)
        return 0

    loop(count, 4, convolve, 0)
    zed[...] = nn(low[...], gates[...])
    line = lax.broadcasted_iota(jnp.int32, (8, width), 0)

    def advance(index, carry):
        state, factor, total = carry
        own = pl.ds(pl.multiple_of(index * STEP, STEP), STEP)
        going = mask[pl.ds(pl.multiple_of(index * STEP + RIM, STEP), STEP), :][:, 0:1]
        rate = sigmoid(zed[own, 0:width] + vec[3:4, :])
        into = sigmoid(zed[own, width:] + vec[4:5, :])
        decay = jnp.exp(vec[5:6, :] * rate)
        r_out[own, :] = rate
        i_out[own, :] = into
        scale = jnp.where(going == 0.0, 1.0, jnp.sqrt(1.01 - decay * decay))
        inject = conv_out[own, :] * into * scale
        carried = decay * going
        total = total + fold(decay)
        for group in range(STEP // 8):
            part = slice(8 * group, 8 * group + 8)
            mul, add = carried[part], inject[part]
            for reach in (1, 2, 4):
                inside = line >= reach
                add = add + mul * jnp.where(inside, pltpu.roll(add, reach, 0), 0.0)
                mul = mul * jnp.where(inside, pltpu.roll(mul, reach, 0), 1.0)
            here = add + mul * state
            gone = mul * factor
            rows = pl.ds(pl.multiple_of(index * STEP + 8 * group, 8), 8)
            h_out[rows, :] = here
            f_out[rows, :] = gone
            state, factor = here[7:8], gone[7:8]
        return state, factor, total

    zero = jnp.zeros((1, width), WIDE)
    _, _, total = loop(
        count, 4, advance, (zero, zero + 1.0, jnp.zeros((8, width), WIDE))
    )
    sum_out[...] = total


def mixer_forward(normed, u_weight, packed, vec, mask, width):
    ext, model = normed.shape
    tokens = ext - RIM
    total = u_weight.shape[0]
    pairs = total // width
    units = packed.shape[0] // pairs
    by_lane = lambda length: pl.BlockSpec((length, width), lambda step: (0, step))
    whole = lambda array: pl.BlockSpec(array.shape, lambda step: (0,) * array.ndim)
    flat = jax.ShapeDtypeStruct((tokens, total), WIDE)
    return pl.pallas_call(
        mixer_forward_kernel,
        grid=(pairs,),
        in_specs=[
            whole(normed),
            pl.BlockSpec((width, model), lambda step: (step, 0)),
            pl.BlockSpec((units, *packed.shape[1:]), lambda step: (step, 0, 0)),
            by_lane(vec.shape[0]),
            whole(mask),
        ],
        out_specs=[by_lane(ext)] + [by_lane(tokens)] * 5 + [by_lane(8)],
        out_shape=[jax.ShapeDtypeStruct((ext, total), WIDE)] + [flat] * 5
        + [jax.ShapeDtypeStruct((8, total), WIDE)],
        scratch_shapes=[
            pltpu.VMEM((tokens, width), LOW),
            pltpu.VMEM((tokens, 2 * width), WIDE),
            pltpu.VMEM((width, 2 * width), LOW),
        ],
        compiler_params=params(),
        cost_estimate=cost(26),
        name="mixer_forward",
    )(normed, u_weight, packed, vec, mask)


def gelu_branch_kernel(normed, weight, vec, active_out, slope_out, held):
    held[...] = nt(normed[RIM:, :], weight[...]) + vec[0:1, :]

    def act(index, _):
        own = pl.ds(pl.multiple_of(index * STEP, STEP), STEP)
        active_out[own, :], slope_out[own, :] = gelu_parts(held[own, :])
        return 0

    loop(held.shape[0] // STEP, 4, act, 0)


def gelu_branch(normed, weight, vec, width):
    length, total = normed.shape[0] - RIM, weight.shape[0]
    model = normed.shape[1]
    lane = lambda lines: pl.BlockSpec((lines, width), lambda step: (0, step))
    return pl.pallas_call(
        gelu_branch_kernel,
        grid=(total // width,),
        in_specs=[
            pl.BlockSpec(normed.shape, lambda step: (0, 0)),
            pl.BlockSpec((width, model), lambda step: (step, 0)),
            lane(vec.shape[0]),
        ],
        out_specs=[lane(length), lane(length)],
        out_shape=[jax.ShapeDtypeStruct((length, total), WIDE)] * 2,
        scratch_shapes=[pltpu.VMEM((length, width), WIDE)],
        compiler_params=params(),
        cost_estimate=cost(8),
        name="gelu_branch",
    )(normed, weight, vec)


def mixer_out_kernel(active, h, f, state, weight, tokens, gain, mixed, middle, normed):
    def gate(index, _):
        own = pl.ds(pl.multiple_of(index * STEP, STEP), STEP)
        mixed[own, :] = ((h[own, :] + f[own, :] * state[...]) * active[own, :]).astype(LOW)
        return 0

    loop(active.shape[0] // STEP, 4, gate, 0)
    total = tokens[...] + nn(mixed[...], weight[...])
    middle[...] = total
    scale = lax.rsqrt(jnp.mean(total * total, axis=-1, keepdims=True) + 1e-06)
    normed[...] = (total * scale * gain[...]).astype(LOW)


def mixer_out(active, h, f, state, weight, tokens, gain):
    length, model = tokens.shape
    total = active.shape[1]
    tile = 256 if length % 256 == 0 else length
    row = lambda lanes: pl.BlockSpec((tile, lanes), lambda step: (step, 0))
    one = lambda array: pl.BlockSpec(array.shape, lambda step: (0, 0))
    return pl.pallas_call(
        mixer_out_kernel,
        grid=(length // tile,),
        in_specs=[
            row(total), row(total), row(total), one(state), one(weight), row(model), one(gain),
        ],
        out_specs=[row(total), row(model), row(model)],
        out_shape=[
            jax.ShapeDtypeStruct((length, total), LOW),
            jax.ShapeDtypeStruct((length, model), WIDE),
            jax.ShapeDtypeStruct((length, model), LOW),
        ],
        compiler_params=params(),
        cost_estimate=cost(9),
        name="mixer_out",
    )(active, h, f, state, weight, tokens, gain)


def spread(place, wide, keep, send, matrix, group, rows, lanes=slice(None), count=None):
    part = rows // 4
    if part % 8:
        value = wide[:, 0:count]
        pieces = [value[begin : begin + part] for begin in range(0, group * rows, part)]
        mine = place[1] * 4 + place[2]
        bit = 1
        while bit < len(pieces):
            turned = (mine & bit) != 0
            pieces = [
                jnp.where(turned, pieces[index ^ bit], pieces[index])
                for index in range(len(pieces))
            ]
            bit *= 2
    for slot in range(group):
        shard = slot ^ place[1]
        for turn in range(4):
            if part % 8:
                value = pieces[4 * slot + turn]
            else:
                begin = pl.multiple_of(shard * rows + (turn ^ place[2]) * part, 8)
                value = wide[pl.ds(begin, part), 0:count]
            (keep, send)[turn & 1][slot, matrix, turn >> 1, :, lanes] = value.astype(LOW)


def feed_kernel(
    group, place, normed, cot, out_in, units, out, grad, keep, send, gate_s, up_s, back_s, hidden_l,
    both_l, held, sems, turned, cot_turned,
):
    model = normed.shape[1]
    width = gate_s.shape[0]
    rows = width // group
    part, half = rows // 4, rows // 2
    step = pl.program_id(0)

    def copies(index):
        for member in range(group):
            for turn in range(4):
                unit = (place[0] ^ (group * index + member)) * 4 + (place[1] ^ turn)
                order = 4 * member + (turn % 2) * 2 + turn // 2
                slot = index % 2
                yield pltpu.make_async_copy(
                    units.at[unit], held.at[slot, :, order], sems.at[slot, 4 * member + turn]
                )

    @pl.when(step == 0)
    def _():
        for copy in copies(0):
            copy.start()
        out[...] = out_in[...]
        grad[...] = jnp.zeros_like(grad)
        turned[...] = jnp.transpose(normed[...])
        cot_turned[...] = jnp.transpose(cot[...])

    @pl.when(step + 1 < pl.num_programs(0))
    def _():
        for copy in copies(step + 1):
            copy.start()

    for copy in copies(step):
        copy.wait()

    def weight(begin, end):
        if part % 16 == 0:
            return held[step % 2, begin:end].reshape((end - begin) * width, model)
        pieces = [
            held[step % 2, matrix, order].astype(WIDE)
            for matrix in range(begin, end)
            for order in range(4 * group)
        ]
        return jnp.concatenate(pieces, 0).astype(LOW)

    first, third = weight(0, 2), weight(2, 3)
    gate_s[...] = nn(first[:width], turned[...])
    up_s[...] = nn(first[width:], turned[...])
    back_s[...] = nn(third, cot_turned[...])

    def act(index, _):
        base = pl.multiple_of(index * STEP, STEP)
        own = pl.ds(base, STEP)
        up, back = up_s[own, :], back_s[own, :]
        value, slope = gelu_parts(gate_s[own, :])
        hidden_l[own, :] = (value * up).astype(LOW)
        both_l[own, :] = (back * up * slope).astype(LOW)
        both_l[pl.ds(base + width, STEP), :] = (back * value).astype(LOW)
        return 0

    loop(width // STEP, 4, act, 0)
    out[...] += tn(hidden_l[...], third)
    grad[...] += tn(both_l[...], first)
    for member in range(group):
        for matrix, (value, offset) in enumerate(((both_l, 0), (both_l, width), (hidden_l, 0))):
            begin = offset + member * rows
            keep[member, matrix] = value[begin : begin + half, :]
            send[member, matrix] = value[begin + half : begin + rows, :]


def feed(place, normed, cot, out_in, units):
    length, model = normed.shape
    part = units.shape[2]
    slots = units.shape[0] // 4
    group = 2
    width = 4 * part * group
    whole = lambda array: pl.BlockSpec(array.shape, lambda step, place: (0,) * array.ndim)
    piece = pl.BlockSpec((group, 3, 2 * part, length), lambda step, place: (step, 0, 0, 0))
    wide = jax.ShapeDtypeStruct((length, model), WIDE)
    grads = jax.ShapeDtypeStruct((slots, 3, 2 * part, length), LOW)
    return pl.pallas_call(
        functools.partial(feed_kernel, group),
        grid_spec=pltpu.PrefetchScalarGridSpec(
            num_scalar_prefetch=1,
            grid=(slots // group,),
            in_specs=[
                whole(normed), whole(cot), whole(out_in), pl.BlockSpec(memory_space=pl.ANY),
            ],
            out_specs=[whole(out_in), whole(out_in), piece, piece],
            scratch_shapes=[pltpu.VMEM((width, length), WIDE)] * 3
            + [pltpu.VMEM((width, length), LOW), pltpu.VMEM((2 * width, length), LOW)]
            + [pltpu.VMEM((2, 3, 4 * group, part, model), LOW)]
            + [pltpu.SemaphoreType.DMA((2, 4 * group))]
            + [pltpu.VMEM((model, length), LOW)] * 2,
        ),
        out_shape=[wide, wide, grads, grads],
        compiler_params=params(),
        cost_estimate=cost(34),
        name="feed",
    )(place, normed, cot, out_in, units)


def feed_grads_kernel(parity, count, mine, theirs, normed, cot, normed_too, cot_too, near, far):
    part = mine.shape[2] // 2
    step = pl.program_id(0)
    for matrix in range(3):
        right, right_too = (cot, cot_too) if matrix == 2 else (normed, normed_too)
        value = nn(mine[0, matrix], right[...]) + nn(theirs[0, matrix], right_too[...])
        value = value.astype(LOW)
        if parity == 0:
            near[0, matrix] = value[:part]
            far[0, matrix] = value[part:]
            continue
        for place, out in ((0, near), (count // 2, far)):

            @pl.when((step >= place) & (step < place + count // 2))
            def _():
                out[0, matrix, 0] = value[:part]
                out[0, matrix, 1] = value[part:]


def feed_grads(parity, mine, theirs, normed, cot, normed_too, cot_too):
    slots, _, rows, length = mine.shape
    model = normed.shape[1]
    count, part = slots // 2, rows // 2
    whole = lambda array: pl.BlockSpec(array.shape, lambda step: (0,) * array.ndim)

    def source(step):
        if parity == 0:
            return 4 * (step // 2) + step % 2, 0, 0, 0
        last = (step >= count // 2).astype(jnp.int32)
        return 4 * (step - last * (count // 2)) + 2 + last, 0, 0, 0

    if parity == 0:
        specs = [pl.BlockSpec((1, 3, part, model), lambda step: (step, 0, 0, 0))] * 2
        shape = jax.ShapeDtypeStruct((count, 3, part, model), LOW)
    else:
        clipped = lambda first: lambda step: (jnp.clip(step - first, 0, count // 2 - 1), 0, 0, 0, 0)
        specs = [
            pl.BlockSpec((1, 3, 2, part, model), clipped(first)) for first in (0, count // 2)
        ]
        shape = jax.ShapeDtypeStruct((count // 2, 3, 2, part, model), LOW)
    return pl.pallas_call(
        functools.partial(feed_grads_kernel, parity, count),
        grid=(count,),
        in_specs=[pl.BlockSpec((1, 3, rows, length), source)] * 2 + [whole(normed)] * 4,
        out_specs=specs,
        out_shape=[shape, shape],
        compiler_params=params(),
        cost_estimate=cost(2000),
        name="feed_grads",
    )(mine, theirs, normed, cot, normed_too, cot_too)


def middle_back_kernel(
    middle, grad, cot, gain, weight, active_in, slope_in, h, f, state, mid_grad, mid_low, state_grad, y_grad,
    gain_sum, back_sum, bias_sum, mixed_s,
):
    @pl.when(pl.program_id(0) == 0)
    def _():
        gain_sum[...] = jnp.zeros_like(gain_sum)
        back_sum[...] = jnp.zeros_like(back_sum)
        bias_sum[...] = jnp.zeros_like(bias_sum)

    value, error = middle[...], grad[...]
    scale = lax.rsqrt(jnp.mean(value * value, axis=-1, keepdims=True) + 1e-06)
    gained = gain[...] * error
    mean = jnp.mean(gained * value, axis=-1, keepdims=True)
    total = cot[...] + scale * gained - value * (scale * scale * scale * mean)
    gain_sum[...] += fold(error * value * scale)
    mid_grad[...] = total
    mid_low[...] = total.astype(LOW)
    mixed_s[...] = nt(mid_low[...], weight[...])

    def turn(index, carry):
        back, bias = carry
        own = pl.ds(pl.multiple_of(index * STEP, STEP), STEP)
        error = mixed_s[own, :]
        active, slope = active_in[own, :], slope_in[own, :]
        gone = f[own, :]
        full = h[own, :] + gone * state[...]
        here = error * active
        state_grad[own, :] = here
        low = (error * full * slope).astype(LOW)
        y_grad[own, :] = low
        return back + fold(here * gone), bias + fold(low.astype(WIDE))

    zero = jnp.zeros(back_sum.shape, WIDE)
    back, bias = loop(middle.shape[0] // STEP, 4, turn, (zero, zero))
    back_sum[...] += back
    bias_sum[...] += bias


def middle_back(middle, grad, cot, gain, weight, active, slope, h, f, state):
    length, model = middle.shape
    total = active.shape[1]
    tile = 256 if length % 256 == 0 else length
    row = lambda lanes: pl.BlockSpec((tile, lanes), lambda step: (step, 0))
    one = lambda lines, lanes: pl.BlockSpec((lines, lanes), lambda step: (0, 0))
    return pl.pallas_call(
        middle_back_kernel,
        grid=(length // tile,),
        in_specs=[
            row(model), row(model), row(model), one(1, model),
            one(total, model), row(total), row(total), row(total), row(total), one(1, total),
        ],
        out_specs=[
            row(model), row(model), row(total), row(total), one(8, model), one(8, total),
            one(8, total),
        ],
        out_shape=[
            jax.ShapeDtypeStruct((length, model), WIDE),
            jax.ShapeDtypeStruct((length, model), LOW),
            jax.ShapeDtypeStruct((length, total), WIDE),
            jax.ShapeDtypeStruct((length, total), LOW),
            jax.ShapeDtypeStruct((8, model), WIDE),
            jax.ShapeDtypeStruct((8, total), WIDE),
            jax.ShapeDtypeStruct((8, total), WIDE),
        ],
        scratch_shapes=[pltpu.VMEM((tile, total), WIDE)],
        compiler_params=params(),
        cost_estimate=cost(13),
        name="middle_back",
    )(middle, grad, cot, gain, weight, active, slope, h, f, state)


def mixer_back_kernel(
    rows, first, place, state_grad, r_in, i_in, conv_in, h, f, u, y_grad, mixed, y_weight, u_weight,
    packed, vec, mask, state, after, normed, mid_low, y_sum, decay_sum, *refs
):
    if not first:
        grad_in, refs = refs[2], refs[3:]
    (
        keep, send, normed_grad, conv_s, low, conv_l, grown, u_low, wide, gate_w, gates, sums,
    ) = refs
    length, width = state_grad.shape
    ext, model = normed.shape
    group = width // rows
    block = width // 2
    count = length // STEP
    line = lax.broadcasted_iota(jnp.int32, (8, width), 0)

    fill_gates(packed, gates, block)

    @pl.when(pl.program_id(0) == 0)
    def _():
        if first:
            normed_grad[...] = jnp.zeros_like(normed_grad)
        else:
            normed_grad[...] = grad_in[...]

    def retreat(index, carry):
        error, rate_sum, into_sum, slope_sum = carry
        base = pl.multiple_of((count - 1 - index) * STEP, STEP)
        own = pl.ds(base, STEP)
        going = mask[pl.ds(base + RIM, STEP), :][:, 0:1]
        rate, into, conv = r_in[own, :], i_in[own, :], conv_in[own, :]
        slope = vec[5:6, :]
        decay = jnp.exp(slope * rate)
        carried = decay * going
        given = state_grad[own, :]
        full = h[own, :] + f[own, :] * state[...]
        ahead = pl.ds(pl.multiple_of(jnp.maximum(base - 8, 0), 8), 8)
        edge = h[ahead, :][7:8] + f[ahead, :][7:8] * state[...]
        edge = jnp.where(base == 0, state[...], edge)
        parts = []
        for part in reversed(range(STEP // 8)):
            place_of = slice(8 * part, 8 * part + 8)
            mul = carried[place_of]
            add = mul * given[place_of]
            for reach in (1, 2, 4):
                inside = line < 8 - reach
                add = add + mul * jnp.where(inside, pltpu.roll(add, 8 - reach, 0), 0.0)
                mul = mul * jnp.where(inside, pltpu.roll(mul, 8 - reach, 0), 1.0)
            here = add + mul * error
            parts.append(given[place_of] + jnp.where(line < 7, pltpu.roll(here, 7, 0), error))
            error = here[0:1]
        grad = jnp.concatenate(parts[::-1], 0)
        befores = []
        for part in range(STEP // 8):
            last = edge if part == 0 else full[8 * part - 1 : 8 * part]
            befores.append(
                jnp.where(line > 0, pltpu.roll(full[8 * part : 8 * part + 8], 1, 0), last)
            )
        before = jnp.concatenate(befores, 0)
        root = lax.rsqrt(1.01 - decay * decay)
        scale = jnp.where(going == 0.0, 1.0, (1.01 - decay * decay) * root)
        through = grad * conv
        into_grad = through * scale
        conv_s[own, :] = grad * into * scale
        decay_grad = going * decay * (grad * before - through * into * decay * root)
        z_rate = decay_grad * slope * rate * (1.0 - rate)
        z_into = into_grad * into * (1.0 - into)
        low[own, 0:width] = z_rate.astype(LOW)
        low[own, width:] = z_into.astype(LOW)
        conv_l[own, :] = conv.astype(LOW)
        return (
            error,
            rate_sum + fold(z_rate),
            into_sum + fold(z_into),
            slope_sum + fold(decay_grad * rate),
        )

    zero = jnp.zeros((8, width), WIDE)
    _, rate_sum, into_sum, slope_sum = loop(
        count, 4, retreat, (after[...], zero, zero, zero)
    )
    conv_s[...] += nt(low[...], gates[...])
    gate_full = tn(conv_l[...], low[...])
    for half in (0, block):
        rows_of = slice(half, half + block)
        gate_w[rows_of, 0:block] = gate_full[rows_of, half : half + block]
        gate_w[rows_of, block:] = gate_full[rows_of, width + half : width + half + block]
    grown[0:RIM, :] = jnp.zeros((RIM, width), WIDE)
    grown[RIM + length :, :] = jnp.zeros((RIM, width), WIDE)

    def taps(index, carry):
        base = pl.multiple_of(index * STEP, STEP)
        window = u[pl.ds(base + 8, STEP + 8), :]
        flags = mask[pl.ds(base + RIM, STEP), :]
        error = conv_s[pl.ds(base, STEP), :] * flags[:, 4:5]
        grown[pl.ds(base + RIM, STEP), :] = error
        out = [carry[0] + fold(error), carry[1] + fold(error * window[8:])]
        for shift in (1, 2, 3):
            moved = window[8 - shift : 8 - shift + STEP]
            out.append(carry[1 + shift] + fold(flags[:, shift : shift + 1] * error * moved))
        return tuple(out)

    bias_sum, *tap_sums = loop(count, 4, taps, (zero,) * 5)

    def spread_back(index, total):
        base = pl.multiple_of(index * STEP, STEP)
        window = grown[pl.ds(base, STEP + 8), :]
        flags = mask[pl.ds(base, STEP + 8), :]
        value = vec[6:7, :] * window[0:STEP]
        for shift in (1, 2, 3):
            masked = flags[:, shift : shift + 1] * window
            value = value + vec[6 + shift : 7 + shift, :] * masked[shift : shift + STEP]
        rounded = value.astype(LOW)
        u_low[pl.ds(base, STEP), :] = rounded
        return total + fold(rounded.astype(WIDE))

    input_sum = loop(ext // STEP, 3, spread_back, zero)
    sums[...] = jnp.zeros_like(sums)
    slope_sum = slope_sum * vec[10:11, :]
    values = (y_sum[...], input_sum, *tap_sums, bias_sum, rate_sum, into_sum, slope_sum, decay_sum[...])
    for row, value in enumerate(values):
        sums[row : row + 1, :] = jnp.sum(value, axis=0, keepdims=True)
    wide[:, 0:128] = jnp.transpose(sums[...])
    spread(place, wide, keep, send, 0, group, rows, slice(3 * model + width, None), 128)
    wide[...] = tn(u_low[...], normed[...])
    spread(place, wide, keep, send, 0, group, rows, slice(0, model))
    spread(place, gate_w, keep, send, 0, group, rows, slice(3 * model, 3 * model + width))
    wide[...] = tn(y_grad[...], normed[RIM:, :])
    spread(place, wide, keep, send, 0, group, rows, slice(model, 2 * model))
    wide[...] = tn(mixed[...], mid_low[...])
    spread(place, wide, keep, send, 0, group, rows, slice(2 * model, 3 * model))
    normed_grad[...] += nn(u_low[...], u_weight[...])
    normed_grad[RIM:, :] += nn(y_grad[...], y_weight[...])


def mixer_back(
    place, state_grad, r, i, conv, h, f, u, y_grad, mixed, y_weight, u_weight, packed, vec, mask,
    state, after, normed, mid_low, y_sum, decay_sum, rows, width, begin, steps, so_far=(),
):
    length, total = state_grad.shape
    ext, model = normed.shape
    group, part = width // rows, rows // 4
    pair = lambda step, place: (step + begin) ^ place[0]
    whole = lambda array: pl.BlockSpec(array.shape, lambda step, place: (0,) * array.ndim)
    lane = lambda lines: pl.BlockSpec((lines, width), lambda step, place: (0, pair(step, place)))
    weight = pl.BlockSpec((width, model), lambda step, place: (pair(step, place), 0))
    units = packed.shape[0] * width // total
    lanes = 3 * model + width + 128
    piece = pl.BlockSpec((group, 1, 2, part, lanes), lambda step, place: (step + begin, 0, 0, 0, 0))
    shape = jax.ShapeDtypeStruct((total // rows, 1, 2, part, lanes), LOW)
    operands = [
        state_grad, r, i, conv, h, f, u, y_grad, mixed, y_weight, u_weight, packed, vec, mask,
        state, after, normed, mid_low, y_sum, decay_sum,
    ]
    kept = pl.BlockSpec(memory_space=pl.ANY)
    return pl.pallas_call(
        functools.partial(mixer_back_kernel, rows, not so_far),
        grid_spec=pltpu.PrefetchScalarGridSpec(
            num_scalar_prefetch=1,
            grid=(steps,),
            in_specs=[
                lane(length), lane(length), lane(length), lane(length), lane(length),
                lane(length), lane(ext), lane(length), lane(length), weight, weight,
                pl.BlockSpec(
                    (units, *packed.shape[1:]), lambda step, place: (pair(step, place), 0, 0)
                ),
                lane(vec.shape[0]), whole(mask), lane(1),
                lane(1), whole(normed), whole(mid_low), lane(8), lane(8),
            ]
            + ([kept, kept, whole(so_far[2])] if so_far else []),
            out_specs=[
                piece, piece, pl.BlockSpec((ext, model), lambda step, place: (0, 0)),
            ],
            scratch_shapes=[
                pltpu.VMEM((length, width), WIDE),
                pltpu.VMEM((length, 2 * width), LOW),
                pltpu.VMEM((length, width), LOW),
                pltpu.VMEM((ext + RIM, width), WIDE),
                pltpu.VMEM((ext, width), LOW),
                pltpu.VMEM((width, model), WIDE),
                pltpu.VMEM((width, width), WIDE),
                pltpu.VMEM((width, 2 * width), LOW),
                pltpu.VMEM((128, width), WIDE),
            ],
        ),
        out_shape=[shape, shape, jax.ShapeDtypeStruct((ext, model), WIDE)],
        input_output_aliases={len(operands) + 1 + k: k for k in range(2)} if so_far else {},
        compiler_params=params(),
        cost_estimate=cost(15 * steps),
        name="mixer_back",
    )(place, *operands, *so_far)


def wide_of(value):
    return value.astype(WIDE)


def pin_kernel(source, target):
    del source, target


class Clock:
    def __init__(self):
        self.time = jnp.zeros((8, 128), WIDE)

    def tick(self, values):
        values, self.time = lax.optimization_barrier((values, self.time))
        return values

    def pin(self):
        self.time = pl.pallas_call(
            pin_kernel,
            in_specs=[pl.BlockSpec(memory_space=pl.ANY)],
            out_specs=pl.BlockSpec(memory_space=pl.ANY),
            out_shape=jax.ShapeDtypeStruct(self.time.shape, WIDE),
            input_output_aliases={0: 0},
            cost_estimate=cost(5000),
            name="pin",
        )(self.time)


class Sums:
    def __init__(self, clock, stages, move=swapped, pin=False, start=True):
        self.clock = clock
        self.stages = stages
        self.move = move
        self.result = self.moving = None
        if start:
            self.begin(pin)

    def begin(self, pin=False):
        self.send(next(self.stages), pin)

    def send(self, transfers, pin):
        meanwhile = transfers.pop() if callable(transfers[-1]) else None
        values = self.clock.tick([transfer[0] for transfer in transfers])
        self.moving = [
            (transfer[3] if len(transfer) > 3 else self.move)(value, *transfer[1:3])
            for value, transfer in zip(values, transfers)
        ]
        if pin:
            self.clock.pin()
        if meanwhile:
            meanwhile()

    def step(self, pin=False):
        try:
            transfers = self.stages.send(self.clock.tick(self.moving))
        except StopIteration as end:
            self.result = end.value
        else:
            self.send(transfers, pin)

    def finish(self):
        while self.result is None:
            self.step()
        return self.result


def lockstep(clock, *groups):
    begun = [group for group in groups if group.moving is not None]
    arrived = clock.tick([group.moving for group in begun])
    transfers = []
    for group in groups:
        if group.moving is None:
            transfers.append(next(group.stages))
        else:
            transfers.append(group.stages.send(arrived[begun.index(group)]))
    values = clock.tick([[transfer[0] for transfer in one] for one in transfers])
    for group, one, own in zip(groups, transfers, values):
        group.moving = [group.move(value, *transfer[1:]) for value, transfer in zip(own, one)]


def halved(clock, keep, send):
    slots, matrices, _, part, lanes = keep.shape
    shape = (slots // 4, 2, 2, matrices, 2, part, lanes)
    keep = keep.reshape(shape)
    (came,) = yield [(send, "rows", 1)]
    came = came.reshape(shape)
    every = slice(None)
    near = {}

    def both(one, other, *where):
        return wide_of(one[where]) + wide_of(other[where])

    def meanwhile():
        one, other = clock.tick((keep, came))
        near["y"] = both(one, other, every, 0, every, every, 0)
        near["x"] = both(one, other, every, 1, 0)
        near.update(clock.tick(dict(near)))

    return (
        yield from owned(
            clock,
            lambda place: near["y"][:, place],
            both(keep, came, every, 0, every, every, 1).astype(LOW),
            lambda place: near["x"][:, :, place],
            both(keep, came, every, 1, 1).astype(LOW),
            meanwhile,
        )
    )


def owned(clock, near_y, far_y, near_x, far_x, meanwhile=None):
    from_y, from_x = yield [(far_y, "rows", 2), (far_x, "chan", 1)] + (
        [meanwhile] if meanwhile else []
    )
    rest = lambda place: wide_of(near_y(place)) + wide_of(from_y[:, place])
    also = lambda place: wide_of(near_x(place)) + wide_of(from_x[:, :, place])
    held = [from_y, from_x]

    def later():
        held[:] = clock.tick(held)

    rest_came, also_came = yield [
        (rest(1).astype(LOW), "chan", 1),
        (also(1).astype(LOW), "rows", 2),
        later,
    ]
    from_y, from_x = held
    rest, also = rest(0), also(0)
    parts = {}
    for index in range(rest.shape[0]):
        parts[2 * index] = rest[index] + wide_of(rest_came[index])
        parts[2 * index + 1] = also[index] + wide_of(also_came[index])
    came = yield [
        (value.astype(LOW), "chan", 2 * distance) for distance, value in parts.items() if distance
    ]
    total = parts[0]
    for value in came:
        total = total + wide_of(value)
    return total


def settled(total):
    total = total.astype(LOW)
    (came,) = yield [(total, "rows", 2)]
    pair = jnp.stack([total, came])
    (came,) = yield [(pair, "rows", 1)]
    return pair, came


def ordered(pair, came):
    four = jnp.stack([pair, came], 1)
    place = lax.axis_index("rows")
    four = jnp.where(place & 1, four[:, ::-1], four)
    four = jnp.where(place & 2, four[::-1], four)
    _, _, matrices, part, lanes = four.shape
    four = four.reshape(4, matrices, part, lanes).transpose(1, 0, 2, 3)
    return four.reshape(matrices, 4 * part, lanes).astype(WIDE)


def finish_rest_kernel(place, pair, came, time, into, gelu, out, decay, gate, lines, held):
    del time
    part, model = pair.shape[2], into.shape[1]
    lanes = decay.shape[1]
    for quarter in range(4):
        turn = quarter ^ place[1]
        own, other = (ref[turn // 2, 0].astype(WIDE) for ref in (pair, came))
        value = jnp.where(turn % 2 == 0, own, other)
        rows = slice(quarter * part, quarter * part + part)
        into[rows, :] = value[:, 0:model]
        gelu[rows, :] = value[:, model : 2 * model]
        out[rows, :] = value[:, 2 * model : 3 * model]
        decay[rows, :] = value[:, 3 * model : 3 * model + lanes]
        gate[rows, :] = value[:, 3 * model + lanes : 3 * model + 2 * lanes]
        held[rows, :] = value[:, 3 * model + 2 * lanes :]
    lines[...] = jnp.transpose(held[...])[:16]


def finish_rest(place, pair, came, time, model, block):
    rows = 4 * pair.shape[2]
    vmem = pl.BlockSpec(memory_space=pltpu.VMEM)
    shape = lambda lanes: jax.ShapeDtypeStruct((rows, lanes), WIDE)
    return pl.pallas_call(
        finish_rest_kernel,
        grid_spec=pltpu.PrefetchScalarGridSpec(
            num_scalar_prefetch=1,
            grid=(1,),
            in_specs=[vmem, vmem, pl.BlockSpec(memory_space=pl.ANY)],
            out_specs=[vmem] * 6,
            scratch_shapes=[pltpu.VMEM((rows, 128), WIDE)],
        ),
        out_shape=[shape(model)] * 3 + [shape(block)] * 2 + [jax.ShapeDtypeStruct((16, rows), WIDE)],
        compiler_params=params(),
        cost_estimate=cost(3),
        name="finish_rest",
    )(place, pair, came, time)


def finish_kernel(place, pair, came, gate, up, down):
    def rows_of(matrix):
        parts = []
        for quarter in range(4):
            turn = quarter ^ place[1]
            own, other = (ref[turn // 2, matrix].astype(WIDE) for ref in (pair, came))
            parts.append(jnp.where(turn % 2 == 0, own, other))
        return jnp.concatenate(parts, 0)

    gate[...] = jnp.transpose(rows_of(0))
    up[...] = jnp.transpose(rows_of(1))
    down[...] = rows_of(2)


def finish(place, pair, came):
    _, _, part, model = pair.shape
    tall = jax.ShapeDtypeStruct((model, 4 * part), WIDE)
    vmem = pl.BlockSpec(memory_space=pltpu.VMEM)
    return pl.pallas_call(
        finish_kernel,
        grid_spec=pltpu.PrefetchScalarGridSpec(
            num_scalar_prefetch=1, grid=(1,), in_specs=[vmem] * 2, out_specs=[vmem] * 3
        ),
        out_shape=[tall, tall, jax.ShapeDtypeStruct((4 * part, model), WIDE)],
        compiler_params=params(),
        cost_estimate=cost(4),
        name="finish",
    )(place, pair, came)


def everywhere(value):
    for axis in ("rows", "chan"):
        bits = 1
        while bits < lax.axis_size(axis):
            (came,) = yield [(value, axis, bits)]
            value = value + came
            bits *= 2
    return value


def gathered(piece):
    parts = lax.axis_size("rows")
    share = piece.shape[0] // parts
    own = lax.dynamic_slice_in_dim(piece, lax.axis_index("rows") * share, share)
    full = lax.all_gather(own, ("chan", "rows"), axis=0, tiled=True)
    return full.reshape(lax.axis_size("chan"), piece.shape[0], piece.shape[1])


def pack_kernel(table, count, *refs):
    sources, outs, sems = refs[:count], refs[count:-1], refs[-1]
    copies = [
        pltpu.make_async_copy(
            sources[source].at[begin : begin + size],
            outs[out].at[at : at + size],
            sems.at[index],
        )
        for index, (out, at, source, begin, size) in enumerate(table)
    ]
    for copy in copies:
        copy.start()
    for copy in copies:
        copy.wait()


def pack(*lists):
    sources, table, shapes = [], [], []
    for out, pieces in enumerate(lists):
        at = 0
        for array, begin, size in pieces:
            known = [index for index, one in enumerate(sources) if one is array]
            if not known:
                known = [len(sources)]
                sources.append(array)
            table.append((out, at, known[0], begin, size))
            at += size
        shapes.append(jax.ShapeDtypeStruct((at, *pieces[0][0].shape[1:]), pieces[0][0].dtype))
    return pl.pallas_call(
        functools.partial(pack_kernel, table, len(sources)),
        in_specs=[pl.BlockSpec(memory_space=pl.ANY)] * len(sources),
        out_specs=[pl.BlockSpec(memory_space=pltpu.VMEM)] * len(shapes),
        scratch_shapes=[pltpu.SemaphoreType.DMA((len(table),))],
        out_shape=shapes,
        compiler_params=params(),
        cost_estimate=cost(0.01),
        name="pack",
    )(*sources)


def spread_units(units):
    pairs = range(2, lax.axis_size("chan") // 2)
    count = len(pairs)
    behind, *came = yield [(units[:2], "chan", 2)] + [
        (units[:1], "chan", 2 * pair) for pair in pairs
    ]
    singles = [(value, 0, 1) for value in came]
    (turned,) = pack([(units, 0, 1), (behind, 0, 2), *singles])
    (corners,) = yield [(turned, "chan", 1)]
    near, away = pack(
        [(behind, 0, 2), (corners, 1, 2)], [(corners, 0, 1), *singles, (corners, 3, count)]
    )
    over, near_too = yield [(away, "rows", 2), (near, "rows", 1)]
    size = 2 * count + 1
    (away,) = pack([(away, 0, size), (over, 0, size)])
    (away_too,) = yield [(away, "rows", 1)]
    return units, near, near_too, away, away_too


def unit_source(pair, side, turn, count):
    upper, other = turn // 2, turn % 2
    if pair == 0 and side == 0:
        return 0, 2 * other + upper
    if pair == 1:
        return 1 + other, 2 * side + upper
    if pair == 0:
        return 3 + other, upper * (2 * count + 1)
    return 3 + other, upper * (2 * count + 1) + 1 + side * count + pair - 2


def assemble_kernel(cuts, pairs, place, *refs):
    sources, outs, sems = refs[:5], refs[5:-1], refs[-1]
    copies = []
    for pair in range(pairs):
        for side in range(2):
            for turn in range(4):
                array, index = unit_source(pair, side, turn, pairs - 2)
                unit = ((2 * pair + side) ^ place[0]) * 4 + (turn ^ place[1])
                for (begin, end), out in zip(cuts, outs):
                    copies.append(
                        pltpu.make_async_copy(
                            sources[array].at[index, begin:end],
                            out.at[unit],
                            sems.at[len(copies)],
                        )
                    )
    for copy in copies:
        copy.start()
    for copy in copies:
        copy.wait()


def assembled(place, sources, cuts):
    pairs = lax.axis_size("chan") // 2
    model = sources[0].shape[2]
    anywhere = pl.BlockSpec(memory_space=pl.ANY)
    return pl.pallas_call(
        functools.partial(assemble_kernel, cuts, pairs),
        grid_spec=pltpu.PrefetchScalarGridSpec(
            num_scalar_prefetch=1,
            grid=(1,),
            in_specs=[anywhere] * 5,
            out_specs=[pl.BlockSpec(memory_space=pltpu.VMEM)] * len(cuts),
            scratch_shapes=[pltpu.SemaphoreType.DMA((8 * pairs * len(cuts),))],
        ),
        out_shape=[
            jax.ShapeDtypeStruct((8 * pairs, end - begin, model), LOW) for begin, end in cuts
        ],
        compiler_params=params(),
        cost_estimate=cost(5),
        name="assemble",
    )(place, *sources)


def local(
    tokens, segments, gelu_weight, gelu_bias, input_weight, input_bias, conv_taps, conv_bias,
    decay_gate, decay_bias, input_gate, ingate_bias, decay_param, out_weight, mixer_gain,
    gate_weight, up_weight, down_weight, feed_gain, cotangent,
):
    length, model = tokens.shape
    rim = conv_taps.shape[0] - 1
    chans = lax.axis_size("chan")
    me, row_place = lax.axis_index("chan"), lax.axis_index("rows")
    rows, block = decay_gate.shape
    total = rows * chans
    width = 2 * block
    group = width // rows

    padded = jnp.concatenate([jnp.full((rim,), -1, jnp.int32), segments])
    window = lax.dynamic_slice_in_dim(padded, me * length, length + rim)
    own = window[rim:]
    same = [own == window[rim - shift : rim - shift + length] for shift in range(1, rim + 1)]
    mask = jnp.stack([same[0], *same, own != 0] + [same[0]] * (7 - rim - 1), 1).astype(WIDE)
    mask = jnp.pad(mask, ((RIM, RIM), (0, 0)))

    small = jnp.concatenate(
        [
            jnp.stack([gelu_bias, input_bias, conv_bias, decay_bias, ingate_bias, decay_param]),
            conv_taps,
        ]
    )
    unit_rows = block // 4
    count = rows // unit_rows
    lines = unit_rows // 2
    place = jnp.stack([me, row_place]).astype(jnp.int32)
    clock = Clock()

    part = gate_weight.shape[1] // 4
    own_columns = lambda weight: lax.dynamic_slice_in_dim(weight, row_place * part, part, 1).T
    own_unit = jnp.stack(
        [
            own_columns(gate_weight),
            own_columns(up_weight),
            lax.dynamic_slice_in_dim(down_weight, row_place * part, part),
        ]
    )
    both = jnp.concatenate([decay_gate, input_gate], 1)
    both = jnp.pad(both, ((0, 0), (0, model // 2 - 2 * block)))
    both = both.reshape(count, 2, lines, model // 2).swapaxes(1, 2).reshape(count, lines, model)
    flat = small.reshape(small.shape[0], count, unit_rows).swapaxes(0, 1).reshape(count, 1, -1)
    flat = jnp.pad(flat, ((0, 0), (0, lines // 3 - 1), (0, model - flat.shape[2])))
    by_unit = lambda weight: weight.reshape(count, unit_rows, model)
    first = jnp.concatenate([by_unit(input_weight.T), both, flat], 1)
    second = jnp.concatenate([by_unit(gelu_weight.T), by_unit(out_weight)], 1)
    first_cuts = ((0, unit_rows), (unit_rows, first.shape[1]))
    second_cuts = ((0, unit_rows), (unit_rows, 2 * unit_rows))
    cot_low = cotangent.astype(LOW)
    rim_tokens = moved_by(tokens[length - rim :], "chan", 1)
    extended = jnp.concatenate([jnp.zeros((RIM - rim, model), WIDE), rim_tokens, tokens])
    if count == 4:
        quarters = lambda units: jnp.stack(
            [
                lax.dynamic_index_in_dim(units, row_place ^ bits, keepdims=False)
                for bits in (0, 2, 1, 3)
            ]
        )
        own_unit = clock.tick(own_unit)
        first = Sums(clock, spread_units(quarters(first)))
        second = Sums(clock, spread_units(quarters(second)), start=False)
        lockstep(clock, first, second)
        normed = clock.tick(rms_norm(clock.tick(extended), mixer_gain).astype(LOW))
        lockstep(clock, first, second)
        lockstep(clock, first, second)
        first.step()
        u_weight, packed = clock.tick(assembled(place, first.result, first_cuts))
    else:
        cut = lambda units, cuts: [
            gathered(units.reshape(-1, model))[:, begin:end] for begin, end in cuts
        ]
        normed = rms_norm(extended, mixer_gain).astype(LOW)
        u_weight, packed = cut(first, first_cuts)
        y_weight, o_weight = cut(second, second_cuts)
        y_weight, o_weight = (w.reshape(total, model) for w in (y_weight, o_weight))
    feed_units = lax.all_gather(own_unit[None], ("chan", "rows"), axis=0, tiled=True)
    u_weight = u_weight.reshape(total, model)
    small_full = packed[:, lines, : small.shape[0] * unit_rows]
    small_full = small_full.reshape(-1, small.shape[0], unit_rows).swapaxes(0, 1)
    small_full = small_full.reshape(small.shape[0], total).astype(WIDE)
    param = small_full[5:6]
    line = lax.broadcasted_iota(jnp.int32, (16, total), 0)
    vec = jnp.pad(small_full, ((0, 6), (0, 0)))
    vec = jnp.where(line == 5, -8.0 * jax.nn.softplus(param), vec)
    vec = jnp.where(line == 10, -8.0 * jax.nn.sigmoid(param), vec)

    u, conv, rate, into, state, factor, decay_sum = clock.tick(
        mixer_forward(normed, u_weight, packed, vec, mask, width)
    )
    carry = Sums(
        clock, entering(jnp.concatenate([factor[-1:], state[-1:]]), "chan", 1), moved_by
    )
    if count == 4:
        second.step()
        carry.step()
        second.step()
        y_weight, o_weight = clock.tick(assembled(place, second.result, second_cuts))
        y_weight, o_weight = (w.reshape(total, model) for w in (y_weight, o_weight))
    active, slope = clock.tick(gelu_branch(normed, y_weight, vec, width))
    carry = clock.tick(carry.finish())
    cot_too = swapped(cot_low, "rows", 1)
    mixed, middle, normed2 = clock.tick(
        mixer_out(active, state, factor, carry, o_weight, tokens, feed_gain[None])
    )
    cot_too = clock.tick(cot_too)
    normed2_too = swapped(normed2, "rows", 1)
    feed_units = clock.tick(feed_units)
    block_output, normed2_grad, mine, send = clock.tick(
        feed(place, normed2, cot_low, middle, feed_units)
    )
    theirs = swapped(send, "rows", 1)

    mid_grad, mid_low, state_grad, y_grad, feed_gain_sum, back_sum, y_sum = clock.tick(
        middle_back(
            middle, normed2_grad, cotangent, feed_gain[None], o_weight, active, slope, state,
            factor, carry,
        )
    )
    after = Sums(
        clock,
        entering(
            jnp.concatenate([factor[-1:], jnp.sum(back_sum, 0, keepdims=True)]), "chan", -1
        ),
        moved_by,
    )
    theirs, normed2_too = clock.tick((theirs, normed2_too))
    operands = (mine, theirs, normed2, cot_low, normed2_too, cot_too)
    near_y, far_y = clock.tick(feed_grads(0, *operands))
    split = lambda value: value.reshape(-1, 2, *value.shape[1:])
    moving = [swapped(split(far_y), "rows", 2)]
    after.step()
    near_x, far_x = clock.tick(feed_grads(1, *operands))
    moving.append(swapped(far_x, "chan", 1))
    stages = owned(
        clock,
        lambda place: split(near_y)[:, place],
        far_y,
        lambda place: near_x[:, :, place],
        far_x,
    )
    next(stages)
    fed = Sums(clock, stages, start=False)
    fed.moving = moving
    after = clock.tick(after.finish())
    place = jnp.stack([me // group, me % group, row_place]).astype(jnp.int32)
    pairs = total // width
    back = lambda after, begin, steps, so_far: clock.tick(
        mixer_back(
            place, state_grad, rate, into, conv, state, factor, u, y_grad, mixed, y_weight, u_weight,
            packed, vec, mask, carry, after, normed, mid_low, y_sum, decay_sum, rows, width, begin, steps, so_far,
        )
    )
    so_far = back(after, 1, pairs - 1, ())
    fed.step()
    so_far = clock.tick(so_far)
    keep, send, normed_grad = back(after, 0, 1, so_far)
    fed.moving = clock.tick(fed.moving)
    rest = Sums(clock, halved(clock, keep, send))
    rim_grad = moved_by(clock.tick(normed_grad[RIM - rim : RIM]), "chan", -1)
    rim_grad = clock.tick(rim_grad)
    error = normed_grad[RIM:] + jnp.concatenate([jnp.zeros((length - rim, model), WIDE), rim_grad])
    scale = lax.rsqrt(jnp.mean(tokens * tokens, axis=-1, keepdims=True) + 1e-06)
    gained = mixer_gain * error
    mean = jnp.mean(gained * tokens, axis=-1, keepdims=True)
    mixer_gain_sum = jnp.sum(error * tokens * scale, 0)

    gains = Sums(clock, everywhere(jnp.stack([mixer_gain_sum, jnp.sum(feed_gain_sum, 0)])))
    gains.step()
    rest.step(pin=True)
    fed.step()
    gains.moving, gained, mean = clock.tick((gains.moving, gained, mean))
    tokens_grad = clock.tick(mid_grad + scale * gained - tokens * (scale * scale * scale * mean))
    rest.step(pin=True)
    rest.step(pin=True)
    gains.step()
    gains.step()
    gains.step()
    fed.step()
    fed = Sums(clock, settled(fed.result))
    fed.step()
    gains = gains.finish()
    rest.step()
    rest = Sums(clock, settled(rest.result))
    fed.step()
    feed_sum = clock.tick(finish(jnp.stack([me, row_place]).astype(jnp.int32), *fed.result))
    pair, came = rest.finish()
    if pair.shape[2] % 8:
        whole = ordered(pair, came)[0]
        gains = gains + clock.time[:1, :1]
        input_sum, gelu_sum, out_sum = (whole[:, k * model : (k + 1) * model] for k in range(3))
        gates_sum = whole[:, 3 * model : 3 * model + width]
        decay_sum, gate_sum = gates_sum[:, :block], gates_sum[:, block:]
        lines = whole[:, 3 * model + width : 3 * model + width + 11].T
    else:
        input_sum, gelu_sum, out_sum, decay_sum, gate_sum, lines = finish_rest(
            jnp.stack([me, row_place]).astype(jnp.int32), pair, came, clock.time, model, block
        )
    mean_decay = lines[10] / (length * lax.axis_size("rows") * chans)
    return (
        block_output,
        tokens_grad,
        gelu_sum.T,
        lines[0],
        input_sum.T,
        lines[1],
        lines[2:6],
        lines[6],
        decay_sum,
        lines[7],
        gate_sum,
        lines[8],
        lines[9],
        out_sum,
        gains[0],
        feed_sum[0],
        feed_sum[1],
        feed_sum[2],
        gains[1],
        mean_decay,
    )


def solution(mesh):
    return jax.shard_map(
        local,
        mesh=mesh,
        in_specs=(
            P(("rows", "chan"), None),
            P("rows"),
            P(None, "chan"),
            P("chan"),
            P(None, "chan"),
            P("chan"),
            P(None, "chan"),
            P("chan"),
            P("chan", None),
            P("chan"),
            P("chan", None),
            P("chan"),
            P("chan"),
            P("chan", None),
            P(),
            P(None, "chan"),
            P(None, "chan"),
            P("chan", None),
            P(),
            P(("rows", "chan"), None),
        ),
        out_specs=(
            P(("rows", "chan"), None),
            P(("rows", "chan"), None),
            P(None, "chan"),
            P("chan"),
            P(None, "chan"),
            P("chan"),
            P(None, "chan"),
            P("chan"),
            P("chan", None),
            P("chan"),
            P("chan", None),
            P("chan"),
            P("chan"),
            P("chan", None),
            P(),
            P(None, "chan"),
            P(None, "chan"),
            P("chan", None),
            P(),
            P("chan"),
        ),
        check_vma=False,
    )
```

```python
import functools

import jax
import jax.numpy as jnp
from jax import lax
from jax.experimental import pallas as pl
from jax.experimental.pallas import tpu as pltpu
from jax.sharding import PartitionSpec as P

LOW = jnp.bfloat16
WIDE = jnp.float32
RIM = 16
STEP = 16
VMEM_BYTES = 56 * 1024 * 1024
GELU_SLOPE = 0.7978845608028654
GELU_CUBE = 0.044715


def params(**more):
    return pltpu.CompilerParams(vmem_limit_bytes=VMEM_BYTES, **more)


def moved_by(value, axis, steps):
    count = lax.axis_size(axis)
    leading, last = (max(0, -steps), min(count, count - steps))
    return lax.ppermute(value, axis, [(source, source + steps) for source in range(leading, last)])


def swapped(value, axis, bits):
    count = lax.axis_size(axis)
    return lax.ppermute(value, axis, [(source, source ^ bits) for source in range(count)])


def join(earlier, later):
    return jnp.concatenate(
        [earlier[0:1] * later[0:1], later[0:1] * earlier[1:2] + later[1:2]], 0
    )


def entering(value, axis, sign):
    count = lax.axis_size(axis)
    if count in (4, 8):
        (partner,) = yield [(value, axis, 1, swapped)]
        later = (lax.axis_index(axis) & 1) == (1 if sign > 0 else 0)
        both = join(jnp.where(later, partner, value), jnp.where(later, value, partner))
        came = yield [(both, axis, 2 * sign * reach) for reach in range(1, count // 2)]
        total = came[-1]
        for one in came[-2::-1]:
            total = join(total, one)
        return jnp.where(later, join(total, partner)[1:2], total[1:2])
    total = value
    came = yield [(value, axis, sign * reach) for reach in (1, 2, 3) if reach < count]
    for one in came:
        total = join(one, total)
    reach = 4
    while 2 * reach < count:
        (one,) = yield [(total, axis, sign * reach)]
        total = join(one, total)
        reach *= 2
    came = yield [(total, axis, sign * far) for far in (1, reach + 1) if far < count]
    last = came[0]
    for one in came[1:]:
        last = join(one, last)
    return last[1:2]


def rms_norm(values, gain):
    return values * lax.rsqrt(jnp.mean(values * values, axis=-1, keepdims=True) + 1e-06) * gain


def nt(left, right):
    return lax.dot_general(left, right, (((1,), (1,)), ((), ())), preferred_element_type=WIDE)


def tn(left, right):
    return lax.dot_general(left, right, (((0,), (0,)), ((), ())), preferred_element_type=WIDE)


def nn(left, right):
    return lax.dot_general(left, right, (((1,), (0,)), ((), ())), preferred_element_type=WIDE)


def sigmoid(value):
    return 0.5 * jnp.tanh(0.5 * value) + 0.5


def gelu_parts(value):
    square = value * value
    bend = jnp.tanh(GELU_SLOPE * value * (1.0 + GELU_CUBE * square))
    half = 0.5 + 0.5 * bend
    slope = half + 0.5 * GELU_SLOPE * value * (1.0 - bend * bend) * (1.0 + 3.0 * GELU_CUBE * square)
    return value * half, slope


def loop(count, unroll, body, init):
    while count % unroll:
        unroll -= 1

    def several(index, carry):
        for turn in range(unroll):
            carry = body(index * unroll + turn, carry)
        return carry

    return lax.fori_loop(0, count // unroll, several, init)


def cost(microseconds):
    return pl.CostEstimate(
        flops=int(microseconds * 1.1e7), bytes_accessed=int(microseconds * 3.5e4), transcendentals=0
    )


def fold(value):
    total = value[0:8]
    for group in range(1, value.shape[0] // 8):
        total = total + value[8 * group : 8 * group + 8]
    return total


def fill_gates(packed, gates, block):
    width = 2 * block
    lines = packed.shape[1] * 3 // 4

    @pl.when(pl.program_id(0) == 0)
    def _():
        gates[...] = jnp.zeros_like(gates)

    parts = []
    for unit in range(packed.shape[0]):
        value = packed[unit].astype(WIDE)[:lines]
        parts += [value[:, 0:width], value[:, 512 : 512 + width]]
    parts = jnp.concatenate(parts, 0).astype(LOW)
    for half in (0, block):
        gates[half : half + block, half : half + block] = parts[half : half + block, 0:block]
        gates[half : half + block, width + half : width + half + block] = parts[
            half : half + block, block:
        ]


def mixer_forward_kernel(
    normed, u_weight, packed, vec, mask, u_out, conv_out, r_out, i_out, h_out, f_out, sum_out,
    low, zed, gates,
):
    ext = normed.shape[0]
    width = u_out.shape[1]
    fill_gates(packed, gates, width // 2)
    count = (ext - RIM) // STEP
    u_out[...] = nt(normed[...], u_weight[...]) + vec[1:2, :]

    def convolve(index, _):
        base = pl.multiple_of(index * STEP, STEP)
        own = pl.ds(base, STEP)
        window = u_out[pl.ds(base + 8, STEP + 8), :]
        flags = mask[pl.ds(base + RIM, STEP), :]
        conv = vec[2:3, :] + vec[6:7, :] * window[8:]
        for shift in (1, 2, 3):
            conv = conv + flags[:, shift : shift + 1] * (
                vec[6 + shift : 7 + shift, :] * window[8 - shift : 8 - shift + STEP]
            )
        conv = conv * flags[:, 4:5]
        conv_out[own, :] = conv
        low[own, :] = conv.astype(LOW)
        return 0

    loop(count, 4, convolve, 0)
    zed[...] = nn(low[...], gates[...])
    line = lax.broadcasted_iota(jnp.int32, (8, width), 0)

    def advance(index, carry):
        state, factor, total = carry
        own = pl.ds(pl.multiple_of(index * STEP, STEP), STEP)
        going = mask[pl.ds(pl.multiple_of(index * STEP + RIM, STEP), STEP), :][:, 0:1]
        rate = sigmoid(zed[own, 0:width] + vec[3:4, :])
        into = sigmoid(zed[own, width:] + vec[4:5, :])
        decay = jnp.exp(vec[5:6, :] * rate)
        r_out[own, :] = rate
        i_out[own, :] = into
        scale = jnp.where(going == 0.0, 1.0, jnp.sqrt(1.01 - decay * decay))
        inject = conv_out[own, :] * into * scale
        carried = decay * going
        total = total + fold(decay)
        for group in range(STEP // 8):
            part = slice(8 * group, 8 * group + 8)
            mul, add = carried[part], inject[part]
            for reach in (1, 2, 4):
                inside = line >= reach
                add = add + mul * jnp.where(inside, pltpu.roll(add, reach, 0), 0.0)
                mul = mul * jnp.where(inside, pltpu.roll(mul, reach, 0), 1.0)
            here = add + mul * state
            gone = mul * factor
            rows = pl.ds(pl.multiple_of(index * STEP + 8 * group, 8), 8)
            h_out[rows, :] = here
            f_out[rows, :] = gone
            state, factor = here[7:8], gone[7:8]
        return state, factor, total

    zero = jnp.zeros((1, width), WIDE)
    _, _, total = loop(
        count, 4, advance, (zero, zero + 1.0, jnp.zeros((8, width), WIDE))
    )
    sum_out[...] = total


def mixer_forward(normed, u_weight, packed, vec, mask, width):
    ext, model = normed.shape
    tokens = ext - RIM
    total = u_weight.shape[0]
    pairs = total // width
    units = packed.shape[0] // pairs
    by_lane = lambda length: pl.BlockSpec((length, width), lambda step: (0, step))
    whole = lambda array: pl.BlockSpec(array.shape, lambda step: (0,) * array.ndim)
    flat = jax.ShapeDtypeStruct((tokens, total), WIDE)
    return pl.pallas_call(
        mixer_forward_kernel,
        grid=(pairs,),
        in_specs=[
            whole(normed),
            pl.BlockSpec((width, model), lambda step: (step, 0)),
            pl.BlockSpec((units, *packed.shape[1:]), lambda step: (step, 0, 0)),
            by_lane(vec.shape[0]),
            whole(mask),
        ],
        out_specs=[by_lane(ext)] + [by_lane(tokens)] * 5 + [by_lane(8)],
        out_shape=[jax.ShapeDtypeStruct((ext, total), WIDE)] + [flat] * 5
        + [jax.ShapeDtypeStruct((8, total), WIDE)],
        scratch_shapes=[
            pltpu.VMEM((tokens, width), LOW),
            pltpu.VMEM((tokens, 2 * width), WIDE),
            pltpu.VMEM((width, 2 * width), LOW),
        ],
        compiler_params=params(),
        cost_estimate=cost(26),
        name="mixer_forward",
    )(normed, u_weight, packed, vec, mask)


def gelu_branch_kernel(normed, weight, vec, active_out, slope_out, held):
    held[...] = nt(normed[RIM:, :], weight[...]) + vec[0:1, :]

    def act(index, _):
        own = pl.ds(pl.multiple_of(index * STEP, STEP), STEP)
        active_out[own, :], slope_out[own, :] = gelu_parts(held[own, :])
        return 0

    loop(held.shape[0] // STEP, 4, act, 0)


def gelu_branch(normed, weight, vec, width):
    length, total = normed.shape[0] - RIM, weight.shape[0]
    model = normed.shape[1]
    lane = lambda lines: pl.BlockSpec((lines, width), lambda step: (0, step))
    return pl.pallas_call(
        gelu_branch_kernel,
        grid=(total // width,),
        in_specs=[
            pl.BlockSpec(normed.shape, lambda step: (0, 0)),
            pl.BlockSpec((width, model), lambda step: (step, 0)),
            lane(vec.shape[0]),
        ],
        out_specs=[lane(length), lane(length)],
        out_shape=[jax.ShapeDtypeStruct((length, total), WIDE)] * 2,
        scratch_shapes=[pltpu.VMEM((length, width), WIDE)],
        compiler_params=params(),
        cost_estimate=cost(8),
        name="gelu_branch",
    )(normed, weight, vec)


def mixer_out_kernel(active, h, f, state, weight, tokens, gain, mixed, middle, normed):
    def gate(index, _):
        own = pl.ds(pl.multiple_of(index * STEP, STEP), STEP)
        mixed[own, :] = ((h[own, :] + f[own, :] * state[...]) * active[own, :]).astype(LOW)
        return 0

    loop(active.shape[0] // STEP, 4, gate, 0)
    total = tokens[...] + nn(mixed[...], weight[...])
    middle[...] = total
    scale = lax.rsqrt(jnp.mean(total * total, axis=-1, keepdims=True) + 1e-06)
    normed[...] = (total * scale * gain[...]).astype(LOW)


def mixer_out(active, h, f, state, weight, tokens, gain):
    length, model = tokens.shape
    total = active.shape[1]
    tile = 256 if length % 256 == 0 else length
    row = lambda lanes: pl.BlockSpec((tile, lanes), lambda step: (step, 0))
    one = lambda array: pl.BlockSpec(array.shape, lambda step: (0, 0))
    return pl.pallas_call(
        mixer_out_kernel,
        grid=(length // tile,),
        in_specs=[
            row(total), row(total), row(total), one(state), one(weight), row(model), one(gain),
        ],
        out_specs=[row(total), row(model), row(model)],
        out_shape=[
            jax.ShapeDtypeStruct((length, total), LOW),
            jax.ShapeDtypeStruct((length, model), WIDE),
            jax.ShapeDtypeStruct((length, model), LOW),
        ],
        compiler_params=params(),
        cost_estimate=cost(9),
        name="mixer_out",
    )(active, h, f, state, weight, tokens, gain)


def spread(place, wide, keep, send, matrix, group, rows, lanes=slice(None), count=None):
    part = rows // 4
    if part % 8:
        value = wide[:, 0:count]
        pieces = [value[begin : begin + part] for begin in range(0, group * rows, part)]
        mine = place[1] * 4 + place[2]
        bit = 1
        while bit < len(pieces):
            turned = (mine & bit) != 0
            pieces = [
                jnp.where(turned, pieces[index ^ bit], pieces[index])
                for index in range(len(pieces))
            ]
            bit *= 2
    for slot in range(group):
        shard = slot ^ place[1]
        for turn in range(4):
            if part % 8:
                value = pieces[4 * slot + turn]
            else:
                begin = pl.multiple_of(shard * rows + (turn ^ place[2]) * part, 8)
                value = wide[pl.ds(begin, part), 0:count]
            (keep, send)[turn & 1][slot, matrix, turn >> 1, :, lanes] = value.astype(LOW)


def feed_kernel(
    group, place, normed, cot, out_in, units, out, grad, keep, send, gate_s, up_s, back_s, hidden_l,
    both_l, held, sems, turned, cot_turned,
):
    model = normed.shape[1]
    width = gate_s.shape[0]
    rows = width // group
    part, half = rows // 4, rows // 2
    step = pl.program_id(0)

    def copies(index):
        for member in range(group):
            for turn in range(4):
                unit = (place[0] ^ (group * index + member)) * 4 + (place[1] ^ turn)
                order = 4 * member + (turn % 2) * 2 + turn // 2
                slot = index % 2
                yield pltpu.make_async_copy(
                    units.at[unit], held.at[slot, :, order], sems.at[slot, 4 * member + turn]
                )

    @pl.when(step == 0)
    def _():
        for copy in copies(0):
            copy.start()
        out[...] = out_in[...]
        grad[...] = jnp.zeros_like(grad)
        turned[...] = jnp.transpose(normed[...])
        cot_turned[...] = jnp.transpose(cot[...])

    @pl.when(step + 1 < pl.num_programs(0))
    def _():
        for copy in copies(step + 1):
            copy.start()

    for copy in copies(step):
        copy.wait()

    def weight(begin, end):
        if part % 16 == 0:
            return held[step % 2, begin:end].reshape((end - begin) * width, model)
        pieces = [
            held[step % 2, matrix, order].astype(WIDE)
            for matrix in range(begin, end)
            for order in range(4 * group)
        ]
        return jnp.concatenate(pieces, 0).astype(LOW)

    first, third = weight(0, 2), weight(2, 3)
    gate_s[...] = nn(first[:width], turned[...])
    up_s[...] = nn(first[width:], turned[...])
    back_s[...] = nn(third, cot_turned[...])

    def act(index, _):
        base = pl.multiple_of(index * STEP, STEP)
        own = pl.ds(base, STEP)
        up, back = up_s[own, :], back_s[own, :]
        value, slope = gelu_parts(gate_s[own, :])
        hidden_l[own, :] = (value * up).astype(LOW)
        both_l[own, :] = (back * up * slope).astype(LOW)
        both_l[pl.ds(base + width, STEP), :] = (back * value).astype(LOW)
        return 0

    loop(width // STEP, 4, act, 0)
    out[...] += tn(hidden_l[...], third)
    grad[...] += tn(both_l[...], first)
    for member in range(group):
        for matrix, (value, offset) in enumerate(((both_l, 0), (both_l, width), (hidden_l, 0))):
            begin = offset + member * rows
            keep[member, matrix] = value[begin : begin + half, :]
            send[member, matrix] = value[begin + half : begin + rows, :]


def feed(place, normed, cot, out_in, units):
    length, model = normed.shape
    part = units.shape[2]
    slots = units.shape[0] // 4
    group = 2
    width = 4 * part * group
    whole = lambda array: pl.BlockSpec(array.shape, lambda step, place: (0,) * array.ndim)
    piece = pl.BlockSpec((group, 3, 2 * part, length), lambda step, place: (step, 0, 0, 0))
    wide = jax.ShapeDtypeStruct((length, model), WIDE)
    grads = jax.ShapeDtypeStruct((slots, 3, 2 * part, length), LOW)
    return pl.pallas_call(
        functools.partial(feed_kernel, group),
        grid_spec=pltpu.PrefetchScalarGridSpec(
            num_scalar_prefetch=1,
            grid=(slots // group,),
            in_specs=[
                whole(normed), whole(cot), whole(out_in), pl.BlockSpec(memory_space=pl.ANY),
            ],
            out_specs=[whole(out_in), whole(out_in), piece, piece],
            scratch_shapes=[pltpu.VMEM((width, length), WIDE)] * 3
            + [pltpu.VMEM((width, length), LOW), pltpu.VMEM((2 * width, length), LOW)]
            + [pltpu.VMEM((2, 3, 4 * group, part, model), LOW)]
            + [pltpu.SemaphoreType.DMA((2, 4 * group))]
            + [pltpu.VMEM((model, length), LOW)] * 2,
        ),
        out_shape=[wide, wide, grads, grads],
        compiler_params=params(),
        cost_estimate=cost(34),
        name="feed",
    )(place, normed, cot, out_in, units)


def feed_grads_kernel(parity, count, mine, theirs, normed, cot, normed_too, cot_too, near, far):
    part = mine.shape[2] // 2
    step = pl.program_id(0)
    for matrix in range(3):
        right, right_too = (cot, cot_too) if matrix == 2 else (normed, normed_too)
        value = nn(mine[0, matrix], right[...]) + nn(theirs[0, matrix], right_too[...])
        value = value.astype(LOW)
        if parity == 0:
            near[0, matrix] = value[:part]
            far[0, matrix] = value[part:]
            continue
        for place, out in ((0, near), (count // 2, far)):

            @pl.when((step >= place) & (step < place + count // 2))
            def _():
                out[0, matrix, 0] = value[:part]
                out[0, matrix, 1] = value[part:]


def feed_grads(parity, mine, theirs, normed, cot, normed_too, cot_too):
    slots, _, rows, length = mine.shape
    model = normed.shape[1]
    count, part = slots // 2, rows // 2
    whole = lambda array: pl.BlockSpec(array.shape, lambda step: (0,) * array.ndim)

    def source(step):
        if parity == 0:
            return 4 * (step // 2) + step % 2, 0, 0, 0
        last = (step >= count // 2).astype(jnp.int32)
        return 4 * (step - last * (count // 2)) + 2 + last, 0, 0, 0

    if parity == 0:
        specs = [pl.BlockSpec((1, 3, part, model), lambda step: (step, 0, 0, 0))] * 2
        shape = jax.ShapeDtypeStruct((count, 3, part, model), LOW)
    else:
        clipped = lambda first: lambda step: (jnp.clip(step - first, 0, count // 2 - 1), 0, 0, 0, 0)
        specs = [
            pl.BlockSpec((1, 3, 2, part, model), clipped(first)) for first in (0, count // 2)
        ]
        shape = jax.ShapeDtypeStruct((count // 2, 3, 2, part, model), LOW)
    return pl.pallas_call(
        functools.partial(feed_grads_kernel, parity, count),
        grid=(count,),
        in_specs=[pl.BlockSpec((1, 3, rows, length), source)] * 2 + [whole(normed)] * 4,
        out_specs=specs,
        out_shape=[shape, shape],
        compiler_params=params(),
        cost_estimate=cost(2000),
        name="feed_grads",
    )(mine, theirs, normed, cot, normed_too, cot_too)


def middle_back_kernel(
    middle, grad, cot, gain, weight, active_in, slope_in, h, f, state, mid_grad, mid_low, state_grad, y_grad,
    gain_sum, back_sum, bias_sum, mixed_s,
):
    @pl.when(pl.program_id(0) == 0)
    def _():
        gain_sum[...] = jnp.zeros_like(gain_sum)
        back_sum[...] = jnp.zeros_like(back_sum)
        bias_sum[...] = jnp.zeros_like(bias_sum)

    value, error = middle[...], grad[...]
    scale = lax.rsqrt(jnp.mean(value * value, axis=-1, keepdims=True) + 1e-06)
    gained = gain[...] * error
    mean = jnp.mean(gained * value, axis=-1, keepdims=True)
    total = cot[...] + scale * gained - value * (scale * scale * scale * mean)
    gain_sum[...] += fold(error * value * scale)
    mid_grad[...] = total
    mid_low[...] = total.astype(LOW)
    mixed_s[...] = nt(mid_low[...], weight[...])

    def turn(index, carry):
        back, bias = carry
        own = pl.ds(pl.multiple_of(index * STEP, STEP), STEP)
        error = mixed_s[own, :]
        active, slope = active_in[own, :], slope_in[own, :]
        gone = f[own, :]
        full = h[own, :] + gone * state[...]
        here = error * active
        state_grad[own, :] = here
        low = (error * full * slope).astype(LOW)
        y_grad[own, :] = low
        return back + fold(here * gone), bias + fold(low.astype(WIDE))

    zero = jnp.zeros(back_sum.shape, WIDE)
    back, bias = loop(middle.shape[0] // STEP, 4, turn, (zero, zero))
    back_sum[...] += back
    bias_sum[...] += bias


def middle_back(middle, grad, cot, gain, weight, active, slope, h, f, state):
    length, model = middle.shape
    total = active.shape[1]
    tile = 256 if length % 256 == 0 else length
    row = lambda lanes: pl.BlockSpec((tile, lanes), lambda step: (step, 0))
    one = lambda lines, lanes: pl.BlockSpec((lines, lanes), lambda step: (0, 0))
    return pl.pallas_call(
        middle_back_kernel,
        grid=(length // tile,),
        in_specs=[
            row(model), row(model), row(model), one(1, model),
            one(total, model), row(total), row(total), row(total), row(total), one(1, total),
        ],
        out_specs=[
            row(model), row(model), row(total), row(total), one(8, model), one(8, total),
            one(8, total),
        ],
        out_shape=[
            jax.ShapeDtypeStruct((length, model), WIDE),
            jax.ShapeDtypeStruct((length, model), LOW),
            jax.ShapeDtypeStruct((length, total), WIDE),
            jax.ShapeDtypeStruct((length, total), LOW),
            jax.ShapeDtypeStruct((8, model), WIDE),
            jax.ShapeDtypeStruct((8, total), WIDE),
            jax.ShapeDtypeStruct((8, total), WIDE),
        ],
        scratch_shapes=[pltpu.VMEM((tile, total), WIDE)],
        compiler_params=params(),
        cost_estimate=cost(13),
        name="middle_back",
    )(middle, grad, cot, gain, weight, active, slope, h, f, state)


def mixer_back_kernel(
    rows, first, place, state_grad, r_in, i_in, conv_in, h, f, u, y_grad, mixed, y_weight, u_weight,
    packed, vec, mask, state, after, normed, mid_low, y_sum, decay_sum, *refs
):
    if not first:
        grad_in, refs = refs[2], refs[3:]
    (
        keep, send, normed_grad, conv_s, low, conv_l, grown, u_low, wide, gate_w, gates, sums,
    ) = refs
    length, width = state_grad.shape
    ext, model = normed.shape
    group = width // rows
    block = width // 2
    count = length // STEP
    line = lax.broadcasted_iota(jnp.int32, (8, width), 0)

    fill_gates(packed, gates, block)

    @pl.when(pl.program_id(0) == 0)
    def _():
        if first:
            normed_grad[...] = jnp.zeros_like(normed_grad)
        else:
            normed_grad[...] = grad_in[...]

    def retreat(index, carry):
        error, rate_sum, into_sum, slope_sum = carry
        base = pl.multiple_of((count - 1 - index) * STEP, STEP)
        own = pl.ds(base, STEP)
        going = mask[pl.ds(base + RIM, STEP), :][:, 0:1]
        rate, into, conv = r_in[own, :], i_in[own, :], conv_in[own, :]
        slope = vec[5:6, :]
        decay = jnp.exp(slope * rate)
        carried = decay * going
        given = state_grad[own, :]
        full = h[own, :] + f[own, :] * state[...]
        ahead = pl.ds(pl.multiple_of(jnp.maximum(base - 8, 0), 8), 8)
        edge = h[ahead, :][7:8] + f[ahead, :][7:8] * state[...]
        edge = jnp.where(base == 0, state[...], edge)
        parts = []
        for part in reversed(range(STEP // 8)):
            place_of = slice(8 * part, 8 * part + 8)
            mul = carried[place_of]
            add = mul * given[place_of]
            for reach in (1, 2, 4):
                inside = line < 8 - reach
                add = add + mul * jnp.where(inside, pltpu.roll(add, 8 - reach, 0), 0.0)
                mul = mul * jnp.where(inside, pltpu.roll(mul, 8 - reach, 0), 1.0)
            here = add + mul * error
            parts.append(given[place_of] + jnp.where(line < 7, pltpu.roll(here, 7, 0), error))
            error = here[0:1]
        grad = jnp.concatenate(parts[::-1], 0)
        befores = []
        for part in range(STEP // 8):
            last = edge if part == 0 else full[8 * part - 1 : 8 * part]
            befores.append(
                jnp.where(line > 0, pltpu.roll(full[8 * part : 8 * part + 8], 1, 0), last)
            )
        before = jnp.concatenate(befores, 0)
        root = lax.rsqrt(1.01 - decay * decay)
        scale = jnp.where(going == 0.0, 1.0, (1.01 - decay * decay) * root)
        through = grad * conv
        into_grad = through * scale
        conv_s[own, :] = grad * into * scale
        decay_grad = going * decay * (grad * before - through * into * decay * root)
        z_rate = decay_grad * slope * rate * (1.0 - rate)
        z_into = into_grad * into * (1.0 - into)
        low[own, 0:width] = z_rate.astype(LOW)
        low[own, width:] = z_into.astype(LOW)
        conv_l[own, :] = conv.astype(LOW)
        return (
            error,
            rate_sum + fold(z_rate),
            into_sum + fold(z_into),
            slope_sum + fold(decay_grad * rate),
        )

    zero = jnp.zeros((8, width), WIDE)
    _, rate_sum, into_sum, slope_sum = loop(
        count, 4, retreat, (after[...], zero, zero, zero)
    )
    conv_s[...] += nt(low[...], gates[...])
    gate_full = tn(conv_l[...], low[...])
    for half in (0, block):
        rows_of = slice(half, half + block)
        gate_w[rows_of, 0:block] = gate_full[rows_of, half : half + block]
        gate_w[rows_of, block:] = gate_full[rows_of, width + half : width + half + block]
    grown[0:RIM, :] = jnp.zeros((RIM, width), WIDE)
    grown[RIM + length :, :] = jnp.zeros((RIM, width), WIDE)

    def taps(index, carry):
        base = pl.multiple_of(index * STEP, STEP)
        window = u[pl.ds(base + 8, STEP + 8), :]
        flags = mask[pl.ds(base + RIM, STEP), :]
        error = conv_s[pl.ds(base, STEP), :] * flags[:, 4:5]
        grown[pl.ds(base + RIM, STEP), :] = error
        out = [carry[0] + fold(error), carry[1] + fold(error * window[8:])]
        for shift in (1, 2, 3):
            moved = window[8 - shift : 8 - shift + STEP]
            out.append(carry[1 + shift] + fold(flags[:, shift : shift + 1] * error * moved))
        return tuple(out)

    bias_sum, *tap_sums = loop(count, 4, taps, (zero,) * 5)

    def spread_back(index, total):
        base = pl.multiple_of(index * STEP, STEP)
        window = grown[pl.ds(base, STEP + 8), :]
        flags = mask[pl.ds(base, STEP + 8), :]
        value = vec[6:7, :] * window[0:STEP]
        for shift in (1, 2, 3):
            masked = flags[:, shift : shift + 1] * window
            value = value + vec[6 + shift : 7 + shift, :] * masked[shift : shift + STEP]
        rounded = value.astype(LOW)
        u_low[pl.ds(base, STEP), :] = rounded
        return total + fold(rounded.astype(WIDE))

    input_sum = loop(ext // STEP, 3, spread_back, zero)
    sums[...] = jnp.zeros_like(sums)
    slope_sum = slope_sum * vec[10:11, :]
    values = (y_sum[...], input_sum, *tap_sums, bias_sum, rate_sum, into_sum, slope_sum, decay_sum[...])
    for row, value in enumerate(values):
        sums[row : row + 1, :] = jnp.sum(value, axis=0, keepdims=True)
    wide[:, 0:128] = jnp.transpose(sums[...])
    spread(place, wide, keep, send, 0, group, rows, slice(3 * model + width, None), 128)
    wide[...] = tn(u_low[...], normed[...])
    spread(place, wide, keep, send, 0, group, rows, slice(0, model))
    spread(place, gate_w, keep, send, 0, group, rows, slice(3 * model, 3 * model + width))
    wide[...] = tn(y_grad[...], normed[RIM:, :])
    spread(place, wide, keep, send, 0, group, rows, slice(model, 2 * model))
    wide[...] = tn(mixed[...], mid_low[...])
    spread(place, wide, keep, send, 0, group, rows, slice(2 * model, 3 * model))
    normed_grad[...] += nn(u_low[...], u_weight[...])
    normed_grad[RIM:, :] += nn(y_grad[...], y_weight[...])


def mixer_back(
    place, state_grad, r, i, conv, h, f, u, y_grad, mixed, y_weight, u_weight, packed, vec, mask,
    state, after, normed, mid_low, y_sum, decay_sum, rows, width, begin, steps, so_far=(),
):
    length, total = state_grad.shape
    ext, model = normed.shape
    group, part = width // rows, rows // 4
    pair = lambda step, place: (step + begin) ^ place[0]
    whole = lambda array: pl.BlockSpec(array.shape, lambda step, place: (0,) * array.ndim)
    lane = lambda lines: pl.BlockSpec((lines, width), lambda step, place: (0, pair(step, place)))
    weight = pl.BlockSpec((width, model), lambda step, place: (pair(step, place), 0))
    units = packed.shape[0] * width // total
    lanes = 3 * model + width + 128
    piece = pl.BlockSpec((group, 1, 2, part, lanes), lambda step, place: (step + begin, 0, 0, 0, 0))
    shape = jax.ShapeDtypeStruct((total // rows, 1, 2, part, lanes), LOW)
    operands = [
        state_grad, r, i, conv, h, f, u, y_grad, mixed, y_weight, u_weight, packed, vec, mask,
        state, after, normed, mid_low, y_sum, decay_sum,
    ]
    kept = pl.BlockSpec(memory_space=pl.ANY)
    return pl.pallas_call(
        functools.partial(mixer_back_kernel, rows, not so_far),
        grid_spec=pltpu.PrefetchScalarGridSpec(
            num_scalar_prefetch=1,
            grid=(steps,),
            in_specs=[
                lane(length), lane(length), lane(length), lane(length), lane(length),
                lane(length), lane(ext), lane(length), lane(length), weight, weight,
                pl.BlockSpec(
                    (units, *packed.shape[1:]), lambda step, place: (pair(step, place), 0, 0)
                ),
                lane(vec.shape[0]), whole(mask), lane(1),
                lane(1), whole(normed), whole(mid_low), lane(8), lane(8),
            ]
            + ([kept, kept, whole(so_far[2])] if so_far else []),
            out_specs=[
                piece, piece, pl.BlockSpec((ext, model), lambda step, place: (0, 0)),
            ],
            scratch_shapes=[
                pltpu.VMEM((length, width), WIDE),
                pltpu.VMEM((length, 2 * width), LOW),
                pltpu.VMEM((length, width), LOW),
                pltpu.VMEM((ext + RIM, width), WIDE),
                pltpu.VMEM((ext, width), LOW),
                pltpu.VMEM((width, model), WIDE),
                pltpu.VMEM((width, width), WIDE),
                pltpu.VMEM((width, 2 * width), LOW),
                pltpu.VMEM((128, width), WIDE),
            ],
        ),
        out_shape=[shape, shape, jax.ShapeDtypeStruct((ext, model), WIDE)],
        input_output_aliases={len(operands) + 1 + k: k for k in range(2)} if so_far else {},
        compiler_params=params(),
        cost_estimate=cost(15 * steps),
        name="mixer_back",
    )(place, *operands, *so_far)


def wide_of(value):
    return value.astype(WIDE)


def pin_kernel(source, target):
    del source, target


class Clock:
    def __init__(self):
        self.time = jnp.zeros((8, 128), WIDE)

    def tick(self, values):
        values, self.time = lax.optimization_barrier((values, self.time))
        return values

    def pin(self):
        self.time = pl.pallas_call(
            pin_kernel,
            in_specs=[pl.BlockSpec(memory_space=pl.ANY)],
            out_specs=pl.BlockSpec(memory_space=pl.ANY),
            out_shape=jax.ShapeDtypeStruct(self.time.shape, WIDE),
            input_output_aliases={0: 0},
            cost_estimate=cost(5000),
            name="pin",
        )(self.time)


class Sums:
    def __init__(self, clock, stages, move=swapped, pin=False, start=True):
        self.clock = clock
        self.stages = stages
        self.move = move
        self.result = self.moving = None
        if start:
            self.begin(pin)

    def begin(self, pin=False):
        self.send(next(self.stages), pin)

    def send(self, transfers, pin):
        meanwhile = transfers.pop() if callable(transfers[-1]) else None
        values = self.clock.tick([transfer[0] for transfer in transfers])
        self.moving = [
            (transfer[3] if len(transfer) > 3 else self.move)(value, *transfer[1:3])
            for value, transfer in zip(values, transfers)
        ]
        if pin:
            self.clock.pin()
        if meanwhile:
            meanwhile()

    def step(self, pin=False):
        try:
            transfers = self.stages.send(self.clock.tick(self.moving))
        except StopIteration as end:
            self.result = end.value
        else:
            self.send(transfers, pin)

    def finish(self):
        while self.result is None:
            self.step()
        return self.result


def lockstep(clock, *groups):
    begun = [group for group in groups if group.moving is not None]
    arrived = clock.tick([group.moving for group in begun])
    transfers = []
    for group in groups:
        if group.moving is None:
            transfers.append(next(group.stages))
        else:
            transfers.append(group.stages.send(arrived[begun.index(group)]))
    values = clock.tick([[transfer[0] for transfer in one] for one in transfers])
    for group, one, own in zip(groups, transfers, values):
        group.moving = [group.move(value, *transfer[1:]) for value, transfer in zip(own, one)]


def halved(clock, keep, send):
    slots, matrices, _, part, lanes = keep.shape
    shape = (slots // 4, 2, 2, matrices, 2, part, lanes)
    keep = keep.reshape(shape)
    (came,) = yield [(send, "rows", 1)]
    came = came.reshape(shape)
    every = slice(None)
    near = {}

    def both(one, other, *where):
        return wide_of(one[where]) + wide_of(other[where])

    def meanwhile():
        one, other = clock.tick((keep, came))
        near["y"] = both(one, other, every, 0, every, every, 0)
        near["x"] = both(one, other, every, 1, 0)
        near.update(clock.tick(dict(near)))

    return (
        yield from owned(
            clock,
            lambda place: near["y"][:, place],
            both(keep, came, every, 0, every, every, 1).astype(LOW),
            lambda place: near["x"][:, :, place],
            both(keep, came, every, 1, 1).astype(LOW),
            meanwhile,
        )
    )


def owned(clock, near_y, far_y, near_x, far_x, meanwhile=None):
    from_y, from_x = yield [(far_y, "rows", 2), (far_x, "chan", 1)] + (
        [meanwhile] if meanwhile else []
    )
    rest = lambda place: wide_of(near_y(place)) + wide_of(from_y[:, place])
    also = lambda place: wide_of(near_x(place)) + wide_of(from_x[:, :, place])
    held = [from_y, from_x]

    def later():
        held[:] = clock.tick(held)

    rest_came, also_came = yield [
        (rest(1).astype(LOW), "chan", 1),
        (also(1).astype(LOW), "rows", 2),
    ] + ([later] if meanwhile else [])
    from_y, from_x = held
    rest, also = rest(0), also(0)
    parts = {}
    for index in range(rest.shape[0]):
        parts[2 * index] = rest[index] + wide_of(rest_came[index])
        parts[2 * index + 1] = also[index] + wide_of(also_came[index])
    came = yield [
        (value.astype(LOW), "chan", 2 * distance) for distance, value in parts.items() if distance
    ]
    total = parts[0]
    for value in came:
        total = total + wide_of(value)
    return total


def settled(total):
    total = total.astype(LOW)
    (came,) = yield [(total, "rows", 2)]
    pair = jnp.stack([total, came])
    (came,) = yield [(pair, "rows", 1)]
    return pair, came


def ordered(pair, came):
    four = jnp.stack([pair, came], 1)
    place = lax.axis_index("rows")
    four = jnp.where(place & 1, four[:, ::-1], four)
    four = jnp.where(place & 2, four[::-1], four)
    _, _, matrices, part, lanes = four.shape
    four = four.reshape(4, matrices, part, lanes).transpose(1, 0, 2, 3)
    return four.reshape(matrices, 4 * part, lanes).astype(WIDE)


def finish_rest_kernel(place, pair, came, time, into, gelu, out, decay, gate, lines, held):
    del time
    part, model = pair.shape[2], into.shape[1]
    lanes = decay.shape[1]
    for quarter in range(4):
        turn = quarter ^ place[1]
        own, other = (ref[turn // 2, 0].astype(WIDE) for ref in (pair, came))
        value = jnp.where(turn % 2 == 0, own, other)
        rows = slice(quarter * part, quarter * part + part)
        into[rows, :] = value[:, 0:model]
        gelu[rows, :] = value[:, model : 2 * model]
        out[rows, :] = value[:, 2 * model : 3 * model]
        decay[rows, :] = value[:, 3 * model : 3 * model + lanes]
        gate[rows, :] = value[:, 3 * model + lanes : 3 * model + 2 * lanes]
        held[rows, :] = value[:, 3 * model + 2 * lanes :]
    lines[...] = jnp.transpose(held[...])[:16]


def finish_rest(place, pair, came, time, model, block):
    rows = 4 * pair.shape[2]
    vmem = pl.BlockSpec(memory_space=pltpu.VMEM)
    shape = lambda lanes: jax.ShapeDtypeStruct((rows, lanes), WIDE)
    return pl.pallas_call(
        finish_rest_kernel,
        grid_spec=pltpu.PrefetchScalarGridSpec(
            num_scalar_prefetch=1,
            grid=(1,),
            in_specs=[vmem, vmem, pl.BlockSpec(memory_space=pl.ANY)],
            out_specs=[vmem] * 6,
            scratch_shapes=[pltpu.VMEM((rows, 128), WIDE)],
        ),
        out_shape=[shape(model)] * 3 + [shape(block)] * 2 + [jax.ShapeDtypeStruct((16, rows), WIDE)],
        compiler_params=params(),
        cost_estimate=cost(3),
        name="finish_rest",
    )(place, pair, came, time)


def finish_kernel(place, pair, came, gate, up, down):
    def rows_of(matrix):
        parts = []
        for quarter in range(4):
            turn = quarter ^ place[1]
            own, other = (ref[turn // 2, matrix].astype(WIDE) for ref in (pair, came))
            parts.append(jnp.where(turn % 2 == 0, own, other))
        return jnp.concatenate(parts, 0)

    gate[...] = jnp.transpose(rows_of(0))
    up[...] = jnp.transpose(rows_of(1))
    down[...] = rows_of(2)


def finish(place, pair, came):
    _, _, part, model = pair.shape
    tall = jax.ShapeDtypeStruct((model, 4 * part), WIDE)
    vmem = pl.BlockSpec(memory_space=pltpu.VMEM)
    return pl.pallas_call(
        finish_kernel,
        grid_spec=pltpu.PrefetchScalarGridSpec(
            num_scalar_prefetch=1, grid=(1,), in_specs=[vmem] * 2, out_specs=[vmem] * 3
        ),
        out_shape=[tall, tall, jax.ShapeDtypeStruct((4 * part, model), WIDE)],
        compiler_params=params(),
        cost_estimate=cost(4),
        name="finish",
    )(place, pair, came)


def everywhere(value):
    for axis in ("rows", "chan"):
        bits = 1
        while bits < lax.axis_size(axis):
            (came,) = yield [(value, axis, bits)]
            value = value + came
            bits *= 2
    return value


def gathered(piece):
    parts = lax.axis_size("rows")
    share = piece.shape[0] // parts
    own = lax.dynamic_slice_in_dim(piece, lax.axis_index("rows") * share, share)
    full = lax.all_gather(own, ("chan", "rows"), axis=0, tiled=True)
    return full.reshape(lax.axis_size("chan"), piece.shape[0], piece.shape[1])


def pack_kernel(table, count, *refs):
    sources, outs, sems = refs[:count], refs[count:-1], refs[-1]
    copies = [
        pltpu.make_async_copy(
            sources[source].at[begin : begin + size],
            outs[out].at[at : at + size],
            sems.at[index],
        )
        for index, (out, at, source, begin, size) in enumerate(table)
    ]
    for copy in copies:
        copy.start()
    for copy in copies:
        copy.wait()


def pack(*lists):
    sources, table, shapes = [], [], []
    for out, pieces in enumerate(lists):
        at = 0
        for array, begin, size in pieces:
            known = [index for index, one in enumerate(sources) if one is array]
            if not known:
                known = [len(sources)]
                sources.append(array)
            table.append((out, at, known[0], begin, size))
            at += size
        shapes.append(jax.ShapeDtypeStruct((at, *pieces[0][0].shape[1:]), pieces[0][0].dtype))
    return pl.pallas_call(
        functools.partial(pack_kernel, table, len(sources)),
        in_specs=[pl.BlockSpec(memory_space=pl.ANY)] * len(sources),
        out_specs=[pl.BlockSpec(memory_space=pltpu.VMEM)] * len(shapes),
        scratch_shapes=[pltpu.SemaphoreType.DMA((len(table),))],
        out_shape=shapes,
        compiler_params=params(),
        cost_estimate=cost(0.01),
        name="pack",
    )(*sources)


def spread_units(units):
    pairs = range(2, lax.axis_size("chan") // 2)
    count = len(pairs)
    behind, *came = yield [(units[:2], "chan", 2)] + [
        (units[:1], "chan", 2 * pair) for pair in pairs
    ]
    singles = [(value, 0, 1) for value in came]
    (turned,) = pack([(units, 0, 1), (behind, 0, 2), *singles])
    (corners,) = yield [(turned, "chan", 1)]
    near, away = pack(
        [(behind, 0, 2), (corners, 1, 2)], [(corners, 0, 1), *singles, (corners, 3, count)]
    )
    over, near_too = yield [(away, "rows", 2), (near, "rows", 1)]
    size = 2 * count + 1
    (away,) = pack([(away, 0, size), (over, 0, size)])
    (away_too,) = yield [(away, "rows", 1)]
    return units, near, near_too, away, away_too


def unit_source(pair, side, turn, count):
    upper, other = turn // 2, turn % 2
    if pair == 0 and side == 0:
        return 0, 2 * other + upper
    if pair == 1:
        return 1 + other, 2 * side + upper
    if pair == 0:
        return 3 + other, upper * (2 * count + 1)
    return 3 + other, upper * (2 * count + 1) + 1 + side * count + pair - 2


def assemble_kernel(cuts, pairs, place, *refs):
    sources, outs, sems = refs[:5], refs[5:-1], refs[-1]
    copies = []
    for pair in range(pairs):
        for side in range(2):
            for turn in range(4):
                array, index = unit_source(pair, side, turn, pairs - 2)
                unit = ((2 * pair + side) ^ place[0]) * 4 + (turn ^ place[1])
                for (begin, end), out in zip(cuts, outs):
                    copies.append(
                        pltpu.make_async_copy(
                            sources[array].at[index, begin:end],
                            out.at[unit],
                            sems.at[len(copies)],
                        )
                    )
    for copy in copies:
        copy.start()
    for copy in copies:
        copy.wait()


def assembled(place, sources, cuts):
    pairs = lax.axis_size("chan") // 2
    model = sources[0].shape[2]
    anywhere = pl.BlockSpec(memory_space=pl.ANY)
    return pl.pallas_call(
        functools.partial(assemble_kernel, cuts, pairs),
        grid_spec=pltpu.PrefetchScalarGridSpec(
            num_scalar_prefetch=1,
            grid=(1,),
            in_specs=[anywhere] * 5,
            out_specs=[pl.BlockSpec(memory_space=pltpu.VMEM)] * len(cuts),
            scratch_shapes=[pltpu.SemaphoreType.DMA((8 * pairs * len(cuts),))],
        ),
        out_shape=[
            jax.ShapeDtypeStruct((8 * pairs, end - begin, model), LOW) for begin, end in cuts
        ],
        compiler_params=params(),
        cost_estimate=cost(5),
        name="assemble",
    )(place, *sources)


def local(
    tokens, segments, gelu_weight, gelu_bias, input_weight, input_bias, conv_taps, conv_bias,
    decay_gate, decay_bias, input_gate, ingate_bias, decay_param, out_weight, mixer_gain,
    gate_weight, up_weight, down_weight, feed_gain, cotangent,
):
    length, model = tokens.shape
    rim = conv_taps.shape[0] - 1
    chans = lax.axis_size("chan")
    me, row_place = lax.axis_index("chan"), lax.axis_index("rows")
    rows, block = decay_gate.shape
    total = rows * chans
    width = 2 * block
    group = width // rows

    padded = jnp.concatenate([jnp.full((rim,), -1, jnp.int32), segments])
    window = lax.dynamic_slice_in_dim(padded, me * length, length + rim)
    own = window[rim:]
    same = [own == window[rim - shift : rim - shift + length] for shift in range(1, rim + 1)]
    mask = jnp.stack([same[0], *same, own != 0] + [same[0]] * (7 - rim - 1), 1).astype(WIDE)
    mask = jnp.pad(mask, ((RIM, RIM), (0, 0)))

    small = jnp.concatenate(
        [
            jnp.stack([gelu_bias, input_bias, conv_bias, decay_bias, ingate_bias, decay_param]),
            conv_taps,
        ]
    )
    unit_rows = block // 4
    count = rows // unit_rows
    lines = unit_rows // 2
    place = jnp.stack([me, row_place]).astype(jnp.int32)
    clock = Clock()

    part = gate_weight.shape[1] // 4
    own_columns = lambda weight: lax.dynamic_slice_in_dim(weight, row_place * part, part, 1).T
    own_unit = jnp.stack(
        [
            own_columns(gate_weight),
            own_columns(up_weight),
            lax.dynamic_slice_in_dim(down_weight, row_place * part, part),
        ]
    )
    both = jnp.concatenate([decay_gate, input_gate], 1)
    both = jnp.pad(both, ((0, 0), (0, model // 2 - 2 * block)))
    both = both.reshape(count, 2, lines, model // 2).swapaxes(1, 2).reshape(count, lines, model)
    flat = small.reshape(small.shape[0], count, unit_rows).swapaxes(0, 1).reshape(count, 1, -1)
    flat = jnp.pad(flat, ((0, 0), (0, lines // 3 - 1), (0, model - flat.shape[2])))
    by_unit = lambda weight: weight.reshape(count, unit_rows, model)
    first = jnp.concatenate([by_unit(input_weight.T), both, flat], 1)
    second = jnp.concatenate([by_unit(gelu_weight.T), by_unit(out_weight)], 1)
    first_cuts = ((0, unit_rows), (unit_rows, first.shape[1]))
    second_cuts = ((0, unit_rows), (unit_rows, 2 * unit_rows))
    cot_low = cotangent.astype(LOW)
    rim_tokens = moved_by(tokens[length - rim :], "chan", 1)
    extended = jnp.concatenate([jnp.zeros((RIM - rim, model), WIDE), rim_tokens, tokens])
    if count == 4:
        quarters = lambda units: jnp.stack(
            [
                lax.dynamic_index_in_dim(units, row_place ^ bits, keepdims=False)
                for bits in (0, 2, 1, 3)
            ]
        )
        own_unit = clock.tick(own_unit)
        first = Sums(clock, spread_units(quarters(first)))
        second = Sums(clock, spread_units(quarters(second)), start=False)
        lockstep(clock, first, second)
        normed = clock.tick(rms_norm(clock.tick(extended), mixer_gain).astype(LOW))
        lockstep(clock, first, second)
        lockstep(clock, first, second)
        first.step()
        u_weight, packed = clock.tick(assembled(place, first.result, first_cuts))
    else:
        cut = lambda units, cuts: [
            gathered(units.reshape(-1, model))[:, begin:end] for begin, end in cuts
        ]
        normed = rms_norm(extended, mixer_gain).astype(LOW)
        u_weight, packed = cut(first, first_cuts)
        y_weight, o_weight = cut(second, second_cuts)
        y_weight, o_weight = (w.reshape(total, model) for w in (y_weight, o_weight))
    feed_units = lax.all_gather(own_unit[None], ("chan", "rows"), axis=0, tiled=True)
    u_weight = u_weight.reshape(total, model)
    small_full = packed[:, lines, : small.shape[0] * unit_rows]
    small_full = small_full.reshape(-1, small.shape[0], unit_rows).swapaxes(0, 1)
    small_full = small_full.reshape(small.shape[0], total).astype(WIDE)
    param = small_full[5:6]
    line = lax.broadcasted_iota(jnp.int32, (16, total), 0)
    vec = jnp.pad(small_full, ((0, 6), (0, 0)))
    vec = jnp.where(line == 5, -8.0 * jax.nn.softplus(param), vec)
    vec = jnp.where(line == 10, -8.0 * jax.nn.sigmoid(param), vec)

    u, conv, rate, into, state, factor, decay_sum = clock.tick(
        mixer_forward(normed, u_weight, packed, vec, mask, width)
    )
    carry = Sums(
        clock, entering(jnp.concatenate([factor[-1:], state[-1:]]), "chan", 1), moved_by
    )
    if count == 4:
        second.step()
        carry.step()
        second.step()
        y_weight, o_weight = clock.tick(assembled(place, second.result, second_cuts))
        y_weight, o_weight = (w.reshape(total, model) for w in (y_weight, o_weight))
    active, slope = clock.tick(gelu_branch(normed, y_weight, vec, width))
    carry = clock.tick(carry.finish())
    cot_too = swapped(cot_low, "rows", 1)
    mixed, middle, normed2 = clock.tick(
        mixer_out(active, state, factor, carry, o_weight, tokens, feed_gain[None])
    )
    cot_too = clock.tick(cot_too)
    normed2_too = swapped(normed2, "rows", 1)
    feed_units = clock.tick(feed_units)
    block_output, normed2_grad, mine, send = clock.tick(
        feed(place, normed2, cot_low, middle, feed_units)
    )
    theirs = swapped(send, "rows", 1)

    mid_grad, mid_low, state_grad, y_grad, feed_gain_sum, back_sum, y_sum = clock.tick(
        middle_back(
            middle, normed2_grad, cotangent, feed_gain[None], o_weight, active, slope, state,
            factor, carry,
        )
    )
    after = Sums(
        clock,
        entering(
            jnp.concatenate([factor[-1:], jnp.sum(back_sum, 0, keepdims=True)]), "chan", -1
        ),
        moved_by,
    )
    theirs, normed2_too = clock.tick((theirs, normed2_too))
    operands = (mine, theirs, normed2, cot_low, normed2_too, cot_too)
    near_y, far_y = clock.tick(feed_grads(0, *operands))
    split = lambda value: value.reshape(-1, 2, *value.shape[1:])
    moving = [swapped(split(far_y), "rows", 2)]
    after.step()
    near_x, far_x = clock.tick(feed_grads(1, *operands))
    moving.append(swapped(far_x, "chan", 1))
    stages = owned(
        clock,
        lambda place: split(near_y)[:, place],
        far_y,
        lambda place: near_x[:, :, place],
        far_x,
    )
    next(stages)
    fed = Sums(clock, stages, start=False)
    fed.moving = moving
    after = clock.tick(after.finish())
    place = jnp.stack([me // group, me % group, row_place]).astype(jnp.int32)
    pairs = total // width
    back = lambda after, begin, steps, so_far: clock.tick(
        mixer_back(
            place, state_grad, rate, into, conv, state, factor, u, y_grad, mixed, y_weight, u_weight,
            packed, vec, mask, carry, after, normed, mid_low, y_sum, decay_sum, rows, width, begin, steps, so_far,
        )
    )
    so_far = back(after, 1, pairs - 1, ())
    fed.step()
    so_far = clock.tick(so_far)
    keep, send, normed_grad = back(after, 0, 1, so_far)
    fed.moving = clock.tick(fed.moving)
    rest = Sums(clock, halved(clock, keep, send))
    rim_grad = moved_by(clock.tick(normed_grad[RIM - rim : RIM]), "chan", -1)
    rim_grad = clock.tick(rim_grad)
    error = normed_grad[RIM:] + jnp.concatenate([jnp.zeros((length - rim, model), WIDE), rim_grad])
    scale = lax.rsqrt(jnp.mean(tokens * tokens, axis=-1, keepdims=True) + 1e-06)
    gained = mixer_gain * error
    mean = jnp.mean(gained * tokens, axis=-1, keepdims=True)
    mixer_gain_sum = jnp.sum(error * tokens * scale, 0)

    gains = Sums(clock, everywhere(jnp.stack([mixer_gain_sum, jnp.sum(feed_gain_sum, 0)])))
    gains.step()
    rest.step(pin=True)
    fed.step()
    gains.moving, gained, mean = clock.tick((gains.moving, gained, mean))
    tokens_grad = clock.tick(mid_grad + scale * gained - tokens * (scale * scale * scale * mean))
    rest.step(pin=True)
    rest.step(pin=True)
    gains.step()
    gains.step()
    gains.step()
    fed.step()
    fed = Sums(clock, settled(fed.result))
    fed.step()
    rest.step()
    rest = Sums(clock, settled(rest.result))
    gains = gains.finish()
    rest.step()
    fed.step()
    feed_sum = clock.tick(finish(jnp.stack([me, row_place]).astype(jnp.int32), *fed.result))
    pair, came = rest.finish()
    if pair.shape[2] % 8:
        whole = ordered(pair, came)[0]
        gains = gains + clock.time[:1, :1]
        input_sum, gelu_sum, out_sum = (whole[:, k * model : (k + 1) * model] for k in range(3))
        gates_sum = whole[:, 3 * model : 3 * model + width]
        decay_sum, gate_sum = gates_sum[:, :block], gates_sum[:, block:]
        lines = whole[:, 3 * model + width : 3 * model + width + 11].T
    else:
        input_sum, gelu_sum, out_sum, decay_sum, gate_sum, lines = finish_rest(
            jnp.stack([me, row_place]).astype(jnp.int32), pair, came, clock.time, model, block
        )
    mean_decay = lines[10] / (length * lax.axis_size("rows") * chans)
    return (
        block_output,
        tokens_grad,
        gelu_sum.T,
        lines[0],
        input_sum.T,
        lines[1],
        lines[2:6],
        lines[6],
        decay_sum,
        lines[7],
        gate_sum,
        lines[8],
        lines[9],
        out_sum,
        gains[0],
        feed_sum[0],
        feed_sum[1],
        feed_sum[2],
        gains[1],
        mean_decay,
    )


def solution(mesh):
    return jax.shard_map(
        local,
        mesh=mesh,
        in_specs=(
            P(("rows", "chan"), None),
            P("rows"),
            P(None, "chan"),
            P("chan"),
            P(None, "chan"),
            P("chan"),
            P(None, "chan"),
            P("chan"),
            P("chan", None),
            P("chan"),
            P("chan", None),
            P("chan"),
            P("chan"),
            P("chan", None),
            P(),
            P(None, "chan"),
            P(None, "chan"),
            P("chan", None),
            P(),
            P(("rows", "chan"), None),
        ),
        out_specs=(
            P(("rows", "chan"), None),
            P(("rows", "chan"), None),
            P(None, "chan"),
            P("chan"),
            P(None, "chan"),
            P("chan"),
            P(None, "chan"),
            P("chan"),
            P("chan", None),
            P("chan"),
            P("chan", None),
            P("chan"),
            P("chan"),
            P("chan", None),
            P(),
            P(None, "chan"),
            P(None, "chan"),
            P("chan", None),
            P(),
            P("chan"),
        ),
        check_vma=False,
    )
```
